32 devices in a mesh: ep: 8 (over z, x), tp: 4 (over y, core).
Axes of the slice: x: 2, y: 2, z: 4, core: 2. Of those that a mesh axis runs over, the one named last changes fastest.
Arguments:
- hidden_in: bfloat16 [4096, 2048], P('ep'), may hold values from -6 to 6
- out_grad: bfloat16 [4096, 2048], P('ep'), may hold values from -6 to 6
- query_weight: bfloat16 [2048, 3072], P('ep', 'tp'), may hold values from -0.125 to 0.125
- latent_weight: bfloat16 [2048, 576], P('ep'), may hold values from -0.125 to 0.125
- expand_weight: bfloat16 [512, 4096], P('ep', 'tp'), may hold values from -0.25 to 0.25
- output_weight: bfloat16 [2048, 2048], P('tp', 'ep'), may hold values from -0.75 to 0.75
- norm_gains: bfloat16 [2, 2048], P(None, 'ep'), may hold values from 0.5 to 1.5
- latent_gain: bfloat16 [512], P('ep'), may hold values from 0.5 to 1.5
- router_weight: bfloat16 [2048, 16], P('ep'), may hold values from -0.0625 to 0.0625
- shared_gate_up: bfloat16 [2, 2048, 2816], P(None, 'ep', 'tp'), may hold values from -0.125 to 0.125
- shared_down: bfloat16 [2816, 2048], P('tp', 'ep'), may hold values from -0.109375 to 0.109375
- expert_gate_up: bfloat16 [16, 2, 2048, 1408], P('ep', None, None, 'tp'), may hold values from -0.125 to 0.125
- expert_down: bfloat16 [16, 1408, 2048], P('ep', 'tp'), may hold values from -0.15625 to 0.15625
- expert_ids: int32 [4096, 6], P('ep'), may hold values from 0 to 15, all different within a row; in each aligned block of 512 rows (0 to 511, 512 to 1023, ...) at most 256 rows name the same one
Outputs:
- block_out: bfloat16 [4096, 2048], P('ep')
- grad_hidden_in: float32 [4096, 2048], P('ep')
- grad_query_weight: float32 [2048, 3072], P('ep', 'tp')
- grad_latent_weight: float32 [2048, 576], P('ep')
- grad_expand_weight: float32 [512, 4096], P('ep', 'tp')
- grad_output_weight: float32 [2048, 2048], P('tp', 'ep')
- grad_norm_gains: float32 [2, 2048], P(None, 'ep')
- grad_latent_gain: float32 [512], P('ep')
- grad_router_weight: float32 [2048, 16], P('ep')
- grad_shared_gate_up: float32 [2, 2048, 2816], P(None, 'ep', 'tp')
- grad_shared_down: float32 [2816, 2048], P('tp', 'ep')
- grad_expert_gate_up: float32 [16, 2, 2048, 1408], P('ep', None, None, 'tp')
- grad_expert_down: float32 [16, 1408, 2048], P('ep', 'tp')
The draws below stay inside these ranges and needn't reach their ends.
Inputs may be any that keep to these rules, and one draw needn't show every extreme that they name: `expert_ids`: each row names 6 different experts; in the rows of one index of ep no expert is named more than 256 times.
All inputs are finite; a program needn't handle non-finite values.
Results may differ from the reference program's by a relative error of at most 0.023.
Values may be sent and summed in bfloat16 or wider, within the bound.
No kernel may reach another device: no remote copies, remote signals or barrier semaphores. Data moves between devices by JAX's collectives and lax.ppermute only.
A program may use at most 320 MiB of HBM per device.

```python
import math
import jax
import jax.numpy as jnp
import numpy as np
from jax import lax

D = 2048
HEADS = 16
NOPE = 128
ROPE = 64
V_DIM = 128
KV_RANK = 512
EXPERT_FF = 1408
TOPK = 6
SEQ_LEN = 512
SHARED_FF = 2816
EXPERTS = 16
TOKENS = 4096
CAP = 256
N_EP = 8
N_TP = 4


def steps_of(stream_key, dims, cuts, least, top_value):
    level, own = 1.0, jax.random.fold_in(stream_key, 6)
    for axis_at, blocks in cuts:
        draws = jnp.exp(jax.random.uniform(jax.random.fold_in(own, axis_at), (blocks,), jnp.float32, least / len(cuts), top_value / len(cuts)))
        level = level * jnp.repeat(draws, dims[axis_at] // blocks).reshape([-1 if axis == axis_at else 1 for axis in range(len(dims))])
    return level


def routed_block(key, own, number, rows, number_of, top, bound, skew):
    order = jax.random.permutation(key, number_of)
    packed, ordinary = load_shares(number_of, rows * top, bound, skew, True), load_shares(number_of, rows * top, bound, skew, False)
    places = jnp.arange(number_of)

    def named(tallies, rotation):
        used = int((tallies > 0).sum())
        fixed = max(1, used // 4)
        passed = fixed + (places - fixed + rotation * (used - fixed)) % max(1, number_of - fixed)
        return jnp.zeros((number_of,), jnp.int32).at[order[jnp.where(places < fixed, places, passed)]].set(jnp.asarray(tallies, jnp.int32))

    tallies = jnp.where(number % 4 == 0, named(packed, number // 4), named(ordinary, number - number // 4 - 1))
    mixed = jax.random.permutation(jax.random.fold_in(own, 3), number_of)
    donor, taker = mixed[0:number_of // 2 * 2:2], mixed[1:number_of // 2 * 2:2]
    slack = jnp.minimum(tallies[donor] - 1, bound - tallies[taker]) // 2
    slack = jnp.where((donor == order[0]) | (taker == order[0]) | (tallies[taker] == 0), 0, jnp.maximum(slack, 0))
    passed = jax.random.randint(jax.random.fold_in(own, 4), (number_of // 2,), 0, 1 << 20) % (slack + 1)
    tallies = tallies.at[donor].add(-passed).at[taker].add(passed)
    items = jnp.searchsorted(jnp.cumsum(tallies), jnp.arange(rows * top), side="right").astype(jnp.int32)
    grid = items.reshape(top, rows).T
    grid = grid[jax.random.permutation(jax.random.fold_in(own, 1), rows)]
    rotation = jax.random.randint(jax.random.fold_in(own, 2), (rows, 1), 0, top)
    return jnp.take_along_axis(grid, (jnp.arange(top)[None, :] + rotation) % top, axis=1)


def load_shares(count, total, most, slope, full):
    weights = [(1 << 20) // math.isqrt(standing ** slope) + 1 for standing in range(1, count + 1)]
    largest = most if full else min(most, max(-(-total // count), total * weights[0] // sum(weights)))
    least = 1 if total - largest >= count - 1 else 0
    given, spare = [largest] + [least] * (count - 1), total - largest - least * (count - 1)
    while spare > 0:
        free = [i for i in range(1, count) if given[i] < largest] or [i for i in range(1, count) if given[i] < most]
        mass, budget = sum([weights[i] for i in free]), spare
        for i in free:
            addition = min(most - given[i], max(1, budget * weights[i] // mass), spare)
            given[i] = given[i] + addition
            spare = spare - addition
    return np.array(given)


def scatter_about(rng, shape, width, reach, shards=(), held_as=jnp.bfloat16):
    loudness = steps_of(rng, shape, shards, -0.22, 0.18) if shards else 1.0
    values = jax.random.normal(rng, shape, jnp.float32) * width * loudness
    return jnp.minimum(jnp.maximum(values, -reach), reach).astype(held_as)


def setup_inputs(seed: int = 0) -> dict:
    seeds = jax.random.split(jax.random.key(seed), 15)
    hidden_in = scatter_about(seeds[0], (TOKENS, D), 1.0, 6.0, ((0, 8),))
    out_grad = scatter_about(seeds[1], (TOKENS, D), 1.0, 6.0, ((0, 8),))
    query_weight = scatter_about(seeds[2], (D, HEADS * (NOPE + ROPE)), D ** -0.5, 0.125, ((0, 8), (1, 4)))
    latent_weight = scatter_about(seeds[3], (D, KV_RANK + ROPE), D ** -0.5, 0.125, ((0, 8),))
    expand_weight = scatter_about(seeds[4], (KV_RANK, HEADS * (NOPE + V_DIM)), KV_RANK ** -0.5, 0.25, ((0, 8), (1, 4)))
    output_weight = scatter_about(seeds[5], (HEADS * V_DIM, D), (HEADS * V_DIM // 32) ** -0.5, 0.75, ((0, 4), (1, 8)))
    norm_gains = jnp.clip(1.0 + 0.1 * jax.random.normal(seeds[6], (2, D), jnp.float32), 0.5, 1.5).astype(jnp.bfloat16)
    latent_gain = jnp.clip(1.0 + 0.1 * jax.random.normal(seeds[7], (KV_RANK,), jnp.float32), 0.5, 1.5).astype(jnp.bfloat16)
    router_weight = scatter_about(seeds[8], (D, EXPERTS), (4 * D) ** -0.5, 0.0625, ((0, 8),))
    shared_gate_up = scatter_about(seeds[9], (2, D, SHARED_FF), D ** -0.5, 0.125, ((1, 8), (2, 4)))
    shared_down = scatter_about(seeds[10], (SHARED_FF, D), SHARED_FF ** -0.5, 0.109375, ((0, 4), (1, 8)))
    expert_gate_up = scatter_about(seeds[11], (EXPERTS, 2, D, EXPERT_FF), D ** -0.5, 0.125, ((0, 8), (3, 4)))
    expert_down = scatter_about(seeds[12], (EXPERTS, EXPERT_FF, D), EXPERT_FF ** -0.5, 0.15625, ((0, 8), (1, 4)))
    expert_ids_keys = jax.random.split(jax.random.fold_in(seeds[13], 1), TOKENS // SEQ_LEN)
    expert_ids_turns = jax.random.permutation(jax.random.fold_in(seeds[13], 3), TOKENS // SEQ_LEN)
    expert_ids = jax.vmap(lambda own, number: routed_block(jax.random.fold_in(seeds[13], 2), own, number, SEQ_LEN, EXPERTS, TOPK, CAP, 2))(expert_ids_keys, expert_ids_turns).reshape((TOKENS, TOPK))
    return {"hidden_in": hidden_in, "out_grad": out_grad, "query_weight": query_weight, "latent_weight": latent_weight, "expand_weight": expand_weight, "output_weight": output_weight, "norm_gains": norm_gains, "latent_gain": latent_gain, "router_weight": router_weight, "shared_gate_up": shared_gate_up, "shared_down": shared_down, "expert_gate_up": expert_gate_up, "expert_down": expert_down, "expert_ids": expert_ids}


EPSILON = 1e-06
ROUTE_SCALE = 2.446
ROPE_BASE = 50000.0
HIGHEST = lax.Precision.HIGHEST

@jax.custom_vjp
def low(v):
    return lax.optimization_barrier(v.astype(jnp.bfloat16)).astype(jnp.float32)

@jax.custom_vjp
def low_back(v):
    return v

def low_keep(v):
    return (low(v), None)

def low_pass(kept, grad):
    return (grad,)

def back_keep(v):
    return (v, None)

def back_low(kept, grad):
    return (low(grad),)
low.defvjp(low_keep, low_pass)
low_back.defvjp(back_keep, back_low)

def matmul_high(left_side, right_side):
    return jnp.dot(left_side, right_side, precision=HIGHEST, preferred_element_type=jnp.float32)

def rms_norm(values, gain_row):
    return values * lax.rsqrt(lax.optimization_barrier(jnp.mean(values * values, axis=-1, keepdims=True)) + EPSILON) * gain_row

def rotate(values, cosine_table, sine_table):
    halfway = values.shape[-1] // 2
    first_half = values[..., :halfway]
    second_half = values[..., halfway:]
    return jnp.concatenate([first_half * cosine_table - second_half * sine_table, second_half * cosine_table + first_half * sine_table], axis=-1)

def rope_tables():
    places = (jnp.arange(TOKENS) % SEQ_LEN).astype(jnp.float32)
    frequency = ROPE_BASE ** (-(jnp.arange(ROPE // 2).astype(jnp.float32) * 2.0 / ROPE))
    angles = places[:, None] * frequency[None, :]
    return (jnp.cos(angles), jnp.sin(angles))

def slot_numbers(expert_ids):
    per_device = expert_ids.reshape(N_EP, SEQ_LEN * TOPK)
    onehot = (per_device[:, :, None] == jnp.arange(EXPERTS)[None, None, :]).astype(jnp.int32)
    running = jnp.cumsum(onehot, axis=1) - onehot
    return lax.optimization_barrier(jnp.sum(running * onehot, axis=2)).reshape(TOKENS, TOPK).astype(jnp.int32)

def forward(hidden_in, query_weight, latent_weight, expand_weight, output_weight, norm_gains, latent_gain, router_weight, shared_gate_up, shared_down, expert_gate_up, expert_down, expert_ids):
    cosine_table, sine_table = rope_tables()
    normed_in = low(rms_norm(hidden_in, norm_gains[0]))
    query_raw = low_back(matmul_high(normed_in, query_weight)).reshape(TOKENS, HEADS, NOPE + ROPE)
    queries = low(jnp.concatenate([query_raw[..., :NOPE], rotate(query_raw[..., NOPE:], cosine_table[:, None, :], sine_table[:, None, :])], axis=-1))
    latent = low_back(matmul_high(normed_in, latent_weight))
    latent_normed = low(rms_norm(latent[:, :KV_RANK], latent_gain))
    key_rope = low(rotate(latent[:, KV_RANK:], cosine_table, sine_table))
    expanded = low(low_back(matmul_high(latent_normed, expand_weight))).reshape(TOKENS, HEADS, NOPE + V_DIM)
    key_rows = jnp.concatenate([expanded[..., :NOPE], jnp.broadcast_to(key_rope[:, None, :], (TOKENS, HEADS, ROPE))], axis=-1)
    values = expanded[..., NOPE:]
    sequences = TOKENS // SEQ_LEN
    query_seq = queries.reshape(sequences, SEQ_LEN, HEADS, NOPE + ROPE)
    key_seq = key_rows.reshape(sequences, SEQ_LEN, HEADS, NOPE + ROPE)
    value_seq = values.reshape(sequences, SEQ_LEN, HEADS, V_DIM)
    scores = jnp.einsum('bqhd,bkhd->bhqk', query_seq, key_seq, precision=HIGHEST) / math.sqrt(NOPE + ROPE)
    scores = low_back(scores)
    causal = jnp.arange(SEQ_LEN)[:, None] >= jnp.arange(SEQ_LEN)[None, :]
    scores = jnp.where(causal[None, None], scores, -1e+30)
    softmax_probs = low(jax.nn.softmax(scores, axis=-1))
    attended = jnp.einsum('bhqk,bkhd->bqhd', softmax_probs, value_seq, precision=HIGHEST)
    attended = low(low_back(attended)).reshape(TOKENS, HEADS * V_DIM)
    resid = hidden_in + low_back(matmul_high(attended, output_weight))
    normed_mid = low(rms_norm(resid, norm_gains[1]))
    logits = low_back(matmul_high(normed_mid, router_weight))
    chosen = jnp.take_along_axis(logits, expert_ids, axis=1)
    sigmoids = jax.nn.sigmoid(chosen)
    gating = ROUTE_SCALE * sigmoids / lax.optimization_barrier(jnp.sum(sigmoids, axis=1, keepdims=True))
    shared_gate = low_back(matmul_high(normed_mid, shared_gate_up[0]))
    shared_upper = low_back(matmul_high(normed_mid, shared_gate_up[1]))
    shared_hidden = low(jax.nn.silu(shared_gate) * shared_upper)
    shared_out = matmul_high(shared_hidden, shared_down)
    slots = slot_numbers(expert_ids)
    owners = (jnp.arange(TOKENS) // SEQ_LEN).astype(jnp.int32)[:, None]
    places = owners * CAP + slots
    token_index = jnp.broadcast_to(jnp.arange(TOKENS, dtype=jnp.int32)[:, None], (TOKENS, TOPK))
    slot_table = jnp.full((EXPERTS, N_EP * CAP), TOKENS, jnp.int32).at[expert_ids, places].set(token_index)
    padded = jnp.concatenate([normed_mid, jnp.zeros((1, D), normed_mid.dtype)], axis=0)
    expert_rows = padded[slot_table]
    block_width = EXPERT_FF // N_TP
    summed = jnp.zeros_like(expert_rows)
    for piece_idx in range(N_TP):
        lower = piece_idx * block_width
        inputs = low_back(expert_rows)
        gate_rows = low_back(jnp.einsum('erd,edf->erf', inputs, expert_gate_up[:, 0, :, lower:lower + block_width], precision=HIGHEST))
        upper = low_back(jnp.einsum('erd,edf->erf', inputs, expert_gate_up[:, 1, :, lower:lower + block_width], precision=HIGHEST))
        hidden = low(jax.nn.silu(gate_rows) * upper)
        summed = summed + low(jnp.einsum('erf,efd->erd', hidden, expert_down[:, lower:lower + block_width, :], precision=HIGHEST))
    expert_result = low_back(summed)
    expert_out = expert_result[expert_ids, places]
    routed = lax.optimization_barrier(jnp.sum(gating[:, :, None] * expert_out, axis=1))
    return resid + shared_out + routed

def reference(hidden_in, out_grad, query_weight, latent_weight, expand_weight, output_weight, norm_gains, latent_gain, router_weight, shared_gate_up, shared_down, expert_gate_up, expert_down, expert_ids):
    floats = tuple((array.astype(jnp.float32) for array in (hidden_in, query_weight, latent_weight, expand_weight, output_weight, norm_gains, latent_gain, router_weight, shared_gate_up, shared_down, expert_gate_up, expert_down)))

    def wrapped(*arrays):
        return forward(*arrays, expert_ids)
    result, pullback = jax.vjp(wrapped, *floats)
    gradients = pullback(out_grad.astype(jnp.float32))
    return (result.astype(jnp.bfloat16), gradients[0], gradients[1], gradients[2], gradients[3], gradients[4], gradients[5], gradients[6], gradients[7], gradients[8], gradients[9], gradients[10], gradients[11])
```

```python
import math

import jax
import jax.numpy as jnp
from jax import lax
from jax.sharding import PartitionSpec as P

NOPE = 128
ROPE = 64
V_DIM = 128
KV_RANK = 512
TOPK = 6
EXP_DEV = 2


EPSILON = 1e-06
ROUTE_SCALE = 2.446
ROPE_BASE = 50000.0


def matmul(left_side, right_side):
    return jnp.dot(left_side, right_side, preferred_element_type=jnp.float32)


def transposed_left(left_side, right_side):
    return lax.dot_general(
        left_side, right_side, (((0,), (0,)), ((), ())), preferred_element_type=jnp.float32
    )


def transposed_right(left_side, right_side):
    return lax.dot_general(
        left_side, right_side, (((1,), (1,)), ((), ())), preferred_element_type=jnp.float32
    )


def rotate(values, cosine_table, sine_table):
    halfway = values.shape[-1] // 2
    first_half = values[..., :halfway]
    second_half = values[..., halfway:]
    return jnp.concatenate(
        [
            first_half * cosine_table - second_half * sine_table,
            second_half * cosine_table + first_half * sine_table,
        ],
        axis=-1,
    )


def norm_forward(values, gain_row):
    inverse = lax.rsqrt(jnp.mean(values * values, axis=-1, keepdims=True) + EPSILON)
    unit_rows = values * inverse
    return (unit_rows * gain_row, unit_rows, inverse)


def norm_backward(incoming, unit_rows, inverse, gain_row):
    scaled = incoming * gain_row
    grad_values = inverse * (
        scaled - unit_rows * jnp.mean(scaled * unit_rows, axis=-1, keepdims=True)
    )
    return (grad_values, jnp.sum(incoming * unit_rows, axis=0))


def on_device_sparse(
    hidden_in,
    out_grad,
    query_weight,
    latent_weight,
    expand_weight,
    output_weight,
    norm_gains,
    latent_gain,
    router_weight,
    shared_gate_up,
    shared_down,
    expert_gate_up,
    expert_down,
    expert_ids,
):
    (
        query_full,
        latent_full,
        expand_full,
        output_full,
        gains_full,
        latent_gain_full,
        router_full,
        shared_gu_full,
        shared_down_full,
    ) = (
        lax.all_gather(query_weight, "ep", axis=0, tiled=True),
        lax.all_gather(latent_weight, "ep", axis=0, tiled=True),
        lax.all_gather(expand_weight, "ep", axis=0, tiled=True),
        lax.all_gather(output_weight, "ep", axis=1, tiled=True),
        lax.all_gather(norm_gains, "ep", axis=1, tiled=True),
        lax.all_gather(latent_gain, "ep", axis=0, tiled=True),
        lax.all_gather(router_weight, "ep", axis=0, tiled=True),
        lax.all_gather(shared_gate_up, "ep", axis=1, tiled=True),
        lax.all_gather(shared_down, "ep", axis=1, tiled=True),
    )
    tokens = hidden_in.shape[0]
    model_width = hidden_in.shape[1]
    heads_local = query_full.shape[1] // (NOPE + ROPE)
    gain_rows = gains_full.astype(jnp.float32)
    gain_latent = latent_gain_full.astype(jnp.float32)
    places = jnp.arange(tokens).astype(jnp.float32)
    frequency = ROPE_BASE ** (-(jnp.arange(ROPE // 2).astype(jnp.float32) * 2.0 / ROPE))
    angles = places[:, None] * frequency[None, :]
    cosine_table = jnp.cos(angles)
    sine_table = jnp.sin(angles)
    resid_in = hidden_in.astype(jnp.float32)
    normed_in, unit_in, inverse_in = norm_forward(resid_in, gain_rows[0])
    normed_low = normed_in.astype(jnp.bfloat16)
    query_raw = matmul(normed_low, query_full).reshape(tokens, heads_local, NOPE + ROPE)
    queries = jnp.concatenate(
        [
            query_raw[..., :NOPE],
            rotate(query_raw[..., NOPE:], cosine_table[:, None, :], sine_table[:, None, :]),
        ],
        axis=-1,
    ).astype(jnp.bfloat16)
    latent = matmul(normed_low, latent_full)
    latent_normed, latent_unit, latent_inverse = norm_forward(latent[:, :KV_RANK], gain_latent)
    latent_low = latent_normed.astype(jnp.bfloat16)
    key_rope = rotate(latent[:, KV_RANK:], cosine_table, sine_table).astype(jnp.bfloat16)
    expanded = (
        matmul(latent_low, expand_full)
        .astype(jnp.bfloat16)
        .reshape(tokens, heads_local, NOPE + V_DIM)
    )
    key_rows = jnp.concatenate(
        [expanded[..., :NOPE], jnp.broadcast_to(key_rope[:, None, :], (tokens, heads_local, ROPE))],
        axis=-1,
    )
    values = expanded[..., NOPE:]
    score_scale = 1.0 / math.sqrt(NOPE + ROPE)
    causal = jnp.arange(tokens)[:, None] >= jnp.arange(tokens)[None, :]

    def attention_scores():
        scores = (
            jnp.einsum("qhd,khd->hqk", queries, key_rows, preferred_element_type=jnp.float32)
            * score_scale
        )
        return jnp.where(causal[None], scores, -1e30)

    scores_first = attention_scores()
    row_max = jnp.max(scores_first, axis=-1, keepdims=True)
    log_total = row_max + jnp.log(jnp.sum(jnp.exp(scores_first - row_max), axis=-1, keepdims=True))
    probs_low = jnp.exp(scores_first - log_total).astype(jnp.bfloat16)
    attended = jnp.einsum("hqk,khd->qhd", probs_low, values, preferred_element_type=jnp.float32)
    attended = attended.astype(jnp.bfloat16).reshape(tokens, heads_local * V_DIM)
    attn_out = lax.psum(matmul(attended, output_full), "tp")
    resid = resid_in + attn_out
    normed_mid, unit_mid, inverse_mid = norm_forward(resid, gain_rows[1])
    mid_low = normed_mid.astype(jnp.bfloat16)
    logits = matmul(mid_low, router_full)
    experts = router_full.shape[1]
    route_mask = (expert_ids[:, :, None] == jnp.arange(experts)[None, None, :]).astype(jnp.float32)
    chosen = jnp.sum(route_mask * logits[:, None, :], axis=2)
    sigmoids = jax.nn.sigmoid(chosen)
    sigmoid_total = jnp.sum(sigmoids, axis=1, keepdims=True)
    gating = ROUTE_SCALE * sigmoids / sigmoid_total
    shared_gate = matmul(mid_low, shared_gu_full[0])
    shared_upper = matmul(mid_low, shared_gu_full[1])
    shared_sig = jax.nn.sigmoid(shared_gate)
    shared_hidden = (shared_gate * shared_sig * shared_upper).astype(jnp.bfloat16)
    shared_part = matmul(shared_hidden, shared_down_full)
    groups = lax.axis_size("ep")
    mean_load = tokens * TOPK // (EXP_DEV * groups)
    capacity = mean_load + mean_load // 3
    choices = tokens * TOPK
    rows_total = groups * capacity
    flat_ids = expert_ids.reshape(-1)
    onehot = (flat_ids[:, None] == jnp.arange(experts)[None, :]).astype(jnp.int32)
    slot_of = jnp.sum((jnp.cumsum(onehot, axis=0) - onehot) * onehot, axis=1)
    target = flat_ids % EXP_DEV * rows_total + flat_ids // EXP_DEV * capacity + slot_of
    slot_table = (
        jnp.full((EXP_DEV * rows_total,), choices, jnp.int32)
        .at[target]
        .set(jnp.arange(choices, dtype=jnp.int32))
        .reshape(EXP_DEV, groups, capacity)
    )
    mid_padded = jnp.concatenate([mid_low, jnp.zeros((1, model_width), jnp.bfloat16)], axis=0)
    outgoing = mid_padded[slot_table.reshape(-1) // TOPK].reshape(EXP_DEV, rows_total, model_width)
    expert_rows = lax.all_to_all(outgoing, "ep", split_axis=1, concat_axis=1, tiled=True)
    expert_gate = jnp.einsum(
        "erd,edf->erf", expert_rows, expert_gate_up[:, 0], preferred_element_type=jnp.float32
    )
    expert_upper = jnp.einsum(
        "erd,edf->erf", expert_rows, expert_gate_up[:, 1], preferred_element_type=jnp.float32
    )
    expert_sig = jax.nn.sigmoid(expert_gate)
    expert_hidden = (expert_gate * expert_sig * expert_upper).astype(jnp.bfloat16)
    expert_part = jnp.einsum(
        "erf,efd->erd", expert_hidden, expert_down, preferred_element_type=jnp.float32
    ).astype(jnp.bfloat16)
    returned = lax.all_to_all(expert_part, "ep", split_axis=1, concat_axis=1, tiled=True)
    per_choice = (
        returned.reshape(-1, model_width)[target]
        .reshape(tokens, TOPK, model_width)
        .astype(jnp.float32)
    )
    routed_part = jnp.sum(gating[:, :, None] * per_choice, axis=1)
    moe_out = lax.psum((shared_part + routed_part).astype(jnp.bfloat16), "tp").astype(jnp.float32)
    block_out = (resid + moe_out).astype(jnp.bfloat16)
    grad_top = out_grad.astype(jnp.float32)
    choice_grad = (gating[:, :, None] * grad_top[:, None, :]).astype(jnp.bfloat16)
    grad_padded = jnp.concatenate(
        [choice_grad.reshape(choices, model_width), jnp.zeros((1, model_width), jnp.bfloat16)],
        axis=0,
    )
    outgoing_grad = grad_padded[slot_table.reshape(-1)].reshape(EXP_DEV, rows_total, model_width)
    rows_grad = lax.all_to_all(outgoing_grad, "ep", split_axis=1, concat_axis=1, tiled=True)
    hidden_grad = jnp.einsum(
        "erd,efd->erf", rows_grad, expert_down, preferred_element_type=jnp.float32
    )
    gate_grad = (
        hidden_grad * expert_upper * expert_sig * (1.0 + expert_gate * (1.0 - expert_sig))
    ).astype(jnp.bfloat16)
    upper_grad = (hidden_grad * expert_gate * expert_sig).astype(jnp.bfloat16)
    grad_expert_down = jnp.einsum(
        "erf,erd->efd", expert_hidden, rows_grad, preferred_element_type=jnp.float32
    )
    grad_expert_gate_up = jnp.stack(
        [
            jnp.einsum("erd,erf->edf", expert_rows, gate_grad, preferred_element_type=jnp.float32),
            jnp.einsum("erd,erf->edf", expert_rows, upper_grad, preferred_element_type=jnp.float32),
        ],
        axis=1,
    )
    row_back = jnp.einsum(
        "erf,edf->erd", gate_grad, expert_gate_up[:, 0], preferred_element_type=jnp.float32
    ) + jnp.einsum(
        "erf,edf->erd", upper_grad, expert_gate_up[:, 1], preferred_element_type=jnp.float32
    )
    row_back_low = row_back.astype(jnp.bfloat16)
    back_rows = lax.all_to_all(row_back_low, "ep", split_axis=1, concat_axis=1, tiled=True)
    choice_back = (
        back_rows.reshape(-1, model_width)[target]
        .reshape(tokens, TOPK, model_width)
        .astype(jnp.float32)
    )
    mid_grad_routed = jnp.sum(choice_back, axis=1)
    gating_grad_part = jnp.sum(per_choice * grad_top[:, None, :], axis=2)
    shared_hidden_grad = transposed_right(out_grad, shared_down_full)
    shared_gate_grad = (
        shared_hidden_grad * shared_upper * shared_sig * (1.0 + shared_gate * (1.0 - shared_sig))
    ).astype(jnp.bfloat16)
    shared_upper_grad = (shared_hidden_grad * shared_gate * shared_sig).astype(jnp.bfloat16)
    grad_shared_down = transposed_left(shared_hidden, out_grad)
    grad_shared_gu = jnp.stack(
        [transposed_left(mid_low, shared_gate_grad), transposed_left(mid_low, shared_upper_grad)],
        axis=0,
    )
    mid_grad_shared = transposed_right(shared_gate_grad, shared_gu_full[0]) + transposed_right(
        shared_upper_grad, shared_gu_full[1]
    )
    mid_grad_sum, gating_grad = (
        lax.psum((mid_grad_routed + mid_grad_shared).astype(jnp.bfloat16), "tp").astype(
            jnp.float32
        ),
        lax.psum(gating_grad_part.astype(jnp.bfloat16), "tp").astype(jnp.float32),
    )
    weighted = jnp.sum(gating_grad * sigmoids, axis=1, keepdims=True) / sigmoid_total
    sigmoid_grad = ROUTE_SCALE / sigmoid_total * (gating_grad - weighted)
    chosen_grad = sigmoid_grad * sigmoids * (1.0 - sigmoids)
    logits_grad = jnp.sum(route_mask * chosen_grad[:, :, None], axis=1).astype(jnp.bfloat16)
    grad_router = transposed_left(mid_low, logits_grad)
    mid_grad = mid_grad_sum + transposed_right(logits_grad, router_full)
    resid_norm_grad, grad_gain_mid = norm_backward(mid_grad, unit_mid, inverse_mid, gain_rows[1])
    resid_grad = grad_top + resid_norm_grad
    attn_grad = resid_grad.astype(jnp.bfloat16)
    grad_output = transposed_left(attended, attn_grad)
    attended_grad = (
        transposed_right(attn_grad, output_full)
        .astype(jnp.bfloat16)
        .reshape(tokens, heads_local, V_DIM)
    )
    softmax_probs = jnp.exp(attention_scores() - log_total)
    values_grad = jnp.einsum(
        "hqk,qhd->khd",
        softmax_probs.astype(jnp.bfloat16),
        attended_grad,
        preferred_element_type=jnp.float32,
    )
    probs_grad = jnp.einsum(
        "qhd,khd->hqk", attended_grad, values, preferred_element_type=jnp.float32
    )
    scores_grad = (
        softmax_probs * (probs_grad - jnp.sum(softmax_probs * probs_grad, axis=-1, keepdims=True))
    ).astype(jnp.bfloat16)
    query_grad = (
        jnp.einsum("hqk,khd->qhd", scores_grad, key_rows, preferred_element_type=jnp.float32)
        * score_scale
    )
    keys_grad = (
        jnp.einsum("hqk,qhd->khd", scores_grad, queries, preferred_element_type=jnp.float32)
        * score_scale
    )
    query_raw_grad = (
        jnp.concatenate(
            [
                query_grad[..., :NOPE],
                rotate(query_grad[..., NOPE:], cosine_table[:, None, :], -sine_table[:, None, :]),
            ],
            axis=-1,
        )
        .astype(jnp.bfloat16)
        .reshape(tokens, heads_local * (NOPE + ROPE))
    )
    expanded_grad = jnp.concatenate([keys_grad[..., :NOPE], values_grad], axis=-1).astype(
        jnp.bfloat16
    )
    expanded_grad = expanded_grad.reshape(tokens, heads_local * (NOPE + V_DIM))
    grad_expand = transposed_left(latent_low, expanded_grad)
    latent_normed_grad = transposed_right(expanded_grad, expand_full)
    latent_part_grad, gain_latent_part = norm_backward(
        latent_normed_grad, latent_unit, latent_inverse, gain_latent
    )
    rope_raw_grad = rotate(jnp.sum(keys_grad[..., NOPE:], axis=1), cosine_table, -sine_table)
    latent_grad_part = jnp.concatenate([latent_part_grad, rope_raw_grad], axis=1)
    in_grad_query = transposed_right(query_raw_grad, query_full)
    in_grad_sum, latent_grad, grad_gain_latent = (
        lax.psum(in_grad_query.astype(jnp.bfloat16), "tp").astype(jnp.float32),
        lax.psum(latent_grad_part.astype(jnp.bfloat16), "tp").astype(jnp.float32),
        lax.psum(gain_latent_part.astype(jnp.bfloat16), "tp").astype(jnp.float32),
    )
    latent_grad_low = latent_grad.astype(jnp.bfloat16)
    grad_latent = transposed_left(normed_low, latent_grad_low)
    grad_query = transposed_left(normed_low, query_raw_grad)
    in_grad = in_grad_sum + transposed_right(latent_grad_low, latent_full)
    input_norm_grad, grad_gain_in = norm_backward(in_grad, unit_in, inverse_in, gain_rows[0])
    grad_hidden = resid_grad + input_norm_grad
    grad_gains = jnp.stack([grad_gain_in, grad_gain_mid], axis=0)
    (
        grad_query_out,
        grad_latent_out,
        grad_expand_out,
        grad_output_out,
        grad_gains_out,
        grad_gain_latent_out,
        grad_router_out,
        grad_shared_gu_out,
        grad_shared_down_out,
    ) = (
        lax.psum_scatter(
            grad_query.astype(jnp.bfloat16), "ep", scatter_dimension=0, tiled=True
        ).astype(jnp.float32),
        lax.psum_scatter(
            grad_latent.astype(jnp.bfloat16), "ep", scatter_dimension=0, tiled=True
        ).astype(jnp.float32),
        lax.psum_scatter(
            grad_expand.astype(jnp.bfloat16), "ep", scatter_dimension=0, tiled=True
        ).astype(jnp.float32),
        lax.psum_scatter(
            grad_output.astype(jnp.bfloat16), "ep", scatter_dimension=1, tiled=True
        ).astype(jnp.float32),
        lax.psum_scatter(
            grad_gains.astype(jnp.bfloat16), "ep", scatter_dimension=1, tiled=True
        ).astype(jnp.float32),
        lax.psum_scatter(
            grad_gain_latent.astype(jnp.bfloat16), "ep", scatter_dimension=0, tiled=True
        ).astype(jnp.float32),
        lax.psum_scatter(
            grad_router.astype(jnp.bfloat16), "ep", scatter_dimension=0, tiled=True
        ).astype(jnp.float32),
        lax.psum_scatter(
            grad_shared_gu.astype(jnp.bfloat16), "ep", scatter_dimension=1, tiled=True
        ).astype(jnp.float32),
        lax.psum_scatter(
            grad_shared_down.astype(jnp.bfloat16), "ep", scatter_dimension=1, tiled=True
        ).astype(jnp.float32),
    )
    return (
        block_out,
        grad_hidden,
        grad_query_out,
        grad_latent_out,
        grad_expand_out,
        grad_output_out,
        grad_gains_out,
        grad_gain_latent_out,
        grad_router_out,
        grad_shared_gu_out,
        grad_shared_down_out,
        grad_expert_gate_up,
        grad_expert_down,
    )


def swap(array, axis, bit):
    size = lax.axis_size(axis)
    return lax.ppermute(array, axis, [(place, place ^ bit) for place in range(size)])


def axis_bits(axis):
    size = lax.axis_size(axis)
    return [(axis, 1 << bit) for bit in reversed(range(size.bit_length() - 1))]


def spread(rows, steps):
    for axis, bit in steps:
        rows = jnp.concatenate([rows, swap(rows, axis, bit)], axis=0)
    return rows


def fold(rows, steps):
    for axis, bit in reversed(steps):
        half = rows.shape[0] // 2
        arrived = swap(rows[half:], axis, bit)
        rows = (rows[:half].astype(jnp.float32) + arrived.astype(jnp.float32)).astype(rows.dtype)
    return rows


def distances(steps):
    found = [0]
    for _, bit in steps:
        found = found + [distance + bit for distance in found]
    return found


def by_distance(blocks, place, order):
    return jnp.concatenate(
        [lax.dynamic_slice_in_dim(blocks, place ^ i, 1, axis=0) for i in order], axis=0
    )


def by_place(blocks, place, order):
    natural = jnp.concatenate([blocks[order.index(i)][None] for i in range(len(order))], axis=0)
    return by_distance(natural, place, range(len(order)))


def pad_columns(array, width):
    return jnp.pad(array, ((0, 0), (0, width - array.shape[1])))


def round_up(size, step=128):
    return -(-size // step) * step


def on_device_dense(
    hidden_in,
    out_grad,
    query_weight,
    latent_weight,
    expand_weight,
    output_weight,
    norm_gains,
    latent_gain,
    router_weight,
    shared_gate_up,
    shared_down,
    expert_gate_up,
    expert_down,
    expert_ids,
):
    groups, parts = lax.axis_size("ep"), lax.axis_size("tp")
    group, part = lax.axis_index("ep"), lax.axis_index("tp")
    tokens, width = hidden_in.shape
    own = tokens // parts
    experts = router_weight.shape[1]
    bf16, f32 = jnp.bfloat16, jnp.float32
    ep_steps, tp_steps = axis_bits("ep"), axis_bits("tp")
    tp_order = distances(tp_steps)
    chunk_steps = [
        ep_steps + tp_steps,
        ep_steps[:-1] + tp_steps[:-1] + ep_steps[-1:] + tp_steps[-1:],
    ]
    chunk_rows = own // len(chunk_steps)

    def own_chunks(rows):
        return [rows[i * chunk_rows : (i + 1) * chunk_rows] for i in range(len(chunk_steps))]

    def relative(rows):
        blocks = rows.reshape(parts, own, rows.shape[1])
        return by_distance(blocks, part, tp_order).reshape(tokens, rows.shape[1])

    hidden_rel = relative(hidden_in)
    grad_own = lax.dynamic_slice_in_dim(out_grad, part * own, own, axis=0)

    small = jnp.concatenate(
        [norm_gains.reshape(-1), latent_gain.reshape(-1), router_weight.reshape(-1)]
    )
    small_full = lax.all_gather(small, "ep", axis=0)
    gain_size, latent_size = norm_gains.size, latent_gain.size
    gain_rows = (
        small_full[:, :gain_size].reshape(groups, 2, -1).transpose(1, 0, 2).reshape(2, width)
    ).astype(f32)
    gain_latent = small_full[:, gain_size : gain_size + latent_size].reshape(-1).astype(f32)
    router_full = small_full[:, gain_size + latent_size :].reshape(width, experts)
    latent_cut = latent_weight.shape[0] // parts
    latent_own = lax.dynamic_slice_in_dim(latent_weight, part * latent_cut, latent_cut, axis=0)
    latent_rel = lax.all_gather(latent_own, "ep", axis=0)[None]
    latent_full = (
        by_place(spread(latent_rel, tp_steps), part, tp_order).transpose(1, 0, 2, 3).reshape(width, -1)
    )
    query_full = lax.all_gather(query_weight, "ep", axis=0, tiled=True)
    expand_full = lax.all_gather(expand_weight, "ep", axis=0, tiled=True)
    output_full = lax.all_gather(output_weight, "ep", axis=1, tiled=True)
    units = shared_down.shape[0] // groups
    shared_gu_own = lax.all_to_all(
        shared_gate_up.reshape(2, -1, groups, units), "ep", split_axis=2, concat_axis=1, tiled=True
    ).reshape(2, width, units)
    shared_down_own = lax.all_to_all(shared_down, "ep", split_axis=0, concat_axis=1, tiled=True)

    hidden_units = expert_down.shape[1]
    expert_pad, shared_pad = round_up(hidden_units), round_up(units)
    block_pads = [expert_pad] * EXP_DEV + [shared_pad]
    total = sum(block_pads)
    side_weights = [
        jnp.concatenate(
            [pad_columns(expert_gate_up[e, side], expert_pad) for e in range(EXP_DEV)]
            + [pad_columns(shared_gu_own[side], shared_pad)],
            axis=1,
        )
        for side in range(2)
    ]
    gu_weight = jnp.concatenate(side_weights, axis=1)
    down_weight = jnp.concatenate(
        [jnp.pad(expert_down[e], ((0, expert_pad - hidden_units), (0, 0))) for e in range(EXP_DEV)]
        + [jnp.pad(shared_down_own, ((0, shared_pad - units), (0, 0)))],
        axis=0,
    )

    grad_chunks = [spread(rows, steps) for rows, steps in zip(own_chunks(grad_own), chunk_steps)]
    mask_own = jnp.sum(
        (expert_ids[:, :, None] == jnp.arange(experts)[None, None, :]).astype(bf16), axis=1
    )
    mask_all = lax.all_gather(mask_own, "ep", axis=0).reshape(groups, parts, own, experts)
    mask_all = by_distance(mask_all, group, range(groups)).transpose(1, 0, 2, 3)
    mask_all = by_distance(mask_all, part, range(parts))
    ep_bits, tp_bits = len(ep_steps), len(tp_steps)
    mask_bits = mask_all.reshape((2,) * (tp_bits + ep_bits) + (own, experts))
    bit_names = tp_steps + ep_steps
    mask_chunks = []
    for i, steps in enumerate(chunk_steps):
        turn = [bit_names.index(step) for step in reversed(steps)]
        cut = mask_bits[..., i * chunk_rows : (i + 1) * chunk_rows, :]
        cut = cut.transpose(turn + [len(turn), len(turn) + 1])
        mask_chunks.append(cut.reshape(-1, experts).astype(f32))

    heads_local = query_full.shape[1] // (NOPE + ROPE)
    places = ((part ^ jnp.array(tp_order))[:, None] * own + jnp.arange(own)[None, :]).reshape(-1)
    frequency = ROPE_BASE ** (-(jnp.arange(ROPE // 2).astype(f32) * 2.0 / ROPE))
    angles = places.astype(f32)[:, None] * frequency[None, :]
    cosine_table = jnp.cos(angles)
    sine_table = jnp.sin(angles)
    resid_in = hidden_rel.astype(f32)
    normed_in, unit_in, inverse_in = norm_forward(resid_in, gain_rows[0])
    normed_low = normed_in.astype(bf16)
    query_raw = matmul(normed_low, query_full).reshape(tokens, heads_local, NOPE + ROPE)
    queries = jnp.concatenate(
        [
            query_raw[..., :NOPE],
            rotate(query_raw[..., NOPE:], cosine_table[:, None, :], sine_table[:, None, :]),
        ],
        axis=-1,
    ).astype(bf16)
    latent = matmul(normed_low, latent_full)
    latent_normed, latent_unit, latent_inverse = norm_forward(latent[:, :KV_RANK], gain_latent)
    latent_low = latent_normed.astype(bf16)
    key_rope = rotate(latent[:, KV_RANK:], cosine_table, sine_table).astype(bf16)
    expanded = (
        matmul(latent_low, expand_full).astype(bf16).reshape(tokens, heads_local, NOPE + V_DIM)
    )
    key_rows = jnp.concatenate(
        [expanded[..., :NOPE], jnp.broadcast_to(key_rope[:, None, :], (tokens, heads_local, ROPE))],
        axis=-1,
    )
    values = expanded[..., NOPE:]
    score_scale = 1.0 / math.sqrt(NOPE + ROPE)
    causal = places[:, None] >= places[None, :]
    scores = (
        jnp.einsum("qhd,khd->hqk", queries, key_rows, preferred_element_type=f32) * score_scale
    )
    scores = jnp.where(causal[None], scores, -1e30)
    row_max = jnp.max(scores, axis=-1, keepdims=True)
    powers = jnp.exp(scores - row_max)
    softmax_probs = powers / jnp.sum(powers, axis=-1, keepdims=True)
    probs_low = softmax_probs.astype(bf16)
    attended = jnp.einsum("hqk,khd->qhd", probs_low, values, preferred_element_type=f32)
    attended = attended.astype(bf16).reshape(tokens, heads_local * V_DIM)
    attn_part = matmul(attended, output_full).astype(bf16)
    resid = hidden_rel[:own].astype(f32) + fold(attn_part, tp_steps).astype(f32)

    normed_mid, unit_mid, inverse_mid = norm_forward(resid, gain_rows[1])
    mid_own = normed_mid.astype(bf16)
    mid_chunks = [spread(rows, steps) for rows, steps in zip(own_chunks(mid_own), chunk_steps)]
    first_expert = group * EXP_DEV
    lanes = jnp.arange(experts)
    out_rows, back_rows, hidden_chunks, grads_chunks = [], [], [], []
    for mid_rows, grad_rows, mask, steps in zip(mid_chunks, grad_chunks, mask_chunks, chunk_steps):
        sigmoids = jax.nn.sigmoid(matmul(mid_rows, router_full)) * mask
        gating = ROUTE_SCALE * sigmoids / jnp.sum(sigmoids, axis=1, keepdims=True)
        local = [
            jnp.sum(jnp.where(lanes == first_expert + e, gating, 0.0), axis=1, keepdims=True)
            for e in range(EXP_DEV)
        ]
        weight_of = jnp.concatenate(
            [jnp.broadcast_to(g, (g.shape[0], expert_pad)) for g in local]
            + [jnp.ones((mask.shape[0], shared_pad), f32)],
            axis=1,
        )
        both = matmul(mid_rows, gu_weight)
        gate, upper = both[:, :total], both[:, total:]
        raw_grad = transposed_right(grad_rows, down_weight)
        sig = jax.nn.sigmoid(gate)
        silu = gate * sig
        hidden = silu * upper
        hidden_grad = weight_of * raw_grad
        gate_grad = hidden_grad * upper * sig * (1.0 + gate * (1.0 - sig))
        upper_grad = hidden_grad * silu
        hidden_low = (weight_of * hidden).astype(bf16)
        grads_low = jnp.concatenate([gate_grad, upper_grad], axis=1).astype(bf16)
        share = hidden * raw_grad
        gating_grad = sum(
            jnp.where(
                lanes == first_expert + e,
                jnp.sum(share[:, e * expert_pad : (e + 1) * expert_pad], axis=1, keepdims=True),
                0.0,
            )
            for e in range(EXP_DEV)
        )
        back = transposed_right(grads_low, gu_weight).astype(bf16)
        back_rows.append(
            fold(jnp.concatenate([back, pad_columns(gating_grad, 128).astype(bf16)], axis=1), steps)
        )
        hidden_chunks.append(hidden_low)
        grads_chunks.append(grads_low)
        out_rows.append(fold(matmul(hidden_low, down_weight).astype(bf16), steps))
    mid_all = jnp.concatenate(mid_chunks, axis=0)
    grad_all = jnp.concatenate(grad_chunks, axis=0)
    grad_gu = transposed_left(mid_all, jnp.concatenate(grads_chunks, axis=0))
    grad_down = transposed_left(jnp.concatenate(hidden_chunks, axis=0), grad_all)
    grad_expert_gate_up = jnp.stack(
        [
            jnp.stack(
                [
                    grad_gu[:, side * total + e * expert_pad :][:, :hidden_units]
                    for side in range(2)
                ]
            )
            for e in range(EXP_DEV)
        ]
    )
    grad_expert_down = jnp.stack(
        [grad_down[e * expert_pad : e * expert_pad + hidden_units] for e in range(EXP_DEV)]
    )
    shared_at = EXP_DEV * expert_pad
    grad_shared_gu = jnp.stack(
        [grad_gu[:, side * total + shared_at :][:, :units] for side in range(2)]
    ).astype(bf16)
    grad_shared_gu_out = (
        lax.all_to_all(
            grad_shared_gu.reshape(2, width, 1, units),
            "ep",
            split_axis=1,
            concat_axis=2,
            tiled=True,
        )
        .reshape(shared_gate_up.shape)
        .astype(f32)
    )
    grad_shared_down_out = lax.all_to_all(
        grad_down[shared_at : shared_at + units].astype(bf16),
        "ep",
        split_axis=1,
        concat_axis=0,
        tiled=True,
    ).astype(f32)

    block_own = (resid + jnp.concatenate(out_rows, axis=0).astype(f32)).astype(bf16)

    back_own = jnp.concatenate(back_rows, axis=0).astype(f32)
    gating_grad = back_own[:, width : width + experts]
    mask = lax.dynamic_slice_in_dim(mask_own, part * own, own, axis=0).astype(f32)
    sigmoids = jax.nn.sigmoid(matmul(mid_own, router_full))
    chosen = sigmoids * mask
    sigmoid_total = jnp.sum(chosen, axis=1, keepdims=True)
    weighted = jnp.sum(gating_grad * chosen, axis=1, keepdims=True) / sigmoid_total
    sigmoid_grad = ROUTE_SCALE / sigmoid_total * (gating_grad - weighted)
    logits_grad = (sigmoid_grad * chosen * (1.0 - sigmoids)).astype(bf16)
    grad_router = transposed_left(mid_own, logits_grad)
    mid_grad = back_own[:, :width] + transposed_right(logits_grad, router_full)
    resid_norm_grad, grad_gain_mid = norm_backward(mid_grad, unit_mid, inverse_mid, gain_rows[1])
    resid_grad = grad_own.astype(f32) + resid_norm_grad

    attn_grad = spread(resid_grad.astype(bf16), tp_steps)
    grad_output = transposed_left(attended, attn_grad)
    attended_grad = (
        transposed_right(attn_grad, output_full).astype(bf16).reshape(tokens, heads_local, V_DIM)
    )
    values_grad = jnp.einsum("hqk,qhd->khd", probs_low, attended_grad, preferred_element_type=f32)
    probs_grad = jnp.einsum("qhd,khd->hqk", attended_grad, values, preferred_element_type=f32)
    scores_grad = (
        softmax_probs * (probs_grad - jnp.sum(softmax_probs * probs_grad, axis=-1, keepdims=True))
    ).astype(bf16)
    query_grad = (
        jnp.einsum("hqk,khd->qhd", scores_grad, key_rows, preferred_element_type=f32) * score_scale
    )
    keys_grad = (
        jnp.einsum("hqk,qhd->khd", scores_grad, queries, preferred_element_type=f32) * score_scale
    )
    query_raw_grad = (
        jnp.concatenate(
            [
                query_grad[..., :NOPE],
                rotate(query_grad[..., NOPE:], cosine_table[:, None, :], -sine_table[:, None, :]),
            ],
            axis=-1,
        )
        .astype(bf16)
        .reshape(tokens, heads_local * (NOPE + ROPE))
    )
    expanded_grad = (
        jnp.concatenate([keys_grad[..., :NOPE], values_grad], axis=-1)
        .astype(bf16)
        .reshape(tokens, heads_local * (NOPE + V_DIM))
    )
    grad_expand = transposed_left(latent_low, expanded_grad)
    latent_normed_grad = transposed_right(expanded_grad, expand_full)
    latent_part_grad, gain_latent_part = norm_backward(
        latent_normed_grad, latent_unit, latent_inverse, gain_latent
    )
    rope_raw_grad = rotate(jnp.sum(keys_grad[..., NOPE:], axis=1), cosine_table, -sine_table)
    latent_grad = jnp.concatenate([latent_part_grad, rope_raw_grad], axis=1).astype(bf16)
    grad_latent = transposed_left(normed_low, latent_grad)
    grad_query = transposed_left(normed_low, query_raw_grad)
    in_grad_part = transposed_right(query_raw_grad, query_full) + transposed_right(
        latent_grad, latent_full
    )
    in_grad = fold(in_grad_part.astype(bf16), tp_steps).astype(f32)
    input_norm_grad, grad_gain_in = norm_backward(
        in_grad, unit_in[:own], inverse_in[:own], gain_rows[0]
    )
    hidden_own = (resid_grad + input_norm_grad).astype(bf16)

    grad_query_out = lax.psum_scatter(
        grad_query.astype(bf16), "ep", scatter_dimension=0, tiled=True
    ).astype(f32)
    grad_expand_out = lax.psum_scatter(
        grad_expand.astype(bf16), "ep", scatter_dimension=0, tiled=True
    ).astype(f32)
    grad_output_out = lax.psum_scatter(
        grad_output.astype(bf16), "ep", scatter_dimension=1, tiled=True
    ).astype(f32)
    latent_blocks = grad_latent.astype(bf16).reshape(groups, parts, latent_cut, -1)
    latent_blocks = by_distance(latent_blocks.transpose(1, 0, 2, 3), part, tp_order)
    latent_blocks = fold(latent_blocks, tp_steps)[0]
    latent_sum = lax.psum_scatter(latent_blocks, "ep", scatter_dimension=0, tiled=True)
    grad_latent_out = (
        by_place(spread(latent_sum, tp_steps), part, tp_order)
        .reshape(latent_weight.shape)
        .astype(f32)
    )
    grad_small = jnp.concatenate(
        [
            jnp.stack([grad_gain_in, grad_gain_mid])
            .reshape(2, groups, -1)
            .transpose(1, 0, 2)
            .reshape(groups, -1),
            gain_latent_part.reshape(groups, -1),
            grad_router.reshape(groups, -1),
        ],
        axis=1,
    )
    small_sum = fold(by_distance(grad_small, group, distances(ep_steps)), ep_steps)
    for axis, bit in tp_steps:
        small_sum = small_sum + swap(small_sum, axis, bit)
    small_sum = small_sum.reshape(-1)
    grad_gains_out = small_sum[:gain_size].reshape(norm_gains.shape)
    grad_gain_latent_out = small_sum[gain_size : gain_size + latent_size]
    grad_router_out = small_sum[gain_size + latent_size :].reshape(router_weight.shape)

    def all_rows(rows):
        blocks = spread(rows[None], tp_steps)
        return by_place(blocks, part, tp_order).reshape(tokens, width)

    return (
        all_rows(block_own),
        all_rows(hidden_own).astype(f32),
        grad_query_out,
        grad_latent_out,
        grad_expand_out,
        grad_output_out,
        grad_gains_out,
        grad_gain_latent_out,
        grad_router_out,
        grad_shared_gu_out,
        grad_shared_down_out,
        grad_expert_gate_up,
        grad_expert_down,
    )


def power_of_two(size):
    return size & (size - 1) == 0


def on_device(hidden_in, *others):
    groups, parts = lax.axis_size("ep"), lax.axis_size("tp")
    tokens = hidden_in.shape[0]
    mean_load = tokens * TOPK // (EXP_DEV * groups)
    capacity = mean_load + mean_load // 3
    if EXP_DEV * capacity >= tokens and power_of_two(groups) and power_of_two(parts):
        return on_device_dense(hidden_in, *others)
    return on_device_sparse(hidden_in, *others)


def solution(mesh):
    placed = (
        P("ep", None),
        P("ep", None),
        P("ep", "tp"),
        P("ep", None),
        P("ep", "tp"),
        P("tp", "ep"),
        P(None, "ep"),
        P("ep"),
        P("ep", None),
        P(None, "ep", "tp"),
        P("tp", "ep"),
        P("ep", None, None, "tp"),
        P("ep", "tp", None),
        P("ep", None),
    )
    return jax.shard_map(
        on_device,
        mesh=mesh,
        in_specs=placed,
        out_specs=(
            P("ep", None),
            P("ep", None),
            P("ep", "tp"),
            P("ep", None),
            P("ep", "tp"),
            P("tp", "ep"),
            P(None, "ep"),
            P("ep"),
            P("ep", None),
            P(None, "ep", "tp"),
            P("tp", "ep"),
            P("ep", None, None, "tp"),
            P("ep", "tp", None),
        ),
        check_vma=False,
    )
```

```python
import functools
import math

import jax
import jax.numpy as jnp
from jax import lax
from jax.experimental import pallas as pl
from jax.experimental.pallas import tpu as pltpu
from jax.sharding import PartitionSpec as P

NOPE = 128
ROPE = 64
V_DIM = 128
KV_RANK = 512
TOPK = 6
EXP_DEV = 2


EPSILON = 1e-06
ROUTE_SCALE = 2.446
ROPE_BASE = 50000.0


def matmul(left_side, right_side):
    return jnp.dot(left_side, right_side, preferred_element_type=jnp.float32)


def transposed_left(left_side, right_side):
    return lax.dot_general(
        left_side, right_side, (((0,), (0,)), ((), ())), preferred_element_type=jnp.float32
    )


def transposed_right(left_side, right_side):
    return lax.dot_general(
        left_side, right_side, (((1,), (1,)), ((), ())), preferred_element_type=jnp.float32
    )


def rotate(values, cosine_table, sine_table):
    halfway = values.shape[-1] // 2
    first_half = values[..., :halfway]
    second_half = values[..., halfway:]
    return jnp.concatenate(
        [
            first_half * cosine_table - second_half * sine_table,
            second_half * cosine_table + first_half * sine_table,
        ],
        axis=-1,
    )


def norm_forward(values, gain_row):
    inverse = lax.rsqrt(jnp.mean(values * values, axis=-1, keepdims=True) + EPSILON)
    unit_rows = values * inverse
    return (unit_rows * gain_row, unit_rows, inverse)


def norm_backward(incoming, unit_rows, inverse, gain_row):
    scaled = incoming * gain_row
    grad_values = inverse * (
        scaled - unit_rows * jnp.mean(scaled * unit_rows, axis=-1, keepdims=True)
    )
    return (grad_values, jnp.sum(incoming * unit_rows, axis=0))


def on_device_sparse(
    hidden_in,
    out_grad,
    query_weight,
    latent_weight,
    expand_weight,
    output_weight,
    norm_gains,
    latent_gain,
    router_weight,
    shared_gate_up,
    shared_down,
    expert_gate_up,
    expert_down,
    expert_ids,
):
    (
        query_full,
        latent_full,
        expand_full,
        output_full,
        gains_full,
        latent_gain_full,
        router_full,
        shared_gu_full,
        shared_down_full,
    ) = (
        lax.all_gather(query_weight, "ep", axis=0, tiled=True),
        lax.all_gather(latent_weight, "ep", axis=0, tiled=True),
        lax.all_gather(expand_weight, "ep", axis=0, tiled=True),
        lax.all_gather(output_weight, "ep", axis=1, tiled=True),
        lax.all_gather(norm_gains, "ep", axis=1, tiled=True),
        lax.all_gather(latent_gain, "ep", axis=0, tiled=True),
        lax.all_gather(router_weight, "ep", axis=0, tiled=True),
        lax.all_gather(shared_gate_up, "ep", axis=1, tiled=True),
        lax.all_gather(shared_down, "ep", axis=1, tiled=True),
    )
    tokens = hidden_in.shape[0]
    model_width = hidden_in.shape[1]
    heads_local = query_full.shape[1] // (NOPE + ROPE)
    gain_rows = gains_full.astype(jnp.float32)
    gain_latent = latent_gain_full.astype(jnp.float32)
    places = jnp.arange(tokens).astype(jnp.float32)
    frequency = ROPE_BASE ** (-(jnp.arange(ROPE // 2).astype(jnp.float32) * 2.0 / ROPE))
    angles = places[:, None] * frequency[None, :]
    cosine_table = jnp.cos(angles)
    sine_table = jnp.sin(angles)
    resid_in = hidden_in.astype(jnp.float32)
    normed_in, unit_in, inverse_in = norm_forward(resid_in, gain_rows[0])
    normed_low = normed_in.astype(jnp.bfloat16)
    query_raw = matmul(normed_low, query_full).reshape(tokens, heads_local, NOPE + ROPE)
    queries = jnp.concatenate(
        [
            query_raw[..., :NOPE],
            rotate(query_raw[..., NOPE:], cosine_table[:, None, :], sine_table[:, None, :]),
        ],
        axis=-1,
    ).astype(jnp.bfloat16)
    latent = matmul(normed_low, latent_full)
    latent_normed, latent_unit, latent_inverse = norm_forward(latent[:, :KV_RANK], gain_latent)
    latent_low = latent_normed.astype(jnp.bfloat16)
    key_rope = rotate(latent[:, KV_RANK:], cosine_table, sine_table).astype(jnp.bfloat16)
    expanded = (
        matmul(latent_low, expand_full)
        .astype(jnp.bfloat16)
        .reshape(tokens, heads_local, NOPE + V_DIM)
    )
    key_rows = jnp.concatenate(
        [expanded[..., :NOPE], jnp.broadcast_to(key_rope[:, None, :], (tokens, heads_local, ROPE))],
        axis=-1,
    )
    values = expanded[..., NOPE:]
    score_scale = 1.0 / math.sqrt(NOPE + ROPE)
    causal = jnp.arange(tokens)[:, None] >= jnp.arange(tokens)[None, :]

    def attention_scores():
        scores = (
            jnp.einsum("qhd,khd->hqk", queries, key_rows, preferred_element_type=jnp.float32)
            * score_scale
        )
        return jnp.where(causal[None], scores, -1e30)

    scores_first = attention_scores()
    row_max = jnp.max(scores_first, axis=-1, keepdims=True)
    log_total = row_max + jnp.log(jnp.sum(jnp.exp(scores_first - row_max), axis=-1, keepdims=True))
    probs_low = jnp.exp(scores_first - log_total).astype(jnp.bfloat16)
    attended = jnp.einsum("hqk,khd->qhd", probs_low, values, preferred_element_type=jnp.float32)
    attended = attended.astype(jnp.bfloat16).reshape(tokens, heads_local * V_DIM)
    attn_out = lax.psum(matmul(attended, output_full), "tp")
    resid = resid_in + attn_out
    normed_mid, unit_mid, inverse_mid = norm_forward(resid, gain_rows[1])
    mid_low = normed_mid.astype(jnp.bfloat16)
    logits = matmul(mid_low, router_full)
    experts = router_full.shape[1]
    route_mask = (expert_ids[:, :, None] == jnp.arange(experts)[None, None, :]).astype(jnp.float32)
    chosen = jnp.sum(route_mask * logits[:, None, :], axis=2)
    sigmoids = jax.nn.sigmoid(chosen)
    sigmoid_total = jnp.sum(sigmoids, axis=1, keepdims=True)
    gating = ROUTE_SCALE * sigmoids / sigmoid_total
    shared_gate = matmul(mid_low, shared_gu_full[0])
    shared_upper = matmul(mid_low, shared_gu_full[1])
    shared_sig = jax.nn.sigmoid(shared_gate)
    shared_hidden = (shared_gate * shared_sig * shared_upper).astype(jnp.bfloat16)
    shared_part = matmul(shared_hidden, shared_down_full)
    groups = lax.axis_size("ep")
    mean_load = tokens * TOPK // (EXP_DEV * groups)
    capacity = mean_load + mean_load // 3
    choices = tokens * TOPK
    rows_total = groups * capacity
    flat_ids = expert_ids.reshape(-1)
    onehot = (flat_ids[:, None] == jnp.arange(experts)[None, :]).astype(jnp.int32)
    slot_of = jnp.sum((jnp.cumsum(onehot, axis=0) - onehot) * onehot, axis=1)
    target = flat_ids % EXP_DEV * rows_total + flat_ids // EXP_DEV * capacity + slot_of
    slot_table = (
        jnp.full((EXP_DEV * rows_total,), choices, jnp.int32)
        .at[target]
        .set(jnp.arange(choices, dtype=jnp.int32))
        .reshape(EXP_DEV, groups, capacity)
    )
    mid_padded = jnp.concatenate([mid_low, jnp.zeros((1, model_width), jnp.bfloat16)], axis=0)
    outgoing = mid_padded[slot_table.reshape(-1) // TOPK].reshape(EXP_DEV, rows_total, model_width)
    expert_rows = lax.all_to_all(outgoing, "ep", split_axis=1, concat_axis=1, tiled=True)
    expert_gate = jnp.einsum(
        "erd,edf->erf", expert_rows, expert_gate_up[:, 0], preferred_element_type=jnp.float32
    )
    expert_upper = jnp.einsum(
        "erd,edf->erf", expert_rows, expert_gate_up[:, 1], preferred_element_type=jnp.float32
    )
    expert_sig = jax.nn.sigmoid(expert_gate)
    expert_hidden = (expert_gate * expert_sig * expert_upper).astype(jnp.bfloat16)
    expert_part = jnp.einsum(
        "erf,efd->erd", expert_hidden, expert_down, preferred_element_type=jnp.float32
    ).astype(jnp.bfloat16)
    returned = lax.all_to_all(expert_part, "ep", split_axis=1, concat_axis=1, tiled=True)
    per_choice = (
        returned.reshape(-1, model_width)[target]
        .reshape(tokens, TOPK, model_width)
        .astype(jnp.float32)
    )
    routed_part = jnp.sum(gating[:, :, None] * per_choice, axis=1)
    moe_out = lax.psum((shared_part + routed_part).astype(jnp.bfloat16), "tp").astype(jnp.float32)
    block_out = (resid + moe_out).astype(jnp.bfloat16)
    grad_top = out_grad.astype(jnp.float32)
    choice_grad = (gating[:, :, None] * grad_top[:, None, :]).astype(jnp.bfloat16)
    grad_padded = jnp.concatenate(
        [choice_grad.reshape(choices, model_width), jnp.zeros((1, model_width), jnp.bfloat16)],
        axis=0,
    )
    outgoing_grad = grad_padded[slot_table.reshape(-1)].reshape(EXP_DEV, rows_total, model_width)
    rows_grad = lax.all_to_all(outgoing_grad, "ep", split_axis=1, concat_axis=1, tiled=True)
    hidden_grad = jnp.einsum(
        "erd,efd->erf", rows_grad, expert_down, preferred_element_type=jnp.float32
    )
    gate_grad = (
        hidden_grad * expert_upper * expert_sig * (1.0 + expert_gate * (1.0 - expert_sig))
    ).astype(jnp.bfloat16)
    upper_grad = (hidden_grad * expert_gate * expert_sig).astype(jnp.bfloat16)
    grad_expert_down = jnp.einsum(
        "erf,erd->efd", expert_hidden, rows_grad, preferred_element_type=jnp.float32
    )
    grad_expert_gate_up = jnp.stack(
        [
            jnp.einsum("erd,erf->edf", expert_rows, gate_grad, preferred_element_type=jnp.float32),
            jnp.einsum("erd,erf->edf", expert_rows, upper_grad, preferred_element_type=jnp.float32),
        ],
        axis=1,
    )
    row_back = jnp.einsum(
        "erf,edf->erd", gate_grad, expert_gate_up[:, 0], preferred_element_type=jnp.float32
    ) + jnp.einsum(
        "erf,edf->erd", upper_grad, expert_gate_up[:, 1], preferred_element_type=jnp.float32
    )
    row_back_low = row_back.astype(jnp.bfloat16)
    back_rows = lax.all_to_all(row_back_low, "ep", split_axis=1, concat_axis=1, tiled=True)
    choice_back = (
        back_rows.reshape(-1, model_width)[target]
        .reshape(tokens, TOPK, model_width)
        .astype(jnp.float32)
    )
    mid_grad_routed = jnp.sum(choice_back, axis=1)
    gating_grad_part = jnp.sum(per_choice * grad_top[:, None, :], axis=2)
    shared_hidden_grad = transposed_right(out_grad, shared_down_full)
    shared_gate_grad = (
        shared_hidden_grad * shared_upper * shared_sig * (1.0 + shared_gate * (1.0 - shared_sig))
    ).astype(jnp.bfloat16)
    shared_upper_grad = (shared_hidden_grad * shared_gate * shared_sig).astype(jnp.bfloat16)
    grad_shared_down = transposed_left(shared_hidden, out_grad)
    grad_shared_gu = jnp.stack(
        [transposed_left(mid_low, shared_gate_grad), transposed_left(mid_low, shared_upper_grad)],
        axis=0,
    )
    mid_grad_shared = transposed_right(shared_gate_grad, shared_gu_full[0]) + transposed_right(
        shared_upper_grad, shared_gu_full[1]
    )
    mid_grad_sum, gating_grad = (
        lax.psum((mid_grad_routed + mid_grad_shared).astype(jnp.bfloat16), "tp").astype(
            jnp.float32
        ),
        lax.psum(gating_grad_part.astype(jnp.bfloat16), "tp").astype(jnp.float32),
    )
    weighted = jnp.sum(gating_grad * sigmoids, axis=1, keepdims=True) / sigmoid_total
    sigmoid_grad = ROUTE_SCALE / sigmoid_total * (gating_grad - weighted)
    chosen_grad = sigmoid_grad * sigmoids * (1.0 - sigmoids)
    logits_grad = jnp.sum(route_mask * chosen_grad[:, :, None], axis=1).astype(jnp.bfloat16)
    grad_router = transposed_left(mid_low, logits_grad)
    mid_grad = mid_grad_sum + transposed_right(logits_grad, router_full)
    resid_norm_grad, grad_gain_mid = norm_backward(mid_grad, unit_mid, inverse_mid, gain_rows[1])
    resid_grad = grad_top + resid_norm_grad
    attn_grad = resid_grad.astype(jnp.bfloat16)
    grad_output = transposed_left(attended, attn_grad)
    attended_grad = (
        transposed_right(attn_grad, output_full)
        .astype(jnp.bfloat16)
        .reshape(tokens, heads_local, V_DIM)
    )
    softmax_probs = jnp.exp(attention_scores() - log_total)
    values_grad = jnp.einsum(
        "hqk,qhd->khd",
        softmax_probs.astype(jnp.bfloat16),
        attended_grad,
        preferred_element_type=jnp.float32,
    )
    probs_grad = jnp.einsum(
        "qhd,khd->hqk", attended_grad, values, preferred_element_type=jnp.float32
    )
    scores_grad = (
        softmax_probs * (probs_grad - jnp.sum(softmax_probs * probs_grad, axis=-1, keepdims=True))
    ).astype(jnp.bfloat16)
    query_grad = (
        jnp.einsum("hqk,khd->qhd", scores_grad, key_rows, preferred_element_type=jnp.float32)
        * score_scale
    )
    keys_grad = (
        jnp.einsum("hqk,qhd->khd", scores_grad, queries, preferred_element_type=jnp.float32)
        * score_scale
    )
    query_raw_grad = (
        jnp.concatenate(
            [
                query_grad[..., :NOPE],
                rotate(query_grad[..., NOPE:], cosine_table[:, None, :], -sine_table[:, None, :]),
            ],
            axis=-1,
        )
        .astype(jnp.bfloat16)
        .reshape(tokens, heads_local * (NOPE + ROPE))
    )
    expanded_grad = jnp.concatenate([keys_grad[..., :NOPE], values_grad], axis=-1).astype(
        jnp.bfloat16
    )
    expanded_grad = expanded_grad.reshape(tokens, heads_local * (NOPE + V_DIM))
    grad_expand = transposed_left(latent_low, expanded_grad)
    latent_normed_grad = transposed_right(expanded_grad, expand_full)
    latent_part_grad, gain_latent_part = norm_backward(
        latent_normed_grad, latent_unit, latent_inverse, gain_latent
    )
    rope_raw_grad = rotate(jnp.sum(keys_grad[..., NOPE:], axis=1), cosine_table, -sine_table)
    latent_grad_part = jnp.concatenate([latent_part_grad, rope_raw_grad], axis=1)
    in_grad_query = transposed_right(query_raw_grad, query_full)
    in_grad_sum, latent_grad, grad_gain_latent = (
        lax.psum(in_grad_query.astype(jnp.bfloat16), "tp").astype(jnp.float32),
        lax.psum(latent_grad_part.astype(jnp.bfloat16), "tp").astype(jnp.float32),
        lax.psum(gain_latent_part.astype(jnp.bfloat16), "tp").astype(jnp.float32),
    )
    latent_grad_low = latent_grad.astype(jnp.bfloat16)
    grad_latent = transposed_left(normed_low, latent_grad_low)
    grad_query = transposed_left(normed_low, query_raw_grad)
    in_grad = in_grad_sum + transposed_right(latent_grad_low, latent_full)
    input_norm_grad, grad_gain_in = norm_backward(in_grad, unit_in, inverse_in, gain_rows[0])
    grad_hidden = resid_grad + input_norm_grad
    grad_gains = jnp.stack([grad_gain_in, grad_gain_mid], axis=0)
    (
        grad_query_out,
        grad_latent_out,
        grad_expand_out,
        grad_output_out,
        grad_gains_out,
        grad_gain_latent_out,
        grad_router_out,
        grad_shared_gu_out,
        grad_shared_down_out,
    ) = (
        lax.psum_scatter(
            grad_query.astype(jnp.bfloat16), "ep", scatter_dimension=0, tiled=True
        ).astype(jnp.float32),
        lax.psum_scatter(
            grad_latent.astype(jnp.bfloat16), "ep", scatter_dimension=0, tiled=True
        ).astype(jnp.float32),
        lax.psum_scatter(
            grad_expand.astype(jnp.bfloat16), "ep", scatter_dimension=0, tiled=True
        ).astype(jnp.float32),
        lax.psum_scatter(
            grad_output.astype(jnp.bfloat16), "ep", scatter_dimension=1, tiled=True
        ).astype(jnp.float32),
        lax.psum_scatter(
            grad_gains.astype(jnp.bfloat16), "ep", scatter_dimension=1, tiled=True
        ).astype(jnp.float32),
        lax.psum_scatter(
            grad_gain_latent.astype(jnp.bfloat16), "ep", scatter_dimension=0, tiled=True
        ).astype(jnp.float32),
        lax.psum_scatter(
            grad_router.astype(jnp.bfloat16), "ep", scatter_dimension=0, tiled=True
        ).astype(jnp.float32),
        lax.psum_scatter(
            grad_shared_gu.astype(jnp.bfloat16), "ep", scatter_dimension=1, tiled=True
        ).astype(jnp.float32),
        lax.psum_scatter(
            grad_shared_down.astype(jnp.bfloat16), "ep", scatter_dimension=1, tiled=True
        ).astype(jnp.float32),
    )
    return (
        block_out,
        grad_hidden,
        grad_query_out,
        grad_latent_out,
        grad_expand_out,
        grad_output_out,
        grad_gains_out,
        grad_gain_latent_out,
        grad_router_out,
        grad_shared_gu_out,
        grad_shared_down_out,
        grad_expert_gate_up,
        grad_expert_down,
    )


CUTS = 4
GATHERS = 2
LANES = 128
VMEM_BYTES = 56 * 1024 * 1024


def swap(array, axis, bit):
    size = lax.axis_size(axis)
    return lax.ppermute(array, axis, [(place, place ^ bit) for place in range(size)])


def axis_bits(axis):
    size = lax.axis_size(axis)
    return [(axis, 1 << bit) for bit in reversed(range(size.bit_length() - 1))]


def spread(rows, steps):
    for axis, bit in steps:
        rows = jnp.concatenate([rows, swap(rows, axis, bit)], axis=0)
    return rows


def add_rounded(left_side, right_side):
    return (left_side.astype(jnp.float32) + right_side.astype(jnp.float32)).astype(
        left_side.dtype
    )


def fold_step(rows, step):
    axis, bit = step
    half = rows.shape[0] // 2
    return add_rounded(rows[:half], swap(rows[half:], axis, bit))


def fold(rows, steps):
    for step in reversed(steps):
        rows = fold_step(rows, step)
    return rows


def distances(steps):
    found = [0]
    for _, bit in steps:
        found = found + [distance + bit for distance in found]
    return found


def by_distance(blocks, place, order):
    return jnp.concatenate(
        [lax.dynamic_slice_in_dim(blocks, place ^ i, 1, axis=0) for i in order], axis=0
    )


def by_place(blocks, place, order):
    natural = jnp.concatenate([blocks[order.index(i)][None] for i in range(len(order))], axis=0)
    return by_distance(natural, place, range(len(order)))


def ring_owner(spot, size):
    return jnp.where(spot < size // 2, 2 * spot, 2 * (size - 1 - spot) + 1)


def ring_spot(place, size):
    return jnp.where(place % 2 == 0, place // 2, size - 1 - place // 2)


def ring_shift(array, axis, by):
    size = lax.axis_size(axis)
    ring = [2 * i for i in range(size // 2)] + [2 * i + 1 for i in reversed(range(size // 2))]
    return lax.ppermute(array, axis, [(ring[i], ring[(i + by) % size]) for i in range(size)])


def ring_gather(array, axis):
    size = lax.axis_size(axis)
    found = [array] + [None] * (size - 1)
    ahead = behind = array
    for k in range(1, size // 2 + 1):
        behind = ring_shift(behind, axis, 1)
        found[size - k] = behind
        if k < size - k:
            ahead = ring_shift(ahead, axis, -1)
            found[k] = ahead
    return found


def ring_begin(parts, axis):
    size = lax.axis_size(axis)
    half = size // 2
    left = [(parts[half - k], parts[half + 1 + k] if k < half - 1 else None) for k in range(1, half)]
    return (parts[half], parts[half + 1]), left + [(parts[0], None)]


def ring_round(ring, axis):
    (ahead, behind), left = ring
    more_ahead, more_behind = left[0]
    ahead = add_rounded(ring_shift(ahead, axis, 1), more_ahead)
    if behind is not None and len(left) > 1:
        behind = ring_shift(behind, axis, -1)
        if more_behind is not None:
            behind = add_rounded(behind, more_behind)
    return (ahead, behind), left[1:]


def ring_end(ring, axis):
    (ahead, behind), left = ring
    while left:
        if len(left) == 1:
            found = ring_shift(ahead, axis, 1).astype(jnp.float32) + left[0][0]
            return found + behind
        (ahead, behind), left = ring_round(((ahead, behind), left), axis)
    return ahead.astype(jnp.float32) + behind


def pad_columns(array, width):
    return jnp.pad(array, ((0, 0), (0, width - array.shape[1])))


def pad_rows(array, height):
    return jnp.pad(array, ((0, height - array.shape[0]), (0, 0)))


def round_up(size, step=LANES):
    return -(-size // step) * step


def feed_forward_kernel(count, wide_steps, sub, *refs):
    first_ref, slot_ref, rows_ref, raw_ref, mask_ref, router_ref, tiles_ref = refs[:7]
    back_out, gate_ref, upper_ref, hidden_ref = refs[7:11]
    gains, shares, kept, tiles, back_ref, arrived, back_left = refs[11:]
    cut, step, last = pl.program_id(0), pl.program_id(1), count + wide_steps - 1
    owners, _, each, width = rows_ref.shape
    half, rows = raw_ref.shape[3], owners * each
    block = sub // each
    f32, bf16 = jnp.float32, jnp.bfloat16

    def arrival(n):
        return pltpu.make_async_copy(tiles_ref.at[n], tiles.at[n], arrived.at[n])

    def back_leaving(n):
        size = width // wide_steps
        extra = back_ref.shape[2] - width if n == wide_steps - 1 else 0
        of = (slice(None), slice(None), pl.ds(n * size, size + extra))
        return pltpu.make_async_copy(back_ref.at[of], back_out.at[(cut, *of)], back_left.at[n])

    @pl.when(step == 0)
    def _():
        @pl.when(cut == 0)
        def _():
            for n in range(count):
                arrival(n).start()

        values = rows_ref[...].reshape(rows, width)
        logits = jnp.dot(values, router_ref[...], preferred_element_type=f32)
        sig = jax.nn.sigmoid(logits) * mask_ref[...].reshape(logits.shape)
        gating = ROUTE_SCALE * sig / jnp.sum(sig, axis=1, keepdims=True)
        lanes = lax.broadcasted_iota(jnp.int32, gating.shape, 1)
        for e in range(EXP_DEV):
            own = jnp.sum(jnp.where(lanes == first_ref[0] + e, gating, 0.0), axis=1, keepdims=True)
            gains[e] = jnp.broadcast_to(own, gains.shape[1:])
        gains[EXP_DEV] = jnp.ones(gains.shape[1:], f32)
        shares[...] = jnp.zeros_like(shares)

    @pl.when(step < count)
    def _():
        @pl.when(cut == 0)
        def _():
            arrival(step).wait()

        kind = jnp.minimum(step // ((count - 1) // EXP_DEV), EXP_DEV)
        for i in range(rows // sub):
            at, of = pl.ds(i * sub, sub), pl.ds(i * block, block)
            values = rows_ref[of].reshape(sub, width)
            both = lax.dot_general(
                values, tiles[step], (((1,), (1,)), ((), ())), preferred_element_type=f32
            )
            gate, upper = both[:, :half], both[:, half:]
            gain, raw = gains[kind, at, :], raw_ref[of].reshape(sub, half).astype(f32)
            sig = jax.nn.sigmoid(gate)
            silu = gate * sig
            hidden = silu * upper
            grad = gain * raw
            shape = (block, 1, each, half)
            hidden_ref[of] = (gain * hidden).astype(bf16).reshape(shape)
            shares[kind, at, :] += hidden * raw
            gate_grad = (grad * upper * (sig + silu * (1.0 - sig))).astype(bf16)
            upper_grad = (grad * silu).astype(bf16)
            gate_ref[of] = gate_grad.reshape(shape)
            upper_ref[of] = upper_grad.reshape(shape)
            kept[step, at, :half] = gate_grad
            kept[step, at, half:] = upper_grad

    @pl.when(step >= count)
    def _():
        size = width // wide_steps
        columns = pl.ds(pl.multiple_of((step - count) * size, size), size)
        for i in range(rows // sub):
            found = sum(
                jnp.dot(
                    kept[n, pl.ds(i * sub, sub), :],
                    tiles[n, :, columns],
                    preferred_element_type=f32,
                )
                for n in range(count)
            ).astype(bf16)
            for j in range(block):
                part = found[j * each : (j + 1) * each]
                back_ref[slot_ref[cut, i * block + j], :, columns] = part

    @pl.when(step == last)
    def _():
        extra = back_ref.shape[2] - width
        lanes = lax.broadcasted_iota(jnp.int32, (rows, extra), 1)
        gating_grad = jnp.zeros(lanes.shape, f32)
        for e in range(EXP_DEV):
            own = jnp.sum(shares[e], axis=1, keepdims=True)
            gating_grad += jnp.where(lanes == first_ref[0] + e, own, 0.0)
        gating_grad = gating_grad.astype(bf16)
        for i in range(owners):
            back_ref[slot_ref[cut, i], :, width:] = gating_grad[i * each : (i + 1) * each]

    for n in range(wide_steps):

        @pl.when(step == count + n)
        def _(n=n):
            back_leaving(n).start()

    @pl.when(step == last)
    def _():
        for n in range(wide_steps):
            back_leaving(n).wait()


def feed_forward(slots, mid_rows, raw_grad, mask, router, tiles, first):
    count, both, width = tiles.shape
    owners, cuts, each, experts = mask.shape
    rows, half, wide_steps = owners * each, both // 2, 4
    bf16, f32 = jnp.bfloat16, jnp.float32

    def tile(step):
        return jnp.minimum(step, count - 1)

    smem, whole = pl.BlockSpec(memory_space=pltpu.SMEM), pl.BlockSpec(memory_space=pl.ANY)
    side = pl.BlockSpec((owners, 1, each, half), lambda c, i: (0, c, 0, tile(i)))
    return pl.pallas_call(
        functools.partial(feed_forward_kernel, count, wide_steps, min(8, owners) * each),
        grid=(cuts, count + wide_steps),
        in_specs=[
            smem,
            smem,
            pl.BlockSpec((owners, 1, each, width), lambda c, i: (0, c, 0, 0)),
            side,
            pl.BlockSpec((owners, 1, each, experts), lambda c, i: (0, c, 0, 0)),
            pl.BlockSpec((width, experts), lambda c, i: (0, 0)),
            whole,
        ],
        out_specs=[whole, side, side, side],
        out_shape=[
            jax.ShapeDtypeStruct((cuts, owners, each, width + LANES), bf16),
            *[jax.ShapeDtypeStruct((owners, cuts, each, count * half), bf16)] * 3,
        ],
        scratch_shapes=[
            pltpu.VMEM((EXP_DEV + 1, rows, half), f32),
            pltpu.VMEM((EXP_DEV + 1, rows, half), f32),
            pltpu.VMEM((count, rows, both), bf16),
            pltpu.VMEM(tiles.shape, bf16),
            pltpu.VMEM((owners, each, width + LANES), bf16),
            pltpu.SemaphoreType.DMA((count,)),
            pltpu.SemaphoreType.DMA((wide_steps,)),
        ],
        compiler_params=pltpu.CompilerParams(vmem_limit_bytes=VMEM_BYTES),
        cost_estimate=pl.CostEstimate(
            flops=4 * cuts * rows * width * both * count,
            bytes_accessed=50_000_000,
            transcendentals=0,
        ),
    )(first, slots, mid_rows, raw_grad, mask, router, tiles)


def rows_by_device_kernel(*refs):
    *left_refs, right_ref, out_ref = refs
    for i, left_ref in enumerate(left_refs):

        @pl.when(pl.program_id(1) == i)
        def _(left_ref=left_ref):
            found = jnp.dot(left_ref[...], right_ref[...], preferred_element_type=jnp.float32)
            out_ref[...] = found.astype(out_ref.dtype).reshape(out_ref.shape)


def rows_by_device(left_parts, right_side, devices):
    rows, depth = left_parts[0].shape
    columns, count = right_side.shape[1], len(left_parts)
    wide = columns // 2
    return pl.pallas_call(
        rows_by_device_kernel,
        grid=(2, count),
        in_specs=[pl.BlockSpec((rows, depth), lambda j, i: (0, 0))] * count
        + [pl.BlockSpec((depth, wide), lambda j, i: (0, j))],
        out_specs=pl.BlockSpec((devices, 1, rows // devices, wide), lambda j, i: (0, i, 0, j)),
        out_shape=jax.ShapeDtypeStruct(
            (devices, count, rows // devices, columns), right_side.dtype
        ),
        compiler_params=pltpu.CompilerParams(vmem_limit_bytes=VMEM_BYTES),
        cost_estimate=pl.CostEstimate(
            flops=2 * count * rows * depth * columns,
            bytes_accessed=2 * count * rows * (depth + columns),
            transcendentals=0,
        ),
    )(*left_parts, right_side).reshape(count * rows, columns)


def place_kernel(places_ref, *refs):
    *pieces, out_ref = refs
    for i, piece in enumerate(pieces):

        @pl.when(pl.program_id(0) == i)
        def _(piece=piece):
            out_ref[0] = piece[...]


def place_blocks(pieces, places):
    shape = pieces[0].shape
    return pl.pallas_call(
        place_kernel,
        grid_spec=pltpu.PrefetchScalarGridSpec(
            num_scalar_prefetch=1,
            grid=(len(pieces),),
            in_specs=[pl.BlockSpec(shape, lambda i, at: (0, 0))] * len(pieces),
            out_specs=pl.BlockSpec((1, *shape), lambda i, at: (at[i], 0, 0)),
        ),
        out_shape=jax.ShapeDtypeStruct((len(pieces), *shape), pieces[0].dtype),
        compiler_params=pltpu.CompilerParams(vmem_limit_bytes=VMEM_BYTES),
    )(jnp.stack(places).astype(jnp.int32), *pieces)


def on_device_dense(
    hidden_in,
    out_grad,
    query_weight,
    latent_weight,
    expand_weight,
    output_weight,
    norm_gains,
    latent_gain,
    router_weight,
    shared_gate_up,
    shared_down,
    expert_gate_up,
    expert_down,
    expert_ids,
):
    groups, parts = lax.axis_size("ep"), lax.axis_size("tp")
    group, part = lax.axis_index("ep"), lax.axis_index("tp")
    tokens, width = hidden_in.shape
    own = tokens // parts
    experts = router_weight.shape[1]
    bf16, f32 = jnp.bfloat16, jnp.float32
    ep_steps, tp_steps = axis_bits("ep"), axis_bits("tp")
    tp_order = distances(tp_steps)
    every = ("ep", "tp")
    devices = groups * parts
    cut_rows = own // CUTS

    spot = ring_spot(group, groups)
    ring_groups = [ring_owner((spot + k) % groups, groups) for k in range(groups)]

    mask_own = jnp.sum(
        (expert_ids[:, :, None] == jnp.arange(experts)[None, None, :]).astype(bf16), axis=1
    )
    sizes = [norm_gains.size, latent_gain.size, router_weight.size, mask_own.size]
    small = jnp.concatenate(
        [array.reshape(1, -1) for array in (norm_gains, latent_gain, router_weight, mask_own)],
        axis=1,
    )
    small_rel = spread(small, ep_steps)
    at = [sum(sizes[:i]) for i in range(len(sizes) + 1)]
    small_full = by_place(small_rel, group, distances(ep_steps))
    gain_rows = (
        small_full[:, : at[1]].reshape(groups, 2, -1).transpose(1, 0, 2).reshape(2, width)
    ).astype(f32)
    gain_latent = small_full[:, at[1] : at[2]].reshape(-1).astype(f32)
    router_full = small_full[:, at[2] : at[3]].reshape(width, experts)

    query_size, latent_width = query_weight.shape[1], latent_weight.shape[1]
    output_size = output_weight.shape[0]
    into_size = round_up(query_size + latent_width)
    into = pad_columns(jnp.concatenate([query_weight, latent_weight], axis=1), into_size)
    out_of = jnp.concatenate(
        [output_weight.T, expand_weight.reshape(output_weight.shape[1], -1)], axis=1
    )
    into_pieces = ring_gather(into, "ep")
    into_full = place_blocks(into_pieces, ring_groups).reshape(width, -1)
    out_of_full = place_blocks(ring_gather(out_of, "ep"), ring_groups).reshape(width, -1)
    expand_full = out_of_full[:, output_size:].reshape(KV_RANK, -1)
    output_turned = out_of_full[:, :output_size]

    units = shared_down.shape[0] // groups
    shared_gu_own = lax.all_to_all(
        shared_gate_up.reshape(2, -1, groups, units), "ep", split_axis=2, concat_axis=1, tiled=True
    ).reshape(2, width, units)
    shared_down_own = lax.all_to_all(shared_down, "ep", split_axis=0, concat_axis=1, tiled=True)

    hidden_units = expert_down.shape[1]
    expert_pad, shared_pad = round_up(hidden_units), round_up(units)
    side_weights = [
        jnp.concatenate(
            [pad_rows(expert_gate_up[e, side].T, expert_pad) for e in range(EXP_DEV)]
            + [pad_rows(shared_gu_own[side].T, shared_pad)],
            axis=0,
        ).reshape(-1, LANES, width)
        for side in range(2)
    ]
    tiles = jnp.concatenate(side_weights, axis=1)
    down_weight = jnp.concatenate(
        [pad_rows(expert_down[e], expert_pad) for e in range(EXP_DEV)]
        + [pad_rows(shared_down_own, shared_pad)],
        axis=0,
    )

    into_full, tiles, down_weight = lax.optimization_barrier((into_full, tiles, down_weight))
    out_grad_late, _ = lax.optimization_barrier((out_grad, into_pieces[groups // 2]))

    gather_rows = own // GATHERS
    cuts = CUTS // GATHERS

    def by_gather(rows):
        rows = rows.reshape(devices, GATHERS, gather_rows, -1).transpose(1, 0, 2, 3)
        return list(rows.reshape(GATHERS, devices * gather_rows, -1))

    grad_own = lax.dynamic_slice_in_dim(out_grad_late, part * own, own, axis=0)
    grad_parts = by_gather(lax.all_gather(grad_own, every, axis=0, tiled=True))
    raw_parts = [
        transposed_right(rows, down_weight).astype(bf16).reshape(devices, cuts, cut_rows, -1)
        for rows in grad_parts
    ]
    mask_parts = [
        rows.astype(f32).reshape(devices, cuts, cut_rows, experts)
        for rows in by_gather(small_full[:, at[3] :])
    ]

    row_blocks = hidden_in.reshape(parts, own, width)
    hidden_rel = by_distance(row_blocks, part, tp_order).reshape(tokens, width)
    heads_local = query_size // (NOPE + ROPE)
    places = ((part ^ jnp.array(tp_order))[:, None] * own + jnp.arange(own)[None, :]).reshape(-1)
    frequency = ROPE_BASE ** (-(jnp.arange(ROPE // 2).astype(f32) * 2.0 / ROPE))
    angles = places.astype(f32)[:, None] * frequency[None, :]
    cosine_table = jnp.cos(angles)
    sine_table = jnp.sin(angles)
    normed_in, unit_in, inverse_in = norm_forward(hidden_rel.astype(f32), gain_rows[0])
    normed_low = normed_in.astype(bf16)
    both_in = matmul(normed_low, into_full)
    query_raw = both_in[:, :query_size].reshape(tokens, heads_local, NOPE + ROPE)
    queries = jnp.concatenate(
        [
            query_raw[..., :NOPE],
            rotate(query_raw[..., NOPE:], cosine_table[:, None, :], sine_table[:, None, :]),
        ],
        axis=-1,
    ).astype(bf16)
    latent = both_in[:, query_size : query_size + latent_width]
    latent_normed, latent_unit, latent_inverse = norm_forward(latent[:, :KV_RANK], gain_latent)
    latent_low = latent_normed.astype(bf16)
    key_rope = rotate(latent[:, KV_RANK:], cosine_table, sine_table).astype(bf16)
    expanded = (
        matmul(latent_low, expand_full).astype(bf16).reshape(tokens, heads_local, NOPE + V_DIM)
    )
    key_rows = jnp.concatenate(
        [expanded[..., :NOPE], jnp.broadcast_to(key_rope[:, None, :], (tokens, heads_local, ROPE))],
        axis=-1,
    )
    values = expanded[..., NOPE:]
    score_scale = 1.0 / math.sqrt(NOPE + ROPE)
    causal = places[:, None] >= places[None, :]
    scores = (
        jnp.einsum("qhd,khd->hqk", queries, key_rows, preferred_element_type=f32) * score_scale
    )
    scores = jnp.where(causal[None], scores, -1e30)
    row_max = jnp.max(scores, axis=-1, keepdims=True)
    powers = jnp.exp(scores - row_max)
    softmax_probs = powers / jnp.sum(powers, axis=-1, keepdims=True)
    probs_low = softmax_probs.astype(bf16)
    attended = jnp.einsum("hqk,khd->qhd", probs_low, values, preferred_element_type=f32)
    attended = attended.astype(bf16).reshape(tokens, heads_local * V_DIM)
    attn_part = transposed_right(attended, output_turned).astype(bf16)
    resid = hidden_rel[:own].astype(f32) + fold(attn_part, tp_steps).astype(f32)

    normed_mid, unit_mid, inverse_mid = norm_forward(resid, gain_rows[1])
    mid_own = normed_mid.astype(bf16)
    first = (group * EXP_DEV).astype(jnp.int32).reshape(1)
    mid_parts = [
        lax.all_gather(
            mid_own[i * gather_rows : (i + 1) * gather_rows], every, axis=0, tiled=True
        )
        for i in range(GATHERS)
    ]
    one_order = (ep_steps + tp_steps)[::-1]
    turn = [0, *range(2, len(tp_steps) + 1), 1, *range(len(tp_steps) + 1, len(one_order))]
    orders = [one_order, [one_order[i] for i in turn]]
    distance = jnp.arange(devices, dtype=jnp.int32) ^ (group * parts + part)
    slots = []
    for order in orders:
        slot = jnp.zeros_like(distance)
        for axis, bit in order:
            slot = 2 * slot + distance // (bit * (parts if axis == "ep" else 1)) % 2
        slots.append(slot)
    slots = jnp.stack([slots[cut % 2] for cut in range(cuts)])

    def on_a_step(sums):
        return [(fold_step(rows, todo[0]), todo[1:]) if todo else (rows, todo) for rows, todo in sums]

    def together(work, sums):
        work, rows = lax.optimization_barrier((work, [rows for rows, _ in sums]))
        return work, [(each, todo) for each, (_, todo) in zip(rows, sums)]

    sums, grad_down, grad_gate, grad_upper, hidden_parts = [], None, None, None, []

    def plus(total, left_side, right_side):
        found = transposed_left(left_side, right_side)
        return found if total is None else total + found

    for mid_rows, raw_grad, mask, grad_rows in zip(mid_parts, raw_parts, mask_parts, grad_parts):
        shape = (devices, cuts, cut_rows, width)
        back, *sides = feed_forward(
            slots, mid_rows.reshape(shape), raw_grad, mask, router_full, tiles, first
        )
        (back, sides), sums = together((back, sides), on_a_step(sums))
        sums += [(back[cut], orders[cut % 2]) for cut in range(cuts)]
        gate_rows, upper_rows, hidden_rows = [side.reshape(mid_rows.shape[0], -1) for side in sides]
        hidden_parts.append(hidden_rows)
        grad_down = plus(grad_down, hidden_rows, grad_rows)
        grad_down, sums = together(grad_down, on_a_step(sums))
        grad_gate = plus(grad_gate, gate_rows, mid_rows)
        grad_gate, sums = together(grad_gate, on_a_step(sums))
        grad_upper = plus(grad_upper, upper_rows, mid_rows)
        grad_upper, sums = together(grad_upper, on_a_step(sums))
    while any(todo for _, todo in sums):
        sums = on_a_step(sums)
    back_own = jnp.concatenate([rows[0] for rows, _ in sums], axis=0)

    back_own = back_own.astype(f32)
    gating_grad = back_own[:, width : width + experts]
    mask = lax.dynamic_slice_in_dim(mask_own, part * own, own, axis=0).astype(f32)
    sigmoids = jax.nn.sigmoid(matmul(mid_own, router_full))
    chosen = sigmoids * mask
    sigmoid_total = jnp.sum(chosen, axis=1, keepdims=True)
    weighted = jnp.sum(gating_grad * chosen, axis=1, keepdims=True) / sigmoid_total
    sigmoid_grad = ROUTE_SCALE / sigmoid_total * (gating_grad - weighted)
    logits_grad = (sigmoid_grad * chosen * (1.0 - sigmoids)).astype(bf16)
    grad_router = transposed_left(mid_own, logits_grad)
    mid_grad = back_own[:, :width] + transposed_right(logits_grad, router_full)
    resid_norm_grad, grad_gain_mid = norm_backward(mid_grad, unit_mid, inverse_mid, gain_rows[1])
    resid_grad = grad_own.astype(f32) + resid_norm_grad

    resid_low, hidden_parts = lax.optimization_barrier((resid_grad.astype(bf16), hidden_parts))
    out_part = rows_by_device(hidden_parts, down_weight, devices)
    attn_rows, out_part = lax.optimization_barrier((spread(resid_low, tp_steps[:1]), out_part))
    out_own = lax.psum_scatter(out_part, every, scatter_dimension=0, tiled=True)
    block_own = (lax.optimization_barrier(resid) + out_own.astype(f32)).astype(bf16)
    attn_grad = spread(attn_rows, tp_steps[1:])

    def ring_columns(left_side, right_side):
        size = left_side.shape[1] // groups
        return [
            transposed_left(
                lax.dynamic_slice_in_dim(left_side, g * size, size, axis=1), right_side
            ).astype(bf16)
            for g in ring_groups
        ]

    def beside(work, rings):
        rounds = [ring_round(ring, "ep") for ring in rings]
        work, states = lax.optimization_barrier((work, [state for state, _ in rounds]))
        return work, [(state, left) for state, (_, left) in zip(states, rounds)]

    output_ring = ring_begin(ring_columns(attn_grad, attended), "ep")
    attended_grad = (
        matmul(attn_grad, output_turned).astype(bf16).reshape(tokens, heads_local, V_DIM)
    )
    values_grad = jnp.einsum("hqk,qhd->khd", probs_low, attended_grad, preferred_element_type=f32)
    probs_grad = jnp.einsum("qhd,khd->hqk", attended_grad, values, preferred_element_type=f32)
    scores_grad = (
        softmax_probs * (probs_grad - jnp.sum(softmax_probs * probs_grad, axis=-1, keepdims=True))
    ).astype(bf16)
    (scores_grad, values_grad), (output_ring,) = beside((scores_grad, values_grad), [output_ring])
    query_grad = (
        jnp.einsum("hqk,khd->qhd", scores_grad, key_rows, preferred_element_type=f32) * score_scale
    )
    keys_grad = (
        jnp.einsum("hqk,qhd->khd", scores_grad, queries, preferred_element_type=f32) * score_scale
    )
    query_raw_grad = (
        jnp.concatenate(
            [
                query_grad[..., :NOPE],
                rotate(query_grad[..., NOPE:], cosine_table[:, None, :], -sine_table[:, None, :]),
            ],
            axis=-1,
        )
        .astype(bf16)
        .reshape(tokens, heads_local * (NOPE + ROPE))
    )
    expanded_grad = (
        jnp.concatenate([keys_grad[..., :NOPE], values_grad], axis=-1)
        .astype(bf16)
        .reshape(tokens, heads_local * (NOPE + V_DIM))
    )
    latent_normed_grad = transposed_right(expanded_grad, expand_full)
    latent_part_grad, gain_latent_part = norm_backward(
        latent_normed_grad, latent_unit, latent_inverse, gain_latent
    )
    rope_raw_grad = rotate(jnp.sum(keys_grad[..., NOPE:], axis=1), cosine_table, -sine_table)
    latent_grad = jnp.concatenate([latent_part_grad, rope_raw_grad], axis=1).astype(bf16)
    both_grad = pad_columns(jnp.concatenate([query_raw_grad, latent_grad], axis=1), into_size)
    both_grad, (output_ring,) = beside(both_grad, [output_ring])
    into_ring = ring_begin(ring_columns(normed_low, both_grad), "ep")
    in_grad_part = transposed_right(both_grad, into_full).astype(bf16)
    expand_blocks = transposed_left(latent_low, expanded_grad).astype(bf16)
    expand_blocks = expand_blocks.reshape(groups, -1, expand_blocks.shape[1])
    expand_ring = ring_begin(
        [lax.dynamic_slice_in_dim(expand_blocks, g, 1, axis=0)[0] for g in ring_groups], "ep"
    )
    work = (in_grad_part, [left for _, left in (into_ring, expand_ring)])
    (in_grad_part, lefts), (into_ring, output_ring) = beside(work, [into_ring, output_ring])
    into_ring, expand_ring = (into_ring[0], lefts[0][1:]), (expand_ring[0], lefts[1])

    grad_sides = (grad_gate, grad_upper)
    shared_at = EXP_DEV * expert_pad
    grad_shared_gu = jnp.stack([grad[shared_at:][:units].T for grad in grad_sides]).astype(bf16)
    shared_down_part = grad_down[shared_at : shared_at + units].astype(bf16)
    grad_sides, grad_down, _ = lax.optimization_barrier((grad_sides, grad_down, in_grad_part))
    grad_expert_gate_up = jnp.stack(
        [
            jnp.stack([grad[e * expert_pad :][:hidden_units].T for grad in grad_sides])
            for e in range(EXP_DEV)
        ]
    )
    in_grad = fold_step(in_grad_part, tp_steps[-1])
    (grad_expert_gate_up, grad_shared_gu, in_grad), (into_ring, expand_ring, output_ring) = beside(
        (grad_expert_gate_up, grad_shared_gu, in_grad), [into_ring, expand_ring, output_ring]
    )
    grad_expert_down = jnp.stack(
        [grad_down[e * expert_pad : e * expert_pad + hidden_units] for e in range(EXP_DEV)]
    )
    grad_shared_gu_out = (
        lax.all_to_all(
            grad_shared_gu.reshape(2, width, 1, units),
            "ep",
            split_axis=1,
            concat_axis=2,
            tiled=True,
        )
        .reshape(shared_gate_up.shape)
        .astype(f32)
    )
    grad_shared_down_out = lax.all_to_all(
        shared_down_part,
        "ep",
        split_axis=1,
        concat_axis=0,
        tiled=True,
    ).astype(f32)

    in_grad = fold(in_grad, tp_steps[:-1]).astype(f32)
    (grad_expert_down, in_grad), (into_ring, expand_ring) = beside(
        (grad_expert_down, in_grad), [into_ring, expand_ring]
    )
    input_norm_grad, grad_gain_in = norm_backward(
        in_grad, unit_in[:own], inverse_in[:own], gain_rows[0]
    )
    hidden_own = (resid_grad + input_norm_grad).astype(bf16)
    into_sum = ring_end(into_ring, "ep")
    grad_expand_out = ring_end(expand_ring, "ep")
    grad_output_out = ring_end(output_ring, "ep").T
    grad_query_out = into_sum[:, :query_size]
    grad_latent_out = into_sum[:, query_size : query_size + latent_width]
    for axis, bit in tp_steps:
        rounded = grad_latent_out.astype(bf16)
        grad_latent_out = rounded.astype(f32) + swap(rounded, axis, bit).astype(f32)
    grad_small = jnp.concatenate(
        [
            jnp.stack([grad_gain_in, grad_gain_mid])
            .reshape(2, groups, -1)
            .transpose(1, 0, 2)
            .reshape(groups, -1),
            gain_latent_part.reshape(groups, -1),
            grad_router.reshape(groups, -1),
        ],
        axis=1,
    )
    small_sum = fold(by_distance(grad_small, group, distances(ep_steps)), ep_steps)
    for axis, bit in tp_steps:
        small_sum = small_sum + swap(small_sum, axis, bit)
    small_sum = small_sum.reshape(-1)
    grad_gains_out = small_sum[: at[1]].reshape(norm_gains.shape)
    grad_gain_latent_out = small_sum[at[1] : at[2]]
    grad_router_out = small_sum[at[2] : at[3]].reshape(router_weight.shape)

    def all_own(rows):
        return lax.all_gather(rows, "tp", axis=0, tiled=True)

    return (
        all_own(block_own),
        all_own(hidden_own).astype(f32),
        grad_query_out,
        grad_latent_out,
        grad_expand_out,
        grad_output_out,
        grad_gains_out,
        grad_gain_latent_out,
        grad_router_out,
        grad_shared_gu_out,
        grad_shared_down_out,
        grad_expert_gate_up,
        grad_expert_down,
    )


def power_of_two(size):
    return size & (size - 1) == 0


def on_device(hidden_in, *others):
    groups, parts = lax.axis_size("ep"), lax.axis_size("tp")
    tokens = hidden_in.shape[0]
    mean_load = tokens * TOPK // (EXP_DEV * groups)
    capacity = mean_load + mean_load // 3
    if EXP_DEV * capacity >= tokens and power_of_two(groups) and power_of_two(parts):
        return on_device_dense(hidden_in, *others)
    return on_device_sparse(hidden_in, *others)


def solution(mesh):
    placed = (
        P("ep", None),
        P("ep", None),
        P("ep", "tp"),
        P("ep", None),
        P("ep", "tp"),
        P("tp", "ep"),
        P(None, "ep"),
        P("ep"),
        P("ep", None),
        P(None, "ep", "tp"),
        P("tp", "ep"),
        P("ep", None, None, "tp"),
        P("ep", "tp", None),
        P("ep", None),
    )
    return jax.shard_map(
        on_device,
        mesh=mesh,
        in_specs=placed,
        out_specs=(
            P("ep", None),
            P("ep", None),
            P("ep", "tp"),
            P("ep", None),
            P("ep", "tp"),
            P("tp", "ep"),
            P(None, "ep"),
            P("ep"),
            P("ep", None),
            P(None, "ep", "tp"),
            P("tp", "ep"),
            P("ep", None, None, "tp"),
            P("ep", "tp", None),
        ),
        check_vma=False,
    )
```

```python
import functools
import math

import jax
import jax.numpy as jnp
from jax import lax
from jax.experimental import pallas as pl
from jax.experimental.pallas import tpu as pltpu
from jax.sharding import PartitionSpec as P

NOPE = 128
ROPE = 64
V_DIM = 128
KV_RANK = 512
TOPK = 6
EXP_DEV = 2


EPSILON = 1e-06
ROUTE_SCALE = 2.446
ROPE_BASE = 50000.0


def matmul(left_side, right_side):
    return jnp.dot(left_side, right_side, preferred_element_type=jnp.float32)


def transposed_left(left_side, right_side):
    return lax.dot_general(
        left_side, right_side, (((0,), (0,)), ((), ())), preferred_element_type=jnp.float32
    )


def transposed_right(left_side, right_side):
    return lax.dot_general(
        left_side, right_side, (((1,), (1,)), ((), ())), preferred_element_type=jnp.float32
    )


def rotate(values, cosine_table, sine_table):
    halfway = values.shape[-1] // 2
    first_half = values[..., :halfway]
    second_half = values[..., halfway:]
    return jnp.concatenate(
        [
            first_half * cosine_table - second_half * sine_table,
            second_half * cosine_table + first_half * sine_table,
        ],
        axis=-1,
    )


def norm_forward(values, gain_row):
    inverse = lax.rsqrt(jnp.mean(values * values, axis=-1, keepdims=True) + EPSILON)
    unit_rows = values * inverse
    return (unit_rows * gain_row, unit_rows, inverse)


def norm_backward(incoming, unit_rows, inverse, gain_row):
    scaled = incoming * gain_row
    grad_values = inverse * (
        scaled - unit_rows * jnp.mean(scaled * unit_rows, axis=-1, keepdims=True)
    )
    return (grad_values, jnp.sum(incoming * unit_rows, axis=0))


def on_device_sparse(
    hidden_in,
    out_grad,
    query_weight,
    latent_weight,
    expand_weight,
    output_weight,
    norm_gains,
    latent_gain,
    router_weight,
    shared_gate_up,
    shared_down,
    expert_gate_up,
    expert_down,
    expert_ids,
):
    (
        query_full,
        latent_full,
        expand_full,
        output_full,
        gains_full,
        latent_gain_full,
        router_full,
        shared_gu_full,
        shared_down_full,
    ) = (
        lax.all_gather(query_weight, "ep", axis=0, tiled=True),
        lax.all_gather(latent_weight, "ep", axis=0, tiled=True),
        lax.all_gather(expand_weight, "ep", axis=0, tiled=True),
        lax.all_gather(output_weight, "ep", axis=1, tiled=True),
        lax.all_gather(norm_gains, "ep", axis=1, tiled=True),
        lax.all_gather(latent_gain, "ep", axis=0, tiled=True),
        lax.all_gather(router_weight, "ep", axis=0, tiled=True),
        lax.all_gather(shared_gate_up, "ep", axis=1, tiled=True),
        lax.all_gather(shared_down, "ep", axis=1, tiled=True),
    )
    tokens = hidden_in.shape[0]
    model_width = hidden_in.shape[1]
    heads_local = query_full.shape[1] // (NOPE + ROPE)
    gain_rows = gains_full.astype(jnp.float32)
    gain_latent = latent_gain_full.astype(jnp.float32)
    places = jnp.arange(tokens).astype(jnp.float32)
    frequency = ROPE_BASE ** (-(jnp.arange(ROPE // 2).astype(jnp.float32) * 2.0 / ROPE))
    angles = places[:, None] * frequency[None, :]
    cosine_table = jnp.cos(angles)
    sine_table = jnp.sin(angles)
    resid_in = hidden_in.astype(jnp.float32)
    normed_in, unit_in, inverse_in = norm_forward(resid_in, gain_rows[0])
    normed_low = normed_in.astype(jnp.bfloat16)
    query_raw = matmul(normed_low, query_full).reshape(tokens, heads_local, NOPE + ROPE)
    queries = jnp.concatenate(
        [
            query_raw[..., :NOPE],
            rotate(query_raw[..., NOPE:], cosine_table[:, None, :], sine_table[:, None, :]),
        ],
        axis=-1,
    ).astype(jnp.bfloat16)
    latent = matmul(normed_low, latent_full)
    latent_normed, latent_unit, latent_inverse = norm_forward(latent[:, :KV_RANK], gain_latent)
    latent_low = latent_normed.astype(jnp.bfloat16)
    key_rope = rotate(latent[:, KV_RANK:], cosine_table, sine_table).astype(jnp.bfloat16)
    expanded = (
        matmul(latent_low, expand_full)
        .astype(jnp.bfloat16)
        .reshape(tokens, heads_local, NOPE + V_DIM)
    )
    key_rows = jnp.concatenate(
        [expanded[..., :NOPE], jnp.broadcast_to(key_rope[:, None, :], (tokens, heads_local, ROPE))],
        axis=-1,
    )
    values = expanded[..., NOPE:]
    score_scale = 1.0 / math.sqrt(NOPE + ROPE)
    causal = jnp.arange(tokens)[:, None] >= jnp.arange(tokens)[None, :]

    def attention_scores():
        scores = (
            jnp.einsum("qhd,khd->hqk", queries, key_rows, preferred_element_type=jnp.float32)
            * score_scale
        )
        return jnp.where(causal[None], scores, -1e30)

    scores_first = attention_scores()
    row_max = jnp.max(scores_first, axis=-1, keepdims=True)
    log_total = row_max + jnp.log(jnp.sum(jnp.exp(scores_first - row_max), axis=-1, keepdims=True))
    probs_low = jnp.exp(scores_first - log_total).astype(jnp.bfloat16)
    attended = jnp.einsum("hqk,khd->qhd", probs_low, values, preferred_element_type=jnp.float32)
    attended = attended.astype(jnp.bfloat16).reshape(tokens, heads_local * V_DIM)
    attn_out = lax.psum(matmul(attended, output_full), "tp")
    resid = resid_in + attn_out
    normed_mid, unit_mid, inverse_mid = norm_forward(resid, gain_rows[1])
    mid_low = normed_mid.astype(jnp.bfloat16)
    logits = matmul(mid_low, router_full)
    experts = router_full.shape[1]
    route_mask = (expert_ids[:, :, None] == jnp.arange(experts)[None, None, :]).astype(jnp.float32)
    chosen = jnp.sum(route_mask * logits[:, None, :], axis=2)
    sigmoids = jax.nn.sigmoid(chosen)
    sigmoid_total = jnp.sum(sigmoids, axis=1, keepdims=True)
    gating = ROUTE_SCALE * sigmoids / sigmoid_total
    shared_gate = matmul(mid_low, shared_gu_full[0])
    shared_upper = matmul(mid_low, shared_gu_full[1])
    shared_sig = jax.nn.sigmoid(shared_gate)
    shared_hidden = (shared_gate * shared_sig * shared_upper).astype(jnp.bfloat16)
    shared_part = matmul(shared_hidden, shared_down_full)
    groups = lax.axis_size("ep")
    mean_load = tokens * TOPK // (EXP_DEV * groups)
    capacity = mean_load + mean_load // 3
    choices = tokens * TOPK
    rows_total = groups * capacity
    flat_ids = expert_ids.reshape(-1)
    onehot = (flat_ids[:, None] == jnp.arange(experts)[None, :]).astype(jnp.int32)
    slot_of = jnp.sum((jnp.cumsum(onehot, axis=0) - onehot) * onehot, axis=1)
    target = flat_ids % EXP_DEV * rows_total + flat_ids // EXP_DEV * capacity + slot_of
    slot_table = (
        jnp.full((EXP_DEV * rows_total,), choices, jnp.int32)
        .at[target]
        .set(jnp.arange(choices, dtype=jnp.int32))
        .reshape(EXP_DEV, groups, capacity)
    )
    mid_padded = jnp.concatenate([mid_low, jnp.zeros((1, model_width), jnp.bfloat16)], axis=0)
    outgoing = mid_padded[slot_table.reshape(-1) // TOPK].reshape(EXP_DEV, rows_total, model_width)
    expert_rows = lax.all_to_all(outgoing, "ep", split_axis=1, concat_axis=1, tiled=True)
    expert_gate = jnp.einsum(
        "erd,edf->erf", expert_rows, expert_gate_up[:, 0], preferred_element_type=jnp.float32
    )
    expert_upper = jnp.einsum(
        "erd,edf->erf", expert_rows, expert_gate_up[:, 1], preferred_element_type=jnp.float32
    )
    expert_sig = jax.nn.sigmoid(expert_gate)
    expert_hidden = (expert_gate * expert_sig * expert_upper).astype(jnp.bfloat16)
    expert_part = jnp.einsum(
        "erf,efd->erd", expert_hidden, expert_down, preferred_element_type=jnp.float32
    ).astype(jnp.bfloat16)
    returned = lax.all_to_all(expert_part, "ep", split_axis=1, concat_axis=1, tiled=True)
    per_choice = (
        returned.reshape(-1, model_width)[target]
        .reshape(tokens, TOPK, model_width)
        .astype(jnp.float32)
    )
    routed_part = jnp.sum(gating[:, :, None] * per_choice, axis=1)
    moe_out = lax.psum((shared_part + routed_part).astype(jnp.bfloat16), "tp").astype(jnp.float32)
    block_out = (resid + moe_out).astype(jnp.bfloat16)
    grad_top = out_grad.astype(jnp.float32)
    choice_grad = (gating[:, :, None] * grad_top[:, None, :]).astype(jnp.bfloat16)
    grad_padded = jnp.concatenate(
        [choice_grad.reshape(choices, model_width), jnp.zeros((1, model_width), jnp.bfloat16)],
        axis=0,
    )
    outgoing_grad = grad_padded[slot_table.reshape(-1)].reshape(EXP_DEV, rows_total, model_width)
    rows_grad = lax.all_to_all(outgoing_grad, "ep", split_axis=1, concat_axis=1, tiled=True)
    hidden_grad = jnp.einsum(
        "erd,efd->erf", rows_grad, expert_down, preferred_element_type=jnp.float32
    )
    gate_grad = (
        hidden_grad * expert_upper * expert_sig * (1.0 + expert_gate * (1.0 - expert_sig))
    ).astype(jnp.bfloat16)
    upper_grad = (hidden_grad * expert_gate * expert_sig).astype(jnp.bfloat16)
    grad_expert_down = jnp.einsum(
        "erf,erd->efd", expert_hidden, rows_grad, preferred_element_type=jnp.float32
    )
    grad_expert_gate_up = jnp.stack(
        [
            jnp.einsum("erd,erf->edf", expert_rows, gate_grad, preferred_element_type=jnp.float32),
            jnp.einsum("erd,erf->edf", expert_rows, upper_grad, preferred_element_type=jnp.float32),
        ],
        axis=1,
    )
    row_back = jnp.einsum(
        "erf,edf->erd", gate_grad, expert_gate_up[:, 0], preferred_element_type=jnp.float32
    ) + jnp.einsum(
        "erf,edf->erd", upper_grad, expert_gate_up[:, 1], preferred_element_type=jnp.float32
    )
    row_back_low = row_back.astype(jnp.bfloat16)
    back_rows = lax.all_to_all(row_back_low, "ep", split_axis=1, concat_axis=1, tiled=True)
    choice_back = (
        back_rows.reshape(-1, model_width)[target]
        .reshape(tokens, TOPK, model_width)
        .astype(jnp.float32)
    )
    mid_grad_routed = jnp.sum(choice_back, axis=1)
    gating_grad_part = jnp.sum(per_choice * grad_top[:, None, :], axis=2)
    shared_hidden_grad = transposed_right(out_grad, shared_down_full)
    shared_gate_grad = (
        shared_hidden_grad * shared_upper * shared_sig * (1.0 + shared_gate * (1.0 - shared_sig))
    ).astype(jnp.bfloat16)
    shared_upper_grad = (shared_hidden_grad * shared_gate * shared_sig).astype(jnp.bfloat16)
    grad_shared_down = transposed_left(shared_hidden, out_grad)
    grad_shared_gu = jnp.stack(
        [transposed_left(mid_low, shared_gate_grad), transposed_left(mid_low, shared_upper_grad)],
        axis=0,
    )
    mid_grad_shared = transposed_right(shared_gate_grad, shared_gu_full[0]) + transposed_right(
        shared_upper_grad, shared_gu_full[1]
    )
    mid_grad_sum, gating_grad = (
        lax.psum((mid_grad_routed + mid_grad_shared).astype(jnp.bfloat16), "tp").astype(
            jnp.float32
        ),
        lax.psum(gating_grad_part.astype(jnp.bfloat16), "tp").astype(jnp.float32),
    )
    weighted = jnp.sum(gating_grad * sigmoids, axis=1, keepdims=True) / sigmoid_total
    sigmoid_grad = ROUTE_SCALE / sigmoid_total * (gating_grad - weighted)
    chosen_grad = sigmoid_grad * sigmoids * (1.0 - sigmoids)
    logits_grad = jnp.sum(route_mask * chosen_grad[:, :, None], axis=1).astype(jnp.bfloat16)
    grad_router = transposed_left(mid_low, logits_grad)
    mid_grad = mid_grad_sum + transposed_right(logits_grad, router_full)
    resid_norm_grad, grad_gain_mid = norm_backward(mid_grad, unit_mid, inverse_mid, gain_rows[1])
    resid_grad = grad_top + resid_norm_grad
    attn_grad = resid_grad.astype(jnp.bfloat16)
    grad_output = transposed_left(attended, attn_grad)
    attended_grad = (
        transposed_right(attn_grad, output_full)
        .astype(jnp.bfloat16)
        .reshape(tokens, heads_local, V_DIM)
    )
    softmax_probs = jnp.exp(attention_scores() - log_total)
    values_grad = jnp.einsum(
        "hqk,qhd->khd",
        softmax_probs.astype(jnp.bfloat16),
        attended_grad,
        preferred_element_type=jnp.float32,
    )
    probs_grad = jnp.einsum(
        "qhd,khd->hqk", attended_grad, values, preferred_element_type=jnp.float32
    )
    scores_grad = (
        softmax_probs * (probs_grad - jnp.sum(softmax_probs * probs_grad, axis=-1, keepdims=True))
    ).astype(jnp.bfloat16)
    query_grad = (
        jnp.einsum("hqk,khd->qhd", scores_grad, key_rows, preferred_element_type=jnp.float32)
        * score_scale
    )
    keys_grad = (
        jnp.einsum("hqk,qhd->khd", scores_grad, queries, preferred_element_type=jnp.float32)
        * score_scale
    )
    query_raw_grad = (
        jnp.concatenate(
            [
                query_grad[..., :NOPE],
                rotate(query_grad[..., NOPE:], cosine_table[:, None, :], -sine_table[:, None, :]),
            ],
            axis=-1,
        )
        .astype(jnp.bfloat16)
        .reshape(tokens, heads_local * (NOPE + ROPE))
    )
    expanded_grad = jnp.concatenate([keys_grad[..., :NOPE], values_grad], axis=-1).astype(
        jnp.bfloat16
    )
    expanded_grad = expanded_grad.reshape(tokens, heads_local * (NOPE + V_DIM))
    grad_expand = transposed_left(latent_low, expanded_grad)
    latent_normed_grad = transposed_right(expanded_grad, expand_full)
    latent_part_grad, gain_latent_part = norm_backward(
        latent_normed_grad, latent_unit, latent_inverse, gain_latent
    )
    rope_raw_grad = rotate(jnp.sum(keys_grad[..., NOPE:], axis=1), cosine_table, -sine_table)
    latent_grad_part = jnp.concatenate([latent_part_grad, rope_raw_grad], axis=1)
    in_grad_query = transposed_right(query_raw_grad, query_full)
    in_grad_sum, latent_grad, grad_gain_latent = (
        lax.psum(in_grad_query.astype(jnp.bfloat16), "tp").astype(jnp.float32),
        lax.psum(latent_grad_part.astype(jnp.bfloat16), "tp").astype(jnp.float32),
        lax.psum(gain_latent_part.astype(jnp.bfloat16), "tp").astype(jnp.float32),
    )
    latent_grad_low = latent_grad.astype(jnp.bfloat16)
    grad_latent = transposed_left(normed_low, latent_grad_low)
    grad_query = transposed_left(normed_low, query_raw_grad)
    in_grad = in_grad_sum + transposed_right(latent_grad_low, latent_full)
    input_norm_grad, grad_gain_in = norm_backward(in_grad, unit_in, inverse_in, gain_rows[0])
    grad_hidden = resid_grad + input_norm_grad
    grad_gains = jnp.stack([grad_gain_in, grad_gain_mid], axis=0)
    (
        grad_query_out,
        grad_latent_out,
        grad_expand_out,
        grad_output_out,
        grad_gains_out,
        grad_gain_latent_out,
        grad_router_out,
        grad_shared_gu_out,
        grad_shared_down_out,
    ) = (
        lax.psum_scatter(
            grad_query.astype(jnp.bfloat16), "ep", scatter_dimension=0, tiled=True
        ).astype(jnp.float32),
        lax.psum_scatter(
            grad_latent.astype(jnp.bfloat16), "ep", scatter_dimension=0, tiled=True
        ).astype(jnp.float32),
        lax.psum_scatter(
            grad_expand.astype(jnp.bfloat16), "ep", scatter_dimension=0, tiled=True
        ).astype(jnp.float32),
        lax.psum_scatter(
            grad_output.astype(jnp.bfloat16), "ep", scatter_dimension=1, tiled=True
        ).astype(jnp.float32),
        lax.psum_scatter(
            grad_gains.astype(jnp.bfloat16), "ep", scatter_dimension=1, tiled=True
        ).astype(jnp.float32),
        lax.psum_scatter(
            grad_gain_latent.astype(jnp.bfloat16), "ep", scatter_dimension=0, tiled=True
        ).astype(jnp.float32),
        lax.psum_scatter(
            grad_router.astype(jnp.bfloat16), "ep", scatter_dimension=0, tiled=True
        ).astype(jnp.float32),
        lax.psum_scatter(
            grad_shared_gu.astype(jnp.bfloat16), "ep", scatter_dimension=1, tiled=True
        ).astype(jnp.float32),
        lax.psum_scatter(
            grad_shared_down.astype(jnp.bfloat16), "ep", scatter_dimension=1, tiled=True
        ).astype(jnp.float32),
    )
    return (
        block_out,
        grad_hidden,
        grad_query_out,
        grad_latent_out,
        grad_expand_out,
        grad_output_out,
        grad_gains_out,
        grad_gain_latent_out,
        grad_router_out,
        grad_shared_gu_out,
        grad_shared_down_out,
        grad_expert_gate_up,
        grad_expert_down,
    )


CUTS = 4
GATHERS = 2
LANES = 128
VMEM_BYTES = 56 * 1024 * 1024


def swap(array, axis, bit):
    size = lax.axis_size(axis)
    return lax.ppermute(array, axis, [(place, place ^ bit) for place in range(size)])


def axis_bits(axis):
    size = lax.axis_size(axis)
    return [(axis, 1 << bit) for bit in reversed(range(size.bit_length() - 1))]


def spread(rows, steps):
    for axis, bit in steps:
        rows = jnp.concatenate([rows, swap(rows, axis, bit)], axis=0)
    return rows


def add_rounded(left_side, right_side):
    return (left_side.astype(jnp.float32) + right_side.astype(jnp.float32)).astype(
        left_side.dtype
    )


def fold_step(rows, step):
    axis, bit = step
    half = rows.shape[0] // 2
    return add_rounded(rows[:half], swap(rows[half:], axis, bit))


def fold(rows, steps):
    for step in reversed(steps):
        rows = fold_step(rows, step)
    return rows


def distances(steps):
    found = [0]
    for _, bit in steps:
        found = found + [distance + bit for distance in found]
    return found


def by_distance(blocks, place, order):
    return jnp.concatenate(
        [lax.dynamic_slice_in_dim(blocks, place ^ i, 1, axis=0) for i in order], axis=0
    )


def by_place(blocks, place, order):
    natural = jnp.concatenate([blocks[order.index(i)][None] for i in range(len(order))], axis=0)
    return by_distance(natural, place, range(len(order)))


def ring_owner(spot, size):
    return jnp.where(spot < size // 2, 2 * spot, 2 * (size - 1 - spot) + 1)


def ring_spot(place, size):
    return jnp.where(place % 2 == 0, place // 2, size - 1 - place // 2)


def ring_shift(array, axis, by):
    size = lax.axis_size(axis)
    ring = [2 * i for i in range(size // 2)] + [2 * i + 1 for i in reversed(range(size // 2))]
    return lax.ppermute(array, axis, [(ring[i], ring[(i + by) % size]) for i in range(size)])


def ring_gather(arrays, axis, beside):
    size = lax.axis_size(axis)
    found = [[array] + [None] * (size - 1) for array in arrays]
    ahead, behind, others, rounds = arrays, arrays, [], []
    for k in range(1, size // 2 + 1):
        behind = [ring_shift(array, axis, 1) for array in behind]
        if k < size - k:
            ahead = [ring_shift(array, axis, -1) for array in ahead]
        other = beside[k - 1](others) if k <= len(beside) else None
        behind, ahead, other = lax.optimization_barrier((behind, ahead, other))
        others.append(other)
        rounds.append(behind)
        for pieces, before, after in zip(found, behind, ahead):
            pieces[size - k] = before
            if k < size - k:
                pieces[k] = after
    return found, others, rounds


def ring_begin(parts, axis):
    size = lax.axis_size(axis)
    half = size // 2
    left = [(parts[half - k], parts[half + 1 + k] if k < half - 1 else None) for k in range(1, half)]
    return (parts[half], parts[half + 1]), left + [(parts[0], None)]


def ring_round(ring, axis):
    (ahead, behind), left = ring
    more_ahead, more_behind = left[0]
    ahead = add_rounded(ring_shift(ahead, axis, 1), more_ahead)
    if behind is not None and len(left) > 1:
        behind = ring_shift(behind, axis, -1)
        if more_behind is not None:
            behind = add_rounded(behind, more_behind)
    return (ahead, behind), left[1:]


def ring_end(ring, axis):
    (ahead, behind), left = ring
    while left:
        if len(left) == 1:
            found = ring_shift(ahead, axis, 1).astype(jnp.float32) + left[0][0]
            return found + behind
        (ahead, behind), left = ring_round(((ahead, behind), left), axis)
    return ahead.astype(jnp.float32) + behind


def pad_columns(array, width):
    return jnp.pad(array, ((0, 0), (0, width - array.shape[1])))


def pad_rows(array, height):
    return jnp.pad(array, ((0, height - array.shape[0]), (0, 0)))


def round_up(size, step=LANES):
    return -(-size // step) * step


def feed_forward_kernel(count, wide_steps, sub, *refs):
    first_ref, slot_ref, rows_ref, raw_ref, mask_ref, router_ref, tiles_ref = refs[:7]
    back_out, gate_ref, upper_ref, hidden_ref = refs[7:11]
    gains, shares, kept, tiles, back_ref, arrived, back_left = refs[11:]
    cut, step, last = pl.program_id(0), pl.program_id(1), count + wide_steps - 1
    owners, _, each, width = rows_ref.shape
    half, rows = raw_ref.shape[3], owners * each
    block = sub // each
    f32, bf16 = jnp.float32, jnp.bfloat16

    def arrival(n):
        return pltpu.make_async_copy(tiles_ref.at[n], tiles.at[n], arrived.at[n])

    def back_leaving(n):
        size = width // wide_steps
        extra = back_ref.shape[2] - width if n == wide_steps - 1 else 0
        of = (slice(None), slice(None), pl.ds(n * size, size + extra))
        return pltpu.make_async_copy(back_ref.at[of], back_out.at[(cut, *of)], back_left.at[n])

    @pl.when(step == 0)
    def _():
        @pl.when(cut == 0)
        def _():
            for n in range(count):
                arrival(n).start()

        values = rows_ref[...].reshape(rows, width)
        logits = jnp.dot(values, router_ref[...], preferred_element_type=f32)
        sig = jax.nn.sigmoid(logits) * mask_ref[...].reshape(logits.shape)
        gating = ROUTE_SCALE * sig / jnp.sum(sig, axis=1, keepdims=True)
        lanes = lax.broadcasted_iota(jnp.int32, gating.shape, 1)
        for e in range(EXP_DEV):
            own = jnp.sum(jnp.where(lanes == first_ref[0] + e, gating, 0.0), axis=1, keepdims=True)
            gains[e] = jnp.broadcast_to(own, gains.shape[1:])
        gains[EXP_DEV] = jnp.ones(gains.shape[1:], f32)
        shares[...] = jnp.zeros_like(shares)

    @pl.when(step < count)
    def _():
        @pl.when(cut == 0)
        def _():
            arrival(step).wait()

        kind = jnp.minimum(step // ((count - 1) // EXP_DEV), EXP_DEV)
        for i in range(rows // sub):
            at, of = pl.ds(i * sub, sub), pl.ds(i * block, block)
            values = rows_ref[of].reshape(sub, width)
            both = lax.dot_general(
                values, tiles[step], (((1,), (1,)), ((), ())), preferred_element_type=f32
            )
            gate, upper = both[:, :half], both[:, half:]
            gain, raw = gains[kind, at, :], raw_ref[of].reshape(sub, half).astype(f32)
            sig = jax.nn.sigmoid(gate)
            silu = gate * sig
            hidden = silu * upper
            grad = gain * raw
            shape = (block, 1, each, half)
            hidden_ref[of] = (gain * hidden).astype(bf16).reshape(shape)
            shares[kind, at, :] += hidden * raw
            gate_grad = (grad * upper * (sig + silu * (1.0 - sig))).astype(bf16)
            upper_grad = (grad * silu).astype(bf16)
            gate_ref[of] = gate_grad.reshape(shape)
            upper_ref[of] = upper_grad.reshape(shape)
            kept[step, at, :half] = gate_grad
            kept[step, at, half:] = upper_grad

    @pl.when(step >= count)
    def _():
        size = width // wide_steps
        columns = pl.ds(pl.multiple_of((step - count) * size, size), size)
        for i in range(rows // sub):
            found = sum(
                jnp.dot(
                    kept[n, pl.ds(i * sub, sub), :],
                    tiles[n, :, columns],
                    preferred_element_type=f32,
                )
                for n in range(count)
            ).astype(bf16)
            for j in range(block):
                part = found[j * each : (j + 1) * each]
                back_ref[slot_ref[cut, i * block + j], :, columns] = part

    @pl.when(step == last)
    def _():
        extra = back_ref.shape[2] - width
        lanes = lax.broadcasted_iota(jnp.int32, (rows, extra), 1)
        gating_grad = jnp.zeros(lanes.shape, f32)
        for e in range(EXP_DEV):
            own = jnp.sum(shares[e], axis=1, keepdims=True)
            gating_grad += jnp.where(lanes == first_ref[0] + e, own, 0.0)
        gating_grad = gating_grad.astype(bf16)
        for i in range(owners):
            back_ref[slot_ref[cut, i], :, width:] = gating_grad[i * each : (i + 1) * each]

    for n in range(wide_steps):

        @pl.when(step == count + n)
        def _(n=n):
            back_leaving(n).start()

    @pl.when(step == last)
    def _():
        for n in range(wide_steps):
            back_leaving(n).wait()


def feed_forward(slots, mid_rows, raw_grad, mask, router, tiles, first):
    count, both, width = tiles.shape
    owners, cuts, each, experts = mask.shape
    rows, half, wide_steps = owners * each, both // 2, 4
    bf16, f32 = jnp.bfloat16, jnp.float32

    def tile(step):
        return jnp.minimum(step, count - 1)

    smem, whole = pl.BlockSpec(memory_space=pltpu.SMEM), pl.BlockSpec(memory_space=pl.ANY)
    side = pl.BlockSpec((owners, 1, each, half), lambda c, i: (0, c, 0, tile(i)))
    return pl.pallas_call(
        functools.partial(feed_forward_kernel, count, wide_steps, min(8, owners) * each),
        grid=(cuts, count + wide_steps),
        in_specs=[
            smem,
            smem,
            pl.BlockSpec((owners, 1, each, width), lambda c, i: (0, c, 0, 0)),
            side,
            pl.BlockSpec((owners, 1, each, experts), lambda c, i: (0, c, 0, 0)),
            pl.BlockSpec((width, experts), lambda c, i: (0, 0)),
            whole,
        ],
        out_specs=[whole, side, side, side],
        out_shape=[
            jax.ShapeDtypeStruct((cuts, owners, each, width + LANES), bf16),
            *[jax.ShapeDtypeStruct((owners, cuts, each, count * half), bf16)] * 3,
        ],
        scratch_shapes=[
            pltpu.VMEM((EXP_DEV + 1, rows, half), f32),
            pltpu.VMEM((EXP_DEV + 1, rows, half), f32),
            pltpu.VMEM((count, rows, both), bf16),
            pltpu.VMEM(tiles.shape, bf16),
            pltpu.VMEM((owners, each, width + LANES), bf16),
            pltpu.SemaphoreType.DMA((count,)),
            pltpu.SemaphoreType.DMA((wide_steps,)),
        ],
        compiler_params=pltpu.CompilerParams(vmem_limit_bytes=VMEM_BYTES),
        cost_estimate=pl.CostEstimate(
            flops=4 * cuts * rows * width * both * count,
            bytes_accessed=50_000_000,
            transcendentals=0,
        ),
    )(first, slots, mid_rows, raw_grad, mask, router, tiles)


def rows_by_device_kernel(*refs):
    *left_refs, right_ref, out_ref = refs
    for i, left_ref in enumerate(left_refs):

        @pl.when(pl.program_id(1) == i)
        def _(left_ref=left_ref):
            found = jnp.dot(left_ref[...], right_ref[...], preferred_element_type=jnp.float32)
            out_ref[...] = found.astype(out_ref.dtype).reshape(out_ref.shape)


def rows_by_device(left_parts, right_side, devices):
    rows, depth = left_parts[0].shape
    columns, count = right_side.shape[1], len(left_parts)
    wide = columns // 2
    return pl.pallas_call(
        rows_by_device_kernel,
        grid=(2, count),
        in_specs=[pl.BlockSpec((rows, depth), lambda j, i: (0, 0))] * count
        + [pl.BlockSpec((depth, wide), lambda j, i: (0, j))],
        out_specs=pl.BlockSpec((devices, 1, rows // devices, wide), lambda j, i: (0, i, 0, j)),
        out_shape=jax.ShapeDtypeStruct(
            (devices, count, rows // devices, columns), right_side.dtype
        ),
        compiler_params=pltpu.CompilerParams(vmem_limit_bytes=VMEM_BYTES),
        cost_estimate=pl.CostEstimate(
            flops=2 * count * rows * depth * columns,
            bytes_accessed=2 * count * rows * (depth + columns),
            transcendentals=0,
        ),
    )(*left_parts, right_side).reshape(count * rows, columns)


def place_kernel(places_ref, *refs):
    *pieces, out_ref = refs
    for i, piece in enumerate(pieces):

        @pl.when(pl.program_id(0) == i)
        def _(piece=piece):
            out_ref[0] = piece[...]


def place_blocks(pieces, places):
    shape = pieces[0].shape
    return pl.pallas_call(
        place_kernel,
        grid_spec=pltpu.PrefetchScalarGridSpec(
            num_scalar_prefetch=1,
            grid=(len(pieces),),
            in_specs=[pl.BlockSpec(shape, lambda i, at: (0, 0))] * len(pieces),
            out_specs=pl.BlockSpec((1, *shape), lambda i, at: (at[i], 0, 0)),
        ),
        out_shape=jax.ShapeDtypeStruct((len(pieces), *shape), pieces[0].dtype),
        compiler_params=pltpu.CompilerParams(vmem_limit_bytes=VMEM_BYTES),
    )(jnp.stack(places).astype(jnp.int32), *pieces)


def on_device_dense(
    hidden_in,
    out_grad,
    query_weight,
    latent_weight,
    expand_weight,
    output_weight,
    norm_gains,
    latent_gain,
    router_weight,
    shared_gate_up,
    shared_down,
    expert_gate_up,
    expert_down,
    expert_ids,
):
    groups, parts = lax.axis_size("ep"), lax.axis_size("tp")
    group, part = lax.axis_index("ep"), lax.axis_index("tp")
    tokens, width = hidden_in.shape
    own = tokens // parts
    experts = router_weight.shape[1]
    bf16, f32 = jnp.bfloat16, jnp.float32
    ep_steps, tp_steps = axis_bits("ep"), axis_bits("tp")
    tp_order = distances(tp_steps)
    every = ("ep", "tp")
    devices = groups * parts
    cut_rows = own // CUTS

    spot = ring_spot(group, groups)
    ring_groups = [ring_owner((spot + k) % groups, groups) for k in range(groups)]

    mask_own = jnp.sum(
        (expert_ids[:, :, None] == jnp.arange(experts)[None, None, :]).astype(bf16), axis=1
    )
    sizes = [norm_gains.size, latent_gain.size, router_weight.size, mask_own.size]
    small = jnp.concatenate(
        [array.reshape(1, -1) for array in (norm_gains, latent_gain, router_weight, mask_own)],
        axis=1,
    )
    query_size, latent_width = query_weight.shape[1], latent_weight.shape[1]
    output_size = output_weight.shape[0]
    into_size = round_up(query_size + latent_width)
    into = pad_columns(jnp.concatenate([query_weight, latent_weight], axis=1), into_size)
    out_of = jnp.concatenate(
        [output_weight.T, expand_weight.reshape(output_weight.shape[1], -1)], axis=1
    )

    units = shared_down.shape[0] // groups
    shared_gu_own = lax.all_to_all(
        shared_gate_up.reshape(2, -1, groups, units), "ep", split_axis=2, concat_axis=1, tiled=True
    ).reshape(2, width, units)
    shared_down_own = lax.all_to_all(shared_down, "ep", split_axis=0, concat_axis=1, tiled=True)


    hidden_units = expert_down.shape[1]
    expert_pad, shared_pad = round_up(hidden_units), round_up(units)

    def dense_weights():
        side_weights = [
            jnp.concatenate(
                [pad_rows(expert_gate_up[e, side].T, expert_pad) for e in range(EXP_DEV)]
                + [pad_rows(shared_gu_own[side].T, shared_pad)],
                axis=0,
            ).reshape(-1, LANES, width)
            for side in range(2)
        ]
        tiles = jnp.concatenate(side_weights, axis=1)
        down_weight = jnp.concatenate(
            [pad_rows(expert_down[e], expert_pad) for e in range(EXP_DEV)]
            + [pad_rows(shared_down_own, shared_pad)],
            axis=0,
        )
        return tiles, down_weight

    (into_pieces, out_of_pieces), others, rounds = ring_gather(
        [into, out_of],
        "ep",
        [
            lambda _: spread(small, ep_steps[:1]),
            lambda done: (spread(done[0], ep_steps[1:2]), shared_gu_own, shared_down_own),
            lambda done: spread(done[1][0], ep_steps[2:]),
            lambda _: dense_weights(),
        ],
    )
    small_rel = others[2]
    tiles, down_weight = others[3]
    at = [sum(sizes[:i]) for i in range(len(sizes) + 1)]
    small_full = by_place(small_rel, group, distances(ep_steps))
    gain_rows = (
        small_full[:, : at[1]].reshape(groups, 2, -1).transpose(1, 0, 2).reshape(2, width)
    ).astype(f32)
    gain_latent = small_full[:, at[1] : at[2]].reshape(-1).astype(f32)
    router_full = small_full[:, at[2] : at[3]].reshape(width, experts)

    into_full = place_blocks(into_pieces, ring_groups).reshape(width, -1)
    out_of_full = place_blocks(out_of_pieces, ring_groups).reshape(width, -1)
    expand_full = out_of_full[:, output_size:].reshape(KV_RANK, -1)
    output_turned = out_of_full[:, :output_size]

    out_grad_late, _ = lax.optimization_barrier((out_grad, rounds[-2][0]))

    gather_rows = own // GATHERS
    cuts = CUTS // GATHERS

    def by_gather(rows):
        rows = rows.reshape(devices, GATHERS, gather_rows, -1).transpose(1, 0, 2, 3)
        return list(rows.reshape(GATHERS, devices * gather_rows, -1))

    grad_own = lax.dynamic_slice_in_dim(out_grad_late, part * own, own, axis=0)
    grad_parts = by_gather(lax.all_gather(grad_own, every, axis=0, tiled=True))
    raw_parts = [
        transposed_right(rows, down_weight).astype(bf16).reshape(devices, cuts, cut_rows, -1)
        for rows in grad_parts
    ]
    mask_parts = [
        rows.astype(f32).reshape(devices, cuts, cut_rows, experts)
        for rows in by_gather(small_full[:, at[3] :])
    ]

    row_blocks = hidden_in.reshape(parts, own, width)
    hidden_rel = by_distance(row_blocks, part, tp_order).reshape(tokens, width)
    heads_local = query_size // (NOPE + ROPE)
    places = ((part ^ jnp.array(tp_order))[:, None] * own + jnp.arange(own)[None, :]).reshape(-1)
    frequency = ROPE_BASE ** (-(jnp.arange(ROPE // 2).astype(f32) * 2.0 / ROPE))
    angles = places.astype(f32)[:, None] * frequency[None, :]
    cosine_table = jnp.cos(angles)
    sine_table = jnp.sin(angles)
    normed_in, unit_in, inverse_in = norm_forward(hidden_rel.astype(f32), gain_rows[0])
    normed_low = normed_in.astype(bf16)
    both_in = matmul(normed_low, into_full)
    query_raw = both_in[:, :query_size].reshape(tokens, heads_local, NOPE + ROPE)
    queries = jnp.concatenate(
        [
            query_raw[..., :NOPE],
            rotate(query_raw[..., NOPE:], cosine_table[:, None, :], sine_table[:, None, :]),
        ],
        axis=-1,
    ).astype(bf16)
    latent = both_in[:, query_size : query_size + latent_width]
    latent_normed, latent_unit, latent_inverse = norm_forward(latent[:, :KV_RANK], gain_latent)
    latent_low = latent_normed.astype(bf16)
    key_rope = rotate(latent[:, KV_RANK:], cosine_table, sine_table).astype(bf16)
    expanded = (
        matmul(latent_low, expand_full).astype(bf16).reshape(tokens, heads_local, NOPE + V_DIM)
    )
    key_rows = jnp.concatenate(
        [expanded[..., :NOPE], jnp.broadcast_to(key_rope[:, None, :], (tokens, heads_local, ROPE))],
        axis=-1,
    )
    values = expanded[..., NOPE:]
    score_scale = 1.0 / math.sqrt(NOPE + ROPE)
    causal = places[:, None] >= places[None, :]
    scores = (
        jnp.einsum("qhd,khd->hqk", queries, key_rows, preferred_element_type=f32) * score_scale
    )
    scores = jnp.where(causal[None], scores, -1e30)
    row_max = jnp.max(scores, axis=-1, keepdims=True)
    powers = jnp.exp(scores - row_max)
    softmax_probs = powers / jnp.sum(powers, axis=-1, keepdims=True)
    probs_low = softmax_probs.astype(bf16)
    attended = jnp.einsum("hqk,khd->qhd", probs_low, values, preferred_element_type=f32)
    attended = attended.astype(bf16).reshape(tokens, heads_local * V_DIM)
    attn_part = transposed_right(attended, output_turned).astype(bf16)
    resid = hidden_rel[:own].astype(f32) + fold(attn_part, tp_steps).astype(f32)

    normed_mid, unit_mid, inverse_mid = norm_forward(resid, gain_rows[1])
    mid_own = normed_mid.astype(bf16)
    first = (group * EXP_DEV).astype(jnp.int32).reshape(1)
    mid_parts = [
        lax.all_gather(
            mid_own[i * gather_rows : (i + 1) * gather_rows], every, axis=0, tiled=True
        )
        for i in range(GATHERS)
    ]
    one_order = (ep_steps + tp_steps)[::-1]
    turn = [0, *range(2, len(tp_steps) + 1), 1, *range(len(tp_steps) + 1, len(one_order))]
    orders = [one_order, [one_order[i] for i in turn]]
    distance = jnp.arange(devices, dtype=jnp.int32) ^ (group * parts + part)
    slots = []
    for order in orders:
        slot = jnp.zeros_like(distance)
        for axis, bit in order:
            slot = 2 * slot + distance // (bit * (parts if axis == "ep" else 1)) % 2
        slots.append(slot)
    slots = jnp.stack([slots[cut % 2] for cut in range(cuts)])

    def on_a_step(sums):
        return [(fold_step(rows, todo[0]), todo[1:]) if todo else (rows, todo) for rows, todo in sums]

    def together(work, sums):
        work, rows = lax.optimization_barrier((work, [rows for rows, _ in sums]))
        return work, [(each, todo) for each, (_, todo) in zip(rows, sums)]

    mid_parts[0], raw_parts = lax.optimization_barrier((mid_parts[0], raw_parts))
    sums, gate_parts, upper_parts, hidden_parts = [], [], [], []
    for i in range(GATHERS):
        mid_rows = mid_parts[i]
        back, *sides = feed_forward(
            slots,
            mid_rows.reshape(devices, cuts, cut_rows, width),
            raw_parts[i],
            mask_parts[i],
            router_full,
            tiles,
            first,
        )
        (back, sides), sums = together((back, sides), on_a_step(sums))
        sums += [(back[cut], orders[cut % 2]) for cut in range(cuts)]
        for parts_of, side in zip((gate_parts, upper_parts, hidden_parts), sides):
            parts_of.append(side.reshape(mid_rows.shape[0], -1))
        if i == 0:
            grad_down = transposed_left(hidden_parts[0], grad_parts[0])
            (grad_down, mid_parts[1:]), sums = together((grad_down, mid_parts[1:]), on_a_step(sums))
    out_part = rows_by_device(hidden_parts, down_weight, devices)
    out_part, sums = together(out_part, on_a_step(sums))
    out_own = lax.psum_scatter(out_part, every, scatter_dimension=0, tiled=True)
    block_own = (lax.optimization_barrier(resid) + out_own.astype(f32)).astype(bf16)
    for hidden_rows, grad_rows in zip(hidden_parts[1:], grad_parts[1:]):
        grad_down = grad_down + transposed_left(hidden_rows, grad_rows)
    grad_gate = transposed_left(gate_parts[0], mid_parts[0])
    (grad_down, grad_gate), sums = together((grad_down, grad_gate), on_a_step(sums))
    for gate_rows, mid_rows in zip(gate_parts[1:], mid_parts[1:]):
        grad_gate = grad_gate + transposed_left(gate_rows, mid_rows)
    grad_gate, sums = together(grad_gate, on_a_step(sums))
    while any(todo for _, todo in sums):
        sums = on_a_step(sums)
    back_own = jnp.concatenate([rows[0] for rows, _ in sums], axis=0)

    back_own = back_own.astype(f32)
    gating_grad = back_own[:, width : width + experts]
    mask = lax.dynamic_slice_in_dim(mask_own, part * own, own, axis=0).astype(f32)
    sigmoids = jax.nn.sigmoid(matmul(mid_own, router_full))
    chosen = sigmoids * mask
    sigmoid_total = jnp.sum(chosen, axis=1, keepdims=True)
    weighted = jnp.sum(gating_grad * chosen, axis=1, keepdims=True) / sigmoid_total
    sigmoid_grad = ROUTE_SCALE / sigmoid_total * (gating_grad - weighted)
    logits_grad = (sigmoid_grad * chosen * (1.0 - sigmoids)).astype(bf16)
    grad_router = transposed_left(mid_own, logits_grad)
    mid_grad = back_own[:, :width] + transposed_right(logits_grad, router_full)
    resid_norm_grad, grad_gain_mid = norm_backward(mid_grad, unit_mid, inverse_mid, gain_rows[1])
    resid_grad = grad_own.astype(f32) + resid_norm_grad

    resid_low, upper_parts = lax.optimization_barrier((resid_grad.astype(bf16), upper_parts))
    grad_upper = sum(transposed_left(*rows) for rows in zip(upper_parts, mid_parts))
    attn_rows, grad_upper = lax.optimization_barrier((spread(resid_low, tp_steps[:1]), grad_upper))
    attn_grad = spread(attn_rows, tp_steps[1:])

    def ring_columns(left_side, right_side):
        size = left_side.shape[1] // groups
        return [
            transposed_left(
                lax.dynamic_slice_in_dim(left_side, g * size, size, axis=1), right_side
            ).astype(bf16)
            for g in ring_groups
        ]

    def beside(work, rings):
        rounds = [ring_round(ring, "ep") for ring in rings]
        work, states = lax.optimization_barrier((work, [state for state, _ in rounds]))
        return work, [(state, left) for state, (_, left) in zip(states, rounds)]

    output_ring = ring_begin(ring_columns(attn_grad, attended), "ep")

    shared_at = EXP_DEV * expert_pad
    shared_gu_back = lax.all_to_all(
        jnp.stack([grad[shared_at:][:units].T for grad in (grad_gate, grad_upper)])
        .astype(bf16)
        .reshape(2, width, 1, units),
        "ep",
        split_axis=1,
        concat_axis=2,
        tiled=True,
    )
    shared_down_back = lax.all_to_all(
        grad_down[shared_at : shared_at + units].astype(bf16),
        "ep",
        split_axis=1,
        concat_axis=0,
        tiled=True,
    )
    attended_grad = (
        matmul(attn_grad, output_turned).astype(bf16).reshape(tokens, heads_local, V_DIM)
    )
    values_grad = jnp.einsum("hqk,qhd->khd", probs_low, attended_grad, preferred_element_type=f32)
    probs_grad = jnp.einsum("qhd,khd->hqk", attended_grad, values, preferred_element_type=f32)
    scores_grad = (
        softmax_probs * (probs_grad - jnp.sum(softmax_probs * probs_grad, axis=-1, keepdims=True))
    ).astype(bf16)
    (scores_grad, values_grad), (output_ring,) = beside((scores_grad, values_grad), [output_ring])
    query_grad = (
        jnp.einsum("hqk,khd->qhd", scores_grad, key_rows, preferred_element_type=f32) * score_scale
    )
    keys_grad = (
        jnp.einsum("hqk,qhd->khd", scores_grad, queries, preferred_element_type=f32) * score_scale
    )
    query_raw_grad = (
        jnp.concatenate(
            [
                query_grad[..., :NOPE],
                rotate(query_grad[..., NOPE:], cosine_table[:, None, :], -sine_table[:, None, :]),
            ],
            axis=-1,
        )
        .astype(bf16)
        .reshape(tokens, heads_local * (NOPE + ROPE))
    )
    expanded_grad = (
        jnp.concatenate([keys_grad[..., :NOPE], values_grad], axis=-1)
        .astype(bf16)
        .reshape(tokens, heads_local * (NOPE + V_DIM))
    )
    latent_normed_grad = transposed_right(expanded_grad, expand_full)
    latent_part_grad, gain_latent_part = norm_backward(
        latent_normed_grad, latent_unit, latent_inverse, gain_latent
    )
    rope_raw_grad = rotate(jnp.sum(keys_grad[..., NOPE:], axis=1), cosine_table, -sine_table)
    latent_grad = jnp.concatenate([latent_part_grad, rope_raw_grad], axis=1).astype(bf16)
    both_grad = pad_columns(jnp.concatenate([query_raw_grad, latent_grad], axis=1), into_size)
    (both_grad, shared_gu_back, shared_down_back), (output_ring,) = beside(
        (both_grad, shared_gu_back, shared_down_back), [output_ring]
    )
    grad_shared_gu_out = shared_gu_back.reshape(shared_gate_up.shape).astype(f32)
    grad_shared_down_out = shared_down_back.astype(f32)
    into_ring = ring_begin(ring_columns(normed_low, both_grad), "ep")
    in_grad_part = transposed_right(both_grad, into_full).astype(bf16)
    expand_blocks = transposed_left(latent_low, expanded_grad).astype(bf16)
    expand_blocks = expand_blocks.reshape(groups, -1, expand_blocks.shape[1])
    expand_ring = ring_begin(
        [lax.dynamic_slice_in_dim(expand_blocks, g, 1, axis=0)[0] for g in ring_groups], "ep"
    )
    work = (in_grad_part, [left for _, left in (into_ring, expand_ring)])
    (in_grad_part, lefts), (into_ring, output_ring) = beside(work, [into_ring, output_ring])
    into_ring, expand_ring = (into_ring[0], lefts[0][1:]), (expand_ring[0], lefts[1])

    grad_sides = (grad_gate, grad_upper)
    grad_sides, grad_down, _ = lax.optimization_barrier((grad_sides, grad_down, in_grad_part))
    grad_expert_gate_up = jnp.stack(
        [
            jnp.stack([grad[e * expert_pad :][:hidden_units].T for grad in grad_sides])
            for e in range(EXP_DEV)
        ]
    )
    in_grad = fold_step(in_grad_part, tp_steps[-1])
    (grad_expert_gate_up, in_grad), (into_ring, expand_ring, output_ring) = beside(
        (grad_expert_gate_up, in_grad), [into_ring, expand_ring, output_ring]
    )
    grad_expert_down = jnp.stack(
        [grad_down[e * expert_pad : e * expert_pad + hidden_units] for e in range(EXP_DEV)]
    )
    in_grad = fold(in_grad, tp_steps[:-1]).astype(f32)
    (grad_expert_down, in_grad), (into_ring, expand_ring) = beside(
        (grad_expert_down, in_grad), [into_ring, expand_ring]
    )
    input_norm_grad, grad_gain_in = norm_backward(
        in_grad, unit_in[:own], inverse_in[:own], gain_rows[0]
    )
    hidden_own = (resid_grad + input_norm_grad).astype(bf16)
    into_sum = ring_end(into_ring, "ep")
    grad_expand_out = ring_end(expand_ring, "ep")
    grad_output_out = ring_end(output_ring, "ep").T
    grad_query_out = into_sum[:, :query_size]
    grad_latent_out = into_sum[:, query_size : query_size + latent_width]
    for axis, bit in tp_steps:
        rounded = grad_latent_out.astype(bf16)
        grad_latent_out = rounded.astype(f32) + swap(rounded, axis, bit).astype(f32)
    grad_small = jnp.concatenate(
        [
            jnp.stack([grad_gain_in, grad_gain_mid])
            .reshape(2, groups, -1)
            .transpose(1, 0, 2)
            .reshape(groups, -1),
            gain_latent_part.reshape(groups, -1),
            grad_router.reshape(groups, -1),
        ],
        axis=1,
    )
    small_sum = fold(by_distance(grad_small, group, distances(ep_steps)), ep_steps)
    for axis, bit in tp_steps:
        small_sum = small_sum + swap(small_sum, axis, bit)
    small_sum = small_sum.reshape(-1)
    grad_gains_out = small_sum[: at[1]].reshape(norm_gains.shape)
    grad_gain_latent_out = small_sum[at[1] : at[2]]
    grad_router_out = small_sum[at[2] : at[3]].reshape(router_weight.shape)

    def all_own(rows):
        return lax.all_gather(rows, "tp", axis=0, tiled=True)

    return (
        all_own(block_own),
        all_own(hidden_own).astype(f32),
        grad_query_out,
        grad_latent_out,
        grad_expand_out,
        grad_output_out,
        grad_gains_out,
        grad_gain_latent_out,
        grad_router_out,
        grad_shared_gu_out,
        grad_shared_down_out,
        grad_expert_gate_up,
        grad_expert_down,
    )


def power_of_two(size):
    return size & (size - 1) == 0


def on_device(hidden_in, *others):
    groups, parts = lax.axis_size("ep"), lax.axis_size("tp")
    tokens = hidden_in.shape[0]
    mean_load = tokens * TOPK // (EXP_DEV * groups)
    capacity = mean_load + mean_load // 3
    if EXP_DEV * capacity >= tokens and power_of_two(groups) and power_of_two(parts):
        return on_device_dense(hidden_in, *others)
    return on_device_sparse(hidden_in, *others)


def solution(mesh):
    placed = (
        P("ep", None),
        P("ep", None),
        P("ep", "tp"),
        P("ep", None),
        P("ep", "tp"),
        P("tp", "ep"),
        P(None, "ep"),
        P("ep"),
        P("ep", None),
        P(None, "ep", "tp"),
        P("tp", "ep"),
        P("ep", None, None, "tp"),
        P("ep", "tp", None),
        P("ep", None),
    )
    return jax.shard_map(
        on_device,
        mesh=mesh,
        in_specs=placed,
        out_specs=(
            P("ep", None),
            P("ep", None),
            P("ep", "tp"),
            P("ep", None),
            P("ep", "tp"),
            P("tp", "ep"),
            P(None, "ep"),
            P("ep"),
            P("ep", None),
            P(None, "ep", "tp"),
            P("tp", "ep"),
            P("ep", None, None, "tp"),
            P("ep", "tp", None),
        ),
        check_vma=False,
    )
```

```python
import functools
import math

import jax
import jax.numpy as jnp
from jax import lax
from jax.experimental import pallas as pl
from jax.experimental.pallas import tpu as pltpu
from jax.sharding import PartitionSpec as P

NOPE = 128
ROPE = 64
V_DIM = 128
KV_RANK = 512
TOPK = 6
EXP_DEV = 2


EPSILON = 1e-06
ROUTE_SCALE = 2.446
ROPE_BASE = 50000.0


def matmul(left_side, right_side):
    return jnp.dot(left_side, right_side, preferred_element_type=jnp.float32)


def transposed_left(left_side, right_side):
    return lax.dot_general(
        left_side, right_side, (((0,), (0,)), ((), ())), preferred_element_type=jnp.float32
    )


def transposed_right(left_side, right_side):
    return lax.dot_general(
        left_side, right_side, (((1,), (1,)), ((), ())), preferred_element_type=jnp.float32
    )


def rotate(values, cosine_table, sine_table):
    halfway = values.shape[-1] // 2
    first_half = values[..., :halfway]
    second_half = values[..., halfway:]
    return jnp.concatenate(
        [
            first_half * cosine_table - second_half * sine_table,
            second_half * cosine_table + first_half * sine_table,
        ],
        axis=-1,
    )


def norm_forward(values, gain_row):
    inverse = lax.rsqrt(jnp.mean(values * values, axis=-1, keepdims=True) + EPSILON)
    unit_rows = values * inverse
    return (unit_rows * gain_row, unit_rows, inverse)


def norm_backward(incoming, unit_rows, inverse, gain_row):
    scaled = incoming * gain_row
    grad_values = inverse * (
        scaled - unit_rows * jnp.mean(scaled * unit_rows, axis=-1, keepdims=True)
    )
    return (grad_values, jnp.sum(incoming * unit_rows, axis=0))


def on_device_sparse(
    hidden_in,
    out_grad,
    query_weight,
    latent_weight,
    expand_weight,
    output_weight,
    norm_gains,
    latent_gain,
    router_weight,
    shared_gate_up,
    shared_down,
    expert_gate_up,
    expert_down,
    expert_ids,
):
    (
        query_full,
        latent_full,
        expand_full,
        output_full,
        gains_full,
        latent_gain_full,
        router_full,
        shared_gu_full,
        shared_down_full,
    ) = (
        lax.all_gather(query_weight, "ep", axis=0, tiled=True),
        lax.all_gather(latent_weight, "ep", axis=0, tiled=True),
        lax.all_gather(expand_weight, "ep", axis=0, tiled=True),
        lax.all_gather(output_weight, "ep", axis=1, tiled=True),
        lax.all_gather(norm_gains, "ep", axis=1, tiled=True),
        lax.all_gather(latent_gain, "ep", axis=0, tiled=True),
        lax.all_gather(router_weight, "ep", axis=0, tiled=True),
        lax.all_gather(shared_gate_up, "ep", axis=1, tiled=True),
        lax.all_gather(shared_down, "ep", axis=1, tiled=True),
    )
    tokens = hidden_in.shape[0]
    model_width = hidden_in.shape[1]
    heads_local = query_full.shape[1] // (NOPE + ROPE)
    gain_rows = gains_full.astype(jnp.float32)
    gain_latent = latent_gain_full.astype(jnp.float32)
    places = jnp.arange(tokens).astype(jnp.float32)
    frequency = ROPE_BASE ** (-(jnp.arange(ROPE // 2).astype(jnp.float32) * 2.0 / ROPE))
    angles = places[:, None] * frequency[None, :]
    cosine_table = jnp.cos(angles)
    sine_table = jnp.sin(angles)
    resid_in = hidden_in.astype(jnp.float32)
    normed_in, unit_in, inverse_in = norm_forward(resid_in, gain_rows[0])
    normed_low = normed_in.astype(jnp.bfloat16)
    query_raw = matmul(normed_low, query_full).reshape(tokens, heads_local, NOPE + ROPE)
    queries = jnp.concatenate(
        [
            query_raw[..., :NOPE],
            rotate(query_raw[..., NOPE:], cosine_table[:, None, :], sine_table[:, None, :]),
        ],
        axis=-1,
    ).astype(jnp.bfloat16)
    latent = matmul(normed_low, latent_full)
    latent_normed, latent_unit, latent_inverse = norm_forward(latent[:, :KV_RANK], gain_latent)
    latent_low = latent_normed.astype(jnp.bfloat16)
    key_rope = rotate(latent[:, KV_RANK:], cosine_table, sine_table).astype(jnp.bfloat16)
    expanded = (
        matmul(latent_low, expand_full)
        .astype(jnp.bfloat16)
        .reshape(tokens, heads_local, NOPE + V_DIM)
    )
    key_rows = jnp.concatenate(
        [expanded[..., :NOPE], jnp.broadcast_to(key_rope[:, None, :], (tokens, heads_local, ROPE))],
        axis=-1,
    )
    values = expanded[..., NOPE:]
    score_scale = 1.0 / math.sqrt(NOPE + ROPE)
    causal = jnp.arange(tokens)[:, None] >= jnp.arange(tokens)[None, :]

    def attention_scores():
        scores = (
            jnp.einsum("qhd,khd->hqk", queries, key_rows, preferred_element_type=jnp.float32)
            * score_scale
        )
        return jnp.where(causal[None], scores, -1e30)

    scores_first = attention_scores()
    row_max = jnp.max(scores_first, axis=-1, keepdims=True)
    log_total = row_max + jnp.log(jnp.sum(jnp.exp(scores_first - row_max), axis=-1, keepdims=True))
    probs_low = jnp.exp(scores_first - log_total).astype(jnp.bfloat16)
    attended = jnp.einsum("hqk,khd->qhd", probs_low, values, preferred_element_type=jnp.float32)
    attended = attended.astype(jnp.bfloat16).reshape(tokens, heads_local * V_DIM)
    attn_out = lax.psum(matmul(attended, output_full), "tp")
    resid = resid_in + attn_out
    normed_mid, unit_mid, inverse_mid = norm_forward(resid, gain_rows[1])
    mid_low = normed_mid.astype(jnp.bfloat16)
    logits = matmul(mid_low, router_full)
    experts = router_full.shape[1]
    route_mask = (expert_ids[:, :, None] == jnp.arange(experts)[None, None, :]).astype(jnp.float32)
    chosen = jnp.sum(route_mask * logits[:, None, :], axis=2)
    sigmoids = jax.nn.sigmoid(chosen)
    sigmoid_total = jnp.sum(sigmoids, axis=1, keepdims=True)
    gating = ROUTE_SCALE * sigmoids / sigmoid_total
    shared_gate = matmul(mid_low, shared_gu_full[0])
    shared_upper = matmul(mid_low, shared_gu_full[1])
    shared_sig = jax.nn.sigmoid(shared_gate)
    shared_hidden = (shared_gate * shared_sig * shared_upper).astype(jnp.bfloat16)
    shared_part = matmul(shared_hidden, shared_down_full)
    groups = lax.axis_size("ep")
    mean_load = tokens * TOPK // (EXP_DEV * groups)
    capacity = mean_load + mean_load // 3
    choices = tokens * TOPK
    rows_total = groups * capacity
    flat_ids = expert_ids.reshape(-1)
    onehot = (flat_ids[:, None] == jnp.arange(experts)[None, :]).astype(jnp.int32)
    slot_of = jnp.sum((jnp.cumsum(onehot, axis=0) - onehot) * onehot, axis=1)
    target = flat_ids % EXP_DEV * rows_total + flat_ids // EXP_DEV * capacity + slot_of
    slot_table = (
        jnp.full((EXP_DEV * rows_total,), choices, jnp.int32)
        .at[target]
        .set(jnp.arange(choices, dtype=jnp.int32))
        .reshape(EXP_DEV, groups, capacity)
    )
    mid_padded = jnp.concatenate([mid_low, jnp.zeros((1, model_width), jnp.bfloat16)], axis=0)
    outgoing = mid_padded[slot_table.reshape(-1) // TOPK].reshape(EXP_DEV, rows_total, model_width)
    expert_rows = lax.all_to_all(outgoing, "ep", split_axis=1, concat_axis=1, tiled=True)
    expert_gate = jnp.einsum(
        "erd,edf->erf", expert_rows, expert_gate_up[:, 0], preferred_element_type=jnp.float32
    )
    expert_upper = jnp.einsum(
        "erd,edf->erf", expert_rows, expert_gate_up[:, 1], preferred_element_type=jnp.float32
    )
    expert_sig = jax.nn.sigmoid(expert_gate)
    expert_hidden = (expert_gate * expert_sig * expert_upper).astype(jnp.bfloat16)
    expert_part = jnp.einsum(
        "erf,efd->erd", expert_hidden, expert_down, preferred_element_type=jnp.float32
    ).astype(jnp.bfloat16)
    returned = lax.all_to_all(expert_part, "ep", split_axis=1, concat_axis=1, tiled=True)
    per_choice = (
        returned.reshape(-1, model_width)[target]
        .reshape(tokens, TOPK, model_width)
        .astype(jnp.float32)
    )
    routed_part = jnp.sum(gating[:, :, None] * per_choice, axis=1)
    moe_out = lax.psum((shared_part + routed_part).astype(jnp.bfloat16), "tp").astype(jnp.float32)
    block_out = (resid + moe_out).astype(jnp.bfloat16)
    grad_top = out_grad.astype(jnp.float32)
    choice_grad = (gating[:, :, None] * grad_top[:, None, :]).astype(jnp.bfloat16)
    grad_padded = jnp.concatenate(
        [choice_grad.reshape(choices, model_width), jnp.zeros((1, model_width), jnp.bfloat16)],
        axis=0,
    )
    outgoing_grad = grad_padded[slot_table.reshape(-1)].reshape(EXP_DEV, rows_total, model_width)
    rows_grad = lax.all_to_all(outgoing_grad, "ep", split_axis=1, concat_axis=1, tiled=True)
    hidden_grad = jnp.einsum(
        "erd,efd->erf", rows_grad, expert_down, preferred_element_type=jnp.float32
    )
    gate_grad = (
        hidden_grad * expert_upper * expert_sig * (1.0 + expert_gate * (1.0 - expert_sig))
    ).astype(jnp.bfloat16)
    upper_grad = (hidden_grad * expert_gate * expert_sig).astype(jnp.bfloat16)
    grad_expert_down = jnp.einsum(
        "erf,erd->efd", expert_hidden, rows_grad, preferred_element_type=jnp.float32
    )
    grad_expert_gate_up = jnp.stack(
        [
            jnp.einsum("erd,erf->edf", expert_rows, gate_grad, preferred_element_type=jnp.float32),
            jnp.einsum("erd,erf->edf", expert_rows, upper_grad, preferred_element_type=jnp.float32),
        ],
        axis=1,
    )
    row_back = jnp.einsum(
        "erf,edf->erd", gate_grad, expert_gate_up[:, 0], preferred_element_type=jnp.float32
    ) + jnp.einsum(
        "erf,edf->erd", upper_grad, expert_gate_up[:, 1], preferred_element_type=jnp.float32
    )
    row_back_low = row_back.astype(jnp.bfloat16)
    back_rows = lax.all_to_all(row_back_low, "ep", split_axis=1, concat_axis=1, tiled=True)
    choice_back = (
        back_rows.reshape(-1, model_width)[target]
        .reshape(tokens, TOPK, model_width)
        .astype(jnp.float32)
    )
    mid_grad_routed = jnp.sum(choice_back, axis=1)
    gating_grad_part = jnp.sum(per_choice * grad_top[:, None, :], axis=2)
    shared_hidden_grad = transposed_right(out_grad, shared_down_full)
    shared_gate_grad = (
        shared_hidden_grad * shared_upper * shared_sig * (1.0 + shared_gate * (1.0 - shared_sig))
    ).astype(jnp.bfloat16)
    shared_upper_grad = (shared_hidden_grad * shared_gate * shared_sig).astype(jnp.bfloat16)
    grad_shared_down = transposed_left(shared_hidden, out_grad)
    grad_shared_gu = jnp.stack(
        [transposed_left(mid_low, shared_gate_grad), transposed_left(mid_low, shared_upper_grad)],
        axis=0,
    )
    mid_grad_shared = transposed_right(shared_gate_grad, shared_gu_full[0]) + transposed_right(
        shared_upper_grad, shared_gu_full[1]
    )
    mid_grad_sum, gating_grad = (
        lax.psum((mid_grad_routed + mid_grad_shared).astype(jnp.bfloat16), "tp").astype(
            jnp.float32
        ),
        lax.psum(gating_grad_part.astype(jnp.bfloat16), "tp").astype(jnp.float32),
    )
    weighted = jnp.sum(gating_grad * sigmoids, axis=1, keepdims=True) / sigmoid_total
    sigmoid_grad = ROUTE_SCALE / sigmoid_total * (gating_grad - weighted)
    chosen_grad = sigmoid_grad * sigmoids * (1.0 - sigmoids)
    logits_grad = jnp.sum(route_mask * chosen_grad[:, :, None], axis=1).astype(jnp.bfloat16)
    grad_router = transposed_left(mid_low, logits_grad)
    mid_grad = mid_grad_sum + transposed_right(logits_grad, router_full)
    resid_norm_grad, grad_gain_mid = norm_backward(mid_grad, unit_mid, inverse_mid, gain_rows[1])
    resid_grad = grad_top + resid_norm_grad
    attn_grad = resid_grad.astype(jnp.bfloat16)
    grad_output = transposed_left(attended, attn_grad)
    attended_grad = (
        transposed_right(attn_grad, output_full)
        .astype(jnp.bfloat16)
        .reshape(tokens, heads_local, V_DIM)
    )
    softmax_probs = jnp.exp(attention_scores() - log_total)
    values_grad = jnp.einsum(
        "hqk,qhd->khd",
        softmax_probs.astype(jnp.bfloat16),
        attended_grad,
        preferred_element_type=jnp.float32,
    )
    probs_grad = jnp.einsum(
        "qhd,khd->hqk", attended_grad, values, preferred_element_type=jnp.float32
    )
    scores_grad = (
        softmax_probs * (probs_grad - jnp.sum(softmax_probs * probs_grad, axis=-1, keepdims=True))
    ).astype(jnp.bfloat16)
    query_grad = (
        jnp.einsum("hqk,khd->qhd", scores_grad, key_rows, preferred_element_type=jnp.float32)
        * score_scale
    )
    keys_grad = (
        jnp.einsum("hqk,qhd->khd", scores_grad, queries, preferred_element_type=jnp.float32)
        * score_scale
    )
    query_raw_grad = (
        jnp.concatenate(
            [
                query_grad[..., :NOPE],
                rotate(query_grad[..., NOPE:], cosine_table[:, None, :], -sine_table[:, None, :]),
            ],
            axis=-1,
        )
        .astype(jnp.bfloat16)
        .reshape(tokens, heads_local * (NOPE + ROPE))
    )
    expanded_grad = jnp.concatenate([keys_grad[..., :NOPE], values_grad], axis=-1).astype(
        jnp.bfloat16
    )
    expanded_grad = expanded_grad.reshape(tokens, heads_local * (NOPE + V_DIM))
    grad_expand = transposed_left(latent_low, expanded_grad)
    latent_normed_grad = transposed_right(expanded_grad, expand_full)
    latent_part_grad, gain_latent_part = norm_backward(
        latent_normed_grad, latent_unit, latent_inverse, gain_latent
    )
    rope_raw_grad = rotate(jnp.sum(keys_grad[..., NOPE:], axis=1), cosine_table, -sine_table)
    latent_grad_part = jnp.concatenate([latent_part_grad, rope_raw_grad], axis=1)
    in_grad_query = transposed_right(query_raw_grad, query_full)
    in_grad_sum, latent_grad, grad_gain_latent = (
        lax.psum(in_grad_query.astype(jnp.bfloat16), "tp").astype(jnp.float32),
        lax.psum(latent_grad_part.astype(jnp.bfloat16), "tp").astype(jnp.float32),
        lax.psum(gain_latent_part.astype(jnp.bfloat16), "tp").astype(jnp.float32),
    )
    latent_grad_low = latent_grad.astype(jnp.bfloat16)
    grad_latent = transposed_left(normed_low, latent_grad_low)
    grad_query = transposed_left(normed_low, query_raw_grad)
    in_grad = in_grad_sum + transposed_right(latent_grad_low, latent_full)
    input_norm_grad, grad_gain_in = norm_backward(in_grad, unit_in, inverse_in, gain_rows[0])
    grad_hidden = resid_grad + input_norm_grad
    grad_gains = jnp.stack([grad_gain_in, grad_gain_mid], axis=0)
    (
        grad_query_out,
        grad_latent_out,
        grad_expand_out,
        grad_output_out,
        grad_gains_out,
        grad_gain_latent_out,
        grad_router_out,
        grad_shared_gu_out,
        grad_shared_down_out,
    ) = (
        lax.psum_scatter(
            grad_query.astype(jnp.bfloat16), "ep", scatter_dimension=0, tiled=True
        ).astype(jnp.float32),
        lax.psum_scatter(
            grad_latent.astype(jnp.bfloat16), "ep", scatter_dimension=0, tiled=True
        ).astype(jnp.float32),
        lax.psum_scatter(
            grad_expand.astype(jnp.bfloat16), "ep", scatter_dimension=0, tiled=True
        ).astype(jnp.float32),
        lax.psum_scatter(
            grad_output.astype(jnp.bfloat16), "ep", scatter_dimension=1, tiled=True
        ).astype(jnp.float32),
        lax.psum_scatter(
            grad_gains.astype(jnp.bfloat16), "ep", scatter_dimension=1, tiled=True
        ).astype(jnp.float32),
        lax.psum_scatter(
            grad_gain_latent.astype(jnp.bfloat16), "ep", scatter_dimension=0, tiled=True
        ).astype(jnp.float32),
        lax.psum_scatter(
            grad_router.astype(jnp.bfloat16), "ep", scatter_dimension=0, tiled=True
        ).astype(jnp.float32),
        lax.psum_scatter(
            grad_shared_gu.astype(jnp.bfloat16), "ep", scatter_dimension=1, tiled=True
        ).astype(jnp.float32),
        lax.psum_scatter(
            grad_shared_down.astype(jnp.bfloat16), "ep", scatter_dimension=1, tiled=True
        ).astype(jnp.float32),
    )
    return (
        block_out,
        grad_hidden,
        grad_query_out,
        grad_latent_out,
        grad_expand_out,
        grad_output_out,
        grad_gains_out,
        grad_gain_latent_out,
        grad_router_out,
        grad_shared_gu_out,
        grad_shared_down_out,
        grad_expert_gate_up,
        grad_expert_down,
    )


CUTS = 4
GATHERS = 2
LANES = 128
VMEM_BYTES = 56 * 1024 * 1024


def swap(array, axis, bit):
    size = lax.axis_size(axis)
    return lax.ppermute(array, axis, [(place, place ^ bit) for place in range(size)])


def axis_bits(axis):
    size = lax.axis_size(axis)
    return [(axis, 1 << bit) for bit in reversed(range(size.bit_length() - 1))]


def spread(rows, steps):
    for axis, bit in steps:
        rows = jnp.concatenate([rows, swap(rows, axis, bit)], axis=0)
    return rows


def add_rounded(left_side, right_side):
    return (left_side.astype(jnp.float32) + right_side.astype(jnp.float32)).astype(
        left_side.dtype
    )


def fold_step(rows, step):
    axis, bit = step
    half = rows.shape[0] // 2
    return add_rounded(rows[:half], swap(rows[half:], axis, bit))


def fold(rows, steps):
    for step in reversed(steps):
        rows = fold_step(rows, step)
    return rows


def distances(steps):
    found = [0]
    for _, bit in steps:
        found = found + [distance + bit for distance in found]
    return found


def by_distance(blocks, place, order):
    return jnp.concatenate(
        [lax.dynamic_slice_in_dim(blocks, place ^ i, 1, axis=0) for i in order], axis=0
    )


def by_place(blocks, place, order):
    natural = jnp.concatenate([blocks[order.index(i)][None] for i in range(len(order))], axis=0)
    return by_distance(natural, place, range(len(order)))


def ring_owner(spot, size):
    return jnp.where(spot < size // 2, 2 * spot, 2 * (size - 1 - spot) + 1)


def ring_spot(place, size):
    return jnp.where(place % 2 == 0, place // 2, size - 1 - place // 2)


def ring_shift(array, axis, by):
    size = lax.axis_size(axis)
    ring = [2 * i for i in range(size // 2)] + [2 * i + 1 for i in reversed(range(size // 2))]
    return lax.ppermute(array, axis, [(ring[i], ring[(i + by) % size]) for i in range(size)])


def ring_gather(arrays, axis, beside):
    size = lax.axis_size(axis)
    found = [[array] + [None] * (size - 1) for array in arrays]
    ahead, behind, others, rounds = arrays, arrays, [], []
    for k in range(1, size // 2 + 1):
        behind = [ring_shift(array, axis, 1) for array in behind]
        if k < size - k:
            ahead = [ring_shift(array, axis, -1) for array in ahead]
        other = beside[k - 1](others) if k <= len(beside) else None
        behind, ahead, other = lax.optimization_barrier((behind, ahead, other))
        others.append(other)
        rounds.append(behind)
        for pieces, before, after in zip(found, behind, ahead):
            pieces[size - k] = before
            if k < size - k:
                pieces[k] = after
    return found, others, rounds


def ring_begin(parts, axis):
    size = lax.axis_size(axis)
    half = size // 2
    left = [(parts[half - k], parts[half + 1 + k] if k < half - 1 else None) for k in range(1, half)]
    return (parts[half], parts[half + 1]), left + [(parts[0], None)]


def ring_round(ring, axis):
    (ahead, behind), left = ring
    more_ahead, more_behind = left[0]
    ahead = add_rounded(ring_shift(ahead, axis, 1), more_ahead)
    if behind is not None and len(left) > 1:
        behind = ring_shift(behind, axis, -1)
        if more_behind is not None:
            behind = add_rounded(behind, more_behind)
    return (ahead, behind), left[1:]


def ring_end(ring, axis):
    (ahead, behind), left = ring
    while left:
        if len(left) == 1:
            found = ring_shift(ahead, axis, 1).astype(jnp.float32) + left[0][0]
            return found + behind
        (ahead, behind), left = ring_round(((ahead, behind), left), axis)
    return ahead.astype(jnp.float32) + behind


def pad_columns(array, width):
    return jnp.pad(array, ((0, 0), (0, width - array.shape[1])))


def pad_rows(array, height):
    return jnp.pad(array, ((0, height - array.shape[0]), (0, 0)))


def round_up(size, step=LANES):
    return -(-size // step) * step


def feed_forward_kernel(count, wide_steps, sub, *refs):
    first_ref, slot_ref, rows_ref, raw_ref, mask_ref, router_ref, tiles_ref = refs[:7]
    back_out, gate_ref, upper_ref, hidden_ref = refs[7:11]
    gains, shares, kept, tiles, back_ref, arrived, back_left = refs[11:]
    cut, step, last = pl.program_id(0), pl.program_id(1), count + wide_steps - 1
    owners, _, each, width = rows_ref.shape
    half, rows = raw_ref.shape[3], owners * each
    block = sub // each
    f32, bf16 = jnp.float32, jnp.bfloat16

    def arrival(n):
        return pltpu.make_async_copy(tiles_ref.at[n], tiles.at[n], arrived.at[n])

    def back_leaving(n):
        size = width // wide_steps
        extra = back_ref.shape[2] - width if n == wide_steps - 1 else 0
        of = (slice(None), slice(None), pl.ds(n * size, size + extra))
        return pltpu.make_async_copy(back_ref.at[of], back_out.at[(cut, *of)], back_left.at[n])

    @pl.when(step == 0)
    def _():
        @pl.when(cut == 0)
        def _():
            for n in range(count):
                arrival(n).start()

        values = rows_ref[...].reshape(rows, width)
        logits = jnp.dot(values, router_ref[...], preferred_element_type=f32)
        sig = jax.nn.sigmoid(logits) * mask_ref[...].reshape(logits.shape)
        gating = ROUTE_SCALE * sig / jnp.sum(sig, axis=1, keepdims=True)
        lanes = lax.broadcasted_iota(jnp.int32, gating.shape, 1)
        for e in range(EXP_DEV):
            own = jnp.sum(jnp.where(lanes == first_ref[0] + e, gating, 0.0), axis=1, keepdims=True)
            gains[e] = jnp.broadcast_to(own, gains.shape[1:])
        gains[EXP_DEV] = jnp.ones(gains.shape[1:], f32)
        shares[...] = jnp.zeros_like(shares)

    @pl.when(step < count)
    def _():
        @pl.when(cut == 0)
        def _():
            arrival(step).wait()

        kind = jnp.minimum(step // ((count - 1) // EXP_DEV), EXP_DEV)
        for i in range(rows // sub):
            at, of = pl.ds(i * sub, sub), pl.ds(i * block, block)
            values = rows_ref[of].reshape(sub, width)
            both = lax.dot_general(
                values, tiles[step], (((1,), (1,)), ((), ())), preferred_element_type=f32
            )
            gate, upper = both[:, :half], both[:, half:]
            gain, raw = gains[kind, at, :], raw_ref[of].reshape(sub, half).astype(f32)
            sig = jax.nn.sigmoid(gate)
            silu = gate * sig
            hidden = silu * upper
            grad = gain * raw
            shape = (block, 1, each, half)
            hidden_ref[of] = (gain * hidden).astype(bf16).reshape(shape)
            shares[kind, at, :] += hidden * raw
            gate_grad = (grad * upper * (sig + silu * (1.0 - sig))).astype(bf16)
            upper_grad = (grad * silu).astype(bf16)
            gate_ref[of] = gate_grad.reshape(shape)
            upper_ref[of] = upper_grad.reshape(shape)
            kept[step, at, :half] = gate_grad
            kept[step, at, half:] = upper_grad

    @pl.when(step >= count)
    def _():
        size = width // wide_steps
        columns = pl.ds(pl.multiple_of((step - count) * size, size), size)
        for i in range(rows // sub):
            found = sum(
                jnp.dot(
                    kept[n, pl.ds(i * sub, sub), :],
                    tiles[n, :, columns],
                    preferred_element_type=f32,
                )
                for n in range(count)
            ).astype(bf16)
            for j in range(block):
                part = found[j * each : (j + 1) * each]
                back_ref[slot_ref[cut, i * block + j], :, columns] = part

    @pl.when(step == last)
    def _():
        extra = back_ref.shape[2] - width
        lanes = lax.broadcasted_iota(jnp.int32, (rows, extra), 1)
        gating_grad = jnp.zeros(lanes.shape, f32)
        for e in range(EXP_DEV):
            own = jnp.sum(shares[e], axis=1, keepdims=True)
            gating_grad += jnp.where(lanes == first_ref[0] + e, own, 0.0)
        gating_grad = gating_grad.astype(bf16)
        for i in range(owners):
            back_ref[slot_ref[cut, i], :, width:] = gating_grad[i * each : (i + 1) * each]

    for n in range(wide_steps):

        @pl.when(step == count + n)
        def _(n=n):
            back_leaving(n).start()

    @pl.when(step == last)
    def _():
        for n in range(wide_steps):
            back_leaving(n).wait()


def feed_forward(slots, mid_rows, raw_grad, mask, router, tiles, first):
    count, both, width = tiles.shape
    owners, cuts, each, experts = mask.shape
    rows, half, wide_steps = owners * each, both // 2, 4
    bf16, f32 = jnp.bfloat16, jnp.float32

    def tile(step):
        return jnp.minimum(step, count - 1)

    smem, whole = pl.BlockSpec(memory_space=pltpu.SMEM), pl.BlockSpec(memory_space=pl.ANY)
    side = pl.BlockSpec((owners, 1, each, half), lambda c, i: (0, c, 0, tile(i)))
    return pl.pallas_call(
        functools.partial(feed_forward_kernel, count, wide_steps, min(8, owners) * each),
        grid=(cuts, count + wide_steps),
        in_specs=[
            smem,
            smem,
            pl.BlockSpec((owners, 1, each, width), lambda c, i: (0, c, 0, 0)),
            side,
            pl.BlockSpec((owners, 1, each, experts), lambda c, i: (0, c, 0, 0)),
            pl.BlockSpec((width, experts), lambda c, i: (0, 0)),
            whole,
        ],
        out_specs=[whole, side, side, side],
        out_shape=[
            jax.ShapeDtypeStruct((cuts, owners, each, width + LANES), bf16),
            *[jax.ShapeDtypeStruct((owners, cuts, each, count * half), bf16)] * 3,
        ],
        scratch_shapes=[
            pltpu.VMEM((EXP_DEV + 1, rows, half), f32),
            pltpu.VMEM((EXP_DEV + 1, rows, half), f32),
            pltpu.VMEM((count, rows, both), bf16),
            pltpu.VMEM(tiles.shape, bf16),
            pltpu.VMEM((owners, each, width + LANES), bf16),
            pltpu.SemaphoreType.DMA((count,)),
            pltpu.SemaphoreType.DMA((wide_steps,)),
        ],
        compiler_params=pltpu.CompilerParams(vmem_limit_bytes=VMEM_BYTES),
        cost_estimate=pl.CostEstimate(
            flops=4 * cuts * rows * width * both * count,
            bytes_accessed=50_000_000,
            transcendentals=0,
        ),
    )(first, slots, mid_rows, raw_grad, mask, router, tiles)


def rows_by_device_kernel(*refs):
    *left_refs, right_ref, out_ref = refs
    for i, left_ref in enumerate(left_refs):

        @pl.when(pl.program_id(1) == i)
        def _(left_ref=left_ref):
            found = jnp.dot(left_ref[...], right_ref[...], preferred_element_type=jnp.float32)
            out_ref[...] = found.astype(out_ref.dtype).reshape(out_ref.shape)


def rows_by_device(left_parts, right_side, devices):
    rows, depth = left_parts[0].shape
    columns, count = right_side.shape[1], len(left_parts)
    wide = columns // 2
    return pl.pallas_call(
        rows_by_device_kernel,
        grid=(2, count),
        in_specs=[pl.BlockSpec((rows, depth), lambda j, i: (0, 0))] * count
        + [pl.BlockSpec((depth, wide), lambda j, i: (0, j))],
        out_specs=pl.BlockSpec((devices, 1, rows // devices, wide), lambda j, i: (0, i, 0, j)),
        out_shape=jax.ShapeDtypeStruct(
            (devices, count, rows // devices, columns), right_side.dtype
        ),
        compiler_params=pltpu.CompilerParams(vmem_limit_bytes=VMEM_BYTES),
        cost_estimate=pl.CostEstimate(
            flops=2 * count * rows * depth * columns,
            bytes_accessed=2 * count * rows * (depth + columns),
            transcendentals=0,
        ),
    )(*left_parts, right_side).reshape(count * rows, columns)


def place_kernel(places_ref, *refs):
    *pieces, out_ref = refs
    for i, piece in enumerate(pieces):

        @pl.when(pl.program_id(0) == i)
        def _(piece=piece):
            out_ref[0] = piece[...]


def place_blocks(pieces, places):
    shape = pieces[0].shape
    return pl.pallas_call(
        place_kernel,
        grid_spec=pltpu.PrefetchScalarGridSpec(
            num_scalar_prefetch=1,
            grid=(len(pieces),),
            in_specs=[pl.BlockSpec(shape, lambda i, at: (0, 0))] * len(pieces),
            out_specs=pl.BlockSpec((1, *shape), lambda i, at: (at[i], 0, 0)),
        ),
        out_shape=jax.ShapeDtypeStruct((len(pieces), *shape), pieces[0].dtype),
        compiler_params=pltpu.CompilerParams(vmem_limit_bytes=VMEM_BYTES),
    )(jnp.stack(places).astype(jnp.int32), *pieces)


def on_device_dense(
    hidden_in,
    out_grad,
    query_weight,
    latent_weight,
    expand_weight,
    output_weight,
    norm_gains,
    latent_gain,
    router_weight,
    shared_gate_up,
    shared_down,
    expert_gate_up,
    expert_down,
    expert_ids,
):
    groups, parts = lax.axis_size("ep"), lax.axis_size("tp")
    group, part = lax.axis_index("ep"), lax.axis_index("tp")
    tokens, width = hidden_in.shape
    own = tokens // parts
    experts = router_weight.shape[1]
    bf16, f32 = jnp.bfloat16, jnp.float32
    ep_steps, tp_steps = axis_bits("ep"), axis_bits("tp")
    tp_order = distances(tp_steps)
    every = ("ep", "tp")
    devices = groups * parts
    cut_rows = own // CUTS

    spot = ring_spot(group, groups)
    ring_groups = [ring_owner((spot + k) % groups, groups) for k in range(groups)]

    mask_own = jnp.sum(
        (expert_ids[:, :, None] == jnp.arange(experts)[None, None, :]).astype(bf16), axis=1
    )
    sizes = [norm_gains.size, latent_gain.size, router_weight.size, mask_own.size]
    small = jnp.concatenate(
        [array.reshape(1, -1) for array in (norm_gains, latent_gain, router_weight, mask_own)],
        axis=1,
    )
    query_size, latent_width = query_weight.shape[1], latent_weight.shape[1]
    output_size = output_weight.shape[0]
    into_size = round_up(query_size + latent_width)
    into = pad_columns(jnp.concatenate([query_weight, latent_weight], axis=1), into_size)
    out_of = jnp.concatenate(
        [output_weight.T, expand_weight.reshape(output_weight.shape[1], -1)], axis=1
    )

    units = shared_down.shape[0] // groups
    shared_gu_own = lax.all_to_all(
        shared_gate_up.reshape(2, -1, groups, units), "ep", split_axis=2, concat_axis=1, tiled=True
    ).reshape(2, width, units)
    shared_down_own = lax.all_to_all(shared_down, "ep", split_axis=0, concat_axis=1, tiled=True)


    hidden_units = expert_down.shape[1]
    expert_pad, shared_pad = round_up(hidden_units), round_up(units)

    def dense_weights(expert_gate_up, expert_down):
        side_weights = [
            jnp.concatenate(
                [pad_rows(expert_gate_up[e, side].T, expert_pad) for e in range(EXP_DEV)]
                + [pad_rows(shared_gu_own[side].T, shared_pad)],
                axis=0,
            ).reshape(-1, LANES, width)
            for side in range(2)
        ]
        tiles = jnp.concatenate(side_weights, axis=1)
        down_weight = jnp.concatenate(
            [pad_rows(expert_down[e], expert_pad) for e in range(EXP_DEV)]
            + [pad_rows(shared_down_own, shared_pad)],
            axis=0,
        )
        return tiles, down_weight

    (into_pieces, out_of_pieces), others, rounds = ring_gather(
        [into, out_of],
        "ep",
        [
            lambda _: spread(small, ep_steps[:1]),
            lambda done: (spread(done[0], ep_steps[1:2]), shared_gu_own, shared_down_own),
            lambda done: spread(done[1][0], ep_steps[2:]),
        ],
    )
    small_rel = others[2]
    _, shared_gu_own, shared_down_own = others[1]
    at = [sum(sizes[:i]) for i in range(len(sizes) + 1)]
    small_full = by_place(small_rel, group, distances(ep_steps))
    gain_rows = (
        small_full[:, : at[1]].reshape(groups, 2, -1).transpose(1, 0, 2).reshape(2, width)
    ).astype(f32)
    gain_latent = small_full[:, at[1] : at[2]].reshape(-1).astype(f32)
    router_full = small_full[:, at[2] : at[3]].reshape(width, experts)

    into_full = place_blocks(into_pieces, ring_groups).reshape(width, -1)
    out_of_full = place_blocks(out_of_pieces, ring_groups).reshape(width, -1)
    expand_full = out_of_full[:, output_size:].reshape(KV_RANK, -1)
    output_turned = out_of_full[:, :output_size]

    out_grad_late, _ = lax.optimization_barrier((out_grad, rounds[-2][0]))

    gather_rows = own // GATHERS
    cuts = CUTS // GATHERS

    def by_gather(rows):
        rows = rows.reshape(devices, GATHERS, gather_rows, -1).transpose(1, 0, 2, 3)
        return list(rows.reshape(GATHERS, devices * gather_rows, -1))

    grad_own = lax.dynamic_slice_in_dim(out_grad_late, part * own, own, axis=0)
    grad_parts = by_gather(lax.all_gather(grad_own, every, axis=0, tiled=True))
    mask_parts = [
        rows.astype(f32).reshape(devices, cuts, cut_rows, experts)
        for rows in by_gather(small_full[:, at[3] :])
    ]

    row_blocks = hidden_in.reshape(parts, own, width)
    hidden_rel = by_distance(row_blocks, part, tp_order).reshape(tokens, width)
    heads_local = query_size // (NOPE + ROPE)
    places = ((part ^ jnp.array(tp_order))[:, None] * own + jnp.arange(own)[None, :]).reshape(-1)
    frequency = ROPE_BASE ** (-(jnp.arange(ROPE // 2).astype(f32) * 2.0 / ROPE))
    angles = places.astype(f32)[:, None] * frequency[None, :]
    cosine_table = jnp.cos(angles)
    sine_table = jnp.sin(angles)
    normed_in, unit_in, inverse_in = norm_forward(hidden_rel.astype(f32), gain_rows[0])
    normed_low = normed_in.astype(bf16)
    both_in = matmul(normed_low, into_full)
    query_raw = both_in[:, :query_size].reshape(tokens, heads_local, NOPE + ROPE)
    queries = jnp.concatenate(
        [
            query_raw[..., :NOPE],
            rotate(query_raw[..., NOPE:], cosine_table[:, None, :], sine_table[:, None, :]),
        ],
        axis=-1,
    ).astype(bf16)
    latent = both_in[:, query_size : query_size + latent_width]
    latent_normed, latent_unit, latent_inverse = norm_forward(latent[:, :KV_RANK], gain_latent)
    latent_low = latent_normed.astype(bf16)
    key_rope = rotate(latent[:, KV_RANK:], cosine_table, sine_table).astype(bf16)
    expanded = (
        matmul(latent_low, expand_full).astype(bf16).reshape(tokens, heads_local, NOPE + V_DIM)
    )
    key_rows = jnp.concatenate(
        [expanded[..., :NOPE], jnp.broadcast_to(key_rope[:, None, :], (tokens, heads_local, ROPE))],
        axis=-1,
    )
    values = expanded[..., NOPE:]
    score_scale = 1.0 / math.sqrt(NOPE + ROPE)
    causal = places[:, None] >= places[None, :]
    scores = (
        jnp.einsum("qhd,khd->hqk", queries, key_rows, preferred_element_type=f32) * score_scale
    )
    scores = jnp.where(causal[None], scores, -1e30)
    row_max = jnp.max(scores, axis=-1, keepdims=True)
    powers = jnp.exp(scores - row_max)
    softmax_probs = powers / jnp.sum(powers, axis=-1, keepdims=True)
    probs_low = softmax_probs.astype(bf16)
    attended = jnp.einsum("hqk,khd->qhd", probs_low, values, preferred_element_type=f32)
    attended = attended.astype(bf16).reshape(tokens, heads_local * V_DIM)
    attn_part = transposed_right(attended, output_turned).astype(bf16)
    resid = hidden_rel[:own].astype(f32) + fold(attn_part, tp_steps).astype(f32)

    normed_mid, unit_mid, inverse_mid = norm_forward(resid, gain_rows[1])
    mid_own, expert_gate_up, expert_down = lax.optimization_barrier(
        (normed_mid.astype(bf16), expert_gate_up, expert_down)
    )
    tiles, down_weight = dense_weights(expert_gate_up, expert_down)
    raw_parts = [
        transposed_right(rows, down_weight).astype(bf16).reshape(devices, cuts, cut_rows, -1)
        for rows in grad_parts
    ]
    first = (group * EXP_DEV).astype(jnp.int32).reshape(1)
    mid_parts = [
        lax.all_gather(
            mid_own[i * gather_rows : (i + 1) * gather_rows], every, axis=0, tiled=True
        )
        for i in range(GATHERS)
    ]
    one_order = (ep_steps + tp_steps)[::-1]
    turn = [0, *range(2, len(tp_steps) + 1), 1, *range(len(tp_steps) + 1, len(one_order))]
    orders = [one_order, [one_order[i] for i in turn]]
    distance = jnp.arange(devices, dtype=jnp.int32) ^ (group * parts + part)
    slots = []
    for order in orders:
        slot = jnp.zeros_like(distance)
        for axis, bit in order:
            slot = 2 * slot + distance // (bit * (parts if axis == "ep" else 1)) % 2
        slots.append(slot)
    slots = jnp.stack([slots[cut % 2] for cut in range(cuts)])

    def on_a_step(sums):
        return [(fold_step(rows, todo[0]), todo[1:]) if todo else (rows, todo) for rows, todo in sums]

    def together(work, sums):
        work, rows = lax.optimization_barrier((work, [rows for rows, _ in sums]))
        return work, [(each, todo) for each, (_, todo) in zip(rows, sums)]

    mid_parts[0], raw_parts = lax.optimization_barrier((mid_parts[0], raw_parts))
    sums, gate_parts, upper_parts, hidden_parts = [], [], [], []
    for i in range(GATHERS):
        mid_rows = mid_parts[i]
        back, *sides = feed_forward(
            slots,
            mid_rows.reshape(devices, cuts, cut_rows, width),
            raw_parts[i],
            mask_parts[i],
            router_full,
            tiles,
            first,
        )
        (back, sides), sums = together((back, sides), on_a_step(sums))
        sums += [(back[cut], orders[cut % 2]) for cut in range(cuts)]
        for parts_of, side in zip((gate_parts, upper_parts, hidden_parts), sides):
            parts_of.append(side.reshape(mid_rows.shape[0], -1))
        if i == 0:
            firsts = [
                transposed_left(parts_of[0], rows[0])
                for parts_of, rows in (
                    (hidden_parts, grad_parts),
                    (gate_parts, mid_parts),
                    (upper_parts, mid_parts),
                )
            ]
            (firsts, mid_parts[1:]), sums = together((firsts, mid_parts[1:]), on_a_step(sums))
    grad_down, grad_gate, grad_upper = firsts
    out_part = rows_by_device(hidden_parts, down_weight, devices)
    out_part, sums = together(out_part, on_a_step(sums))
    out_own = lax.psum_scatter(out_part, every, scatter_dimension=0, tiled=True)
    block_own = (lax.optimization_barrier(resid) + out_own.astype(f32)).astype(bf16)
    while any(todo for _, todo in sums):
        sums = on_a_step(sums)
    back_own = jnp.concatenate([rows[0] for rows, _ in sums], axis=0)

    back_own = back_own.astype(f32)
    gating_grad = back_own[:, width : width + experts]
    mask = lax.dynamic_slice_in_dim(mask_own, part * own, own, axis=0).astype(f32)
    sigmoids = jax.nn.sigmoid(matmul(mid_own, router_full))
    chosen = sigmoids * mask
    sigmoid_total = jnp.sum(chosen, axis=1, keepdims=True)
    weighted = jnp.sum(gating_grad * chosen, axis=1, keepdims=True) / sigmoid_total
    sigmoid_grad = ROUTE_SCALE / sigmoid_total * (gating_grad - weighted)
    logits_grad = (sigmoid_grad * chosen * (1.0 - sigmoids)).astype(bf16)
    grad_router = transposed_left(mid_own, logits_grad)
    mid_grad = back_own[:, :width] + transposed_right(logits_grad, router_full)
    resid_norm_grad, grad_gain_mid = norm_backward(mid_grad, unit_mid, inverse_mid, gain_rows[1])
    resid_grad = grad_own.astype(f32) + resid_norm_grad

    resid_low, hidden_parts = lax.optimization_barrier((resid_grad.astype(bf16), hidden_parts))
    grad_down = grad_down + transposed_left(hidden_parts[1], grad_parts[1])
    attn_rows, gate_parts, grad_down = lax.optimization_barrier(
        (spread(resid_low, tp_steps[:1]), gate_parts, grad_down)
    )
    grad_gate = grad_gate + transposed_left(gate_parts[1], mid_parts[1])
    attn_grad, grad_gate = lax.optimization_barrier((spread(attn_rows, tp_steps[1:]), grad_gate))

    def ring_columns(left_side, right_side):
        size = left_side.shape[1] // groups
        return [
            transposed_left(
                lax.dynamic_slice_in_dim(left_side, g * size, size, axis=1), right_side
            ).astype(bf16)
            for g in ring_groups
        ]

    def beside(work, rings):
        rounds = [ring_round(ring, "ep") for ring in rings]
        work, states = lax.optimization_barrier((work, [state for state, _ in rounds]))
        return work, [(state, left) for state, (_, left) in zip(states, rounds)]

    output_ring = ring_begin(ring_columns(attn_grad, attended), "ep")
    attended_grad = (
        matmul(attn_grad, output_turned).astype(bf16).reshape(tokens, heads_local, V_DIM)
    )
    values_grad = jnp.einsum("hqk,qhd->khd", probs_low, attended_grad, preferred_element_type=f32)
    probs_grad = jnp.einsum("qhd,khd->hqk", attended_grad, values, preferred_element_type=f32)
    scores_grad = (
        softmax_probs * (probs_grad - jnp.sum(softmax_probs * probs_grad, axis=-1, keepdims=True))
    ).astype(bf16)
    (scores_grad, values_grad), (output_ring,) = beside((scores_grad, values_grad), [output_ring])
    query_grad = (
        jnp.einsum("hqk,khd->qhd", scores_grad, key_rows, preferred_element_type=f32) * score_scale
    )
    keys_grad = (
        jnp.einsum("hqk,qhd->khd", scores_grad, queries, preferred_element_type=f32) * score_scale
    )
    query_raw_grad = (
        jnp.concatenate(
            [
                query_grad[..., :NOPE],
                rotate(query_grad[..., NOPE:], cosine_table[:, None, :], -sine_table[:, None, :]),
            ],
            axis=-1,
        )
        .astype(bf16)
        .reshape(tokens, heads_local * (NOPE + ROPE))
    )
    expanded_grad = (
        jnp.concatenate([keys_grad[..., :NOPE], values_grad], axis=-1)
        .astype(bf16)
        .reshape(tokens, heads_local * (NOPE + V_DIM))
    )
    latent_normed_grad = transposed_right(expanded_grad, expand_full)
    latent_part_grad, gain_latent_part = norm_backward(
        latent_normed_grad, latent_unit, latent_inverse, gain_latent
    )
    rope_raw_grad = rotate(jnp.sum(keys_grad[..., NOPE:], axis=1), cosine_table, -sine_table)
    latent_grad = jnp.concatenate([latent_part_grad, rope_raw_grad], axis=1).astype(bf16)
    both_grad = pad_columns(jnp.concatenate([query_raw_grad, latent_grad], axis=1), into_size)
    both_grad, (output_ring,) = beside(both_grad, [output_ring])
    into_ring = ring_begin(ring_columns(normed_low, both_grad), "ep")
    in_grad_part = transposed_right(both_grad, into_full).astype(bf16)
    expand_blocks = transposed_left(latent_low, expanded_grad).astype(bf16)
    expand_blocks = expand_blocks.reshape(groups, -1, expand_blocks.shape[1])
    expand_ring = ring_begin(
        [lax.dynamic_slice_in_dim(expand_blocks, g, 1, axis=0)[0] for g in ring_groups], "ep"
    )
    work = (in_grad_part, [left for _, left in (into_ring, expand_ring)])
    (in_grad_part, lefts), (into_ring, output_ring) = beside(work, [into_ring, output_ring])
    into_ring, expand_ring = (into_ring[0], lefts[0][1:]), (expand_ring[0], lefts[1])

    upper_rows, _ = lax.optimization_barrier((upper_parts[1], in_grad_part))
    grad_upper = grad_upper + transposed_left(upper_rows, mid_parts[1])
    in_grad = fold_step(in_grad_part, tp_steps[-1])
    (grad_sides, in_grad), (into_ring, expand_ring, output_ring) = beside(
        ((grad_gate, grad_upper), in_grad), [into_ring, expand_ring, output_ring]
    )

    shared_at = EXP_DEV * expert_pad
    shared_gu_back = lax.all_to_all(
        jnp.stack([grad[shared_at:][:units].T for grad in grad_sides])
        .astype(bf16)
        .reshape(2, width, 1, units),
        "ep",
        split_axis=1,
        concat_axis=2,
        tiled=True,
    )
    shared_down_back = lax.all_to_all(
        grad_down[shared_at : shared_at + units].astype(bf16),
        "ep",
        split_axis=1,
        concat_axis=0,
        tiled=True,
    )
    grad_expert_gate_up = jnp.stack(
        [
            jnp.stack([grad[e * expert_pad :][:hidden_units].T for grad in grad_sides])
            for e in range(EXP_DEV)
        ]
    )
    grad_expert_down = jnp.stack(
        [grad_down[e * expert_pad : e * expert_pad + hidden_units] for e in range(EXP_DEV)]
    )
    grad_shared_gu_out = shared_gu_back.reshape(shared_gate_up.shape).astype(f32)
    grad_shared_down_out = shared_down_back.astype(f32)
    in_grad = fold(in_grad, tp_steps[:-1]).astype(f32)
    in_grad, (into_ring, expand_ring) = beside(in_grad, [into_ring, expand_ring])
    input_norm_grad, grad_gain_in = norm_backward(
        in_grad, unit_in[:own], inverse_in[:own], gain_rows[0]
    )
    hidden_own = (resid_grad + input_norm_grad).astype(bf16)
    into_sum = ring_end(into_ring, "ep")
    grad_expand_out = ring_end(expand_ring, "ep")
    grad_output_out = ring_end(output_ring, "ep").T
    grad_query_out = into_sum[:, :query_size]
    grad_latent_out = into_sum[:, query_size : query_size + latent_width]
    for axis, bit in tp_steps:
        rounded = grad_latent_out.astype(bf16)
        grad_latent_out = rounded.astype(f32) + swap(rounded, axis, bit).astype(f32)
    grad_small = jnp.concatenate(
        [
            jnp.stack([grad_gain_in, grad_gain_mid])
            .reshape(2, groups, -1)
            .transpose(1, 0, 2)
            .reshape(groups, -1),
            gain_latent_part.reshape(groups, -1),
            grad_router.reshape(groups, -1),
        ],
        axis=1,
    )
    small_sum = fold(by_distance(grad_small, group, distances(ep_steps)), ep_steps)
    for axis, bit in tp_steps:
        small_sum = small_sum + swap(small_sum, axis, bit)
    small_sum = small_sum.reshape(-1)
    grad_gains_out = small_sum[: at[1]].reshape(norm_gains.shape)
    grad_gain_latent_out = small_sum[at[1] : at[2]]
    grad_router_out = small_sum[at[2] : at[3]].reshape(router_weight.shape)

    def all_own(rows):
        return lax.all_gather(rows, "tp", axis=0, tiled=True)

    return (
        all_own(block_own),
        all_own(hidden_own).astype(f32),
        grad_query_out,
        grad_latent_out,
        grad_expand_out,
        grad_output_out,
        grad_gains_out,
        grad_gain_latent_out,
        grad_router_out,
        grad_shared_gu_out,
        grad_shared_down_out,
        grad_expert_gate_up,
        grad_expert_down,
    )


def power_of_two(size):
    return size & (size - 1) == 0


def on_device(hidden_in, *others):
    groups, parts = lax.axis_size("ep"), lax.axis_size("tp")
    tokens = hidden_in.shape[0]
    mean_load = tokens * TOPK // (EXP_DEV * groups)
    capacity = mean_load + mean_load // 3
    if EXP_DEV * capacity >= tokens and power_of_two(groups) and power_of_two(parts):
        return on_device_dense(hidden_in, *others)
    return on_device_sparse(hidden_in, *others)


def solution(mesh):
    placed = (
        P("ep", None),
        P("ep", None),
        P("ep", "tp"),
        P("ep", None),
        P("ep", "tp"),
        P("tp", "ep"),
        P(None, "ep"),
        P("ep"),
        P("ep", None),
        P(None, "ep", "tp"),
        P("tp", "ep"),
        P("ep", None, None, "tp"),
        P("ep", "tp", None),
        P("ep", None),
    )
    return jax.shard_map(
        on_device,
        mesh=mesh,
        in_specs=placed,
        out_specs=(
            P("ep", None),
            P("ep", None),
            P("ep", "tp"),
            P("ep", None),
            P("ep", "tp"),
            P("tp", "ep"),
            P(None, "ep"),
            P("ep"),
            P("ep", None),
            P(None, "ep", "tp"),
            P("tp", "ep"),
            P("ep", None, None, "tp"),
            P("ep", "tp", None),
        ),
        check_vma=False,
    )
```

```python
import functools
import math

import jax
import jax.numpy as jnp
from jax import lax
from jax.experimental import pallas as pl
from jax.experimental.pallas import tpu as pltpu
from jax.sharding import PartitionSpec as P

NOPE = 128
ROPE = 64
V_DIM = 128
KV_RANK = 512
TOPK = 6
EXP_DEV = 2


EPSILON = 1e-06
ROUTE_SCALE = 2.446
ROPE_BASE = 50000.0


def matmul(left_side, right_side):
    return jnp.dot(left_side, right_side, preferred_element_type=jnp.float32)


def transposed_left(left_side, right_side):
    return lax.dot_general(
        left_side, right_side, (((0,), (0,)), ((), ())), preferred_element_type=jnp.float32
    )


def transposed_right(left_side, right_side):
    return lax.dot_general(
        left_side, right_side, (((1,), (1,)), ((), ())), preferred_element_type=jnp.float32
    )


def rotate(values, cosine_table, sine_table):
    halfway = values.shape[-1] // 2
    first_half = values[..., :halfway]
    second_half = values[..., halfway:]
    return jnp.concatenate(
        [
            first_half * cosine_table - second_half * sine_table,
            second_half * cosine_table + first_half * sine_table,
        ],
        axis=-1,
    )


def norm_forward(values, gain_row):
    inverse = lax.rsqrt(jnp.mean(values * values, axis=-1, keepdims=True) + EPSILON)
    unit_rows = values * inverse
    return (unit_rows * gain_row, unit_rows, inverse)


def norm_backward(incoming, unit_rows, inverse, gain_row):
    scaled = incoming * gain_row
    grad_values = inverse * (
        scaled - unit_rows * jnp.mean(scaled * unit_rows, axis=-1, keepdims=True)
    )
    return (grad_values, jnp.sum(incoming * unit_rows, axis=0))


def on_device_sparse(
    hidden_in,
    out_grad,
    query_weight,
    latent_weight,
    expand_weight,
    output_weight,
    norm_gains,
    latent_gain,
    router_weight,
    shared_gate_up,
    shared_down,
    expert_gate_up,
    expert_down,
    expert_ids,
):
    (
        query_full,
        latent_full,
        expand_full,
        output_full,
        gains_full,
        latent_gain_full,
        router_full,
        shared_gu_full,
        shared_down_full,
    ) = (
        lax.all_gather(query_weight, "ep", axis=0, tiled=True),
        lax.all_gather(latent_weight, "ep", axis=0, tiled=True),
        lax.all_gather(expand_weight, "ep", axis=0, tiled=True),
        lax.all_gather(output_weight, "ep", axis=1, tiled=True),
        lax.all_gather(norm_gains, "ep", axis=1, tiled=True),
        lax.all_gather(latent_gain, "ep", axis=0, tiled=True),
        lax.all_gather(router_weight, "ep", axis=0, tiled=True),
        lax.all_gather(shared_gate_up, "ep", axis=1, tiled=True),
        lax.all_gather(shared_down, "ep", axis=1, tiled=True),
    )
    tokens = hidden_in.shape[0]
    model_width = hidden_in.shape[1]
    heads_local = query_full.shape[1] // (NOPE + ROPE)
    gain_rows = gains_full.astype(jnp.float32)
    gain_latent = latent_gain_full.astype(jnp.float32)
    places = jnp.arange(tokens).astype(jnp.float32)
    frequency = ROPE_BASE ** (-(jnp.arange(ROPE // 2).astype(jnp.float32) * 2.0 / ROPE))
    angles = places[:, None] * frequency[None, :]
    cosine_table = jnp.cos(angles)
    sine_table = jnp.sin(angles)
    resid_in = hidden_in.astype(jnp.float32)
    normed_in, unit_in, inverse_in = norm_forward(resid_in, gain_rows[0])
    normed_low = normed_in.astype(jnp.bfloat16)
    query_raw = matmul(normed_low, query_full).reshape(tokens, heads_local, NOPE + ROPE)
    queries = jnp.concatenate(
        [
            query_raw[..., :NOPE],
            rotate(query_raw[..., NOPE:], cosine_table[:, None, :], sine_table[:, None, :]),
        ],
        axis=-1,
    ).astype(jnp.bfloat16)
    latent = matmul(normed_low, latent_full)
    latent_normed, latent_unit, latent_inverse = norm_forward(latent[:, :KV_RANK], gain_latent)
    latent_low = latent_normed.astype(jnp.bfloat16)
    key_rope = rotate(latent[:, KV_RANK:], cosine_table, sine_table).astype(jnp.bfloat16)
    expanded = (
        matmul(latent_low, expand_full)
        .astype(jnp.bfloat16)
        .reshape(tokens, heads_local, NOPE + V_DIM)
    )
    key_rows = jnp.concatenate(
        [expanded[..., :NOPE], jnp.broadcast_to(key_rope[:, None, :], (tokens, heads_local, ROPE))],
        axis=-1,
    )
    values = expanded[..., NOPE:]
    score_scale = 1.0 / math.sqrt(NOPE + ROPE)
    causal = jnp.arange(tokens)[:, None] >= jnp.arange(tokens)[None, :]

    def attention_scores():
        scores = (
            jnp.einsum("qhd,khd->hqk", queries, key_rows, preferred_element_type=jnp.float32)
            * score_scale
        )
        return jnp.where(causal[None], scores, -1e30)

    scores_first = attention_scores()
    row_max = jnp.max(scores_first, axis=-1, keepdims=True)
    log_total = row_max + jnp.log(jnp.sum(jnp.exp(scores_first - row_max), axis=-1, keepdims=True))
    probs_low = jnp.exp(scores_first - log_total).astype(jnp.bfloat16)
    attended = jnp.einsum("hqk,khd->qhd", probs_low, values, preferred_element_type=jnp.float32)
    attended = attended.astype(jnp.bfloat16).reshape(tokens, heads_local * V_DIM)
    attn_out = lax.psum(matmul(attended, output_full), "tp")
    resid = resid_in + attn_out
    normed_mid, unit_mid, inverse_mid = norm_forward(resid, gain_rows[1])
    mid_low = normed_mid.astype(jnp.bfloat16)
    logits = matmul(mid_low, router_full)
    experts = router_full.shape[1]
    route_mask = (expert_ids[:, :, None] == jnp.arange(experts)[None, None, :]).astype(jnp.float32)
    chosen = jnp.sum(route_mask * logits[:, None, :], axis=2)
    sigmoids = jax.nn.sigmoid(chosen)
    sigmoid_total = jnp.sum(sigmoids, axis=1, keepdims=True)
    gating = ROUTE_SCALE * sigmoids / sigmoid_total
    shared_gate = matmul(mid_low, shared_gu_full[0])
    shared_upper = matmul(mid_low, shared_gu_full[1])
    shared_sig = jax.nn.sigmoid(shared_gate)
    shared_hidden = (shared_gate * shared_sig * shared_upper).astype(jnp.bfloat16)
    shared_part = matmul(shared_hidden, shared_down_full)
    groups = lax.axis_size("ep")
    mean_load = tokens * TOPK // (EXP_DEV * groups)
    capacity = mean_load + mean_load // 3
    choices = tokens * TOPK
    rows_total = groups * capacity
    flat_ids = expert_ids.reshape(-1)
    onehot = (flat_ids[:, None] == jnp.arange(experts)[None, :]).astype(jnp.int32)
    slot_of = jnp.sum((jnp.cumsum(onehot, axis=0) - onehot) * onehot, axis=1)
    target = flat_ids % EXP_DEV * rows_total + flat_ids // EXP_DEV * capacity + slot_of
    slot_table = (
        jnp.full((EXP_DEV * rows_total,), choices, jnp.int32)
        .at[target]
        .set(jnp.arange(choices, dtype=jnp.int32))
        .reshape(EXP_DEV, groups, capacity)
    )
    mid_padded = jnp.concatenate([mid_low, jnp.zeros((1, model_width), jnp.bfloat16)], axis=0)
    outgoing = mid_padded[slot_table.reshape(-1) // TOPK].reshape(EXP_DEV, rows_total, model_width)
    expert_rows = lax.all_to_all(outgoing, "ep", split_axis=1, concat_axis=1, tiled=True)
    expert_gate = jnp.einsum(
        "erd,edf->erf", expert_rows, expert_gate_up[:, 0], preferred_element_type=jnp.float32
    )
    expert_upper = jnp.einsum(
        "erd,edf->erf", expert_rows, expert_gate_up[:, 1], preferred_element_type=jnp.float32
    )
    expert_sig = jax.nn.sigmoid(expert_gate)
    expert_hidden = (expert_gate * expert_sig * expert_upper).astype(jnp.bfloat16)
    expert_part = jnp.einsum(
        "erf,efd->erd", expert_hidden, expert_down, preferred_element_type=jnp.float32
    ).astype(jnp.bfloat16)
    returned = lax.all_to_all(expert_part, "ep", split_axis=1, concat_axis=1, tiled=True)
    per_choice = (
        returned.reshape(-1, model_width)[target]
        .reshape(tokens, TOPK, model_width)
        .astype(jnp.float32)
    )
    routed_part = jnp.sum(gating[:, :, None] * per_choice, axis=1)
    moe_out = lax.psum((shared_part + routed_part).astype(jnp.bfloat16), "tp").astype(jnp.float32)
    block_out = (resid + moe_out).astype(jnp.bfloat16)
    grad_top = out_grad.astype(jnp.float32)
    choice_grad = (gating[:, :, None] * grad_top[:, None, :]).astype(jnp.bfloat16)
    grad_padded = jnp.concatenate(
        [choice_grad.reshape(choices, model_width), jnp.zeros((1, model_width), jnp.bfloat16)],
        axis=0,
    )
    outgoing_grad = grad_padded[slot_table.reshape(-1)].reshape(EXP_DEV, rows_total, model_width)
    rows_grad = lax.all_to_all(outgoing_grad, "ep", split_axis=1, concat_axis=1, tiled=True)
    hidden_grad = jnp.einsum(
        "erd,efd->erf", rows_grad, expert_down, preferred_element_type=jnp.float32
    )
    gate_grad = (
        hidden_grad * expert_upper * expert_sig * (1.0 + expert_gate * (1.0 - expert_sig))
    ).astype(jnp.bfloat16)
    upper_grad = (hidden_grad * expert_gate * expert_sig).astype(jnp.bfloat16)
    grad_expert_down = jnp.einsum(
        "erf,erd->efd", expert_hidden, rows_grad, preferred_element_type=jnp.float32
    )
    grad_expert_gate_up = jnp.stack(
        [
            jnp.einsum("erd,erf->edf", expert_rows, gate_grad, preferred_element_type=jnp.float32),
            jnp.einsum("erd,erf->edf", expert_rows, upper_grad, preferred_element_type=jnp.float32),
        ],
        axis=1,
    )
    row_back = jnp.einsum(
        "erf,edf->erd", gate_grad, expert_gate_up[:, 0], preferred_element_type=jnp.float32
    ) + jnp.einsum(
        "erf,edf->erd", upper_grad, expert_gate_up[:, 1], preferred_element_type=jnp.float32
    )
    row_back_low = row_back.astype(jnp.bfloat16)
    back_rows = lax.all_to_all(row_back_low, "ep", split_axis=1, concat_axis=1, tiled=True)
    choice_back = (
        back_rows.reshape(-1, model_width)[target]
        .reshape(tokens, TOPK, model_width)
        .astype(jnp.float32)
    )
    mid_grad_routed = jnp.sum(choice_back, axis=1)
    gating_grad_part = jnp.sum(per_choice * grad_top[:, None, :], axis=2)
    shared_hidden_grad = transposed_right(out_grad, shared_down_full)
    shared_gate_grad = (
        shared_hidden_grad * shared_upper * shared_sig * (1.0 + shared_gate * (1.0 - shared_sig))
    ).astype(jnp.bfloat16)
    shared_upper_grad = (shared_hidden_grad * shared_gate * shared_sig).astype(jnp.bfloat16)
    grad_shared_down = transposed_left(shared_hidden, out_grad)
    grad_shared_gu = jnp.stack(
        [transposed_left(mid_low, shared_gate_grad), transposed_left(mid_low, shared_upper_grad)],
        axis=0,
    )
    mid_grad_shared = transposed_right(shared_gate_grad, shared_gu_full[0]) + transposed_right(
        shared_upper_grad, shared_gu_full[1]
    )
    mid_grad_sum, gating_grad = (
        lax.psum((mid_grad_routed + mid_grad_shared).astype(jnp.bfloat16), "tp").astype(
            jnp.float32
        ),
        lax.psum(gating_grad_part.astype(jnp.bfloat16), "tp").astype(jnp.float32),
    )
    weighted = jnp.sum(gating_grad * sigmoids, axis=1, keepdims=True) / sigmoid_total
    sigmoid_grad = ROUTE_SCALE / sigmoid_total * (gating_grad - weighted)
    chosen_grad = sigmoid_grad * sigmoids * (1.0 - sigmoids)
    logits_grad = jnp.sum(route_mask * chosen_grad[:, :, None], axis=1).astype(jnp.bfloat16)
    grad_router = transposed_left(mid_low, logits_grad)
    mid_grad = mid_grad_sum + transposed_right(logits_grad, router_full)
    resid_norm_grad, grad_gain_mid = norm_backward(mid_grad, unit_mid, inverse_mid, gain_rows[1])
    resid_grad = grad_top + resid_norm_grad
    attn_grad = resid_grad.astype(jnp.bfloat16)
    grad_output = transposed_left(attended, attn_grad)
    attended_grad = (
        transposed_right(attn_grad, output_full)
        .astype(jnp.bfloat16)
        .reshape(tokens, heads_local, V_DIM)
    )
    softmax_probs = jnp.exp(attention_scores() - log_total)
    values_grad = jnp.einsum(
        "hqk,qhd->khd",
        softmax_probs.astype(jnp.bfloat16),
        attended_grad,
        preferred_element_type=jnp.float32,
    )
    probs_grad = jnp.einsum(
        "qhd,khd->hqk", attended_grad, values, preferred_element_type=jnp.float32
    )
    scores_grad = (
        softmax_probs * (probs_grad - jnp.sum(softmax_probs * probs_grad, axis=-1, keepdims=True))
    ).astype(jnp.bfloat16)
    query_grad = (
        jnp.einsum("hqk,khd->qhd", scores_grad, key_rows, preferred_element_type=jnp.float32)
        * score_scale
    )
    keys_grad = (
        jnp.einsum("hqk,qhd->khd", scores_grad, queries, preferred_element_type=jnp.float32)
        * score_scale
    )
    query_raw_grad = (
        jnp.concatenate(
            [
                query_grad[..., :NOPE],
                rotate(query_grad[..., NOPE:], cosine_table[:, None, :], -sine_table[:, None, :]),
            ],
            axis=-1,
        )
        .astype(jnp.bfloat16)
        .reshape(tokens, heads_local * (NOPE + ROPE))
    )
    expanded_grad = jnp.concatenate([keys_grad[..., :NOPE], values_grad], axis=-1).astype(
        jnp.bfloat16
    )
    expanded_grad = expanded_grad.reshape(tokens, heads_local * (NOPE + V_DIM))
    grad_expand = transposed_left(latent_low, expanded_grad)
    latent_normed_grad = transposed_right(expanded_grad, expand_full)
    latent_part_grad, gain_latent_part = norm_backward(
        latent_normed_grad, latent_unit, latent_inverse, gain_latent
    )
    rope_raw_grad = rotate(jnp.sum(keys_grad[..., NOPE:], axis=1), cosine_table, -sine_table)
    latent_grad_part = jnp.concatenate([latent_part_grad, rope_raw_grad], axis=1)
    in_grad_query = transposed_right(query_raw_grad, query_full)
    in_grad_sum, latent_grad, grad_gain_latent = (
        lax.psum(in_grad_query.astype(jnp.bfloat16), "tp").astype(jnp.float32),
        lax.psum(latent_grad_part.astype(jnp.bfloat16), "tp").astype(jnp.float32),
        lax.psum(gain_latent_part.astype(jnp.bfloat16), "tp").astype(jnp.float32),
    )
    latent_grad_low = latent_grad.astype(jnp.bfloat16)
    grad_latent = transposed_left(normed_low, latent_grad_low)
    grad_query = transposed_left(normed_low, query_raw_grad)
    in_grad = in_grad_sum + transposed_right(latent_grad_low, latent_full)
    input_norm_grad, grad_gain_in = norm_backward(in_grad, unit_in, inverse_in, gain_rows[0])
    grad_hidden = resid_grad + input_norm_grad
    grad_gains = jnp.stack([grad_gain_in, grad_gain_mid], axis=0)
    (
        grad_query_out,
        grad_latent_out,
        grad_expand_out,
        grad_output_out,
        grad_gains_out,
        grad_gain_latent_out,
        grad_router_out,
        grad_shared_gu_out,
        grad_shared_down_out,
    ) = (
        lax.psum_scatter(
            grad_query.astype(jnp.bfloat16), "ep", scatter_dimension=0, tiled=True
        ).astype(jnp.float32),
        lax.psum_scatter(
            grad_latent.astype(jnp.bfloat16), "ep", scatter_dimension=0, tiled=True
        ).astype(jnp.float32),
        lax.psum_scatter(
            grad_expand.astype(jnp.bfloat16), "ep", scatter_dimension=0, tiled=True
        ).astype(jnp.float32),
        lax.psum_scatter(
            grad_output.astype(jnp.bfloat16), "ep", scatter_dimension=1, tiled=True
        ).astype(jnp.float32),
        lax.psum_scatter(
            grad_gains.astype(jnp.bfloat16), "ep", scatter_dimension=1, tiled=True
        ).astype(jnp.float32),
        lax.psum_scatter(
            grad_gain_latent.astype(jnp.bfloat16), "ep", scatter_dimension=0, tiled=True
        ).astype(jnp.float32),
        lax.psum_scatter(
            grad_router.astype(jnp.bfloat16), "ep", scatter_dimension=0, tiled=True
        ).astype(jnp.float32),
        lax.psum_scatter(
            grad_shared_gu.astype(jnp.bfloat16), "ep", scatter_dimension=1, tiled=True
        ).astype(jnp.float32),
        lax.psum_scatter(
            grad_shared_down.astype(jnp.bfloat16), "ep", scatter_dimension=1, tiled=True
        ).astype(jnp.float32),
    )
    return (
        block_out,
        grad_hidden,
        grad_query_out,
        grad_latent_out,
        grad_expand_out,
        grad_output_out,
        grad_gains_out,
        grad_gain_latent_out,
        grad_router_out,
        grad_shared_gu_out,
        grad_shared_down_out,
        grad_expert_gate_up,
        grad_expert_down,
    )


CUTS = 4
GATHERS = 2
LANES = 128
VMEM_BYTES = 56 * 1024 * 1024


def swap(array, axis, bit):
    size = lax.axis_size(axis)
    return lax.ppermute(array, axis, [(place, place ^ bit) for place in range(size)])


def axis_bits(axis):
    size = lax.axis_size(axis)
    return [(axis, 1 << bit) for bit in reversed(range(size.bit_length() - 1))]


def spread(rows, steps):
    for axis, bit in steps:
        rows = jnp.concatenate([rows, swap(rows, axis, bit)], axis=0)
    return rows


def add_rounded(left_side, right_side):
    return (left_side.astype(jnp.float32) + right_side.astype(jnp.float32)).astype(
        left_side.dtype
    )


def fold_step(rows, step):
    axis, bit = step
    half = rows.shape[0] // 2
    return add_rounded(rows[:half], swap(rows[half:], axis, bit))


def fold(rows, steps):
    for step in reversed(steps):
        rows = fold_step(rows, step)
    return rows


def distances(steps):
    found = [0]
    for _, bit in steps:
        found = found + [distance + bit for distance in found]
    return found


def by_distance(blocks, place, order):
    return jnp.concatenate(
        [lax.dynamic_slice_in_dim(blocks, place ^ i, 1, axis=0) for i in order], axis=0
    )


def by_place(blocks, place, order):
    natural = jnp.concatenate([blocks[order.index(i)][None] for i in range(len(order))], axis=0)
    return by_distance(natural, place, range(len(order)))


def ring_owner(spot, size):
    return jnp.where(spot < size // 2, 2 * spot, 2 * (size - 1 - spot) + 1)


def ring_spot(place, size):
    return jnp.where(place % 2 == 0, place // 2, size - 1 - place // 2)


def ring_shift(array, axis, by):
    size = lax.axis_size(axis)
    ring = [2 * i for i in range(size // 2)] + [2 * i + 1 for i in reversed(range(size // 2))]
    return lax.ppermute(array, axis, [(ring[i], ring[(i + by) % size]) for i in range(size)])


def ring_gather(arrays, axis, beside):
    size = lax.axis_size(axis)
    found = [[array] + [None] * (size - 1) for array in arrays]
    ahead, behind, others, rounds = arrays, arrays, [], []
    for k in range(1, size // 2 + 1):
        behind = [ring_shift(array, axis, 1) for array in behind]
        if k < size - k:
            ahead = [ring_shift(array, axis, -1) for array in ahead]
        other = beside[k - 1](others) if k <= len(beside) else None
        behind, ahead, other = lax.optimization_barrier((behind, ahead, other))
        others.append(other)
        rounds.append(behind)
        for pieces, before, after in zip(found, behind, ahead):
            pieces[size - k] = before
            if k < size - k:
                pieces[k] = after
    return found, others, rounds


def ring_begin(parts, axis):
    size = lax.axis_size(axis)
    half = size // 2
    left = [(parts[half - k], parts[half + 1 + k] if k < half - 1 else None) for k in range(1, half)]
    return (parts[half], parts[half + 1]), left + [(parts[0], None)]


def ring_round(ring, axis):
    (ahead, behind), left = ring
    more_ahead, more_behind = left[0]
    ahead = add_rounded(ring_shift(ahead, axis, 1), more_ahead)
    if behind is not None and len(left) > 1:
        behind = ring_shift(behind, axis, -1)
        if more_behind is not None:
            behind = add_rounded(behind, more_behind)
    return (ahead, behind), left[1:]


def ring_end(ring, axis):
    (ahead, behind), left = ring
    while left:
        if len(left) == 1:
            found = ring_shift(ahead, axis, 1).astype(jnp.float32) + left[0][0]
            return found + behind
        (ahead, behind), left = ring_round(((ahead, behind), left), axis)
    return ahead.astype(jnp.float32) + behind


def pad_columns(array, width):
    return jnp.pad(array, ((0, 0), (0, width - array.shape[1])))


def pad_rows(array, height):
    return jnp.pad(array, ((0, height - array.shape[0]), (0, 0)))


def round_up(size, step=LANES):
    return -(-size // step) * step


def feed_forward_kernel(count, wide_steps, sub, *refs):
    first_ref, slot_ref, rows_ref, raw_ref, mask_ref, router_ref, tiles_ref = refs[:7]
    back_out, gate_ref, upper_ref, hidden_ref = refs[7:11]
    gains, shares, kept, tiles, back_ref, even, odd, arrived, back_left = refs[11:]
    cut, step, last = pl.program_id(0), pl.program_id(1), count + wide_steps
    owners, _, each, width = rows_ref.shape
    half, rows = raw_ref.shape[3], owners * each
    block = sub // each
    f32, bf16 = jnp.float32, jnp.bfloat16

    def arrival(n):
        return pltpu.make_async_copy(tiles_ref.at[n], tiles.at[n], arrived.at[n])

    def back_leaving(n):
        size = width // wide_steps
        extra = back_ref.shape[2] - width if n == wide_steps - 1 else 0
        of = (slice(None), slice(None), pl.ds(n * size, size + extra))
        return pltpu.make_async_copy(back_ref.at[of], back_out.at[(cut, *of)], back_left.at[n])

    @pl.when(step == 0)
    def _():
        @pl.when(cut == 0)
        def _():
            for n in range(count):
                arrival(n).start()

        values = rows_ref[...].reshape(rows, width)
        logits = jnp.dot(values, router_ref[...], preferred_element_type=f32)
        sig = jax.nn.sigmoid(logits) * mask_ref[...].reshape(logits.shape)
        gating = ROUTE_SCALE * sig / jnp.sum(sig, axis=1, keepdims=True)
        lanes = lax.broadcasted_iota(jnp.int32, gating.shape, 1)
        for e in range(EXP_DEV):
            own = jnp.sum(jnp.where(lanes == first_ref[0] + e, gating, 0.0), axis=1, keepdims=True)
            gains[e] = jnp.broadcast_to(own, gains.shape[1:])
        gains[EXP_DEV] = jnp.ones(gains.shape[1:], f32)
        shares[...] = jnp.zeros_like(shares)

    def products(i, into):
        values = rows_ref[pl.ds(i * block, block)].reshape(sub, width)
        into[pl.ds(i * sub, sub), :] = lax.dot_general(
            values, tiles[step], (((1,), (1,)), ((), ())), preferred_element_type=f32
        )

    def units(i, both):
        at, of = pl.ds(i * sub, sub), pl.ds(i * block, block)
        kind = jnp.minimum((step - 1) // ((count - 1) // EXP_DEV), EXP_DEV)
        gate, upper = both[at, :half], both[at, half:]
        gain, raw = gains[kind, at, :], raw_ref[of].reshape(sub, half).astype(f32)
        sig = jax.nn.sigmoid(gate)
        silu = gate * sig
        hidden = silu * upper
        grad = gain * raw
        shape = (block, 1, each, half)
        hidden_ref[of] = (gain * hidden).astype(bf16).reshape(shape)
        shares[kind, at, :] += hidden * raw
        gate_grad = (grad * upper * (sig + silu * (1.0 - sig))).astype(bf16)
        upper_grad = (grad * silu).astype(bf16)
        gate_ref[of] = gate_grad.reshape(shape)
        upper_ref[of] = upper_grad.reshape(shape)
        kept[step - 1, at, :half] = gate_grad
        kept[step - 1, at, half:] = upper_grad

    @pl.when((cut == 0) & (step < count))
    def _():
        arrival(step).wait()

    @pl.when(step == 0)
    def _():
        for i in range(rows // sub):
            products(i, even)

    for parity, (now, before) in enumerate(((even, odd), (odd, even))):

        @pl.when((step > 0) & (step < count) & (step % 2 == parity))
        def _(now=now, before=before):
            for i in range(rows // sub):
                products(i, now)
                units(i, before)

    @pl.when(step == count)
    def _():
        for i in range(rows // sub):
            units(i, odd if count % 2 == 0 else even)

    @pl.when(step > count)
    def _():
        size = width // wide_steps
        columns = pl.ds(pl.multiple_of((step - count - 1) * size, size), size)
        for i in range(rows // sub):
            found = sum(
                jnp.dot(
                    kept[n, pl.ds(i * sub, sub), :],
                    tiles[n, :, columns],
                    preferred_element_type=f32,
                )
                for n in range(count)
            ).astype(bf16)
            for j in range(block):
                part = found[j * each : (j + 1) * each]
                back_ref[slot_ref[cut, i * block + j], :, columns] = part

    @pl.when(step == last)
    def _():
        extra = back_ref.shape[2] - width
        lanes = lax.broadcasted_iota(jnp.int32, (rows, extra), 1)
        gating_grad = jnp.zeros(lanes.shape, f32)
        for e in range(EXP_DEV):
            own = jnp.sum(shares[e], axis=1, keepdims=True)
            gating_grad += jnp.where(lanes == first_ref[0] + e, own, 0.0)
        gating_grad = gating_grad.astype(bf16)
        for i in range(owners):
            back_ref[slot_ref[cut, i], :, width:] = gating_grad[i * each : (i + 1) * each]

    for n in range(wide_steps):

        @pl.when(step == count + 1 + n)
        def _(n=n):
            back_leaving(n).start()

    @pl.when(step == last)
    def _():
        for n in range(wide_steps):
            back_leaving(n).wait()


def feed_forward(slots, mid_rows, raw_grad, mask, router, tiles, first):
    count, both, width = tiles.shape
    owners, cuts, each, experts = mask.shape
    rows, half, wide_steps = owners * each, both // 2, 4
    bf16, f32 = jnp.bfloat16, jnp.float32

    def tile(step):
        return jnp.clip(step - 1, 0, count - 1)

    smem, whole = pl.BlockSpec(memory_space=pltpu.SMEM), pl.BlockSpec(memory_space=pl.ANY)
    side = pl.BlockSpec((owners, 1, each, half), lambda c, i: (0, c, 0, tile(i)))
    return pl.pallas_call(
        functools.partial(feed_forward_kernel, count, wide_steps, min(8, owners) * each),
        grid=(cuts, count + 1 + wide_steps),
        in_specs=[
            smem,
            smem,
            pl.BlockSpec((owners, 1, each, width), lambda c, i: (0, c, 0, 0)),
            side,
            pl.BlockSpec((owners, 1, each, experts), lambda c, i: (0, c, 0, 0)),
            pl.BlockSpec((width, experts), lambda c, i: (0, 0)),
            whole,
        ],
        out_specs=[whole, side, side, side],
        out_shape=[
            jax.ShapeDtypeStruct((cuts, owners, each, width + LANES), bf16),
            *[jax.ShapeDtypeStruct((owners, cuts, each, count * half), bf16)] * 3,
        ],
        scratch_shapes=[
            pltpu.VMEM((EXP_DEV + 1, rows, half), f32),
            pltpu.VMEM((EXP_DEV + 1, rows, half), f32),
            pltpu.VMEM((count, rows, both), bf16),
            pltpu.VMEM(tiles.shape, bf16),
            pltpu.VMEM((owners, each, width + LANES), bf16),
            pltpu.VMEM((rows, both), f32),
            pltpu.VMEM((rows, both), f32),
            pltpu.SemaphoreType.DMA((count,)),
            pltpu.SemaphoreType.DMA((wide_steps,)),
        ],
        compiler_params=pltpu.CompilerParams(vmem_limit_bytes=VMEM_BYTES),
        cost_estimate=pl.CostEstimate(
            flops=4 * cuts * rows * width * both * count,
            bytes_accessed=50_000_000,
            transcendentals=0,
        ),
    )(first, slots, mid_rows, raw_grad, mask, router, tiles)


def rows_by_device_kernel(*refs):
    *left_refs, right_ref, out_ref = refs
    for i, left_ref in enumerate(left_refs):

        @pl.when(pl.program_id(1) == i)
        def _(left_ref=left_ref):
            found = jnp.dot(left_ref[...], right_ref[...], preferred_element_type=jnp.float32)
            out_ref[...] = found.astype(out_ref.dtype).reshape(out_ref.shape)


def rows_by_device(left_parts, right_side, devices):
    rows, depth = left_parts[0].shape
    columns, count = right_side.shape[1], len(left_parts)
    wide = columns // 2
    return pl.pallas_call(
        rows_by_device_kernel,
        grid=(2, count),
        in_specs=[pl.BlockSpec((rows, depth), lambda j, i: (0, 0))] * count
        + [pl.BlockSpec((depth, wide), lambda j, i: (0, j))],
        out_specs=pl.BlockSpec((devices, 1, rows // devices, wide), lambda j, i: (0, i, 0, j)),
        out_shape=jax.ShapeDtypeStruct(
            (devices, count, rows // devices, columns), right_side.dtype
        ),
        compiler_params=pltpu.CompilerParams(vmem_limit_bytes=VMEM_BYTES),
        cost_estimate=pl.CostEstimate(
            flops=2 * count * rows * depth * columns,
            bytes_accessed=2 * count * rows * (depth + columns),
            transcendentals=0,
        ),
    )(*left_parts, right_side).reshape(count * rows, columns)


def place_kernel(places_ref, *refs):
    *pieces, out_ref = refs
    for i, piece in enumerate(pieces):

        @pl.when(pl.program_id(0) == i)
        def _(piece=piece):
            out_ref[0] = piece[...]


def place_blocks(pieces, places):
    shape = pieces[0].shape
    return pl.pallas_call(
        place_kernel,
        grid_spec=pltpu.PrefetchScalarGridSpec(
            num_scalar_prefetch=1,
            grid=(len(pieces),),
            in_specs=[pl.BlockSpec(shape, lambda i, at: (0, 0))] * len(pieces),
            out_specs=pl.BlockSpec((1, *shape), lambda i, at: (at[i], 0, 0)),
        ),
        out_shape=jax.ShapeDtypeStruct((len(pieces), *shape), pieces[0].dtype),
        compiler_params=pltpu.CompilerParams(vmem_limit_bytes=VMEM_BYTES),
    )(jnp.stack(places).astype(jnp.int32), *pieces)


def on_device_dense(
    hidden_in,
    out_grad,
    query_weight,
    latent_weight,
    expand_weight,
    output_weight,
    norm_gains,
    latent_gain,
    router_weight,
    shared_gate_up,
    shared_down,
    expert_gate_up,
    expert_down,
    expert_ids,
):
    groups, parts = lax.axis_size("ep"), lax.axis_size("tp")
    group, part = lax.axis_index("ep"), lax.axis_index("tp")
    tokens, width = hidden_in.shape
    own = tokens // parts
    experts = router_weight.shape[1]
    bf16, f32 = jnp.bfloat16, jnp.float32
    ep_steps, tp_steps = axis_bits("ep"), axis_bits("tp")
    tp_order = distances(tp_steps)
    every = ("ep", "tp")
    devices = groups * parts
    cut_rows = own // CUTS

    spot = ring_spot(group, groups)
    ring_groups = [ring_owner((spot + k) % groups, groups) for k in range(groups)]

    mask_own = jnp.sum(
        (expert_ids[:, :, None] == jnp.arange(experts)[None, None, :]).astype(bf16), axis=1
    )
    sizes = [norm_gains.size, latent_gain.size, router_weight.size, mask_own.size]
    small = jnp.concatenate(
        [array.reshape(1, -1) for array in (norm_gains, latent_gain, router_weight, mask_own)],
        axis=1,
    )
    query_size, latent_width = query_weight.shape[1], latent_weight.shape[1]
    output_size = output_weight.shape[0]
    into_size = round_up(query_size + latent_width)
    into = pad_columns(jnp.concatenate([query_weight, latent_weight], axis=1), into_size)
    out_of = jnp.concatenate(
        [output_weight.T, expand_weight.reshape(output_weight.shape[1], -1)], axis=1
    )

    units = shared_down.shape[0] // groups
    shared_gu_own = lax.all_to_all(
        shared_gate_up.reshape(2, -1, groups, units), "ep", split_axis=2, concat_axis=1, tiled=True
    ).reshape(2, width, units)
    shared_down_own = lax.all_to_all(shared_down, "ep", split_axis=0, concat_axis=1, tiled=True)


    hidden_units = expert_down.shape[1]
    expert_pad, shared_pad = round_up(hidden_units), round_up(units)

    def dense_weights(shared_gu_own, shared_down_own, expert_gate_up, expert_down):
        side_weights = [
            jnp.concatenate(
                [pad_rows(expert_gate_up[e, side].T, expert_pad) for e in range(EXP_DEV)]
                + [pad_rows(shared_gu_own[side].T, shared_pad)],
                axis=0,
            ).reshape(-1, LANES, width)
            for side in range(2)
        ]
        tiles = jnp.concatenate(side_weights, axis=1)
        down_weight = jnp.concatenate(
            [pad_rows(expert_down[e], expert_pad) for e in range(EXP_DEV)]
            + [pad_rows(shared_down_own, shared_pad)],
            axis=0,
        )
        return tiles, down_weight

    (into_pieces, out_of_pieces), others, rounds = ring_gather(
        [into, out_of],
        "ep",
        [
            lambda _: spread(small, ep_steps[:1]),
            lambda done: spread(done[0], ep_steps[1:2]),
            lambda done: spread(done[1], ep_steps[2:]),
        ],
    )
    small_rel = others[2]
    at = [sum(sizes[:i]) for i in range(len(sizes) + 1)]
    small_full = by_place(small_rel, group, distances(ep_steps))
    gain_rows = (
        small_full[:, : at[1]].reshape(groups, 2, -1).transpose(1, 0, 2).reshape(2, width)
    ).astype(f32)
    gain_latent = small_full[:, at[1] : at[2]].reshape(-1).astype(f32)
    router_full = small_full[:, at[2] : at[3]].reshape(width, experts)

    into_full = place_blocks(into_pieces, ring_groups).reshape(width, -1)
    out_of_full = place_blocks(out_of_pieces, ring_groups).reshape(width, -1)
    expand_full = out_of_full[:, output_size:].reshape(KV_RANK, -1)
    output_turned = out_of_full[:, :output_size]

    out_grad_late, _ = lax.optimization_barrier((out_grad, rounds[-2][0]))

    gather_rows = own // GATHERS
    cuts = CUTS // GATHERS

    def by_gather(rows):
        rows = rows.reshape(devices, GATHERS, gather_rows, -1).transpose(1, 0, 2, 3)
        return list(rows.reshape(GATHERS, devices * gather_rows, -1))

    grad_own = lax.dynamic_slice_in_dim(out_grad_late, part * own, own, axis=0)
    grad_parts = by_gather(lax.all_gather(grad_own, every, axis=0, tiled=True))
    mask_parts = [
        rows.astype(f32).reshape(devices, cuts, cut_rows, experts)
        for rows in by_gather(small_full[:, at[3] :])
    ]

    row_blocks = hidden_in.reshape(parts, own, width)
    hidden_rel = by_distance(row_blocks, part, tp_order).reshape(tokens, width)
    heads_local = query_size // (NOPE + ROPE)
    places = ((part ^ jnp.array(tp_order))[:, None] * own + jnp.arange(own)[None, :]).reshape(-1)
    frequency = ROPE_BASE ** (-(jnp.arange(ROPE // 2).astype(f32) * 2.0 / ROPE))
    angles = places.astype(f32)[:, None] * frequency[None, :]
    cosine_table = jnp.cos(angles)
    sine_table = jnp.sin(angles)
    normed_in, unit_in, inverse_in = norm_forward(hidden_rel.astype(f32), gain_rows[0])
    normed_low = normed_in.astype(bf16)
    both_in = matmul(normed_low, into_full)
    query_raw = both_in[:, :query_size].reshape(tokens, heads_local, NOPE + ROPE)
    queries = jnp.concatenate(
        [
            query_raw[..., :NOPE],
            rotate(query_raw[..., NOPE:], cosine_table[:, None, :], sine_table[:, None, :]),
        ],
        axis=-1,
    ).astype(bf16)
    latent = both_in[:, query_size : query_size + latent_width]
    latent_normed, latent_unit, latent_inverse = norm_forward(latent[:, :KV_RANK], gain_latent)
    latent_low = latent_normed.astype(bf16)
    key_rope = rotate(latent[:, KV_RANK:], cosine_table, sine_table).astype(bf16)
    expanded = (
        matmul(latent_low, expand_full).astype(bf16).reshape(tokens, heads_local, NOPE + V_DIM)
    )
    key_rows = jnp.concatenate(
        [expanded[..., :NOPE], jnp.broadcast_to(key_rope[:, None, :], (tokens, heads_local, ROPE))],
        axis=-1,
    )
    values = expanded[..., NOPE:]
    score_scale = 1.0 / math.sqrt(NOPE + ROPE)
    causal = places[:, None] >= places[None, :]
    scores = (
        jnp.einsum("qhd,khd->hqk", queries, key_rows, preferred_element_type=f32) * score_scale
    )
    scores = jnp.where(causal[None], scores, -1e30)
    row_max = jnp.max(scores, axis=-1, keepdims=True)
    powers = jnp.exp(scores - row_max)
    softmax_probs = powers / jnp.sum(powers, axis=-1, keepdims=True)
    probs_low = softmax_probs.astype(bf16)
    attended = jnp.einsum("hqk,khd->qhd", probs_low, values, preferred_element_type=f32)
    attended = attended.astype(bf16).reshape(tokens, heads_local * V_DIM)
    attended, shared_gu_own, shared_down_own = lax.optimization_barrier(
        (attended, shared_gu_own, shared_down_own)
    )
    attn_part = transposed_right(attended, output_turned).astype(bf16)
    resid = hidden_rel[:own].astype(f32) + fold(attn_part, tp_steps).astype(f32)

    normed_mid, unit_mid, inverse_mid = norm_forward(resid, gain_rows[1])
    mid_own, expert_gate_up, expert_down = lax.optimization_barrier(
        (normed_mid.astype(bf16), expert_gate_up, expert_down)
    )
    tiles, down_weight = dense_weights(
        shared_gu_own, shared_down_own, expert_gate_up, expert_down
    )
    raw_parts = [
        transposed_right(rows, down_weight).astype(bf16).reshape(devices, cuts, cut_rows, -1)
        for rows in grad_parts
    ]
    first = (group * EXP_DEV).astype(jnp.int32).reshape(1)
    mid_parts = [
        lax.all_gather(
            mid_own[i * gather_rows : (i + 1) * gather_rows], every, axis=0, tiled=True
        )
        for i in range(GATHERS)
    ]
    one_order = (ep_steps + tp_steps)[::-1]
    turn = [0, *range(2, len(tp_steps) + 1), 1, *range(len(tp_steps) + 1, len(one_order))]
    orders = [one_order, [one_order[i] for i in turn]]
    distance = jnp.arange(devices, dtype=jnp.int32) ^ (group * parts + part)
    slots = []
    for order in orders:
        slot = jnp.zeros_like(distance)
        for axis, bit in order:
            slot = 2 * slot + distance // (bit * (parts if axis == "ep" else 1)) % 2
        slots.append(slot)
    slots = jnp.stack([slots[cut % 2] for cut in range(cuts)])

    def on_a_step(sums):
        return [(fold_step(rows, todo[0]), todo[1:]) if todo else (rows, todo) for rows, todo in sums]

    def together(work, sums):
        work, rows = lax.optimization_barrier((work, [rows for rows, _ in sums]))
        return work, [(each, todo) for each, (_, todo) in zip(rows, sums)]

    mid_parts[0], raw_parts = lax.optimization_barrier((mid_parts[0], raw_parts))
    sums, gate_parts, upper_parts, hidden_parts = [], [], [], []
    for i in range(GATHERS):
        mid_rows = mid_parts[i]
        back, *sides = feed_forward(
            slots,
            mid_rows.reshape(devices, cuts, cut_rows, width),
            raw_parts[i],
            mask_parts[i],
            router_full,
            tiles,
            first,
        )
        (back, sides), sums = together((back, sides), on_a_step(sums))
        sums += [(back[cut], orders[cut % 2]) for cut in range(cuts)]
        for parts_of, side in zip((gate_parts, upper_parts, hidden_parts), sides):
            parts_of.append(side.reshape(mid_rows.shape[0], -1))
        if i == 0:
            firsts = [
                transposed_left(parts_of[0], rows[0])
                for parts_of, rows in (
                    (hidden_parts, grad_parts),
                    (gate_parts, mid_parts),
                    (upper_parts, mid_parts),
                )
            ]
            (firsts, mid_parts[1:]), sums = together((firsts, mid_parts[1:]), on_a_step(sums))
    out_part = rows_by_device(hidden_parts, down_weight, devices)
    out_part, sums = together(out_part, on_a_step(sums))
    for _ in range(2):
        out_part, sums = together(out_part, on_a_step(sums))
    out_own = lax.psum_scatter(out_part, every, scatter_dimension=0, tiled=True)
    block_own = (lax.optimization_barrier(resid) + out_own.astype(f32)).astype(bf16)
    while any(todo for _, todo in sums):
        sums = on_a_step(sums)
    back_own = jnp.concatenate([rows[0] for rows, _ in sums], axis=0)

    back_own = back_own.astype(f32)
    gating_grad = back_own[:, width : width + experts]
    mask = lax.dynamic_slice_in_dim(mask_own, part * own, own, axis=0).astype(f32)
    sigmoids = jax.nn.sigmoid(matmul(mid_own, router_full))
    chosen = sigmoids * mask
    sigmoid_total = jnp.sum(chosen, axis=1, keepdims=True)
    weighted = jnp.sum(gating_grad * chosen, axis=1, keepdims=True) / sigmoid_total
    sigmoid_grad = ROUTE_SCALE / sigmoid_total * (gating_grad - weighted)
    logits_grad = (sigmoid_grad * chosen * (1.0 - sigmoids)).astype(bf16)
    grad_router = transposed_left(mid_own, logits_grad)
    mid_grad = back_own[:, :width] + transposed_right(logits_grad, router_full)
    resid_norm_grad, grad_gain_mid = norm_backward(mid_grad, unit_mid, inverse_mid, gain_rows[1])
    resid_grad = grad_own.astype(f32) + resid_norm_grad

    resid_low, hidden_parts = lax.optimization_barrier((resid_grad.astype(bf16), hidden_parts))
    down_second = transposed_left(hidden_parts[1], grad_parts[1])
    attn_rows, gate_parts, down_second = lax.optimization_barrier(
        (spread(resid_low, tp_steps[:1]), gate_parts, down_second)
    )
    gate_second = transposed_left(gate_parts[1], mid_parts[1])
    attn_grad, gate_second = lax.optimization_barrier(
        (spread(attn_rows, tp_steps[1:]), gate_second)
    )

    def ring_columns(left_side, right_side):
        size = left_side.shape[1] // groups
        return [
            transposed_left(
                lax.dynamic_slice_in_dim(left_side, g * size, size, axis=1), right_side
            ).astype(bf16)
            for g in ring_groups
        ]

    def beside(work, rings):
        rounds = [ring_round(ring, "ep") for ring in rings]
        work, states = lax.optimization_barrier((work, [state for state, _ in rounds]))
        return work, [(state, left) for state, (_, left) in zip(states, rounds)]

    output_ring = ring_begin(ring_columns(attn_grad, attended), "ep")
    attended_grad = (
        matmul(attn_grad, output_turned).astype(bf16).reshape(tokens, heads_local, V_DIM)
    )
    values_grad = jnp.einsum("hqk,qhd->khd", probs_low, attended_grad, preferred_element_type=f32)
    probs_grad = jnp.einsum("qhd,khd->hqk", attended_grad, values, preferred_element_type=f32)
    scores_grad = (
        softmax_probs * (probs_grad - jnp.sum(softmax_probs * probs_grad, axis=-1, keepdims=True))
    ).astype(bf16)
    (scores_grad, values_grad), (output_ring,) = beside((scores_grad, values_grad), [output_ring])
    query_grad = (
        jnp.einsum("hqk,khd->qhd", scores_grad, key_rows, preferred_element_type=f32) * score_scale
    )
    keys_grad = (
        jnp.einsum("hqk,qhd->khd", scores_grad, queries, preferred_element_type=f32) * score_scale
    )
    query_raw_grad = (
        jnp.concatenate(
            [
                query_grad[..., :NOPE],
                rotate(query_grad[..., NOPE:], cosine_table[:, None, :], -sine_table[:, None, :]),
            ],
            axis=-1,
        )
        .astype(bf16)
        .reshape(tokens, heads_local * (NOPE + ROPE))
    )
    expanded_grad = (
        jnp.concatenate([keys_grad[..., :NOPE], values_grad], axis=-1)
        .astype(bf16)
        .reshape(tokens, heads_local * (NOPE + V_DIM))
    )
    latent_normed_grad = transposed_right(expanded_grad, expand_full)
    latent_part_grad, gain_latent_part = norm_backward(
        latent_normed_grad, latent_unit, latent_inverse, gain_latent
    )
    rope_raw_grad = rotate(jnp.sum(keys_grad[..., NOPE:], axis=1), cosine_table, -sine_table)
    latent_grad = jnp.concatenate([latent_part_grad, rope_raw_grad], axis=1).astype(bf16)
    both_grad = pad_columns(jnp.concatenate([query_raw_grad, latent_grad], axis=1), into_size)
    both_grad, (output_ring,) = beside(both_grad, [output_ring])
    into_ring = ring_begin(ring_columns(normed_low, both_grad), "ep")
    in_grad_part = transposed_right(both_grad, into_full).astype(bf16)
    expand_blocks = transposed_left(latent_low, expanded_grad).astype(bf16)
    expand_blocks = expand_blocks.reshape(groups, -1, expand_blocks.shape[1])
    expand_ring = ring_begin(
        [lax.dynamic_slice_in_dim(expand_blocks, g, 1, axis=0)[0] for g in ring_groups], "ep"
    )
    work = (in_grad_part, [left for _, left in (into_ring, expand_ring)])
    (in_grad_part, lefts), (into_ring, output_ring) = beside(work, [into_ring, output_ring])
    into_ring, expand_ring = (into_ring[0], lefts[0][1:]), (expand_ring[0], lefts[1])

    upper_rows, _ = lax.optimization_barrier((upper_parts[1], in_grad_part))
    upper_second = transposed_left(upper_rows, mid_parts[1])
    in_grad = fold_step(in_grad_part, tp_steps[-1])
    halves = (firsts, [down_second, gate_second, upper_second])
    (halves, in_grad), (into_ring, expand_ring, output_ring) = beside(
        (halves, in_grad), [into_ring, expand_ring, output_ring]
    )

    def grad_units(kind, start, count):
        return sum(half[kind][start : start + count] for half in halves)

    shared_at = EXP_DEV * expert_pad
    shared_gu_back = lax.all_to_all(
        jnp.stack([grad_units(kind, shared_at, units).T for kind in (1, 2)])
        .astype(bf16)
        .reshape(2, width, 1, units),
        "ep",
        split_axis=1,
        concat_axis=2,
        tiled=True,
    )
    shared_down_back = lax.all_to_all(
        grad_units(0, shared_at, units).astype(bf16),
        "ep",
        split_axis=1,
        concat_axis=0,
        tiled=True,
    )
    grad_expert_gate_up = jnp.stack(
        [
            jnp.stack([grad_units(kind, e * expert_pad, hidden_units).T for kind in (1, 2)])
            for e in range(EXP_DEV)
        ]
    )
    grad_expert_down = jnp.stack(
        [grad_units(0, e * expert_pad, hidden_units) for e in range(EXP_DEV)]
    )
    grad_shared_gu_out = shared_gu_back.reshape(shared_gate_up.shape).astype(f32)
    grad_shared_down_out = shared_down_back.astype(f32)
    in_grad = fold(in_grad, tp_steps[:-1]).astype(f32)
    in_grad, (into_ring, expand_ring) = beside(in_grad, [into_ring, expand_ring])
    input_norm_grad, grad_gain_in = norm_backward(
        in_grad, unit_in[:own], inverse_in[:own], gain_rows[0]
    )
    hidden_own = (resid_grad + input_norm_grad).astype(bf16)
    grad_small = jnp.concatenate(
        [
            jnp.stack([grad_gain_in, grad_gain_mid])
            .reshape(2, groups, -1)
            .transpose(1, 0, 2)
            .reshape(groups, -1),
            gain_latent_part.reshape(groups, -1),
            grad_router.reshape(groups, -1),
        ],
        axis=1,
    )
    small_sum = by_distance(grad_small, group, distances(ep_steps))
    small_sum = fold_step(small_sum, ep_steps[-1])
    (hidden_own, small_sum), (into_ring, expand_ring) = beside(
        (hidden_own, small_sum), [into_ring, expand_ring]
    )
    small_sum = fold(small_sum, ep_steps[:-1])
    into_sum = ring_end(into_ring, "ep")
    grad_expand_out = ring_end(expand_ring, "ep")
    grad_output_out = ring_end(output_ring, "ep").T
    grad_query_out = into_sum[:, :query_size]
    grad_latent_out = into_sum[:, query_size : query_size + latent_width]
    for axis, bit in tp_steps:
        rounded = grad_latent_out.astype(bf16)
        grad_latent_out = rounded.astype(f32) + swap(rounded, axis, bit).astype(f32)
    for axis, bit in tp_steps:
        small_sum = small_sum + swap(small_sum, axis, bit)
    small_sum = small_sum.reshape(-1)
    grad_gains_out = small_sum[: at[1]].reshape(norm_gains.shape)
    grad_gain_latent_out = small_sum[at[1] : at[2]]
    grad_router_out = small_sum[at[2] : at[3]].reshape(router_weight.shape)

    def all_own(rows):
        return lax.all_gather(rows, "tp", axis=0, tiled=True)

    return (
        all_own(block_own),
        all_own(hidden_own).astype(f32),
        grad_query_out,
        grad_latent_out,
        grad_expand_out,
        grad_output_out,
        grad_gains_out,
        grad_gain_latent_out,
        grad_router_out,
        grad_shared_gu_out,
        grad_shared_down_out,
        grad_expert_gate_up,
        grad_expert_down,
    )


def power_of_two(size):
    return size & (size - 1) == 0


def on_device(hidden_in, *others):
    groups, parts = lax.axis_size("ep"), lax.axis_size("tp")
    tokens = hidden_in.shape[0]
    mean_load = tokens * TOPK // (EXP_DEV * groups)
    capacity = mean_load + mean_load // 3
    if EXP_DEV * capacity >= tokens and power_of_two(groups) and power_of_two(parts):
        return on_device_dense(hidden_in, *others)
    return on_device_sparse(hidden_in, *others)


def solution(mesh):
    placed = (
        P("ep", None),
        P("ep", None),
        P("ep", "tp"),
        P("ep", None),
        P("ep", "tp"),
        P("tp", "ep"),
        P(None, "ep"),
        P("ep"),
        P("ep", None),
        P(None, "ep", "tp"),
        P("tp", "ep"),
        P("ep", None, None, "tp"),
        P("ep", "tp", None),
        P("ep", None),
    )
    return jax.shard_map(
        on_device,
        mesh=mesh,
        in_specs=placed,
        out_specs=(
            P("ep", None),
            P("ep", None),
            P("ep", "tp"),
            P("ep", None),
            P("ep", "tp"),
            P("tp", "ep"),
            P(None, "ep"),
            P("ep"),
            P("ep", None),
            P(None, "ep", "tp"),
            P("tp", "ep"),
            P("ep", None, None, "tp"),
            P("ep", "tp", None),
        ),
        check_vma=False,
    )
```

```python
import functools
import math

import jax
import jax.numpy as jnp
from jax import lax
from jax.experimental import pallas as pl
from jax.experimental.pallas import tpu as pltpu
from jax.sharding import PartitionSpec as P

NOPE = 128
ROPE = 64
V_DIM = 128
KV_RANK = 512
TOPK = 6
EXP_DEV = 2


EPSILON = 1e-06
ROUTE_SCALE = 2.446
ROPE_BASE = 50000.0


def matmul(left_side, right_side):
    return jnp.dot(left_side, right_side, preferred_element_type=jnp.float32)


def transposed_left(left_side, right_side):
    return lax.dot_general(
        left_side, right_side, (((0,), (0,)), ((), ())), preferred_element_type=jnp.float32
    )


def transposed_right(left_side, right_side):
    return lax.dot_general(
        left_side, right_side, (((1,), (1,)), ((), ())), preferred_element_type=jnp.float32
    )


def rotate(values, cosine_table, sine_table):
    halfway = values.shape[-1] // 2
    first_half = values[..., :halfway]
    second_half = values[..., halfway:]
    return jnp.concatenate(
        [
            first_half * cosine_table - second_half * sine_table,
            second_half * cosine_table + first_half * sine_table,
        ],
        axis=-1,
    )


def norm_forward(values, gain_row):
    inverse = lax.rsqrt(jnp.mean(values * values, axis=-1, keepdims=True) + EPSILON)
    unit_rows = values * inverse
    return (unit_rows * gain_row, unit_rows, inverse)


def norm_backward(incoming, unit_rows, inverse, gain_row):
    scaled = incoming * gain_row
    grad_values = inverse * (
        scaled - unit_rows * jnp.mean(scaled * unit_rows, axis=-1, keepdims=True)
    )
    return (grad_values, jnp.sum(incoming * unit_rows, axis=0))


def on_device_sparse(
    hidden_in,
    out_grad,
    query_weight,
    latent_weight,
    expand_weight,
    output_weight,
    norm_gains,
    latent_gain,
    router_weight,
    shared_gate_up,
    shared_down,
    expert_gate_up,
    expert_down,
    expert_ids,
):
    (
        query_full,
        latent_full,
        expand_full,
        output_full,
        gains_full,
        latent_gain_full,
        router_full,
        shared_gu_full,
        shared_down_full,
    ) = (
        lax.all_gather(query_weight, "ep", axis=0, tiled=True),
        lax.all_gather(latent_weight, "ep", axis=0, tiled=True),
        lax.all_gather(expand_weight, "ep", axis=0, tiled=True),
        lax.all_gather(output_weight, "ep", axis=1, tiled=True),
        lax.all_gather(norm_gains, "ep", axis=1, tiled=True),
        lax.all_gather(latent_gain, "ep", axis=0, tiled=True),
        lax.all_gather(router_weight, "ep", axis=0, tiled=True),
        lax.all_gather(shared_gate_up, "ep", axis=1, tiled=True),
        lax.all_gather(shared_down, "ep", axis=1, tiled=True),
    )
    tokens = hidden_in.shape[0]
    model_width = hidden_in.shape[1]
    heads_local = query_full.shape[1] // (NOPE + ROPE)
    gain_rows = gains_full.astype(jnp.float32)
    gain_latent = latent_gain_full.astype(jnp.float32)
    places = jnp.arange(tokens).astype(jnp.float32)
    frequency = ROPE_BASE ** (-(jnp.arange(ROPE // 2).astype(jnp.float32) * 2.0 / ROPE))
    angles = places[:, None] * frequency[None, :]
    cosine_table = jnp.cos(angles)
    sine_table = jnp.sin(angles)
    resid_in = hidden_in.astype(jnp.float32)
    normed_in, unit_in, inverse_in = norm_forward(resid_in, gain_rows[0])
    normed_low = normed_in.astype(jnp.bfloat16)
    query_raw = matmul(normed_low, query_full).reshape(tokens, heads_local, NOPE + ROPE)
    queries = jnp.concatenate(
        [
            query_raw[..., :NOPE],
            rotate(query_raw[..., NOPE:], cosine_table[:, None, :], sine_table[:, None, :]),
        ],
        axis=-1,
    ).astype(jnp.bfloat16)
    latent = matmul(normed_low, latent_full)
    latent_normed, latent_unit, latent_inverse = norm_forward(latent[:, :KV_RANK], gain_latent)
    latent_low = latent_normed.astype(jnp.bfloat16)
    key_rope = rotate(latent[:, KV_RANK:], cosine_table, sine_table).astype(jnp.bfloat16)
    expanded = (
        matmul(latent_low, expand_full)
        .astype(jnp.bfloat16)
        .reshape(tokens, heads_local, NOPE + V_DIM)
    )
    key_rows = jnp.concatenate(
        [expanded[..., :NOPE], jnp.broadcast_to(key_rope[:, None, :], (tokens, heads_local, ROPE))],
        axis=-1,
    )
    values = expanded[..., NOPE:]
    score_scale = 1.0 / math.sqrt(NOPE + ROPE)
    causal = jnp.arange(tokens)[:, None] >= jnp.arange(tokens)[None, :]

    def attention_scores():
        scores = (
            jnp.einsum("qhd,khd->hqk", queries, key_rows, preferred_element_type=jnp.float32)
            * score_scale
        )
        return jnp.where(causal[None], scores, -1e30)

    scores_first = attention_scores()
    row_max = jnp.max(scores_first, axis=-1, keepdims=True)
    log_total = row_max + jnp.log(jnp.sum(jnp.exp(scores_first - row_max), axis=-1, keepdims=True))
    probs_low = jnp.exp(scores_first - log_total).astype(jnp.bfloat16)
    attended = jnp.einsum("hqk,khd->qhd", probs_low, values, preferred_element_type=jnp.float32)
    attended = attended.astype(jnp.bfloat16).reshape(tokens, heads_local * V_DIM)
    attn_out = lax.psum(matmul(attended, output_full), "tp")
    resid = resid_in + attn_out
    normed_mid, unit_mid, inverse_mid = norm_forward(resid, gain_rows[1])
    mid_low = normed_mid.astype(jnp.bfloat16)
    logits = matmul(mid_low, router_full)
    experts = router_full.shape[1]
    route_mask = (expert_ids[:, :, None] == jnp.arange(experts)[None, None, :]).astype(jnp.float32)
    chosen = jnp.sum(route_mask * logits[:, None, :], axis=2)
    sigmoids = jax.nn.sigmoid(chosen)
    sigmoid_total = jnp.sum(sigmoids, axis=1, keepdims=True)
    gating = ROUTE_SCALE * sigmoids / sigmoid_total
    shared_gate = matmul(mid_low, shared_gu_full[0])
    shared_upper = matmul(mid_low, shared_gu_full[1])
    shared_sig = jax.nn.sigmoid(shared_gate)
    shared_hidden = (shared_gate * shared_sig * shared_upper).astype(jnp.bfloat16)
    shared_part = matmul(shared_hidden, shared_down_full)
    groups = lax.axis_size("ep")
    mean_load = tokens * TOPK // (EXP_DEV * groups)
    capacity = mean_load + mean_load // 3
    choices = tokens * TOPK
    rows_total = groups * capacity
    flat_ids = expert_ids.reshape(-1)
    onehot = (flat_ids[:, None] == jnp.arange(experts)[None, :]).astype(jnp.int32)
    slot_of = jnp.sum((jnp.cumsum(onehot, axis=0) - onehot) * onehot, axis=1)
    target = flat_ids % EXP_DEV * rows_total + flat_ids // EXP_DEV * capacity + slot_of
    slot_table = (
        jnp.full((EXP_DEV * rows_total,), choices, jnp.int32)
        .at[target]
        .set(jnp.arange(choices, dtype=jnp.int32))
        .reshape(EXP_DEV, groups, capacity)
    )
    mid_padded = jnp.concatenate([mid_low, jnp.zeros((1, model_width), jnp.bfloat16)], axis=0)
    outgoing = mid_padded[slot_table.reshape(-1) // TOPK].reshape(EXP_DEV, rows_total, model_width)
    expert_rows = lax.all_to_all(outgoing, "ep", split_axis=1, concat_axis=1, tiled=True)
    expert_gate = jnp.einsum(
        "erd,edf->erf", expert_rows, expert_gate_up[:, 0], preferred_element_type=jnp.float32
    )
    expert_upper = jnp.einsum(
        "erd,edf->erf", expert_rows, expert_gate_up[:, 1], preferred_element_type=jnp.float32
    )
    expert_sig = jax.nn.sigmoid(expert_gate)
    expert_hidden = (expert_gate * expert_sig * expert_upper).astype(jnp.bfloat16)
    expert_part = jnp.einsum(
        "erf,efd->erd", expert_hidden, expert_down, preferred_element_type=jnp.float32
    ).astype(jnp.bfloat16)
    returned = lax.all_to_all(expert_part, "ep", split_axis=1, concat_axis=1, tiled=True)
    per_choice = (
        returned.reshape(-1, model_width)[target]
        .reshape(tokens, TOPK, model_width)
        .astype(jnp.float32)
    )
    routed_part = jnp.sum(gating[:, :, None] * per_choice, axis=1)
    moe_out = lax.psum((shared_part + routed_part).astype(jnp.bfloat16), "tp").astype(jnp.float32)
    block_out = (resid + moe_out).astype(jnp.bfloat16)
    grad_top = out_grad.astype(jnp.float32)
    choice_grad = (gating[:, :, None] * grad_top[:, None, :]).astype(jnp.bfloat16)
    grad_padded = jnp.concatenate(
        [choice_grad.reshape(choices, model_width), jnp.zeros((1, model_width), jnp.bfloat16)],
        axis=0,
    )
    outgoing_grad = grad_padded[slot_table.reshape(-1)].reshape(EXP_DEV, rows_total, model_width)
    rows_grad = lax.all_to_all(outgoing_grad, "ep", split_axis=1, concat_axis=1, tiled=True)
    hidden_grad = jnp.einsum(
        "erd,efd->erf", rows_grad, expert_down, preferred_element_type=jnp.float32
    )
    gate_grad = (
        hidden_grad * expert_upper * expert_sig * (1.0 + expert_gate * (1.0 - expert_sig))
    ).astype(jnp.bfloat16)
    upper_grad = (hidden_grad * expert_gate * expert_sig).astype(jnp.bfloat16)
    grad_expert_down = jnp.einsum(
        "erf,erd->efd", expert_hidden, rows_grad, preferred_element_type=jnp.float32
    )
    grad_expert_gate_up = jnp.stack(
        [
            jnp.einsum("erd,erf->edf", expert_rows, gate_grad, preferred_element_type=jnp.float32),
            jnp.einsum("erd,erf->edf", expert_rows, upper_grad, preferred_element_type=jnp.float32),
        ],
        axis=1,
    )
    row_back = jnp.einsum(
        "erf,edf->erd", gate_grad, expert_gate_up[:, 0], preferred_element_type=jnp.float32
    ) + jnp.einsum(
        "erf,edf->erd", upper_grad, expert_gate_up[:, 1], preferred_element_type=jnp.float32
    )
    row_back_low = row_back.astype(jnp.bfloat16)
    back_rows = lax.all_to_all(row_back_low, "ep", split_axis=1, concat_axis=1, tiled=True)
    choice_back = (
        back_rows.reshape(-1, model_width)[target]
        .reshape(tokens, TOPK, model_width)
        .astype(jnp.float32)
    )
    mid_grad_routed = jnp.sum(choice_back, axis=1)
    gating_grad_part = jnp.sum(per_choice * grad_top[:, None, :], axis=2)
    shared_hidden_grad = transposed_right(out_grad, shared_down_full)
    shared_gate_grad = (
        shared_hidden_grad * shared_upper * shared_sig * (1.0 + shared_gate * (1.0 - shared_sig))
    ).astype(jnp.bfloat16)
    shared_upper_grad = (shared_hidden_grad * shared_gate * shared_sig).astype(jnp.bfloat16)
    grad_shared_down = transposed_left(shared_hidden, out_grad)
    grad_shared_gu = jnp.stack(
        [transposed_left(mid_low, shared_gate_grad), transposed_left(mid_low, shared_upper_grad)],
        axis=0,
    )
    mid_grad_shared = transposed_right(shared_gate_grad, shared_gu_full[0]) + transposed_right(
        shared_upper_grad, shared_gu_full[1]
    )
    mid_grad_sum, gating_grad = (
        lax.psum((mid_grad_routed + mid_grad_shared).astype(jnp.bfloat16), "tp").astype(
            jnp.float32
        ),
        lax.psum(gating_grad_part.astype(jnp.bfloat16), "tp").astype(jnp.float32),
    )
    weighted = jnp.sum(gating_grad * sigmoids, axis=1, keepdims=True) / sigmoid_total
    sigmoid_grad = ROUTE_SCALE / sigmoid_total * (gating_grad - weighted)
    chosen_grad = sigmoid_grad * sigmoids * (1.0 - sigmoids)
    logits_grad = jnp.sum(route_mask * chosen_grad[:, :, None], axis=1).astype(jnp.bfloat16)
    grad_router = transposed_left(mid_low, logits_grad)
    mid_grad = mid_grad_sum + transposed_right(logits_grad, router_full)
    resid_norm_grad, grad_gain_mid = norm_backward(mid_grad, unit_mid, inverse_mid, gain_rows[1])
    resid_grad = grad_top + resid_norm_grad
    attn_grad = resid_grad.astype(jnp.bfloat16)
    grad_output = transposed_left(attended, attn_grad)
    attended_grad = (
        transposed_right(attn_grad, output_full)
        .astype(jnp.bfloat16)
        .reshape(tokens, heads_local, V_DIM)
    )
    softmax_probs = jnp.exp(attention_scores() - log_total)
    values_grad = jnp.einsum(
        "hqk,qhd->khd",
        softmax_probs.astype(jnp.bfloat16),
        attended_grad,
        preferred_element_type=jnp.float32,
    )
    probs_grad = jnp.einsum(
        "qhd,khd->hqk", attended_grad, values, preferred_element_type=jnp.float32
    )
    scores_grad = (
        softmax_probs * (probs_grad - jnp.sum(softmax_probs * probs_grad, axis=-1, keepdims=True))
    ).astype(jnp.bfloat16)
    query_grad = (
        jnp.einsum("hqk,khd->qhd", scores_grad, key_rows, preferred_element_type=jnp.float32)
        * score_scale
    )
    keys_grad = (
        jnp.einsum("hqk,qhd->khd", scores_grad, queries, preferred_element_type=jnp.float32)
        * score_scale
    )
    query_raw_grad = (
        jnp.concatenate(
            [
                query_grad[..., :NOPE],
                rotate(query_grad[..., NOPE:], cosine_table[:, None, :], -sine_table[:, None, :]),
            ],
            axis=-1,
        )
        .astype(jnp.bfloat16)
        .reshape(tokens, heads_local * (NOPE + ROPE))
    )
    expanded_grad = jnp.concatenate([keys_grad[..., :NOPE], values_grad], axis=-1).astype(
        jnp.bfloat16
    )
    expanded_grad = expanded_grad.reshape(tokens, heads_local * (NOPE + V_DIM))
    grad_expand = transposed_left(latent_low, expanded_grad)
    latent_normed_grad = transposed_right(expanded_grad, expand_full)
    latent_part_grad, gain_latent_part = norm_backward(
        latent_normed_grad, latent_unit, latent_inverse, gain_latent
    )
    rope_raw_grad = rotate(jnp.sum(keys_grad[..., NOPE:], axis=1), cosine_table, -sine_table)
    latent_grad_part = jnp.concatenate([latent_part_grad, rope_raw_grad], axis=1)
    in_grad_query = transposed_right(query_raw_grad, query_full)
    in_grad_sum, latent_grad, grad_gain_latent = (
        lax.psum(in_grad_query.astype(jnp.bfloat16), "tp").astype(jnp.float32),
        lax.psum(latent_grad_part.astype(jnp.bfloat16), "tp").astype(jnp.float32),
        lax.psum(gain_latent_part.astype(jnp.bfloat16), "tp").astype(jnp.float32),
    )
    latent_grad_low = latent_grad.astype(jnp.bfloat16)
    grad_latent = transposed_left(normed_low, latent_grad_low)
    grad_query = transposed_left(normed_low, query_raw_grad)
    in_grad = in_grad_sum + transposed_right(latent_grad_low, latent_full)
    input_norm_grad, grad_gain_in = norm_backward(in_grad, unit_in, inverse_in, gain_rows[0])
    grad_hidden = resid_grad + input_norm_grad
    grad_gains = jnp.stack([grad_gain_in, grad_gain_mid], axis=0)
    (
        grad_query_out,
        grad_latent_out,
        grad_expand_out,
        grad_output_out,
        grad_gains_out,
        grad_gain_latent_out,
        grad_router_out,
        grad_shared_gu_out,
        grad_shared_down_out,
    ) = (
        lax.psum_scatter(
            grad_query.astype(jnp.bfloat16), "ep", scatter_dimension=0, tiled=True
        ).astype(jnp.float32),
        lax.psum_scatter(
            grad_latent.astype(jnp.bfloat16), "ep", scatter_dimension=0, tiled=True
        ).astype(jnp.float32),
        lax.psum_scatter(
            grad_expand.astype(jnp.bfloat16), "ep", scatter_dimension=0, tiled=True
        ).astype(jnp.float32),
        lax.psum_scatter(
            grad_output.astype(jnp.bfloat16), "ep", scatter_dimension=1, tiled=True
        ).astype(jnp.float32),
        lax.psum_scatter(
            grad_gains.astype(jnp.bfloat16), "ep", scatter_dimension=1, tiled=True
        ).astype(jnp.float32),
        lax.psum_scatter(
            grad_gain_latent.astype(jnp.bfloat16), "ep", scatter_dimension=0, tiled=True
        ).astype(jnp.float32),
        lax.psum_scatter(
            grad_router.astype(jnp.bfloat16), "ep", scatter_dimension=0, tiled=True
        ).astype(jnp.float32),
        lax.psum_scatter(
            grad_shared_gu.astype(jnp.bfloat16), "ep", scatter_dimension=1, tiled=True
        ).astype(jnp.float32),
        lax.psum_scatter(
            grad_shared_down.astype(jnp.bfloat16), "ep", scatter_dimension=1, tiled=True
        ).astype(jnp.float32),
    )
    return (
        block_out,
        grad_hidden,
        grad_query_out,
        grad_latent_out,
        grad_expand_out,
        grad_output_out,
        grad_gains_out,
        grad_gain_latent_out,
        grad_router_out,
        grad_shared_gu_out,
        grad_shared_down_out,
        grad_expert_gate_up,
        grad_expert_down,
    )


CUTS = 4
GATHERS = 2
LANES = 128
VMEM_BYTES = 56 * 1024 * 1024


def swap(array, axis, bit):
    size = lax.axis_size(axis)
    return lax.ppermute(array, axis, [(place, place ^ bit) for place in range(size)])


def axis_bits(axis):
    size = lax.axis_size(axis)
    return [(axis, 1 << bit) for bit in reversed(range(size.bit_length() - 1))]


def spread(rows, steps):
    for axis, bit in steps:
        rows = jnp.concatenate([rows, swap(rows, axis, bit)], axis=0)
    return rows


def add_rounded(left_side, right_side):
    return (left_side.astype(jnp.float32) + right_side.astype(jnp.float32)).astype(
        left_side.dtype
    )


def fold_step(rows, step):
    axis, bit = step
    half = rows.shape[0] // 2
    return add_rounded(rows[:half], swap(rows[half:], axis, bit))


def fold(rows, steps):
    for step in reversed(steps):
        rows = fold_step(rows, step)
    return rows


def distances(steps):
    found = [0]
    for _, bit in steps:
        found = found + [distance + bit for distance in found]
    return found


def by_distance(blocks, place, order):
    return jnp.concatenate(
        [lax.dynamic_slice_in_dim(blocks, place ^ i, 1, axis=0) for i in order], axis=0
    )


def by_place(blocks, place, order):
    natural = jnp.concatenate([blocks[order.index(i)][None] for i in range(len(order))], axis=0)
    return by_distance(natural, place, range(len(order)))


def ring_owner(spot, size):
    return jnp.where(spot < size // 2, 2 * spot, 2 * (size - 1 - spot) + 1)


def ring_spot(place, size):
    return jnp.where(place % 2 == 0, place // 2, size - 1 - place // 2)


def ring_shift(array, axis, by):
    size = lax.axis_size(axis)
    ring = [2 * i for i in range(size // 2)] + [2 * i + 1 for i in reversed(range(size // 2))]
    return lax.ppermute(array, axis, [(ring[i], ring[(i + by) % size]) for i in range(size)])


def ring_gather(arrays, axis, beside):
    size = lax.axis_size(axis)
    found = [[array] + [None] * (size - 1) for array in arrays]
    ahead, behind, others, rounds = arrays, arrays, [], []
    for k in range(1, size // 2 + 1):
        behind = [ring_shift(array, axis, 1) for array in behind]
        if k < size - k:
            ahead = [ring_shift(array, axis, -1) for array in ahead]
        other = beside[k - 1](others) if k <= len(beside) else None
        behind, ahead, other = lax.optimization_barrier((behind, ahead, other))
        others.append(other)
        rounds.append(behind)
        for pieces, before, after in zip(found, behind, ahead):
            pieces[size - k] = before
            if k < size - k:
                pieces[k] = after
    return found, others, rounds


def ring_begin(parts, axis):
    size = lax.axis_size(axis)
    half = size // 2
    left = [(parts[half - k], parts[half + 1 + k] if k < half - 1 else None) for k in range(1, half)]
    return (parts[half], parts[half + 1]), left + [(parts[0], None)]


def ring_round(ring, axis):
    (ahead, behind), left = ring
    more_ahead, more_behind = left[0]
    ahead = add_rounded(ring_shift(ahead, axis, 1), more_ahead)
    if behind is not None and len(left) > 1:
        behind = ring_shift(behind, axis, -1)
        if more_behind is not None:
            behind = add_rounded(behind, more_behind)
    return (ahead, behind), left[1:]


def ring_end(ring, axis):
    (ahead, behind), left = ring
    while left:
        if len(left) == 1:
            found = ring_shift(ahead, axis, 1).astype(jnp.float32) + left[0][0]
            return found + behind
        (ahead, behind), left = ring_round(((ahead, behind), left), axis)
    return ahead.astype(jnp.float32) + behind


def pad_columns(array, width):
    return jnp.pad(array, ((0, 0), (0, width - array.shape[1])))


def pad_rows(array, height):
    return jnp.pad(array, ((0, height - array.shape[0]), (0, 0)))


def round_up(size, step=LANES):
    return -(-size // step) * step


def feed_forward_kernel(count, wide_steps, sub, *refs):
    first_ref, slot_ref, rows_ref, raw_ref, mask_ref, router_ref, tiles_ref = refs[:7]
    back_out, gate_ref, upper_ref, hidden_ref = refs[7:11]
    gains, shares, kept, tiles, back_ref, arrived, back_left = refs[11:]
    cut, step, last = pl.program_id(0), pl.program_id(1), count + wide_steps - 1
    owners, _, each, width = rows_ref.shape
    half, rows = raw_ref.shape[3], owners * each
    block = sub // each
    f32, bf16 = jnp.float32, jnp.bfloat16

    def arrival(n):
        return pltpu.make_async_copy(tiles_ref.at[n], tiles.at[n], arrived.at[n])

    def back_leaving(n):
        size = width // wide_steps
        extra = back_ref.shape[2] - width if n == wide_steps - 1 else 0
        of = (slice(None), slice(None), pl.ds(n * size, size + extra))
        return pltpu.make_async_copy(back_ref.at[of], back_out.at[(cut, *of)], back_left.at[n])

    @pl.when(step == 0)
    def _():
        @pl.when(cut == 0)
        def _():
            for n in range(count):
                arrival(n).start()

        values = rows_ref[...].reshape(rows, width)
        logits = jnp.dot(values, router_ref[...], preferred_element_type=f32)
        sig = jax.nn.sigmoid(logits) * mask_ref[...].reshape(logits.shape)
        gating = ROUTE_SCALE * sig / jnp.sum(sig, axis=1, keepdims=True)
        lanes = lax.broadcasted_iota(jnp.int32, gating.shape, 1)
        for e in range(EXP_DEV):
            own = jnp.sum(jnp.where(lanes == first_ref[0] + e, gating, 0.0), axis=1, keepdims=True)
            gains[e] = jnp.broadcast_to(own, gains.shape[1:])
        gains[EXP_DEV] = jnp.ones(gains.shape[1:], f32)
        shares[...] = jnp.zeros_like(shares)

    @pl.when(step < count)
    def _():
        @pl.when(cut == 0)
        def _():
            arrival(step).wait()

        kind = jnp.minimum(step // ((count - 1) // EXP_DEV), EXP_DEV)
        for i in range(rows // sub):
            at, of = pl.ds(i * sub, sub), pl.ds(i * block, block)
            values = rows_ref[of].reshape(sub, width)
            both = lax.dot_general(
                values, tiles[step], (((1,), (1,)), ((), ())), preferred_element_type=f32
            )
            gate, upper = both[:, :half], both[:, half:]
            gain, raw = gains[kind, at, :], raw_ref[of].reshape(sub, half).astype(f32)
            sig = jax.nn.sigmoid(gate)
            silu = gate * sig
            hidden = silu * upper
            grad = gain * raw
            shape = (block, 1, each, half)
            hidden_ref[of] = (gain * hidden).astype(bf16).reshape(shape)
            shares[kind, at, :] += hidden * raw
            gate_grad = (grad * upper * (sig + silu * (1.0 - sig))).astype(bf16)
            upper_grad = (grad * silu).astype(bf16)
            gate_ref[of] = gate_grad.reshape(shape)
            upper_ref[of] = upper_grad.reshape(shape)
            kept[step, at, :half] = gate_grad
            kept[step, at, half:] = upper_grad

    @pl.when(step >= count)
    def _():
        size = width // wide_steps
        columns = pl.ds(pl.multiple_of((step - count) * size, size), size)
        for i in range(rows // sub):
            found = sum(
                jnp.dot(
                    kept[n, pl.ds(i * sub, sub), :],
                    tiles[n, :, columns],
                    preferred_element_type=f32,
                )
                for n in range(count)
            ).astype(bf16)
            for j in range(block):
                part = found[j * each : (j + 1) * each]
                back_ref[slot_ref[cut, i * block + j], :, columns] = part

    @pl.when(step == last)
    def _():
        extra = back_ref.shape[2] - width
        lanes = lax.broadcasted_iota(jnp.int32, (rows, extra), 1)
        gating_grad = jnp.zeros(lanes.shape, f32)
        for e in range(EXP_DEV):
            own = jnp.sum(shares[e], axis=1, keepdims=True)
            gating_grad += jnp.where(lanes == first_ref[0] + e, own, 0.0)
        gating_grad = gating_grad.astype(bf16)
        for i in range(owners):
            back_ref[slot_ref[cut, i], :, width:] = gating_grad[i * each : (i + 1) * each]

    for n in range(wide_steps):

        @pl.when(step == count + n)
        def _(n=n):
            back_leaving(n).start()

    @pl.when(step == last)
    def _():
        for n in range(wide_steps):
            back_leaving(n).wait()


def feed_forward(slots, mid_rows, raw_grad, mask, router, tiles, first):
    count, both, width = tiles.shape
    owners, cuts, each, experts = mask.shape
    rows, half, wide_steps = owners * each, both // 2, 4
    bf16, f32 = jnp.bfloat16, jnp.float32

    def tile(step):
        return jnp.minimum(step, count - 1)

    smem, whole = pl.BlockSpec(memory_space=pltpu.SMEM), pl.BlockSpec(memory_space=pl.ANY)
    side = pl.BlockSpec((owners, 1, each, half), lambda c, i: (0, c, 0, tile(i)))
    return pl.pallas_call(
        functools.partial(feed_forward_kernel, count, wide_steps, min(8, owners) * each),
        grid=(cuts, count + wide_steps),
        in_specs=[
            smem,
            smem,
            pl.BlockSpec((owners, 1, each, width), lambda c, i: (0, c, 0, 0)),
            side,
            pl.BlockSpec((owners, 1, each, experts), lambda c, i: (0, c, 0, 0)),
            pl.BlockSpec((width, experts), lambda c, i: (0, 0)),
            whole,
        ],
        out_specs=[whole, side, side, side],
        out_shape=[
            jax.ShapeDtypeStruct((cuts, owners, each, width + LANES), bf16),
            *[jax.ShapeDtypeStruct((owners, cuts, each, count * half), bf16)] * 3,
        ],
        scratch_shapes=[
            pltpu.VMEM((EXP_DEV + 1, rows, half), f32),
            pltpu.VMEM((EXP_DEV + 1, rows, half), f32),
            pltpu.VMEM((count, rows, both), bf16),
            pltpu.VMEM(tiles.shape, bf16),
            pltpu.VMEM((owners, each, width + LANES), bf16),
            pltpu.SemaphoreType.DMA((count,)),
            pltpu.SemaphoreType.DMA((wide_steps,)),
        ],
        compiler_params=pltpu.CompilerParams(vmem_limit_bytes=VMEM_BYTES),
        cost_estimate=pl.CostEstimate(
            flops=4 * cuts * rows * width * both * count,
            bytes_accessed=50_000_000,
            transcendentals=0,
        ),
    )(first, slots, mid_rows, raw_grad, mask, router, tiles)


def rows_by_device_kernel(*refs):
    *left_refs, right_ref, out_ref = refs
    for i, left_ref in enumerate(left_refs):

        @pl.when(pl.program_id(1) == i)
        def _(left_ref=left_ref):
            found = jnp.dot(left_ref[...], right_ref[...], preferred_element_type=jnp.float32)
            out_ref[...] = found.astype(out_ref.dtype).reshape(out_ref.shape)


def rows_by_device(left_parts, right_side, devices):
    rows, depth = left_parts[0].shape
    columns, count = right_side.shape[1], len(left_parts)
    wide = columns // 2
    return pl.pallas_call(
        rows_by_device_kernel,
        grid=(2, count),
        in_specs=[pl.BlockSpec((rows, depth), lambda j, i: (0, 0))] * count
        + [pl.BlockSpec((depth, wide), lambda j, i: (0, j))],
        out_specs=pl.BlockSpec((devices, 1, rows // devices, wide), lambda j, i: (0, i, 0, j)),
        out_shape=jax.ShapeDtypeStruct(
            (devices, count, rows // devices, columns), right_side.dtype
        ),
        compiler_params=pltpu.CompilerParams(vmem_limit_bytes=VMEM_BYTES),
        cost_estimate=pl.CostEstimate(
            flops=2 * count * rows * depth * columns,
            bytes_accessed=2 * count * rows * (depth + columns),
            transcendentals=0,
        ),
    )(*left_parts, right_side).reshape(count * rows, columns)


def place_kernel(places_ref, *refs):
    *pieces, out_ref = refs
    for i, piece in enumerate(pieces):

        @pl.when(pl.program_id(0) == i)
        def _(piece=piece):
            out_ref[0] = piece[...]


def place_blocks(pieces, places):
    shape = pieces[0].shape
    return pl.pallas_call(
        place_kernel,
        grid_spec=pltpu.PrefetchScalarGridSpec(
            num_scalar_prefetch=1,
            grid=(len(pieces),),
            in_specs=[pl.BlockSpec(shape, lambda i, at: (0, 0))] * len(pieces),
            out_specs=pl.BlockSpec((1, *shape), lambda i, at: (at[i], 0, 0)),
        ),
        out_shape=jax.ShapeDtypeStruct((len(pieces), *shape), pieces[0].dtype),
        compiler_params=pltpu.CompilerParams(vmem_limit_bytes=VMEM_BYTES),
    )(jnp.stack(places).astype(jnp.int32), *pieces)


def on_device_dense(
    hidden_in,
    out_grad,
    query_weight,
    latent_weight,
    expand_weight,
    output_weight,
    norm_gains,
    latent_gain,
    router_weight,
    shared_gate_up,
    shared_down,
    expert_gate_up,
    expert_down,
    expert_ids,
):
    groups, parts = lax.axis_size("ep"), lax.axis_size("tp")
    group, part = lax.axis_index("ep"), lax.axis_index("tp")
    tokens, width = hidden_in.shape
    own = tokens // parts
    experts = router_weight.shape[1]
    bf16, f32 = jnp.bfloat16, jnp.float32
    ep_steps, tp_steps = axis_bits("ep"), axis_bits("tp")
    tp_order = distances(tp_steps)
    every = ("ep", "tp")
    devices = groups * parts
    cut_rows = own // CUTS

    spot = ring_spot(group, groups)
    ring_groups = [ring_owner((spot + k) % groups, groups) for k in range(groups)]

    mask_own = jnp.sum(
        (expert_ids[:, :, None] == jnp.arange(experts)[None, None, :]).astype(bf16), axis=1
    )
    sizes = [norm_gains.size, latent_gain.size, router_weight.size, mask_own.size]
    small = jnp.concatenate(
        [array.reshape(1, -1) for array in (norm_gains, latent_gain, router_weight, mask_own)],
        axis=1,
    )
    query_size, latent_width = query_weight.shape[1], latent_weight.shape[1]
    output_size = output_weight.shape[0]
    into_size = round_up(query_size + latent_width)
    into = pad_columns(jnp.concatenate([query_weight, latent_weight], axis=1), into_size)
    out_of = jnp.concatenate(
        [output_weight.T, expand_weight.reshape(output_weight.shape[1], -1)], axis=1
    )

    units = shared_down.shape[0] // groups

    hidden_units = expert_down.shape[1]
    expert_pad, shared_pad = round_up(hidden_units), round_up(units)

    def dense_weights(shared_gu_own, shared_down_own, expert_gate_up, expert_down):
        side_weights = [
            jnp.concatenate(
                [pad_rows(expert_gate_up[e, side].T, expert_pad) for e in range(EXP_DEV)]
                + [pad_rows(shared_gu_own[side].T, shared_pad)],
                axis=0,
            ).reshape(-1, LANES, width)
            for side in range(2)
        ]
        tiles = jnp.concatenate(side_weights, axis=1)
        down_weight = jnp.concatenate(
            [pad_rows(expert_down[e], expert_pad) for e in range(EXP_DEV)]
            + [pad_rows(shared_down_own, shared_pad)],
            axis=0,
        )
        return tiles, down_weight

    (into_pieces, out_of_pieces), others, rounds = ring_gather(
        [into, out_of],
        "ep",
        [
            lambda _: spread(small, ep_steps[:1]),
            lambda done: spread(done[0], ep_steps[1:2]),
            lambda done: spread(done[1], ep_steps[2:]),
        ],
    )
    shared_gate_up_late, shared_down_late, _ = lax.optimization_barrier(
        (shared_gate_up, shared_down, rounds[-1])
    )
    shared_gu_own = lax.all_to_all(
        shared_gate_up_late.reshape(2, -1, groups, units), "ep", split_axis=2, concat_axis=1, tiled=True
    ).reshape(2, width, units)
    shared_down_own = lax.all_to_all(shared_down_late, "ep", split_axis=0, concat_axis=1, tiled=True)


    small_rel = others[2]
    at = [sum(sizes[:i]) for i in range(len(sizes) + 1)]
    small_full = by_place(small_rel, group, distances(ep_steps))
    gain_rows = (
        small_full[:, : at[1]].reshape(groups, 2, -1).transpose(1, 0, 2).reshape(2, width)
    ).astype(f32)
    gain_latent = small_full[:, at[1] : at[2]].reshape(-1).astype(f32)
    router_full = small_full[:, at[2] : at[3]].reshape(width, experts)

    into_full = place_blocks(into_pieces, ring_groups).reshape(width, -1)
    out_of_full = place_blocks(out_of_pieces, ring_groups).reshape(width, -1)
    expand_full = out_of_full[:, output_size:].reshape(KV_RANK, -1)
    output_turned = out_of_full[:, :output_size]

    out_grad_late, _ = lax.optimization_barrier((out_grad, rounds[-2][0]))

    gather_rows = own // GATHERS
    cuts = CUTS // GATHERS

    def by_gather(rows):
        rows = rows.reshape(devices, GATHERS, gather_rows, -1).transpose(1, 0, 2, 3)
        return list(rows.reshape(GATHERS, devices * gather_rows, -1))

    grad_own = lax.dynamic_slice_in_dim(out_grad_late, part * own, own, axis=0)
    grad_parts = by_gather(lax.all_gather(grad_own, every, axis=0, tiled=True))
    mask_parts = [
        rows.astype(f32).reshape(devices, cuts, cut_rows, experts)
        for rows in by_gather(small_full[:, at[3] :])
    ]

    row_blocks = hidden_in.reshape(parts, own, width)
    hidden_rel = by_distance(row_blocks, part, tp_order).reshape(tokens, width)
    heads_local = query_size // (NOPE + ROPE)
    places = ((part ^ jnp.array(tp_order))[:, None] * own + jnp.arange(own)[None, :]).reshape(-1)
    frequency = ROPE_BASE ** (-(jnp.arange(ROPE // 2).astype(f32) * 2.0 / ROPE))
    angles = places.astype(f32)[:, None] * frequency[None, :]
    cosine_table = jnp.cos(angles)
    sine_table = jnp.sin(angles)
    normed_in, unit_in, inverse_in = norm_forward(hidden_rel.astype(f32), gain_rows[0])
    normed_low = normed_in.astype(bf16)
    both_in = matmul(normed_low, into_full)
    query_raw = both_in[:, :query_size].reshape(tokens, heads_local, NOPE + ROPE)
    queries = jnp.concatenate(
        [
            query_raw[..., :NOPE],
            rotate(query_raw[..., NOPE:], cosine_table[:, None, :], sine_table[:, None, :]),
        ],
        axis=-1,
    ).astype(bf16)
    latent = both_in[:, query_size : query_size + latent_width]
    latent_normed, latent_unit, latent_inverse = norm_forward(latent[:, :KV_RANK], gain_latent)
    latent_low = latent_normed.astype(bf16)
    key_rope = rotate(latent[:, KV_RANK:], cosine_table, sine_table).astype(bf16)
    expanded = (
        matmul(latent_low, expand_full).astype(bf16).reshape(tokens, heads_local, NOPE + V_DIM)
    )
    key_rows = jnp.concatenate(
        [expanded[..., :NOPE], jnp.broadcast_to(key_rope[:, None, :], (tokens, heads_local, ROPE))],
        axis=-1,
    )
    values = expanded[..., NOPE:]
    score_scale = 1.0 / math.sqrt(NOPE + ROPE)
    causal = places[:, None] >= places[None, :]
    scores = (
        jnp.einsum("qhd,khd->hqk", queries, key_rows, preferred_element_type=f32) * score_scale
    )
    scores = jnp.where(causal[None], scores, -1e30)
    row_max = jnp.max(scores, axis=-1, keepdims=True)
    powers = jnp.exp(scores - row_max)
    softmax_probs = powers / jnp.sum(powers, axis=-1, keepdims=True)
    probs_low = softmax_probs.astype(bf16)
    attended = jnp.einsum("hqk,khd->qhd", probs_low, values, preferred_element_type=f32)
    attended = attended.astype(bf16).reshape(tokens, heads_local * V_DIM)
    attended, shared_gu_own, shared_down_own = lax.optimization_barrier(
        (attended, shared_gu_own, shared_down_own)
    )
    attn_part = transposed_right(attended, output_turned).astype(bf16)
    resid = hidden_rel[:own].astype(f32) + fold(attn_part, tp_steps).astype(f32)

    normed_mid, unit_mid, inverse_mid = norm_forward(resid, gain_rows[1])
    mid_own, expert_gate_up, expert_down = lax.optimization_barrier(
        (normed_mid.astype(bf16), expert_gate_up, expert_down)
    )
    tiles, down_weight = dense_weights(
        shared_gu_own, shared_down_own, expert_gate_up, expert_down
    )
    raw_parts = [
        transposed_right(rows, down_weight).astype(bf16).reshape(devices, cuts, cut_rows, -1)
        for rows in grad_parts
    ]
    first = (group * EXP_DEV).astype(jnp.int32).reshape(1)
    mid_parts = [
        lax.all_gather(
            mid_own[i * gather_rows : (i + 1) * gather_rows], every, axis=0, tiled=True
        )
        for i in range(GATHERS)
    ]
    one_order = (ep_steps + tp_steps)[::-1]
    turn = [0, *range(2, len(tp_steps) + 1), 1, *range(len(tp_steps) + 1, len(one_order))]
    orders = [one_order, [one_order[i] for i in turn]]
    distance = jnp.arange(devices, dtype=jnp.int32) ^ (group * parts + part)
    slots = []
    for order in orders:
        slot = jnp.zeros_like(distance)
        for axis, bit in order:
            slot = 2 * slot + distance // (bit * (parts if axis == "ep" else 1)) % 2
        slots.append(slot)
    slots = jnp.stack([slots[cut % 2] for cut in range(cuts)])

    def on_a_step(sums):
        return [(fold_step(rows, todo[0]), todo[1:]) if todo else (rows, todo) for rows, todo in sums]

    def together(work, sums):
        work, rows = lax.optimization_barrier((work, [rows for rows, _ in sums]))
        return work, [(each, todo) for each, (_, todo) in zip(rows, sums)]

    mid_parts[0], raw_parts = lax.optimization_barrier((mid_parts[0], raw_parts))
    sums, gate_parts, upper_parts, hidden_parts = [], [], [], []
    for i in range(GATHERS):
        mid_rows = mid_parts[i]
        back, *sides = feed_forward(
            slots,
            mid_rows.reshape(devices, cuts, cut_rows, width),
            raw_parts[i],
            mask_parts[i],
            router_full,
            tiles,
            first,
        )
        (back, sides), sums = together((back, sides), on_a_step(sums))
        sums += [(back[cut], orders[cut % 2]) for cut in range(cuts)]
        for parts_of, side in zip((gate_parts, upper_parts, hidden_parts), sides):
            parts_of.append(side.reshape(mid_rows.shape[0], -1))
        if i == 0:
            firsts = [
                transposed_left(parts_of[0], rows[0])
                for parts_of, rows in ((hidden_parts, grad_parts), (gate_parts, mid_parts))
            ]
            (firsts, mid_parts[1:]), sums = together((firsts, mid_parts[1:]), on_a_step(sums))
    out_part = rows_by_device(hidden_parts, down_weight, devices)
    out_part, sums = together(out_part, on_a_step(sums))
    for _ in range(2):
        out_part, sums = together(out_part, on_a_step(sums))
    out_own = lax.psum_scatter(out_part, every, scatter_dimension=0, tiled=True)
    block_own = (lax.optimization_barrier(resid) + out_own.astype(f32)).astype(bf16)
    while any(todo for _, todo in sums):
        sums = on_a_step(sums)
    back_own = jnp.concatenate([rows[0] for rows, _ in sums], axis=0)

    back_own = back_own.astype(f32)
    gating_grad = back_own[:, width : width + experts]
    mask = lax.dynamic_slice_in_dim(mask_own, part * own, own, axis=0).astype(f32)
    sigmoids = jax.nn.sigmoid(matmul(mid_own, router_full))
    chosen = sigmoids * mask
    sigmoid_total = jnp.sum(chosen, axis=1, keepdims=True)
    weighted = jnp.sum(gating_grad * chosen, axis=1, keepdims=True) / sigmoid_total
    sigmoid_grad = ROUTE_SCALE / sigmoid_total * (gating_grad - weighted)
    logits_grad = (sigmoid_grad * chosen * (1.0 - sigmoids)).astype(bf16)
    grad_router = transposed_left(mid_own, logits_grad)
    mid_grad = back_own[:, :width] + transposed_right(logits_grad, router_full)
    resid_norm_grad, grad_gain_mid = norm_backward(mid_grad, unit_mid, inverse_mid, gain_rows[1])
    resid_grad = grad_own.astype(f32) + resid_norm_grad

    resid_low, hidden_parts, upper_parts = lax.optimization_barrier(
        (resid_grad.astype(bf16), hidden_parts, upper_parts)
    )
    down_second = transposed_left(hidden_parts[1], grad_parts[1])
    upper_first = transposed_left(upper_parts[0], mid_parts[0])
    attn_rows, gate_parts, down_second, upper_first = lax.optimization_barrier(
        (spread(resid_low, tp_steps[:1]), gate_parts, down_second, upper_first)
    )
    firsts = [*firsts, upper_first]
    gate_second = transposed_left(gate_parts[1], mid_parts[1])
    attn_grad, gate_second = lax.optimization_barrier(
        (spread(attn_rows, tp_steps[1:]), gate_second)
    )

    def ring_columns(left_side, right_side):
        size = left_side.shape[1] // groups
        return [
            transposed_left(
                lax.dynamic_slice_in_dim(left_side, g * size, size, axis=1), right_side
            ).astype(bf16)
            for g in ring_groups
        ]

    def beside(work, rings):
        rounds = [ring_round(ring, "ep") for ring in rings]
        work, states = lax.optimization_barrier((work, [state for state, _ in rounds]))
        return work, [(state, left) for state, (_, left) in zip(states, rounds)]

    output_ring = ring_begin(ring_columns(attn_grad, attended), "ep")
    attended_grad = (
        matmul(attn_grad, output_turned).astype(bf16).reshape(tokens, heads_local, V_DIM)
    )
    values_grad = jnp.einsum("hqk,qhd->khd", probs_low, attended_grad, preferred_element_type=f32)
    probs_grad = jnp.einsum("qhd,khd->hqk", attended_grad, values, preferred_element_type=f32)
    scores_grad = (
        softmax_probs * (probs_grad - jnp.sum(softmax_probs * probs_grad, axis=-1, keepdims=True))
    ).astype(bf16)
    (scores_grad, values_grad), (output_ring,) = beside((scores_grad, values_grad), [output_ring])
    query_grad = (
        jnp.einsum("hqk,khd->qhd", scores_grad, key_rows, preferred_element_type=f32) * score_scale
    )
    keys_grad = (
        jnp.einsum("hqk,qhd->khd", scores_grad, queries, preferred_element_type=f32) * score_scale
    )
    query_raw_grad = (
        jnp.concatenate(
            [
                query_grad[..., :NOPE],
                rotate(query_grad[..., NOPE:], cosine_table[:, None, :], -sine_table[:, None, :]),
            ],
            axis=-1,
        )
        .astype(bf16)
        .reshape(tokens, heads_local * (NOPE + ROPE))
    )
    expanded_grad = (
        jnp.concatenate([keys_grad[..., :NOPE], values_grad], axis=-1)
        .astype(bf16)
        .reshape(tokens, heads_local * (NOPE + V_DIM))
    )
    latent_normed_grad = transposed_right(expanded_grad, expand_full)
    latent_part_grad, gain_latent_part = norm_backward(
        latent_normed_grad, latent_unit, latent_inverse, gain_latent
    )
    rope_raw_grad = rotate(jnp.sum(keys_grad[..., NOPE:], axis=1), cosine_table, -sine_table)
    latent_grad = jnp.concatenate([latent_part_grad, rope_raw_grad], axis=1).astype(bf16)
    both_grad = pad_columns(jnp.concatenate([query_raw_grad, latent_grad], axis=1), into_size)
    both_grad, (output_ring,) = beside(both_grad, [output_ring])
    into_ring = ring_begin(ring_columns(normed_low, both_grad), "ep")
    in_grad_part = transposed_right(both_grad, into_full).astype(bf16)
    expand_blocks = transposed_left(latent_low, expanded_grad).astype(bf16)
    expand_blocks = expand_blocks.reshape(groups, -1, expand_blocks.shape[1])
    expand_ring = ring_begin(
        [lax.dynamic_slice_in_dim(expand_blocks, g, 1, axis=0)[0] for g in ring_groups], "ep"
    )
    work = (in_grad_part, [left for _, left in (into_ring, expand_ring)])
    (in_grad_part, lefts), (into_ring, output_ring) = beside(work, [into_ring, output_ring])
    into_ring, expand_ring = (into_ring[0], lefts[0][1:]), (expand_ring[0], lefts[1])

    upper_rows, _ = lax.optimization_barrier((upper_parts[1], in_grad_part))
    upper_second = transposed_left(upper_rows, mid_parts[1])
    in_grad = fold_step(in_grad_part, tp_steps[-1])
    halves = (firsts, [down_second, gate_second, upper_second])
    (halves, in_grad), (into_ring, expand_ring, output_ring) = beside(
        (halves, in_grad), [into_ring, expand_ring, output_ring]
    )

    def grad_units(kind, start, count):
        return sum(half[kind][start : start + count] for half in halves)

    in_grad = fold(in_grad, tp_steps[:-1]).astype(f32)
    (in_grad, halves), (into_ring, expand_ring) = beside((in_grad, halves), [into_ring, expand_ring])

    shared_at = EXP_DEV * expert_pad
    shared_gu_back = lax.all_to_all(
        jnp.stack([grad_units(kind, shared_at, units).T for kind in (1, 2)])
        .astype(bf16)
        .reshape(2, width, 1, units),
        "ep",
        split_axis=1,
        concat_axis=2,
        tiled=True,
    )
    shared_down_back = lax.all_to_all(
        grad_units(0, shared_at, units).astype(bf16),
        "ep",
        split_axis=1,
        concat_axis=0,
        tiled=True,
    )
    input_norm_grad, grad_gain_in = norm_backward(
        in_grad, unit_in[:own], inverse_in[:own], gain_rows[0]
    )
    hidden_own = (resid_grad + input_norm_grad).astype(bf16)
    grad_small = jnp.concatenate(
        [
            jnp.stack([grad_gain_in, grad_gain_mid])
            .reshape(2, groups, -1)
            .transpose(1, 0, 2)
            .reshape(groups, -1),
            gain_latent_part.reshape(groups, -1),
            grad_router.reshape(groups, -1),
        ],
        axis=1,
    )
    small_sum = by_distance(grad_small, group, distances(ep_steps))
    small_sum = fold_step(small_sum, ep_steps[-1])
    hidden_rows = spread(hidden_own[None], tp_steps[:1])
    (hidden_rows, small_sum, halves), (into_ring, expand_ring) = beside(
        (hidden_rows, small_sum, halves), [into_ring, expand_ring]
    )
    hidden_rows = by_place(spread(hidden_rows, tp_steps[1:]), part, tp_order)

    grad_expert_gate_up = jnp.stack(
        [
            jnp.stack([grad_units(kind, e * expert_pad, hidden_units).T for kind in (1, 2)])
            for e in range(EXP_DEV)
        ]
    )
    grad_expert_down = jnp.stack(
        [grad_units(0, e * expert_pad, hidden_units) for e in range(EXP_DEV)]
    )
    grad_shared_gu_out = shared_gu_back.reshape(shared_gate_up.shape).astype(f32)
    grad_shared_down_out = shared_down_back.astype(f32)
    small_sum = fold(small_sum, ep_steps[:-1])
    into_sum = ring_end(into_ring, "ep")
    grad_expand_out = ring_end(expand_ring, "ep")
    grad_output_out = ring_end(output_ring, "ep").T
    grad_query_out = into_sum[:, :query_size]
    grad_latent_out = into_sum[:, query_size : query_size + latent_width]
    for axis, bit in tp_steps:
        rounded = grad_latent_out.astype(bf16)
        grad_latent_out = rounded.astype(f32) + swap(rounded, axis, bit).astype(f32)
    for axis, bit in tp_steps:
        small_sum = small_sum + swap(small_sum, axis, bit)
    small_sum = small_sum.reshape(-1)
    grad_gains_out = small_sum[: at[1]].reshape(norm_gains.shape)
    grad_gain_latent_out = small_sum[at[1] : at[2]]
    grad_router_out = small_sum[at[2] : at[3]].reshape(router_weight.shape)

    return (
        lax.all_gather(block_own, "tp", axis=0, tiled=True),
        hidden_rows.reshape(tokens, width).astype(f32),
        grad_query_out,
        grad_latent_out,
        grad_expand_out,
        grad_output_out,
        grad_gains_out,
        grad_gain_latent_out,
        grad_router_out,
        grad_shared_gu_out,
        grad_shared_down_out,
        grad_expert_gate_up,
        grad_expert_down,
    )


def power_of_two(size):
    return size & (size - 1) == 0


def on_device(hidden_in, *others):
    groups, parts = lax.axis_size("ep"), lax.axis_size("tp")
    tokens = hidden_in.shape[0]
    mean_load = tokens * TOPK // (EXP_DEV * groups)
    capacity = mean_load + mean_load // 3
    if EXP_DEV * capacity >= tokens and power_of_two(groups) and power_of_two(parts):
        return on_device_dense(hidden_in, *others)
    return on_device_sparse(hidden_in, *others)


def solution(mesh):
    placed = (
        P("ep", None),
        P("ep", None),
        P("ep", "tp"),
        P("ep", None),
        P("ep", "tp"),
        P("tp", "ep"),
        P(None, "ep"),
        P("ep"),
        P("ep", None),
        P(None, "ep", "tp"),
        P("tp", "ep"),
        P("ep", None, None, "tp"),
        P("ep", "tp", None),
        P("ep", None),
    )
    return jax.shard_map(
        on_device,
        mesh=mesh,
        in_specs=placed,
        out_specs=(
            P("ep", None),
            P("ep", None),
            P("ep", "tp"),
            P("ep", None),
            P("ep", "tp"),
            P("tp", "ep"),
            P(None, "ep"),
            P("ep"),
            P("ep", None),
            P(None, "ep", "tp"),
            P("tp", "ep"),
            P("ep", None, None, "tp"),
            P("ep", "tp", None),
        ),
        check_vma=False,
    )
```

```python
import functools
import math

import jax
import jax.numpy as jnp
from jax import lax
from jax.experimental import pallas as pl
from jax.experimental.pallas import tpu as pltpu
from jax.sharding import PartitionSpec as P

NOPE = 128
ROPE = 64
V_DIM = 128
KV_RANK = 512
TOPK = 6
EXP_DEV = 2


EPSILON = 1e-06
ROUTE_SCALE = 2.446
ROPE_BASE = 50000.0


def matmul(left_side, right_side):
    return jnp.dot(left_side, right_side, preferred_element_type=jnp.float32)


def transposed_left(left_side, right_side):
    return lax.dot_general(
        left_side, right_side, (((0,), (0,)), ((), ())), preferred_element_type=jnp.float32
    )


def transposed_right(left_side, right_side):
    return lax.dot_general(
        left_side, right_side, (((1,), (1,)), ((), ())), preferred_element_type=jnp.float32
    )


def rotate(values, cosine_table, sine_table):
    halfway = values.shape[-1] // 2
    first_half = values[..., :halfway]
    second_half = values[..., halfway:]
    return jnp.concatenate(
        [
            first_half * cosine_table - second_half * sine_table,
            second_half * cosine_table + first_half * sine_table,
        ],
        axis=-1,
    )


def norm_forward(values, gain_row):
    inverse = lax.rsqrt(jnp.mean(values * values, axis=-1, keepdims=True) + EPSILON)
    unit_rows = values * inverse
    return (unit_rows * gain_row, unit_rows, inverse)


def norm_backward(incoming, unit_rows, inverse, gain_row):
    scaled = incoming * gain_row
    grad_values = inverse * (
        scaled - unit_rows * jnp.mean(scaled * unit_rows, axis=-1, keepdims=True)
    )
    return (grad_values, jnp.sum(incoming * unit_rows, axis=0))


def on_device_sparse(
    hidden_in,
    out_grad,
    query_weight,
    latent_weight,
    expand_weight,
    output_weight,
    norm_gains,
    latent_gain,
    router_weight,
    shared_gate_up,
    shared_down,
    expert_gate_up,
    expert_down,
    expert_ids,
):
    (
        query_full,
        latent_full,
        expand_full,
        output_full,
        gains_full,
        latent_gain_full,
        router_full,
        shared_gu_full,
        shared_down_full,
    ) = (
        lax.all_gather(query_weight, "ep", axis=0, tiled=True),
        lax.all_gather(latent_weight, "ep", axis=0, tiled=True),
        lax.all_gather(expand_weight, "ep", axis=0, tiled=True),
        lax.all_gather(output_weight, "ep", axis=1, tiled=True),
        lax.all_gather(norm_gains, "ep", axis=1, tiled=True),
        lax.all_gather(latent_gain, "ep", axis=0, tiled=True),
        lax.all_gather(router_weight, "ep", axis=0, tiled=True),
        lax.all_gather(shared_gate_up, "ep", axis=1, tiled=True),
        lax.all_gather(shared_down, "ep", axis=1, tiled=True),
    )
    tokens = hidden_in.shape[0]
    model_width = hidden_in.shape[1]
    heads_local = query_full.shape[1] // (NOPE + ROPE)
    gain_rows = gains_full.astype(jnp.float32)
    gain_latent = latent_gain_full.astype(jnp.float32)
    places = jnp.arange(tokens).astype(jnp.float32)
    frequency = ROPE_BASE ** (-(jnp.arange(ROPE // 2).astype(jnp.float32) * 2.0 / ROPE))
    angles = places[:, None] * frequency[None, :]
    cosine_table = jnp.cos(angles)
    sine_table = jnp.sin(angles)
    resid_in = hidden_in.astype(jnp.float32)
    normed_in, unit_in, inverse_in = norm_forward(resid_in, gain_rows[0])
    normed_low = normed_in.astype(jnp.bfloat16)
    query_raw = matmul(normed_low, query_full).reshape(tokens, heads_local, NOPE + ROPE)
    queries = jnp.concatenate(
        [
            query_raw[..., :NOPE],
            rotate(query_raw[..., NOPE:], cosine_table[:, None, :], sine_table[:, None, :]),
        ],
        axis=-1,
    ).astype(jnp.bfloat16)
    latent = matmul(normed_low, latent_full)
    latent_normed, latent_unit, latent_inverse = norm_forward(latent[:, :KV_RANK], gain_latent)
    latent_low = latent_normed.astype(jnp.bfloat16)
    key_rope = rotate(latent[:, KV_RANK:], cosine_table, sine_table).astype(jnp.bfloat16)
    expanded = (
        matmul(latent_low, expand_full)
        .astype(jnp.bfloat16)
        .reshape(tokens, heads_local, NOPE + V_DIM)
    )
    key_rows = jnp.concatenate(
        [expanded[..., :NOPE], jnp.broadcast_to(key_rope[:, None, :], (tokens, heads_local, ROPE))],
        axis=-1,
    )
    values = expanded[..., NOPE:]
    score_scale = 1.0 / math.sqrt(NOPE + ROPE)
    causal = jnp.arange(tokens)[:, None] >= jnp.arange(tokens)[None, :]

    def attention_scores():
        scores = (
            jnp.einsum("qhd,khd->hqk", queries, key_rows, preferred_element_type=jnp.float32)
            * score_scale
        )
        return jnp.where(causal[None], scores, -1e30)

    scores_first = attention_scores()
    row_max = jnp.max(scores_first, axis=-1, keepdims=True)
    log_total = row_max + jnp.log(jnp.sum(jnp.exp(scores_first - row_max), axis=-1, keepdims=True))
    probs_low = jnp.exp(scores_first - log_total).astype(jnp.bfloat16)
    attended = jnp.einsum("hqk,khd->qhd", probs_low, values, preferred_element_type=jnp.float32)
    attended = attended.astype(jnp.bfloat16).reshape(tokens, heads_local * V_DIM)
    attn_out = lax.psum(matmul(attended, output_full), "tp")
    resid = resid_in + attn_out
    normed_mid, unit_mid, inverse_mid = norm_forward(resid, gain_rows[1])
    mid_low = normed_mid.astype(jnp.bfloat16)
    logits = matmul(mid_low, router_full)
    experts = router_full.shape[1]
    route_mask = (expert_ids[:, :, None] == jnp.arange(experts)[None, None, :]).astype(jnp.float32)
    chosen = jnp.sum(route_mask * logits[:, None, :], axis=2)
    sigmoids = jax.nn.sigmoid(chosen)
    sigmoid_total = jnp.sum(sigmoids, axis=1, keepdims=True)
    gating = ROUTE_SCALE * sigmoids / sigmoid_total
    shared_gate = matmul(mid_low, shared_gu_full[0])
    shared_upper = matmul(mid_low, shared_gu_full[1])
    shared_sig = jax.nn.sigmoid(shared_gate)
    shared_hidden = (shared_gate * shared_sig * shared_upper).astype(jnp.bfloat16)
    shared_part = matmul(shared_hidden, shared_down_full)
    groups = lax.axis_size("ep")
    mean_load = tokens * TOPK // (EXP_DEV * groups)
    capacity = mean_load + mean_load // 3
    choices = tokens * TOPK
    rows_total = groups * capacity
    flat_ids = expert_ids.reshape(-1)
    onehot = (flat_ids[:, None] == jnp.arange(experts)[None, :]).astype(jnp.int32)
    slot_of = jnp.sum((jnp.cumsum(onehot, axis=0) - onehot) * onehot, axis=1)
    target = flat_ids % EXP_DEV * rows_total + flat_ids // EXP_DEV * capacity + slot_of
    slot_table = (
        jnp.full((EXP_DEV * rows_total,), choices, jnp.int32)
        .at[target]
        .set(jnp.arange(choices, dtype=jnp.int32))
        .reshape(EXP_DEV, groups, capacity)
    )
    mid_padded = jnp.concatenate([mid_low, jnp.zeros((1, model_width), jnp.bfloat16)], axis=0)
    outgoing = mid_padded[slot_table.reshape(-1) // TOPK].reshape(EXP_DEV, rows_total, model_width)
    expert_rows = lax.all_to_all(outgoing, "ep", split_axis=1, concat_axis=1, tiled=True)
    expert_gate = jnp.einsum(
        "erd,edf->erf", expert_rows, expert_gate_up[:, 0], preferred_element_type=jnp.float32
    )
    expert_upper = jnp.einsum(
        "erd,edf->erf", expert_rows, expert_gate_up[:, 1], preferred_element_type=jnp.float32
    )
    expert_sig = jax.nn.sigmoid(expert_gate)
    expert_hidden = (expert_gate * expert_sig * expert_upper).astype(jnp.bfloat16)
    expert_part = jnp.einsum(
        "erf,efd->erd", expert_hidden, expert_down, preferred_element_type=jnp.float32
    ).astype(jnp.bfloat16)
    returned = lax.all_to_all(expert_part, "ep", split_axis=1, concat_axis=1, tiled=True)
    per_choice = (
        returned.reshape(-1, model_width)[target]
        .reshape(tokens, TOPK, model_width)
        .astype(jnp.float32)
    )
    routed_part = jnp.sum(gating[:, :, None] * per_choice, axis=1)
    moe_out = lax.psum((shared_part + routed_part).astype(jnp.bfloat16), "tp").astype(jnp.float32)
    block_out = (resid + moe_out).astype(jnp.bfloat16)
    grad_top = out_grad.astype(jnp.float32)
    choice_grad = (gating[:, :, None] * grad_top[:, None, :]).astype(jnp.bfloat16)
    grad_padded = jnp.concatenate(
        [choice_grad.reshape(choices, model_width), jnp.zeros((1, model_width), jnp.bfloat16)],
        axis=0,
    )
    outgoing_grad = grad_padded[slot_table.reshape(-1)].reshape(EXP_DEV, rows_total, model_width)
    rows_grad = lax.all_to_all(outgoing_grad, "ep", split_axis=1, concat_axis=1, tiled=True)
    hidden_grad = jnp.einsum(
        "erd,efd->erf", rows_grad, expert_down, preferred_element_type=jnp.float32
    )
    gate_grad = (
        hidden_grad * expert_upper * expert_sig * (1.0 + expert_gate * (1.0 - expert_sig))
    ).astype(jnp.bfloat16)
    upper_grad = (hidden_grad * expert_gate * expert_sig).astype(jnp.bfloat16)
    grad_expert_down = jnp.einsum(
        "erf,erd->efd", expert_hidden, rows_grad, preferred_element_type=jnp.float32
    )
    grad_expert_gate_up = jnp.stack(
        [
            jnp.einsum("erd,erf->edf", expert_rows, gate_grad, preferred_element_type=jnp.float32),
            jnp.einsum("erd,erf->edf", expert_rows, upper_grad, preferred_element_type=jnp.float32),
        ],
        axis=1,
    )
    row_back = jnp.einsum(
        "erf,edf->erd", gate_grad, expert_gate_up[:, 0], preferred_element_type=jnp.float32
    ) + jnp.einsum(
        "erf,edf->erd", upper_grad, expert_gate_up[:, 1], preferred_element_type=jnp.float32
    )
    row_back_low = row_back.astype(jnp.bfloat16)
    back_rows = lax.all_to_all(row_back_low, "ep", split_axis=1, concat_axis=1, tiled=True)
    choice_back = (
        back_rows.reshape(-1, model_width)[target]
        .reshape(tokens, TOPK, model_width)
        .astype(jnp.float32)
    )
    mid_grad_routed = jnp.sum(choice_back, axis=1)
    gating_grad_part = jnp.sum(per_choice * grad_top[:, None, :], axis=2)
    shared_hidden_grad = transposed_right(out_grad, shared_down_full)
    shared_gate_grad = (
        shared_hidden_grad * shared_upper * shared_sig * (1.0 + shared_gate * (1.0 - shared_sig))
    ).astype(jnp.bfloat16)
    shared_upper_grad = (shared_hidden_grad * shared_gate * shared_sig).astype(jnp.bfloat16)
    grad_shared_down = transposed_left(shared_hidden, out_grad)
    grad_shared_gu = jnp.stack(
        [transposed_left(mid_low, shared_gate_grad), transposed_left(mid_low, shared_upper_grad)],
        axis=0,
    )
    mid_grad_shared = transposed_right(shared_gate_grad, shared_gu_full[0]) + transposed_right(
        shared_upper_grad, shared_gu_full[1]
    )
    mid_grad_sum, gating_grad = (
        lax.psum((mid_grad_routed + mid_grad_shared).astype(jnp.bfloat16), "tp").astype(
            jnp.float32
        ),
        lax.psum(gating_grad_part.astype(jnp.bfloat16), "tp").astype(jnp.float32),
    )
    weighted = jnp.sum(gating_grad * sigmoids, axis=1, keepdims=True) / sigmoid_total
    sigmoid_grad = ROUTE_SCALE / sigmoid_total * (gating_grad - weighted)
    chosen_grad = sigmoid_grad * sigmoids * (1.0 - sigmoids)
    logits_grad = jnp.sum(route_mask * chosen_grad[:, :, None], axis=1).astype(jnp.bfloat16)
    grad_router = transposed_left(mid_low, logits_grad)
    mid_grad = mid_grad_sum + transposed_right(logits_grad, router_full)
    resid_norm_grad, grad_gain_mid = norm_backward(mid_grad, unit_mid, inverse_mid, gain_rows[1])
    resid_grad = grad_top + resid_norm_grad
    attn_grad = resid_grad.astype(jnp.bfloat16)
    grad_output = transposed_left(attended, attn_grad)
    attended_grad = (
        transposed_right(attn_grad, output_full)
        .astype(jnp.bfloat16)
        .reshape(tokens, heads_local, V_DIM)
    )
    softmax_probs = jnp.exp(attention_scores() - log_total)
    values_grad = jnp.einsum(
        "hqk,qhd->khd",
        softmax_probs.astype(jnp.bfloat16),
        attended_grad,
        preferred_element_type=jnp.float32,
    )
    probs_grad = jnp.einsum(
        "qhd,khd->hqk", attended_grad, values, preferred_element_type=jnp.float32
    )
    scores_grad = (
        softmax_probs * (probs_grad - jnp.sum(softmax_probs * probs_grad, axis=-1, keepdims=True))
    ).astype(jnp.bfloat16)
    query_grad = (
        jnp.einsum("hqk,khd->qhd", scores_grad, key_rows, preferred_element_type=jnp.float32)
        * score_scale
    )
    keys_grad = (
        jnp.einsum("hqk,qhd->khd", scores_grad, queries, preferred_element_type=jnp.float32)
        * score_scale
    )
    query_raw_grad = (
        jnp.concatenate(
            [
                query_grad[..., :NOPE],
                rotate(query_grad[..., NOPE:], cosine_table[:, None, :], -sine_table[:, None, :]),
            ],
            axis=-1,
        )
        .astype(jnp.bfloat16)
        .reshape(tokens, heads_local * (NOPE + ROPE))
    )
    expanded_grad = jnp.concatenate([keys_grad[..., :NOPE], values_grad], axis=-1).astype(
        jnp.bfloat16
    )
    expanded_grad = expanded_grad.reshape(tokens, heads_local * (NOPE + V_DIM))
    grad_expand = transposed_left(latent_low, expanded_grad)
    latent_normed_grad = transposed_right(expanded_grad, expand_full)
    latent_part_grad, gain_latent_part = norm_backward(
        latent_normed_grad, latent_unit, latent_inverse, gain_latent
    )
    rope_raw_grad = rotate(jnp.sum(keys_grad[..., NOPE:], axis=1), cosine_table, -sine_table)
    latent_grad_part = jnp.concatenate([latent_part_grad, rope_raw_grad], axis=1)
    in_grad_query = transposed_right(query_raw_grad, query_full)
    in_grad_sum, latent_grad, grad_gain_latent = (
        lax.psum(in_grad_query.astype(jnp.bfloat16), "tp").astype(jnp.float32),
        lax.psum(latent_grad_part.astype(jnp.bfloat16), "tp").astype(jnp.float32),
        lax.psum(gain_latent_part.astype(jnp.bfloat16), "tp").astype(jnp.float32),
    )
    latent_grad_low = latent_grad.astype(jnp.bfloat16)
    grad_latent = transposed_left(normed_low, latent_grad_low)
    grad_query = transposed_left(normed_low, query_raw_grad)
    in_grad = in_grad_sum + transposed_right(latent_grad_low, latent_full)
    input_norm_grad, grad_gain_in = norm_backward(in_grad, unit_in, inverse_in, gain_rows[0])
    grad_hidden = resid_grad + input_norm_grad
    grad_gains = jnp.stack([grad_gain_in, grad_gain_mid], axis=0)
    (
        grad_query_out,
        grad_latent_out,
        grad_expand_out,
        grad_output_out,
        grad_gains_out,
        grad_gain_latent_out,
        grad_router_out,
        grad_shared_gu_out,
        grad_shared_down_out,
    ) = (
        lax.psum_scatter(
            grad_query.astype(jnp.bfloat16), "ep", scatter_dimension=0, tiled=True
        ).astype(jnp.float32),
        lax.psum_scatter(
            grad_latent.astype(jnp.bfloat16), "ep", scatter_dimension=0, tiled=True
        ).astype(jnp.float32),
        lax.psum_scatter(
            grad_expand.astype(jnp.bfloat16), "ep", scatter_dimension=0, tiled=True
        ).astype(jnp.float32),
        lax.psum_scatter(
            grad_output.astype(jnp.bfloat16), "ep", scatter_dimension=1, tiled=True
        ).astype(jnp.float32),
        lax.psum_scatter(
            grad_gains.astype(jnp.bfloat16), "ep", scatter_dimension=1, tiled=True
        ).astype(jnp.float32),
        lax.psum_scatter(
            grad_gain_latent.astype(jnp.bfloat16), "ep", scatter_dimension=0, tiled=True
        ).astype(jnp.float32),
        lax.psum_scatter(
            grad_router.astype(jnp.bfloat16), "ep", scatter_dimension=0, tiled=True
        ).astype(jnp.float32),
        lax.psum_scatter(
            grad_shared_gu.astype(jnp.bfloat16), "ep", scatter_dimension=1, tiled=True
        ).astype(jnp.float32),
        lax.psum_scatter(
            grad_shared_down.astype(jnp.bfloat16), "ep", scatter_dimension=1, tiled=True
        ).astype(jnp.float32),
    )
    return (
        block_out,
        grad_hidden,
        grad_query_out,
        grad_latent_out,
        grad_expand_out,
        grad_output_out,
        grad_gains_out,
        grad_gain_latent_out,
        grad_router_out,
        grad_shared_gu_out,
        grad_shared_down_out,
        grad_expert_gate_up,
        grad_expert_down,
    )


CUTS = 4
GATHERS = 2
LANES = 128
VMEM_BYTES = 56 * 1024 * 1024


def swap(array, axis, bit):
    size = lax.axis_size(axis)
    return lax.ppermute(array, axis, [(place, place ^ bit) for place in range(size)])


def axis_bits(axis):
    size = lax.axis_size(axis)
    return [(axis, 1 << bit) for bit in reversed(range(size.bit_length() - 1))]


def spread(rows, steps):
    for axis, bit in steps:
        rows = jnp.concatenate([rows, swap(rows, axis, bit)], axis=0)
    return rows


def add_rounded(left_side, right_side):
    return (left_side.astype(jnp.float32) + right_side.astype(jnp.float32)).astype(
        left_side.dtype
    )


def fold_step(rows, step):
    axis, bit = step
    half = rows.shape[0] // 2
    return add_rounded(rows[:half], swap(rows[half:], axis, bit))


def fold(rows, steps):
    for step in reversed(steps):
        rows = fold_step(rows, step)
    return rows


def distances(steps):
    found = [0]
    for _, bit in steps:
        found = found + [distance + bit for distance in found]
    return found


def by_distance(blocks, place, order):
    return jnp.concatenate(
        [lax.dynamic_slice_in_dim(blocks, place ^ i, 1, axis=0) for i in order], axis=0
    )


def by_place(blocks, place, order):
    natural = jnp.concatenate([blocks[order.index(i)][None] for i in range(len(order))], axis=0)
    return by_distance(natural, place, range(len(order)))


def ring_owner(spot, size):
    return jnp.where(spot < size // 2, 2 * spot, 2 * (size - 1 - spot) + 1)


def ring_spot(place, size):
    return jnp.where(place % 2 == 0, place // 2, size - 1 - place // 2)


def ring_shift(array, axis, by):
    size = lax.axis_size(axis)
    ring = [2 * i for i in range(size // 2)] + [2 * i + 1 for i in reversed(range(size // 2))]
    return lax.ppermute(array, axis, [(ring[i], ring[(i + by) % size]) for i in range(size)])


def ring_gather(arrays, axis, beside):
    size = lax.axis_size(axis)
    found = [[array] + [None] * (size - 1) for array in arrays]
    ahead, behind, others, rounds = arrays, arrays, [], []
    for k in range(1, size // 2 + 1):
        behind = [ring_shift(array, axis, 1) for array in behind]
        if k < size - k:
            ahead = [ring_shift(array, axis, -1) for array in ahead]
        other = beside[k - 1](others) if k <= len(beside) else None
        behind, ahead, other = lax.optimization_barrier((behind, ahead, other))
        others.append(other)
        rounds.append(behind)
        for pieces, before, after in zip(found, behind, ahead):
            pieces[size - k] = before
            if k < size - k:
                pieces[k] = after
    return found, others, rounds


def ring_begin(parts, axis):
    size = lax.axis_size(axis)
    half = size // 2
    left = [(parts[half - k], parts[half + 1 + k] if k < half - 1 else None) for k in range(1, half)]
    return (parts[half], parts[half + 1]), left + [(parts[0], None)]


def ring_round(ring, axis):
    (ahead, behind), left = ring
    more_ahead, more_behind = left[0]
    ahead = add_rounded(ring_shift(ahead, axis, 1), more_ahead)
    if behind is not None and len(left) > 1:
        behind = ring_shift(behind, axis, -1)
        if more_behind is not None:
            behind = add_rounded(behind, more_behind)
    return (ahead, behind), left[1:]


def ring_end(ring, axis):
    (ahead, behind), left = ring
    while left:
        if len(left) == 1:
            found = ring_shift(ahead, axis, 1).astype(jnp.float32) + left[0][0]
            return found + behind
        (ahead, behind), left = ring_round(((ahead, behind), left), axis)
    return ahead.astype(jnp.float32) + behind


def pad_columns(array, width):
    return jnp.pad(array, ((0, 0), (0, width - array.shape[1])))


def pad_rows(array, height):
    return jnp.pad(array, ((0, height - array.shape[0]), (0, 0)))


def round_up(size, step=LANES):
    return -(-size // step) * step


def feed_forward_kernel(count, wide_steps, sub, *refs):
    first_ref, slot_ref, rows_ref, raw_ref, mask_ref, router_ref, tiles_ref = refs[:7]
    back_out, gate_ref, upper_ref, hidden_ref = refs[7:11]
    gains, shares, kept, tiles, back_ref, arrived, back_left = refs[11:]
    cut, step, last = pl.program_id(0), pl.program_id(1), count + wide_steps - 1
    owners, _, each, width = rows_ref.shape
    half, rows = raw_ref.shape[3], owners * each
    block = sub // each
    f32, bf16 = jnp.float32, jnp.bfloat16

    def arrival(n):
        return pltpu.make_async_copy(tiles_ref.at[n], tiles.at[n], arrived.at[n])

    def back_leaving(n):
        size = width // wide_steps
        extra = back_ref.shape[2] - width if n == wide_steps - 1 else 0
        of = (slice(None), slice(None), pl.ds(n * size, size + extra))
        return pltpu.make_async_copy(back_ref.at[of], back_out.at[(cut, *of)], back_left.at[n])

    @pl.when(step == 0)
    def _():
        @pl.when(cut == 0)
        def _():
            for n in range(count):
                arrival(n).start()

        values = rows_ref[...].reshape(rows, width)
        logits = jnp.dot(values, router_ref[...], preferred_element_type=f32)
        sig = jax.nn.sigmoid(logits) * mask_ref[...].reshape(logits.shape)
        gating = ROUTE_SCALE * sig / jnp.sum(sig, axis=1, keepdims=True)
        lanes = lax.broadcasted_iota(jnp.int32, gating.shape, 1)
        for e in range(EXP_DEV):
            own = jnp.sum(jnp.where(lanes == first_ref[0] + e, gating, 0.0), axis=1, keepdims=True)
            gains[e] = jnp.broadcast_to(own, gains.shape[1:])
        gains[EXP_DEV] = jnp.ones(gains.shape[1:], f32)
        shares[...] = jnp.zeros_like(shares)

    @pl.when(step < count)
    def _():
        @pl.when(cut == 0)
        def _():
            arrival(step).wait()

        kind = jnp.minimum(step // ((count - 1) // EXP_DEV), EXP_DEV)
        for i in range(rows // sub):
            at, of = pl.ds(i * sub, sub), pl.ds(i * block, block)
            values = rows_ref[of].reshape(sub, width)
            both = lax.dot_general(
                values, tiles[step], (((1,), (1,)), ((), ())), preferred_element_type=f32
            )
            gate, upper = both[:, :half], both[:, half:]
            gain, raw = gains[kind, at, :], raw_ref[of].reshape(sub, half).astype(f32)
            sig = jax.nn.sigmoid(gate)
            silu = gate * sig
            hidden = silu * upper
            grad = gain * raw
            shape = (block, 1, each, half)
            hidden_ref[of] = (gain * hidden).astype(bf16).reshape(shape)
            shares[kind, at, :] += hidden * raw
            gate_grad = (grad * upper * (sig + silu * (1.0 - sig))).astype(bf16)
            upper_grad = (grad * silu).astype(bf16)
            gate_ref[of] = gate_grad.reshape(shape)
            upper_ref[of] = upper_grad.reshape(shape)
            kept[step, at, :half] = gate_grad
            kept[step, at, half:] = upper_grad

    @pl.when(step >= count)
    def _():
        size = width // wide_steps
        columns = pl.ds(pl.multiple_of((step - count) * size, size), size)
        for i in range(rows // sub):
            found = sum(
                jnp.dot(
                    kept[n, pl.ds(i * sub, sub), :],
                    tiles[n, :, columns],
                    preferred_element_type=f32,
                )
                for n in range(count)
            ).astype(bf16)
            for j in range(block):
                part = found[j * each : (j + 1) * each]
                back_ref[slot_ref[cut, i * block + j], :, columns] = part

    @pl.when(step == last)
    def _():
        extra = back_ref.shape[2] - width
        lanes = lax.broadcasted_iota(jnp.int32, (rows, extra), 1)
        gating_grad = jnp.zeros(lanes.shape, f32)
        for e in range(EXP_DEV):
            own = jnp.sum(shares[e], axis=1, keepdims=True)
            gating_grad += jnp.where(lanes == first_ref[0] + e, own, 0.0)
        gating_grad = gating_grad.astype(bf16)
        for i in range(owners):
            back_ref[slot_ref[cut, i], :, width:] = gating_grad[i * each : (i + 1) * each]

    for n in range(wide_steps):

        @pl.when(step == count + n)
        def _(n=n):
            back_leaving(n).start()

    @pl.when(step == last)
    def _():
        for n in range(wide_steps):
            back_leaving(n).wait()


def feed_forward(slots, mid_rows, raw_grad, mask, router, tiles, first):
    count, both, width = tiles.shape
    owners, cuts, each, experts = mask.shape
    rows, half, wide_steps = owners * each, both // 2, 4
    bf16, f32 = jnp.bfloat16, jnp.float32

    def tile(step):
        return jnp.minimum(step, count - 1)

    smem, whole = pl.BlockSpec(memory_space=pltpu.SMEM), pl.BlockSpec(memory_space=pl.ANY)
    side = pl.BlockSpec((owners, 1, each, half), lambda c, i: (0, c, 0, tile(i)))
    return pl.pallas_call(
        functools.partial(feed_forward_kernel, count, wide_steps, min(8, owners) * each),
        grid=(cuts, count + wide_steps),
        in_specs=[
            smem,
            smem,
            pl.BlockSpec((owners, 1, each, width), lambda c, i: (0, c, 0, 0)),
            side,
            pl.BlockSpec((owners, 1, each, experts), lambda c, i: (0, c, 0, 0)),
            pl.BlockSpec((width, experts), lambda c, i: (0, 0)),
            whole,
        ],
        out_specs=[whole, side, side, side],
        out_shape=[
            jax.ShapeDtypeStruct((cuts, owners, each, width + LANES), bf16),
            *[jax.ShapeDtypeStruct((owners, cuts, each, count * half), bf16)] * 3,
        ],
        scratch_shapes=[
            pltpu.VMEM((EXP_DEV + 1, rows, half), f32),
            pltpu.VMEM((EXP_DEV + 1, rows, half), f32),
            pltpu.VMEM((count, rows, both), bf16),
            pltpu.VMEM(tiles.shape, bf16),
            pltpu.VMEM((owners, each, width + LANES), bf16),
            pltpu.SemaphoreType.DMA((count,)),
            pltpu.SemaphoreType.DMA((wide_steps,)),
        ],
        compiler_params=pltpu.CompilerParams(vmem_limit_bytes=VMEM_BYTES),
        cost_estimate=pl.CostEstimate(
            flops=4 * cuts * rows * width * both * count,
            bytes_accessed=50_000_000,
            transcendentals=0,
        ),
    )(first, slots, mid_rows, raw_grad, mask, router, tiles)


def rows_by_device_kernel(*refs):
    *left_refs, right_ref, out_ref = refs
    for i, left_ref in enumerate(left_refs):

        @pl.when(pl.program_id(1) == i)
        def _(left_ref=left_ref):
            found = jnp.dot(left_ref[...], right_ref[...], preferred_element_type=jnp.float32)
            out_ref[...] = found.astype(out_ref.dtype).reshape(out_ref.shape)


def rows_by_device(left_parts, right_side, devices):
    rows, depth = left_parts[0].shape
    columns, count = right_side.shape[1], len(left_parts)
    wide = columns // 2
    return pl.pallas_call(
        rows_by_device_kernel,
        grid=(2, count),
        in_specs=[pl.BlockSpec((rows, depth), lambda j, i: (0, 0))] * count
        + [pl.BlockSpec((depth, wide), lambda j, i: (0, j))],
        out_specs=pl.BlockSpec((devices, 1, rows // devices, wide), lambda j, i: (0, i, 0, j)),
        out_shape=jax.ShapeDtypeStruct(
            (devices, count, rows // devices, columns), right_side.dtype
        ),
        compiler_params=pltpu.CompilerParams(vmem_limit_bytes=VMEM_BYTES),
        cost_estimate=pl.CostEstimate(
            flops=2 * count * rows * depth * columns,
            bytes_accessed=2 * count * rows * (depth + columns),
            transcendentals=0,
        ),
    )(*left_parts, right_side).reshape(count * rows, columns)


def place_kernel(places_ref, *refs):
    *pieces, out_ref = refs
    for i, piece in enumerate(pieces):

        @pl.when(pl.program_id(0) == i)
        def _(piece=piece):
            out_ref[0] = piece[...]


def place_blocks(pieces, places):
    shape = pieces[0].shape
    return pl.pallas_call(
        place_kernel,
        grid_spec=pltpu.PrefetchScalarGridSpec(
            num_scalar_prefetch=1,
            grid=(len(pieces),),
            in_specs=[pl.BlockSpec(shape, lambda i, at: (0, 0))] * len(pieces),
            out_specs=pl.BlockSpec((1, *shape), lambda i, at: (at[i], 0, 0)),
        ),
        out_shape=jax.ShapeDtypeStruct((len(pieces), *shape), pieces[0].dtype),
        compiler_params=pltpu.CompilerParams(vmem_limit_bytes=VMEM_BYTES),
    )(jnp.stack(places).astype(jnp.int32), *pieces)


def on_device_dense(
    hidden_in,
    out_grad,
    query_weight,
    latent_weight,
    expand_weight,
    output_weight,
    norm_gains,
    latent_gain,
    router_weight,
    shared_gate_up,
    shared_down,
    expert_gate_up,
    expert_down,
    expert_ids,
):
    groups, parts = lax.axis_size("ep"), lax.axis_size("tp")
    group, part = lax.axis_index("ep"), lax.axis_index("tp")
    tokens, width = hidden_in.shape
    own = tokens // parts
    experts = router_weight.shape[1]
    bf16, f32 = jnp.bfloat16, jnp.float32
    ep_steps, tp_steps = axis_bits("ep"), axis_bits("tp")
    tp_order = distances(tp_steps)
    every = ("ep", "tp")
    devices = groups * parts
    cut_rows = own // CUTS

    spot = ring_spot(group, groups)
    ring_groups = [ring_owner((spot + k) % groups, groups) for k in range(groups)]

    mask_own = jnp.sum(
        (expert_ids[:, :, None] == jnp.arange(experts)[None, None, :]).astype(bf16), axis=1
    )
    sizes = [norm_gains.size, latent_gain.size, router_weight.size, mask_own.size]
    small = jnp.concatenate(
        [array.reshape(1, -1) for array in (norm_gains, latent_gain, router_weight, mask_own)],
        axis=1,
    )
    query_size, latent_width = query_weight.shape[1], latent_weight.shape[1]
    output_size = output_weight.shape[0]
    into_size = round_up(query_size + latent_width)
    into = pad_columns(jnp.concatenate([query_weight, latent_weight], axis=1), into_size)
    out_of = jnp.concatenate(
        [output_weight.T, expand_weight.reshape(output_weight.shape[1], -1)], axis=1
    )

    units = shared_down.shape[0] // groups

    hidden_units = expert_down.shape[1]
    expert_pad, shared_pad = round_up(hidden_units), round_up(units)

    def dense_weights(shared_gu_own, shared_down_own, expert_gate_up, expert_down):
        side_weights = [
            jnp.concatenate(
                [pad_rows(expert_gate_up[e, side].T, expert_pad) for e in range(EXP_DEV)]
                + [pad_rows(shared_gu_own[side].T, shared_pad)],
                axis=0,
            ).reshape(-1, LANES, width)
            for side in range(2)
        ]
        tiles = jnp.concatenate(side_weights, axis=1)
        down_weight = jnp.concatenate(
            [pad_rows(expert_down[e], expert_pad) for e in range(EXP_DEV)]
            + [pad_rows(shared_down_own, shared_pad)],
            axis=0,
        )
        return tiles, down_weight

    (into_pieces, out_of_pieces), others, rounds = ring_gather(
        [into, out_of],
        "ep",
        [
            lambda _: spread(small, ep_steps[:1]),
            lambda done: spread(done[0], ep_steps[1:2]),
            lambda done: spread(done[1], ep_steps[2:]),
        ],
    )
    shared_gate_up_late, shared_down_late, _ = lax.optimization_barrier(
        (shared_gate_up, shared_down, rounds[-1])
    )
    shared_gu_own = lax.all_to_all(
        shared_gate_up_late.reshape(2, -1, groups, units), "ep", split_axis=2, concat_axis=1, tiled=True
    ).reshape(2, width, units)
    shared_down_own = lax.all_to_all(shared_down_late, "ep", split_axis=0, concat_axis=1, tiled=True)


    small_rel = others[2]
    at = [sum(sizes[:i]) for i in range(len(sizes) + 1)]
    small_full = by_place(small_rel, group, distances(ep_steps))
    gain_rows = (
        small_full[:, : at[1]].reshape(groups, 2, -1).transpose(1, 0, 2).reshape(2, width)
    ).astype(f32)
    gain_latent = small_full[:, at[1] : at[2]].reshape(-1).astype(f32)
    router_full = small_full[:, at[2] : at[3]].reshape(width, experts)

    into_full = place_blocks(into_pieces, ring_groups).reshape(width, -1)
    out_of_full = place_blocks(out_of_pieces, ring_groups).reshape(width, -1)
    expand_full = out_of_full[:, output_size:].reshape(KV_RANK, -1)
    output_turned = out_of_full[:, :output_size]

    out_grad_late, _ = lax.optimization_barrier((out_grad, rounds[-2][0]))

    gather_rows = own // GATHERS
    cuts = CUTS // GATHERS

    def by_gather(rows):
        rows = rows.reshape(devices, GATHERS, gather_rows, -1).transpose(1, 0, 2, 3)
        return list(rows.reshape(GATHERS, devices * gather_rows, -1))

    grad_own = lax.dynamic_slice_in_dim(out_grad_late, part * own, own, axis=0)
    grad_parts = by_gather(lax.all_gather(grad_own, every, axis=0, tiled=True))
    mask_parts = [
        rows.astype(f32).reshape(devices, cuts, cut_rows, experts)
        for rows in by_gather(small_full[:, at[3] :])
    ]

    row_blocks = hidden_in.reshape(parts, own, width)
    hidden_rel = by_distance(row_blocks, part, tp_order).reshape(tokens, width)
    heads_local = query_size // (NOPE + ROPE)
    places = ((part ^ jnp.array(tp_order))[:, None] * own + jnp.arange(own)[None, :]).reshape(-1)
    frequency = ROPE_BASE ** (-(jnp.arange(ROPE // 2).astype(f32) * 2.0 / ROPE))
    angles = places.astype(f32)[:, None] * frequency[None, :]
    cosine_table = jnp.cos(angles)
    sine_table = jnp.sin(angles)
    normed_in, unit_in, inverse_in = norm_forward(hidden_rel.astype(f32), gain_rows[0])
    normed_low = normed_in.astype(bf16)
    both_in = matmul(normed_low, into_full)
    query_raw = both_in[:, :query_size].reshape(tokens, heads_local, NOPE + ROPE)
    queries = jnp.concatenate(
        [
            query_raw[..., :NOPE],
            rotate(query_raw[..., NOPE:], cosine_table[:, None, :], sine_table[:, None, :]),
        ],
        axis=-1,
    ).astype(bf16)
    latent = both_in[:, query_size : query_size + latent_width]
    latent_normed, latent_unit, latent_inverse = norm_forward(latent[:, :KV_RANK], gain_latent)
    latent_low = latent_normed.astype(bf16)
    key_rope = rotate(latent[:, KV_RANK:], cosine_table, sine_table).astype(bf16)
    expanded = (
        matmul(latent_low, expand_full).astype(bf16).reshape(tokens, heads_local, NOPE + V_DIM)
    )
    key_rows = jnp.concatenate(
        [expanded[..., :NOPE], jnp.broadcast_to(key_rope[:, None, :], (tokens, heads_local, ROPE))],
        axis=-1,
    )
    values = expanded[..., NOPE:]
    score_scale = 1.0 / math.sqrt(NOPE + ROPE)
    causal = places[:, None] >= places[None, :]
    scores = (
        jnp.einsum("qhd,khd->hqk", queries, key_rows, preferred_element_type=f32) * score_scale
    )
    scores = jnp.where(causal[None], scores, -1e30)
    row_max = jnp.max(scores, axis=-1, keepdims=True)
    powers = jnp.exp(scores - row_max)
    softmax_probs = powers / jnp.sum(powers, axis=-1, keepdims=True)
    probs_low = softmax_probs.astype(bf16)
    attended = jnp.einsum("hqk,khd->qhd", probs_low, values, preferred_element_type=f32)
    attended = attended.astype(bf16).reshape(tokens, heads_local * V_DIM)
    attn_part = transposed_right(attended, output_turned).astype(bf16)
    attn_sum, shared_gu_own, shared_down_own = lax.optimization_barrier(
        (fold(attn_part, tp_steps), shared_gu_own, shared_down_own)
    )
    resid = hidden_rel[:own].astype(f32) + attn_sum.astype(f32)

    normed_mid, unit_mid, inverse_mid = norm_forward(resid, gain_rows[1])
    mid_own, expert_gate_up, expert_down = lax.optimization_barrier(
        (normed_mid.astype(bf16), expert_gate_up, expert_down)
    )
    tiles, down_weight = dense_weights(
        shared_gu_own, shared_down_own, expert_gate_up, expert_down
    )
    raw_parts = [
        transposed_right(rows, down_weight).astype(bf16).reshape(devices, cuts, cut_rows, -1)
        for rows in grad_parts
    ]
    first = (group * EXP_DEV).astype(jnp.int32).reshape(1)
    mid_parts = [
        lax.all_gather(
            mid_own[i * gather_rows : (i + 1) * gather_rows], every, axis=0, tiled=True
        )
        for i in range(GATHERS)
    ]
    one_order = (ep_steps + tp_steps)[::-1]
    turn = [0, *range(2, len(tp_steps) + 1), 1, *range(len(tp_steps) + 1, len(one_order))]
    orders = [one_order, [one_order[i] for i in turn]]
    distance = jnp.arange(devices, dtype=jnp.int32) ^ (group * parts + part)
    slots = []
    for order in orders:
        slot = jnp.zeros_like(distance)
        for axis, bit in order:
            slot = 2 * slot + distance // (bit * (parts if axis == "ep" else 1)) % 2
        slots.append(slot)
    slots = jnp.stack([slots[cut % 2] for cut in range(cuts)])

    def on_a_step(sums):
        return [(fold_step(rows, todo[0]), todo[1:]) if todo else (rows, todo) for rows, todo in sums]

    def together(work, sums):
        work, rows = lax.optimization_barrier((work, [rows for rows, _ in sums]))
        return work, [(each, todo) for each, (_, todo) in zip(rows, sums)]

    mid_parts[0], raw_parts = lax.optimization_barrier((mid_parts[0], raw_parts))
    sums, gate_parts, upper_parts, hidden_parts = [], [], [], []
    for i in range(GATHERS):
        mid_rows = mid_parts[i]
        back, *sides = feed_forward(
            slots,
            mid_rows.reshape(devices, cuts, cut_rows, width),
            raw_parts[i],
            mask_parts[i],
            router_full,
            tiles,
            first,
        )
        (back, sides), sums = together((back, sides), on_a_step(sums))
        sums += [(back[cut], orders[cut % 2]) for cut in range(cuts)]
        for parts_of, side in zip((gate_parts, upper_parts, hidden_parts), sides):
            parts_of.append(side.reshape(mid_rows.shape[0], -1))
        if i == 0:
            firsts = [
                transposed_left(parts_of[0], rows[0])
                for parts_of, rows in ((hidden_parts, grad_parts), (gate_parts, mid_parts))
            ]
            (firsts, mid_parts[1:]), sums = together((firsts, mid_parts[1:]), on_a_step(sums))
    firsts.append(transposed_left(upper_parts[0], mid_parts[0]))
    (firsts, hidden_parts), sums = together((firsts, hidden_parts), on_a_step(sums))
    out_part = rows_by_device(hidden_parts, down_weight, devices)
    for _ in range(2):
        out_part, sums = together(out_part, on_a_step(sums))
    out_own = lax.psum_scatter(out_part, every, scatter_dimension=0, tiled=True)
    block_own = (lax.optimization_barrier(resid) + out_own.astype(f32)).astype(bf16)
    while any(todo for _, todo in sums):
        sums = on_a_step(sums)
    back_own = jnp.concatenate([rows[0] for rows, _ in sums], axis=0)

    back_own = back_own.astype(f32)
    gating_grad = back_own[:, width : width + experts]
    mask = lax.dynamic_slice_in_dim(mask_own, part * own, own, axis=0).astype(f32)
    sigmoids = jax.nn.sigmoid(matmul(mid_own, router_full))
    chosen = sigmoids * mask
    sigmoid_total = jnp.sum(chosen, axis=1, keepdims=True)
    weighted = jnp.sum(gating_grad * chosen, axis=1, keepdims=True) / sigmoid_total
    sigmoid_grad = ROUTE_SCALE / sigmoid_total * (gating_grad - weighted)
    logits_grad = (sigmoid_grad * chosen * (1.0 - sigmoids)).astype(bf16)
    grad_router = transposed_left(mid_own, logits_grad)
    mid_grad = back_own[:, :width] + transposed_right(logits_grad, router_full)
    resid_norm_grad, grad_gain_mid = norm_backward(mid_grad, unit_mid, inverse_mid, gain_rows[1])
    resid_grad = grad_own.astype(f32) + resid_norm_grad

    resid_low, hidden_parts = lax.optimization_barrier((resid_grad.astype(bf16), hidden_parts))
    down_second = transposed_left(hidden_parts[1], grad_parts[1])
    attn_rows, gate_parts, down_second = lax.optimization_barrier(
        (spread(resid_low, tp_steps[:1]), gate_parts, down_second)
    )
    gate_second = transposed_left(gate_parts[1], mid_parts[1])
    attn_grad, gate_second = lax.optimization_barrier(
        (spread(attn_rows, tp_steps[1:]), gate_second)
    )

    def ring_columns(left_side, right_side):
        size = left_side.shape[1] // groups
        return [
            transposed_left(
                lax.dynamic_slice_in_dim(left_side, g * size, size, axis=1), right_side
            ).astype(bf16)
            for g in ring_groups
        ]

    def beside(work, rings):
        rounds = [ring_round(ring, "ep") for ring in rings]
        work, states = lax.optimization_barrier((work, [state for state, _ in rounds]))
        return work, [(state, left) for state, (_, left) in zip(states, rounds)]

    output_ring = ring_begin(ring_columns(attn_grad, attended), "ep")
    attended_grad = (
        matmul(attn_grad, output_turned).astype(bf16).reshape(tokens, heads_local, V_DIM)
    )
    values_grad = jnp.einsum("hqk,qhd->khd", probs_low, attended_grad, preferred_element_type=f32)
    probs_grad = jnp.einsum("qhd,khd->hqk", attended_grad, values, preferred_element_type=f32)
    scores_grad = (
        softmax_probs * (probs_grad - jnp.sum(softmax_probs * probs_grad, axis=-1, keepdims=True))
    ).astype(bf16)
    (scores_grad, values_grad), (output_ring,) = beside((scores_grad, values_grad), [output_ring])
    query_grad = (
        jnp.einsum("hqk,khd->qhd", scores_grad, key_rows, preferred_element_type=f32) * score_scale
    )
    keys_grad = (
        jnp.einsum("hqk,qhd->khd", scores_grad, queries, preferred_element_type=f32) * score_scale
    )
    query_raw_grad = (
        jnp.concatenate(
            [
                query_grad[..., :NOPE],
                rotate(query_grad[..., NOPE:], cosine_table[:, None, :], -sine_table[:, None, :]),
            ],
            axis=-1,
        )
        .astype(bf16)
        .reshape(tokens, heads_local * (NOPE + ROPE))
    )
    expanded_grad = (
        jnp.concatenate([keys_grad[..., :NOPE], values_grad], axis=-1)
        .astype(bf16)
        .reshape(tokens, heads_local * (NOPE + V_DIM))
    )
    latent_normed_grad = transposed_right(expanded_grad, expand_full)
    latent_part_grad, gain_latent_part = norm_backward(
        latent_normed_grad, latent_unit, latent_inverse, gain_latent
    )
    rope_raw_grad = rotate(jnp.sum(keys_grad[..., NOPE:], axis=1), cosine_table, -sine_table)
    latent_grad = jnp.concatenate([latent_part_grad, rope_raw_grad], axis=1).astype(bf16)
    both_grad = pad_columns(jnp.concatenate([query_raw_grad, latent_grad], axis=1), into_size)
    both_grad, (output_ring,) = beside(both_grad, [output_ring])
    into_ring = ring_begin(ring_columns(normed_low, both_grad), "ep")
    in_grad_part = transposed_right(both_grad, into_full).astype(bf16)
    expand_blocks = transposed_left(latent_low, expanded_grad).astype(bf16)
    expand_blocks = expand_blocks.reshape(groups, -1, expand_blocks.shape[1])
    expand_ring = ring_begin(
        [lax.dynamic_slice_in_dim(expand_blocks, g, 1, axis=0)[0] for g in ring_groups], "ep"
    )
    work = (in_grad_part, [left for _, left in (into_ring, expand_ring)])
    (in_grad_part, lefts), (into_ring, output_ring) = beside(work, [into_ring, output_ring])
    into_ring, expand_ring = (into_ring[0], lefts[0][1:]), (expand_ring[0], lefts[1])

    upper_rows, _ = lax.optimization_barrier((upper_parts[1], in_grad_part))
    upper_second = transposed_left(upper_rows, mid_parts[1])
    in_grad = fold_step(in_grad_part, tp_steps[-1])
    halves = (firsts, [down_second, gate_second, upper_second])
    (halves, in_grad), (into_ring, expand_ring, output_ring) = beside(
        (halves, in_grad), [into_ring, expand_ring, output_ring]
    )

    def grad_units(kind, start, count):
        return halves[0][kind][start : start + count] + halves[1][kind][start : start + count]

    in_grad = fold(in_grad, tp_steps[:-1]).astype(f32)
    grad_expert_down = jnp.stack(
        [grad_units(0, e * expert_pad, hidden_units) for e in range(EXP_DEV)]
    )
    (in_grad, halves, grad_expert_down), (into_ring, expand_ring) = beside(
        (in_grad, halves, grad_expert_down), [into_ring, expand_ring]
    )

    shared_at = EXP_DEV * expert_pad
    shared_gu_back = lax.all_to_all(
        jnp.stack([grad_units(kind, shared_at, units).T for kind in (1, 2)])
        .astype(bf16)
        .reshape(2, width, 1, units),
        "ep",
        split_axis=1,
        concat_axis=2,
        tiled=True,
    )
    shared_down_back = lax.all_to_all(
        grad_units(0, shared_at, units).astype(bf16),
        "ep",
        split_axis=1,
        concat_axis=0,
        tiled=True,
    )
    input_norm_grad, grad_gain_in = norm_backward(
        in_grad, unit_in[:own], inverse_in[:own], gain_rows[0]
    )
    hidden_own = (resid_grad + input_norm_grad).astype(bf16)
    grad_small = jnp.concatenate(
        [
            jnp.stack([grad_gain_in, grad_gain_mid])
            .reshape(2, groups, -1)
            .transpose(1, 0, 2)
            .reshape(groups, -1),
            gain_latent_part.reshape(groups, -1),
            grad_router.reshape(groups, -1),
        ],
        axis=1,
    )
    small_sum = by_distance(grad_small, group, distances(ep_steps))
    small_sum = fold_step(small_sum, ep_steps[-1])
    hidden_rows = spread(hidden_own[None], tp_steps[:1])
    block_rows = spread(block_own[None], tp_steps[:1])
    (hidden_rows, block_rows, small_sum, halves), (into_ring, expand_ring) = beside(
        (hidden_rows, block_rows, small_sum, halves), [into_ring, expand_ring]
    )
    hidden_rows = by_place(spread(hidden_rows, tp_steps[1:]), part, tp_order)
    block_rows = by_place(spread(block_rows, tp_steps[1:]), part, tp_order)

    grad_expert_gate_up = jnp.stack(
        [
            jnp.stack([grad_units(kind, e * expert_pad, hidden_units).T for kind in (1, 2)])
            for e in range(EXP_DEV)
        ]
    )
    grad_shared_gu_out = shared_gu_back.reshape(shared_gate_up.shape).astype(f32)
    grad_shared_down_out = shared_down_back.astype(f32)
    small_sum = fold(small_sum, ep_steps[:-1])
    into_sum = ring_end(into_ring, "ep")
    grad_expand_out = ring_end(expand_ring, "ep")
    grad_output_out = ring_end(output_ring, "ep").T
    grad_query_out = into_sum[:, :query_size]
    grad_latent_out = into_sum[:, query_size : query_size + latent_width]
    for axis, bit in tp_steps:
        rounded = grad_latent_out.astype(bf16)
        grad_latent_out = rounded.astype(f32) + swap(rounded, axis, bit).astype(f32)
    for axis, bit in tp_steps:
        small_sum = small_sum + swap(small_sum, axis, bit)
    small_sum = small_sum.reshape(-1)
    grad_gains_out = small_sum[: at[1]].reshape(norm_gains.shape)
    grad_gain_latent_out = small_sum[at[1] : at[2]]
    grad_router_out = small_sum[at[2] : at[3]].reshape(router_weight.shape)

    return (
        block_rows.reshape(tokens, width),
        hidden_rows.reshape(tokens, width).astype(f32),
        grad_query_out,
        grad_latent_out,
        grad_expand_out,
        grad_output_out,
        grad_gains_out,
        grad_gain_latent_out,
        grad_router_out,
        grad_shared_gu_out,
        grad_shared_down_out,
        grad_expert_gate_up,
        grad_expert_down,
    )


def power_of_two(size):
    return size & (size - 1) == 0


def on_device(hidden_in, *others):
    groups, parts = lax.axis_size("ep"), lax.axis_size("tp")
    tokens = hidden_in.shape[0]
    mean_load = tokens * TOPK // (EXP_DEV * groups)
    capacity = mean_load + mean_load // 3
    if EXP_DEV * capacity >= tokens and power_of_two(groups) and power_of_two(parts):
        return on_device_dense(hidden_in, *others)
    return on_device_sparse(hidden_in, *others)


def solution(mesh):
    placed = (
        P("ep", None),
        P("ep", None),
        P("ep", "tp"),
        P("ep", None),
        P("ep", "tp"),
        P("tp", "ep"),
        P(None, "ep"),
        P("ep"),
        P("ep", None),
        P(None, "ep", "tp"),
        P("tp", "ep"),
        P("ep", None, None, "tp"),
        P("ep", "tp", None),
        P("ep", None),
    )
    return jax.shard_map(
        on_device,
        mesh=mesh,
        in_specs=placed,
        out_specs=(
            P("ep", None),
            P("ep", None),
            P("ep", "tp"),
            P("ep", None),
            P("ep", "tp"),
            P("tp", "ep"),
            P(None, "ep"),
            P("ep"),
            P("ep", None),
            P(None, "ep", "tp"),
            P("tp", "ep"),
            P("ep", None, None, "tp"),
            P("ep", "tp", None),
        ),
        check_vma=False,
    )
```

```python
import functools
import math

import jax
import jax.numpy as jnp
from jax import lax
from jax.experimental import pallas as pl
from jax.experimental.pallas import tpu as pltpu
from jax.sharding import PartitionSpec as P

NOPE = 128
ROPE = 64
V_DIM = 128
KV_RANK = 512
TOPK = 6
EXP_DEV = 2


EPSILON = 1e-06
ROUTE_SCALE = 2.446
ROPE_BASE = 50000.0


def matmul(left_side, right_side):
    return jnp.dot(left_side, right_side, preferred_element_type=jnp.float32)


def transposed_left(left_side, right_side):
    return lax.dot_general(
        left_side, right_side, (((0,), (0,)), ((), ())), preferred_element_type=jnp.float32
    )


def transposed_right(left_side, right_side):
    return lax.dot_general(
        left_side, right_side, (((1,), (1,)), ((), ())), preferred_element_type=jnp.float32
    )


def rotate(values, cosine_table, sine_table):
    halfway = values.shape[-1] // 2
    first_half = values[..., :halfway]
    second_half = values[..., halfway:]
    return jnp.concatenate(
        [
            first_half * cosine_table - second_half * sine_table,
            second_half * cosine_table + first_half * sine_table,
        ],
        axis=-1,
    )


def norm_forward(values, gain_row):
    inverse = lax.rsqrt(jnp.mean(values * values, axis=-1, keepdims=True) + EPSILON)
    unit_rows = values * inverse
    return (unit_rows * gain_row, unit_rows, inverse)


def norm_backward(incoming, unit_rows, inverse, gain_row):
    scaled = incoming * gain_row
    grad_values = inverse * (
        scaled - unit_rows * jnp.mean(scaled * unit_rows, axis=-1, keepdims=True)
    )
    return (grad_values, jnp.sum(incoming * unit_rows, axis=0))


def on_device_sparse(
    hidden_in,
    out_grad,
    query_weight,
    latent_weight,
    expand_weight,
    output_weight,
    norm_gains,
    latent_gain,
    router_weight,
    shared_gate_up,
    shared_down,
    expert_gate_up,
    expert_down,
    expert_ids,
):
    (
        query_full,
        latent_full,
        expand_full,
        output_full,
        gains_full,
        latent_gain_full,
        router_full,
        shared_gu_full,
        shared_down_full,
    ) = (
        lax.all_gather(query_weight, "ep", axis=0, tiled=True),
        lax.all_gather(latent_weight, "ep", axis=0, tiled=True),
        lax.all_gather(expand_weight, "ep", axis=0, tiled=True),
        lax.all_gather(output_weight, "ep", axis=1, tiled=True),
        lax.all_gather(norm_gains, "ep", axis=1, tiled=True),
        lax.all_gather(latent_gain, "ep", axis=0, tiled=True),
        lax.all_gather(router_weight, "ep", axis=0, tiled=True),
        lax.all_gather(shared_gate_up, "ep", axis=1, tiled=True),
        lax.all_gather(shared_down, "ep", axis=1, tiled=True),
    )
    tokens = hidden_in.shape[0]
    model_width = hidden_in.shape[1]
    heads_local = query_full.shape[1] // (NOPE + ROPE)
    gain_rows = gains_full.astype(jnp.float32)
    gain_latent = latent_gain_full.astype(jnp.float32)
    places = jnp.arange(tokens).astype(jnp.float32)
    frequency = ROPE_BASE ** (-(jnp.arange(ROPE // 2).astype(jnp.float32) * 2.0 / ROPE))
    angles = places[:, None] * frequency[None, :]
    cosine_table = jnp.cos(angles)
    sine_table = jnp.sin(angles)
    resid_in = hidden_in.astype(jnp.float32)
    normed_in, unit_in, inverse_in = norm_forward(resid_in, gain_rows[0])
    normed_low = normed_in.astype(jnp.bfloat16)
    query_raw = matmul(normed_low, query_full).reshape(tokens, heads_local, NOPE + ROPE)
    queries = jnp.concatenate(
        [
            query_raw[..., :NOPE],
            rotate(query_raw[..., NOPE:], cosine_table[:, None, :], sine_table[:, None, :]),
        ],
        axis=-1,
    ).astype(jnp.bfloat16)
    latent = matmul(normed_low, latent_full)
    latent_normed, latent_unit, latent_inverse = norm_forward(latent[:, :KV_RANK], gain_latent)
    latent_low = latent_normed.astype(jnp.bfloat16)
    key_rope = rotate(latent[:, KV_RANK:], cosine_table, sine_table).astype(jnp.bfloat16)
    expanded = (
        matmul(latent_low, expand_full)
        .astype(jnp.bfloat16)
        .reshape(tokens, heads_local, NOPE + V_DIM)
    )
    key_rows = jnp.concatenate(
        [expanded[..., :NOPE], jnp.broadcast_to(key_rope[:, None, :], (tokens, heads_local, ROPE))],
        axis=-1,
    )
    values = expanded[..., NOPE:]
    score_scale = 1.0 / math.sqrt(NOPE + ROPE)
    causal = jnp.arange(tokens)[:, None] >= jnp.arange(tokens)[None, :]

    def attention_scores():
        scores = (
            jnp.einsum("qhd,khd->hqk", queries, key_rows, preferred_element_type=jnp.float32)
            * score_scale
        )
        return jnp.where(causal[None], scores, -1e30)

    scores_first = attention_scores()
    row_max = jnp.max(scores_first, axis=-1, keepdims=True)
    log_total = row_max + jnp.log(jnp.sum(jnp.exp(scores_first - row_max), axis=-1, keepdims=True))
    probs_low = jnp.exp(scores_first - log_total).astype(jnp.bfloat16)
    attended = jnp.einsum("hqk,khd->qhd", probs_low, values, preferred_element_type=jnp.float32)
    attended = attended.astype(jnp.bfloat16).reshape(tokens, heads_local * V_DIM)
    attn_out = lax.psum(matmul(attended, output_full), "tp")
    resid = resid_in + attn_out
    normed_mid, unit_mid, inverse_mid = norm_forward(resid, gain_rows[1])
    mid_low = normed_mid.astype(jnp.bfloat16)
    logits = matmul(mid_low, router_full)
    experts = router_full.shape[1]
    route_mask = (expert_ids[:, :, None] == jnp.arange(experts)[None, None, :]).astype(jnp.float32)
    chosen = jnp.sum(route_mask * logits[:, None, :], axis=2)
    sigmoids = jax.nn.sigmoid(chosen)
    sigmoid_total = jnp.sum(sigmoids, axis=1, keepdims=True)
    gating = ROUTE_SCALE * sigmoids / sigmoid_total
    shared_gate = matmul(mid_low, shared_gu_full[0])
    shared_upper = matmul(mid_low, shared_gu_full[1])
    shared_sig = jax.nn.sigmoid(shared_gate)
    shared_hidden = (shared_gate * shared_sig * shared_upper).astype(jnp.bfloat16)
    shared_part = matmul(shared_hidden, shared_down_full)
    groups = lax.axis_size("ep")
    mean_load = tokens * TOPK // (EXP_DEV * groups)
    capacity = mean_load + mean_load // 3
    choices = tokens * TOPK
    rows_total = groups * capacity
    flat_ids = expert_ids.reshape(-1)
    onehot = (flat_ids[:, None] == jnp.arange(experts)[None, :]).astype(jnp.int32)
    slot_of = jnp.sum((jnp.cumsum(onehot, axis=0) - onehot) * onehot, axis=1)
    target = flat_ids % EXP_DEV * rows_total + flat_ids // EXP_DEV * capacity + slot_of
    slot_table = (
        jnp.full((EXP_DEV * rows_total,), choices, jnp.int32)
        .at[target]
        .set(jnp.arange(choices, dtype=jnp.int32))
        .reshape(EXP_DEV, groups, capacity)
    )
    mid_padded = jnp.concatenate([mid_low, jnp.zeros((1, model_width), jnp.bfloat16)], axis=0)
    outgoing = mid_padded[slot_table.reshape(-1) // TOPK].reshape(EXP_DEV, rows_total, model_width)
    expert_rows = lax.all_to_all(outgoing, "ep", split_axis=1, concat_axis=1, tiled=True)
    expert_gate = jnp.einsum(
        "erd,edf->erf", expert_rows, expert_gate_up[:, 0], preferred_element_type=jnp.float32
    )
    expert_upper = jnp.einsum(
        "erd,edf->erf", expert_rows, expert_gate_up[:, 1], preferred_element_type=jnp.float32
    )
    expert_sig = jax.nn.sigmoid(expert_gate)
    expert_hidden = (expert_gate * expert_sig * expert_upper).astype(jnp.bfloat16)
    expert_part = jnp.einsum(
        "erf,efd->erd", expert_hidden, expert_down, preferred_element_type=jnp.float32
    ).astype(jnp.bfloat16)
    returned = lax.all_to_all(expert_part, "ep", split_axis=1, concat_axis=1, tiled=True)
    per_choice = (
        returned.reshape(-1, model_width)[target]
        .reshape(tokens, TOPK, model_width)
        .astype(jnp.float32)
    )
    routed_part = jnp.sum(gating[:, :, None] * per_choice, axis=1)
    moe_out = lax.psum((shared_part + routed_part).astype(jnp.bfloat16), "tp").astype(jnp.float32)
    block_out = (resid + moe_out).astype(jnp.bfloat16)
    grad_top = out_grad.astype(jnp.float32)
    choice_grad = (gating[:, :, None] * grad_top[:, None, :]).astype(jnp.bfloat16)
    grad_padded = jnp.concatenate(
        [choice_grad.reshape(choices, model_width), jnp.zeros((1, model_width), jnp.bfloat16)],
        axis=0,
    )
    outgoing_grad = grad_padded[slot_table.reshape(-1)].reshape(EXP_DEV, rows_total, model_width)
    rows_grad = lax.all_to_all(outgoing_grad, "ep", split_axis=1, concat_axis=1, tiled=True)
    hidden_grad = jnp.einsum(
        "erd,efd->erf", rows_grad, expert_down, preferred_element_type=jnp.float32
    )
    gate_grad = (
        hidden_grad * expert_upper * expert_sig * (1.0 + expert_gate * (1.0 - expert_sig))
    ).astype(jnp.bfloat16)
    upper_grad = (hidden_grad * expert_gate * expert_sig).astype(jnp.bfloat16)
    grad_expert_down = jnp.einsum(
        "erf,erd->efd", expert_hidden, rows_grad, preferred_element_type=jnp.float32
    )
    grad_expert_gate_up = jnp.stack(
        [
            jnp.einsum("erd,erf->edf", expert_rows, gate_grad, preferred_element_type=jnp.float32),
            jnp.einsum("erd,erf->edf", expert_rows, upper_grad, preferred_element_type=jnp.float32),
        ],
        axis=1,
    )
    row_back = jnp.einsum(
        "erf,edf->erd", gate_grad, expert_gate_up[:, 0], preferred_element_type=jnp.float32
    ) + jnp.einsum(
        "erf,edf->erd", upper_grad, expert_gate_up[:, 1], preferred_element_type=jnp.float32
    )
    row_back_low = row_back.astype(jnp.bfloat16)
    back_rows = lax.all_to_all(row_back_low, "ep", split_axis=1, concat_axis=1, tiled=True)
    choice_back = (
        back_rows.reshape(-1, model_width)[target]
        .reshape(tokens, TOPK, model_width)
        .astype(jnp.float32)
    )
    mid_grad_routed = jnp.sum(choice_back, axis=1)
    gating_grad_part = jnp.sum(per_choice * grad_top[:, None, :], axis=2)
    shared_hidden_grad = transposed_right(out_grad, shared_down_full)
    shared_gate_grad = (
        shared_hidden_grad * shared_upper * shared_sig * (1.0 + shared_gate * (1.0 - shared_sig))
    ).astype(jnp.bfloat16)
    shared_upper_grad = (shared_hidden_grad * shared_gate * shared_sig).astype(jnp.bfloat16)
    grad_shared_down = transposed_left(shared_hidden, out_grad)
    grad_shared_gu = jnp.stack(
        [transposed_left(mid_low, shared_gate_grad), transposed_left(mid_low, shared_upper_grad)],
        axis=0,
    )
    mid_grad_shared = transposed_right(shared_gate_grad, shared_gu_full[0]) + transposed_right(
        shared_upper_grad, shared_gu_full[1]
    )
    mid_grad_sum, gating_grad = (
        lax.psum((mid_grad_routed + mid_grad_shared).astype(jnp.bfloat16), "tp").astype(
            jnp.float32
        ),
        lax.psum(gating_grad_part.astype(jnp.bfloat16), "tp").astype(jnp.float32),
    )
    weighted = jnp.sum(gating_grad * sigmoids, axis=1, keepdims=True) / sigmoid_total
    sigmoid_grad = ROUTE_SCALE / sigmoid_total * (gating_grad - weighted)
    chosen_grad = sigmoid_grad * sigmoids * (1.0 - sigmoids)
    logits_grad = jnp.sum(route_mask * chosen_grad[:, :, None], axis=1).astype(jnp.bfloat16)
    grad_router = transposed_left(mid_low, logits_grad)
    mid_grad = mid_grad_sum + transposed_right(logits_grad, router_full)
    resid_norm_grad, grad_gain_mid = norm_backward(mid_grad, unit_mid, inverse_mid, gain_rows[1])
    resid_grad = grad_top + resid_norm_grad
    attn_grad = resid_grad.astype(jnp.bfloat16)
    grad_output = transposed_left(attended, attn_grad)
    attended_grad = (
        transposed_right(attn_grad, output_full)
        .astype(jnp.bfloat16)
        .reshape(tokens, heads_local, V_DIM)
    )
    softmax_probs = jnp.exp(attention_scores() - log_total)
    values_grad = jnp.einsum(
        "hqk,qhd->khd",
        softmax_probs.astype(jnp.bfloat16),
        attended_grad,
        preferred_element_type=jnp.float32,
    )
    probs_grad = jnp.einsum(
        "qhd,khd->hqk", attended_grad, values, preferred_element_type=jnp.float32
    )
    scores_grad = (
        softmax_probs * (probs_grad - jnp.sum(softmax_probs * probs_grad, axis=-1, keepdims=True))
    ).astype(jnp.bfloat16)
    query_grad = (
        jnp.einsum("hqk,khd->qhd", scores_grad, key_rows, preferred_element_type=jnp.float32)
        * score_scale
    )
    keys_grad = (
        jnp.einsum("hqk,qhd->khd", scores_grad, queries, preferred_element_type=jnp.float32)
        * score_scale
    )
    query_raw_grad = (
        jnp.concatenate(
            [
                query_grad[..., :NOPE],
                rotate(query_grad[..., NOPE:], cosine_table[:, None, :], -sine_table[:, None, :]),
            ],
            axis=-1,
        )
        .astype(jnp.bfloat16)
        .reshape(tokens, heads_local * (NOPE + ROPE))
    )
    expanded_grad = jnp.concatenate([keys_grad[..., :NOPE], values_grad], axis=-1).astype(
        jnp.bfloat16
    )
    expanded_grad = expanded_grad.reshape(tokens, heads_local * (NOPE + V_DIM))
    grad_expand = transposed_left(latent_low, expanded_grad)
    latent_normed_grad = transposed_right(expanded_grad, expand_full)
    latent_part_grad, gain_latent_part = norm_backward(
        latent_normed_grad, latent_unit, latent_inverse, gain_latent
    )
    rope_raw_grad = rotate(jnp.sum(keys_grad[..., NOPE:], axis=1), cosine_table, -sine_table)
    latent_grad_part = jnp.concatenate([latent_part_grad, rope_raw_grad], axis=1)
    in_grad_query = transposed_right(query_raw_grad, query_full)
    in_grad_sum, latent_grad, grad_gain_latent = (
        lax.psum(in_grad_query.astype(jnp.bfloat16), "tp").astype(jnp.float32),
        lax.psum(latent_grad_part.astype(jnp.bfloat16), "tp").astype(jnp.float32),
        lax.psum(gain_latent_part.astype(jnp.bfloat16), "tp").astype(jnp.float32),
    )
    latent_grad_low = latent_grad.astype(jnp.bfloat16)
    grad_latent = transposed_left(normed_low, latent_grad_low)
    grad_query = transposed_left(normed_low, query_raw_grad)
    in_grad = in_grad_sum + transposed_right(latent_grad_low, latent_full)
    input_norm_grad, grad_gain_in = norm_backward(in_grad, unit_in, inverse_in, gain_rows[0])
    grad_hidden = resid_grad + input_norm_grad
    grad_gains = jnp.stack([grad_gain_in, grad_gain_mid], axis=0)
    (
        grad_query_out,
        grad_latent_out,
        grad_expand_out,
        grad_output_out,
        grad_gains_out,
        grad_gain_latent_out,
        grad_router_out,
        grad_shared_gu_out,
        grad_shared_down_out,
    ) = (
        lax.psum_scatter(
            grad_query.astype(jnp.bfloat16), "ep", scatter_dimension=0, tiled=True
        ).astype(jnp.float32),
        lax.psum_scatter(
            grad_latent.astype(jnp.bfloat16), "ep", scatter_dimension=0, tiled=True
        ).astype(jnp.float32),
        lax.psum_scatter(
            grad_expand.astype(jnp.bfloat16), "ep", scatter_dimension=0, tiled=True
        ).astype(jnp.float32),
        lax.psum_scatter(
            grad_output.astype(jnp.bfloat16), "ep", scatter_dimension=1, tiled=True
        ).astype(jnp.float32),
        lax.psum_scatter(
            grad_gains.astype(jnp.bfloat16), "ep", scatter_dimension=1, tiled=True
        ).astype(jnp.float32),
        lax.psum_scatter(
            grad_gain_latent.astype(jnp.bfloat16), "ep", scatter_dimension=0, tiled=True
        ).astype(jnp.float32),
        lax.psum_scatter(
            grad_router.astype(jnp.bfloat16), "ep", scatter_dimension=0, tiled=True
        ).astype(jnp.float32),
        lax.psum_scatter(
            grad_shared_gu.astype(jnp.bfloat16), "ep", scatter_dimension=1, tiled=True
        ).astype(jnp.float32),
        lax.psum_scatter(
            grad_shared_down.astype(jnp.bfloat16), "ep", scatter_dimension=1, tiled=True
        ).astype(jnp.float32),
    )
    return (
        block_out,
        grad_hidden,
        grad_query_out,
        grad_latent_out,
        grad_expand_out,
        grad_output_out,
        grad_gains_out,
        grad_gain_latent_out,
        grad_router_out,
        grad_shared_gu_out,
        grad_shared_down_out,
        grad_expert_gate_up,
        grad_expert_down,
    )


CUTS = 4
GATHERS = 2
LANES = 128
VMEM_BYTES = 56 * 1024 * 1024


def swap(array, axis, bit):
    size = lax.axis_size(axis)
    return lax.ppermute(array, axis, [(place, place ^ bit) for place in range(size)])


def axis_bits(axis):
    size = lax.axis_size(axis)
    return [(axis, 1 << bit) for bit in reversed(range(size.bit_length() - 1))]


def spread(rows, steps):
    for axis, bit in steps:
        rows = jnp.concatenate([rows, swap(rows, axis, bit)], axis=0)
    return rows


def add_rounded(left_side, right_side):
    return (left_side.astype(jnp.float32) + right_side.astype(jnp.float32)).astype(
        left_side.dtype
    )


def fold_step(rows, step):
    axis, bit = step
    half = rows.shape[0] // 2
    return add_rounded(rows[:half], swap(rows[half:], axis, bit))


def fold(rows, steps):
    for step in reversed(steps):
        rows = fold_step(rows, step)
    return rows


def distances(steps):
    found = [0]
    for _, bit in steps:
        found = found + [distance + bit for distance in found]
    return found


def by_distance(blocks, place, order):
    return jnp.concatenate(
        [lax.dynamic_slice_in_dim(blocks, place ^ i, 1, axis=0) for i in order], axis=0
    )


def by_place(blocks, place, order):
    natural = jnp.concatenate([blocks[order.index(i)][None] for i in range(len(order))], axis=0)
    return by_distance(natural, place, range(len(order)))


def ring_owner(spot, size):
    return jnp.where(spot < size // 2, 2 * spot, 2 * (size - 1 - spot) + 1)


def ring_spot(place, size):
    return jnp.where(place % 2 == 0, place // 2, size - 1 - place // 2)


def ring_shift(array, axis, by):
    size = lax.axis_size(axis)
    ring = [2 * i for i in range(size // 2)] + [2 * i + 1 for i in reversed(range(size // 2))]
    return lax.ppermute(array, axis, [(ring[i], ring[(i + by) % size]) for i in range(size)])


def ring_gather(arrays, axis, beside):
    size = lax.axis_size(axis)
    found = [[array] + [None] * (size - 1) for array in arrays]
    ahead, behind, others, rounds = arrays, arrays, [], []
    for k in range(1, size // 2 + 1):
        behind = [ring_shift(array, axis, 1) for array in behind]
        if k < size - k:
            ahead = [ring_shift(array, axis, -1) for array in ahead]
        other = beside[k - 1](others) if k <= len(beside) else None
        behind, ahead, other = lax.optimization_barrier((behind, ahead, other))
        others.append(other)
        rounds.append(behind)
        for pieces, before, after in zip(found, behind, ahead):
            pieces[size - k] = before
            if k < size - k:
                pieces[k] = after
    return found, others, rounds


def ring_begin(parts, axis):
    size = lax.axis_size(axis)
    half = size // 2
    left = [(parts[half - k], parts[half + 1 + k] if k < half - 1 else None) for k in range(1, half)]
    return (parts[half], parts[half + 1]), left + [(parts[0], None)]


def ring_round(ring, axis):
    (ahead, behind), left = ring
    more_ahead, more_behind = left[0]
    ahead = add_rounded(ring_shift(ahead, axis, 1), more_ahead)
    if behind is not None and len(left) > 1:
        behind = ring_shift(behind, axis, -1)
        if more_behind is not None:
            behind = add_rounded(behind, more_behind)
    return (ahead, behind), left[1:]


def ring_end(ring, axis):
    (ahead, behind), left = ring
    while left:
        if len(left) == 1:
            found = ring_shift(ahead, axis, 1).astype(jnp.float32) + left[0][0]
            return found + behind
        (ahead, behind), left = ring_round(((ahead, behind), left), axis)
    return ahead.astype(jnp.float32) + behind


def pad_columns(array, width):
    return jnp.pad(array, ((0, 0), (0, width - array.shape[1])))


def pad_rows(array, height):
    return jnp.pad(array, ((0, height - array.shape[0]), (0, 0)))


def round_up(size, step=LANES):
    return -(-size // step) * step


def feed_forward_kernel(count, wide_steps, sub, *refs):
    first_ref, slot_ref, rows_ref, raw_ref, mask_ref, router_ref, tiles_ref = refs[:7]
    back_out, gate_ref, upper_ref, hidden_ref = refs[7:11]
    gains, shares, kept, tiles, back_ref, arrived, back_left = refs[11:]
    cut, step, last = pl.program_id(0), pl.program_id(1), count + wide_steps - 1
    owners, _, each, width = rows_ref.shape
    half, rows = raw_ref.shape[3], owners * each
    block = sub // each
    f32, bf16 = jnp.float32, jnp.bfloat16

    def arrival(n):
        return pltpu.make_async_copy(tiles_ref.at[n], tiles.at[n], arrived.at[n])

    def back_leaving(n):
        size = width // wide_steps
        extra = back_ref.shape[2] - width if n == wide_steps - 1 else 0
        of = (slice(None), slice(None), pl.ds(n * size, size + extra))
        return pltpu.make_async_copy(back_ref.at[of], back_out.at[(cut, *of)], back_left.at[n])

    @pl.when(step == 0)
    def _():
        @pl.when(cut == 0)
        def _():
            for n in range(count):
                arrival(n).start()

        values = rows_ref[...].reshape(rows, width)
        logits = jnp.dot(values, router_ref[...], preferred_element_type=f32)
        sig = jax.nn.sigmoid(logits) * mask_ref[...].reshape(logits.shape)
        gating = ROUTE_SCALE * sig / jnp.sum(sig, axis=1, keepdims=True)
        lanes = lax.broadcasted_iota(jnp.int32, gating.shape, 1)
        for e in range(EXP_DEV):
            own = jnp.sum(jnp.where(lanes == first_ref[0] + e, gating, 0.0), axis=1, keepdims=True)
            gains[e] = jnp.broadcast_to(own, gains.shape[1:])
        gains[EXP_DEV] = jnp.ones(gains.shape[1:], f32)
        shares[...] = jnp.zeros_like(shares)

    @pl.when(step < count)
    def _():
        @pl.when(cut == 0)
        def _():
            arrival(step).wait()

        kind = jnp.minimum(step // ((count - 1) // EXP_DEV), EXP_DEV)
        for i in range(rows // sub):
            at, of = pl.ds(i * sub, sub), pl.ds(i * block, block)
            values = rows_ref[of].reshape(sub, width)
            both = lax.dot_general(
                values, tiles[step], (((1,), (1,)), ((), ())), preferred_element_type=f32
            )
            gate, upper = both[:, :half], both[:, half:]
            gain, raw = gains[kind, at, :], raw_ref[of].reshape(sub, half).astype(f32)
            sig = jax.nn.sigmoid(gate)
            silu = gate * sig
            hidden = silu * upper
            grad = gain * raw
            shape = (block, 1, each, half)
            hidden_ref[of] = (gain * hidden).astype(bf16).reshape(shape)
            shares[kind, at, :] += hidden * raw
            gate_grad = (grad * upper * (sig + silu * (1.0 - sig))).astype(bf16)
            upper_grad = (grad * silu).astype(bf16)
            gate_ref[of] = gate_grad.reshape(shape)
            upper_ref[of] = upper_grad.reshape(shape)
            kept[step, at, :half] = gate_grad
            kept[step, at, half:] = upper_grad

    @pl.when(step >= count)
    def _():
        size = width // wide_steps
        columns = pl.ds(pl.multiple_of((step - count) * size, size), size)
        for i in range(rows // sub):
            found = sum(
                jnp.dot(
                    kept[n, pl.ds(i * sub, sub), :],
                    tiles[n, :, columns],
                    preferred_element_type=f32,
                )
                for n in range(count)
            ).astype(bf16)
            for j in range(block):
                part = found[j * each : (j + 1) * each]
                back_ref[slot_ref[cut, i * block + j], :, columns] = part

    @pl.when(step == last)
    def _():
        extra = back_ref.shape[2] - width
        lanes = lax.broadcasted_iota(jnp.int32, (rows, extra), 1)
        gating_grad = jnp.zeros(lanes.shape, f32)
        for e in range(EXP_DEV):
            own = jnp.sum(shares[e], axis=1, keepdims=True)
            gating_grad += jnp.where(lanes == first_ref[0] + e, own, 0.0)
        gating_grad = gating_grad.astype(bf16)
        for i in range(owners):
            back_ref[slot_ref[cut, i], :, width:] = gating_grad[i * each : (i + 1) * each]

    for n in range(wide_steps):

        @pl.when(step == count + n)
        def _(n=n):
            back_leaving(n).start()

    @pl.when(step == last)
    def _():
        for n in range(wide_steps):
            back_leaving(n).wait()


def feed_forward(slots, mid_rows, raw_grad, mask, router, tiles, first):
    count, both, width = tiles.shape
    owners, cuts, each, experts = mask.shape
    rows, half, wide_steps = owners * each, both // 2, 4
    bf16, f32 = jnp.bfloat16, jnp.float32

    def tile(step):
        return jnp.minimum(step, count - 1)

    smem, whole = pl.BlockSpec(memory_space=pltpu.SMEM), pl.BlockSpec(memory_space=pl.ANY)
    side = pl.BlockSpec((owners, 1, each, half), lambda c, i: (0, c, 0, tile(i)))
    return pl.pallas_call(
        functools.partial(feed_forward_kernel, count, wide_steps, min(8, owners) * each),
        grid=(cuts, count + wide_steps),
        in_specs=[
            smem,
            smem,
            pl.BlockSpec((owners, 1, each, width), lambda c, i: (0, c, 0, 0)),
            side,
            pl.BlockSpec((owners, 1, each, experts), lambda c, i: (0, c, 0, 0)),
            pl.BlockSpec((width, experts), lambda c, i: (0, 0)),
            whole,
        ],
        out_specs=[whole, side, side, side],
        out_shape=[
            jax.ShapeDtypeStruct((cuts, owners, each, width + LANES), bf16),
            *[jax.ShapeDtypeStruct((owners, cuts, each, count * half), bf16)] * 3,
        ],
        scratch_shapes=[
            pltpu.VMEM((EXP_DEV + 1, rows, half), f32),
            pltpu.VMEM((EXP_DEV + 1, rows, half), f32),
            pltpu.VMEM((count, rows, both), bf16),
            pltpu.VMEM(tiles.shape, bf16),
            pltpu.VMEM((owners, each, width + LANES), bf16),
            pltpu.SemaphoreType.DMA((count,)),
            pltpu.SemaphoreType.DMA((wide_steps,)),
        ],
        compiler_params=pltpu.CompilerParams(vmem_limit_bytes=VMEM_BYTES),
        cost_estimate=pl.CostEstimate(
            flops=4 * cuts * rows * width * both * count,
            bytes_accessed=50_000_000,
            transcendentals=0,
        ),
    )(first, slots, mid_rows, raw_grad, mask, router, tiles)


def rows_by_device_kernel(*refs):
    *left_refs, right_ref, out_ref = refs
    for i, left_ref in enumerate(left_refs):

        @pl.when(pl.program_id(1) == i)
        def _(left_ref=left_ref):
            found = jnp.dot(left_ref[...], right_ref[...], preferred_element_type=jnp.float32)
            out_ref[...] = found.astype(out_ref.dtype).reshape(out_ref.shape)


def rows_by_device(left_parts, right_side, devices):
    rows, depth = left_parts[0].shape
    columns, count = right_side.shape[1], len(left_parts)
    wide = columns // 2
    return pl.pallas_call(
        rows_by_device_kernel,
        grid=(2, count),
        in_specs=[pl.BlockSpec((rows, depth), lambda j, i: (0, 0))] * count
        + [pl.BlockSpec((depth, wide), lambda j, i: (0, j))],
        out_specs=pl.BlockSpec((devices, 1, rows // devices, wide), lambda j, i: (0, i, 0, j)),
        out_shape=jax.ShapeDtypeStruct(
            (devices, count, rows // devices, columns), right_side.dtype
        ),
        compiler_params=pltpu.CompilerParams(vmem_limit_bytes=VMEM_BYTES),
        cost_estimate=pl.CostEstimate(
            flops=2 * count * rows * depth * columns,
            bytes_accessed=2 * count * rows * (depth + columns),
            transcendentals=0,
        ),
    )(*left_parts, right_side).reshape(count * rows, columns)


def place_kernel(places_ref, *refs):
    *pieces, out_ref = refs
    for i, piece in enumerate(pieces):

        @pl.when(pl.program_id(0) == i)
        def _(piece=piece):
            out_ref[0] = piece[...]


def place_blocks(pieces, places):
    shape = pieces[0].shape
    return pl.pallas_call(
        place_kernel,
        grid_spec=pltpu.PrefetchScalarGridSpec(
            num_scalar_prefetch=1,
            grid=(len(pieces),),
            in_specs=[pl.BlockSpec(shape, lambda i, at: (0, 0))] * len(pieces),
            out_specs=pl.BlockSpec((1, *shape), lambda i, at: (at[i], 0, 0)),
        ),
        out_shape=jax.ShapeDtypeStruct((len(pieces), *shape), pieces[0].dtype),
        compiler_params=pltpu.CompilerParams(vmem_limit_bytes=VMEM_BYTES),
    )(jnp.stack(places).astype(jnp.int32), *pieces)


def on_device_dense(
    hidden_in,
    out_grad,
    query_weight,
    latent_weight,
    expand_weight,
    output_weight,
    norm_gains,
    latent_gain,
    router_weight,
    shared_gate_up,
    shared_down,
    expert_gate_up,
    expert_down,
    expert_ids,
):
    groups, parts = lax.axis_size("ep"), lax.axis_size("tp")
    group, part = lax.axis_index("ep"), lax.axis_index("tp")
    tokens, width = hidden_in.shape
    own = tokens // parts
    experts = router_weight.shape[1]
    bf16, f32 = jnp.bfloat16, jnp.float32
    ep_steps, tp_steps = axis_bits("ep"), axis_bits("tp")
    tp_order = distances(tp_steps)
    every = ("ep", "tp")
    devices = groups * parts
    cut_rows = own // CUTS

    spot = ring_spot(group, groups)
    ring_groups = [ring_owner((spot + k) % groups, groups) for k in range(groups)]

    mask_own = jnp.sum(
        (expert_ids[:, :, None] == jnp.arange(experts)[None, None, :]).astype(bf16), axis=1
    )
    sizes = [norm_gains.size, latent_gain.size, router_weight.size, mask_own.size]
    small = jnp.concatenate(
        [array.reshape(1, -1) for array in (norm_gains, latent_gain, router_weight, mask_own)],
        axis=1,
    )
    query_size, latent_width = query_weight.shape[1], latent_weight.shape[1]
    output_size = output_weight.shape[0]
    into_size = round_up(query_size + latent_width)
    into = pad_columns(jnp.concatenate([query_weight, latent_weight], axis=1), into_size)
    out_of = jnp.concatenate(
        [output_weight.T, expand_weight.reshape(output_weight.shape[1], -1)], axis=1
    )

    units = shared_down.shape[0] // groups

    hidden_units = expert_down.shape[1]
    expert_pad, shared_pad = round_up(hidden_units), round_up(units)

    def dense_weights(shared_gu_own, shared_down_own, expert_gate_up, expert_down):
        side_weights = [
            jnp.concatenate(
                [pad_rows(expert_gate_up[e, side].T, expert_pad) for e in range(EXP_DEV)]
                + [pad_rows(shared_gu_own[side].T, shared_pad)],
                axis=0,
            ).reshape(-1, LANES, width)
            for side in range(2)
        ]
        tiles = jnp.concatenate(side_weights, axis=1)
        down_weight = jnp.concatenate(
            [pad_rows(expert_down[e], expert_pad) for e in range(EXP_DEV)]
            + [pad_rows(shared_down_own, shared_pad)],
            axis=0,
        )
        return tiles, down_weight

    (into_pieces, out_of_pieces), others, rounds = ring_gather(
        [into, out_of],
        "ep",
        [
            lambda _: spread(small, ep_steps[:1]),
            lambda done: spread(done[0], ep_steps[1:2]),
            lambda done: spread(done[1], ep_steps[2:]),
        ],
    )
    shared_gate_up_late, shared_down_late, _ = lax.optimization_barrier(
        (shared_gate_up, shared_down, rounds[-1])
    )
    shared_gu_own = lax.all_to_all(
        shared_gate_up_late.reshape(2, -1, groups, units), "ep", split_axis=2, concat_axis=1, tiled=True
    ).reshape(2, width, units)
    shared_down_own = lax.all_to_all(shared_down_late, "ep", split_axis=0, concat_axis=1, tiled=True)


    small_rel = others[2]
    at = [sum(sizes[:i]) for i in range(len(sizes) + 1)]
    small_full = by_place(small_rel, group, distances(ep_steps))
    gain_rows = (
        small_full[:, : at[1]].reshape(groups, 2, -1).transpose(1, 0, 2).reshape(2, width)
    ).astype(f32)
    gain_latent = small_full[:, at[1] : at[2]].reshape(-1).astype(f32)
    router_full = small_full[:, at[2] : at[3]].reshape(width, experts)

    into_full = place_blocks(into_pieces, ring_groups).reshape(width, -1)
    out_of_full = place_blocks(out_of_pieces, ring_groups).reshape(width, -1)
    expand_full = out_of_full[:, output_size:].reshape(KV_RANK, -1)
    output_turned = out_of_full[:, :output_size]

    out_grad_late, _ = lax.optimization_barrier((out_grad, rounds[-2][0]))

    gather_rows = own // GATHERS
    cuts = CUTS // GATHERS

    def by_gather(rows):
        rows = rows.reshape(devices, GATHERS, gather_rows, -1).transpose(1, 0, 2, 3)
        return list(rows.reshape(GATHERS, devices * gather_rows, -1))

    grad_own = lax.dynamic_slice_in_dim(out_grad_late, part * own, own, axis=0)
    grad_parts = by_gather(lax.all_gather(grad_own, every, axis=0, tiled=True))
    mask_parts = [
        rows.astype(f32).reshape(devices, cuts, cut_rows, experts)
        for rows in by_gather(small_full[:, at[3] :])
    ]

    row_blocks = hidden_in.reshape(parts, own, width)
    hidden_rel = by_distance(row_blocks, part, tp_order).reshape(tokens, width)
    heads_local = query_size // (NOPE + ROPE)
    places = ((part ^ jnp.array(tp_order))[:, None] * own + jnp.arange(own)[None, :]).reshape(-1)
    frequency = ROPE_BASE ** (-(jnp.arange(ROPE // 2).astype(f32) * 2.0 / ROPE))
    angles = places.astype(f32)[:, None] * frequency[None, :]
    cosine_table = jnp.cos(angles)
    sine_table = jnp.sin(angles)
    normed_in, unit_in, inverse_in = norm_forward(hidden_rel.astype(f32), gain_rows[0])
    normed_low = normed_in.astype(bf16)
    both_in = matmul(normed_low, into_full)
    query_raw = both_in[:, :query_size].reshape(tokens, heads_local, NOPE + ROPE)
    queries = jnp.concatenate(
        [
            query_raw[..., :NOPE],
            rotate(query_raw[..., NOPE:], cosine_table[:, None, :], sine_table[:, None, :]),
        ],
        axis=-1,
    ).astype(bf16)
    latent = both_in[:, query_size : query_size + latent_width]
    latent_normed, latent_unit, latent_inverse = norm_forward(latent[:, :KV_RANK], gain_latent)
    latent_low = latent_normed.astype(bf16)
    key_rope = rotate(latent[:, KV_RANK:], cosine_table, sine_table).astype(bf16)
    expanded = (
        matmul(latent_low, expand_full).astype(bf16).reshape(tokens, heads_local, NOPE + V_DIM)
    )
    key_rows = jnp.concatenate(
        [expanded[..., :NOPE], jnp.broadcast_to(key_rope[:, None, :], (tokens, heads_local, ROPE))],
        axis=-1,
    )
    values = expanded[..., NOPE:]
    score_scale = 1.0 / math.sqrt(NOPE + ROPE)
    causal = places[:, None] >= places[None, :]
    scores = (
        jnp.einsum("qhd,khd->hqk", queries, key_rows, preferred_element_type=f32) * score_scale
    )
    scores = jnp.where(causal[None], scores, -1e30)
    row_max = jnp.max(scores, axis=-1, keepdims=True)
    powers = jnp.exp(scores - row_max)
    softmax_probs = powers / jnp.sum(powers, axis=-1, keepdims=True)
    probs_low = softmax_probs.astype(bf16)
    attended = jnp.einsum("hqk,khd->qhd", probs_low, values, preferred_element_type=f32)
    attended = attended.astype(bf16).reshape(tokens, heads_local * V_DIM)
    attn_part = transposed_right(attended, output_turned).astype(bf16)
    resid = hidden_rel[:own].astype(f32) + fold(attn_part, tp_steps).astype(f32)

    normed_mid, unit_mid, inverse_mid = norm_forward(resid, gain_rows[1])
    mid_own, expert_gate_up, expert_down = lax.optimization_barrier(
        (normed_mid.astype(bf16), expert_gate_up, expert_down)
    )
    tiles, down_weight = dense_weights(
        shared_gu_own, shared_down_own, expert_gate_up, expert_down
    )
    raw_parts = [
        transposed_right(rows, down_weight).astype(bf16).reshape(devices, cuts, cut_rows, -1)
        for rows in grad_parts
    ]
    first = (group * EXP_DEV).astype(jnp.int32).reshape(1)
    mid_parts = [
        lax.all_gather(
            mid_own[i * gather_rows : (i + 1) * gather_rows], every, axis=0, tiled=True
        )
        for i in range(GATHERS)
    ]
    one_order = (ep_steps + tp_steps)[::-1]
    turn = [0, *range(2, len(tp_steps) + 1), 1, *range(len(tp_steps) + 1, len(one_order))]
    orders = [one_order, [one_order[i] for i in turn]]
    distance = jnp.arange(devices, dtype=jnp.int32) ^ (group * parts + part)
    slots = []
    for order in orders:
        slot = jnp.zeros_like(distance)
        for axis, bit in order:
            slot = 2 * slot + distance // (bit * (parts if axis == "ep" else 1)) % 2
        slots.append(slot)
    slots = jnp.stack([slots[cut % 2] for cut in range(cuts)])

    def on_a_step(sums):
        return [(fold_step(rows, todo[0]), todo[1:]) if todo else (rows, todo) for rows, todo in sums]

    def together(work, sums):
        work, rows = lax.optimization_barrier((work, [rows for rows, _ in sums]))
        return work, [(each, todo) for each, (_, todo) in zip(rows, sums)]

    mid_parts[0], raw_parts = lax.optimization_barrier((mid_parts[0], raw_parts))
    sums, gate_parts, upper_parts, hidden_parts = [], [], [], []
    for i in range(GATHERS):
        mid_rows = mid_parts[i]
        back, *sides = feed_forward(
            slots,
            mid_rows.reshape(devices, cuts, cut_rows, width),
            raw_parts[i],
            mask_parts[i],
            router_full,
            tiles,
            first,
        )
        (back, sides), sums = together((back, sides), on_a_step(sums))
        sums += [(back[cut], orders[cut % 2]) for cut in range(cuts)]
        for parts_of, side in zip((gate_parts, upper_parts, hidden_parts), sides):
            parts_of.append(side.reshape(mid_rows.shape[0], -1))
        if i == 0:
            firsts = [
                transposed_left(parts_of[0], rows[0])
                for parts_of, rows in ((hidden_parts, grad_parts), (gate_parts, mid_parts))
            ]
            (firsts, mid_parts[1:]), sums = together((firsts, mid_parts[1:]), on_a_step(sums))
    firsts.append(transposed_left(upper_parts[0], mid_parts[0]))
    (firsts, hidden_parts), sums = together((firsts, hidden_parts), on_a_step(sums))
    out_part = rows_by_device(hidden_parts, down_weight, devices)
    for _ in range(2):
        out_part, sums = together(out_part, on_a_step(sums))
    out_own = lax.psum_scatter(out_part, every, scatter_dimension=0, tiled=True)
    block_own = (lax.optimization_barrier(resid) + out_own.astype(f32)).astype(bf16)
    while any(todo for _, todo in sums):
        sums = on_a_step(sums)
    back_own = jnp.concatenate([rows[0] for rows, _ in sums], axis=0)

    back_own = back_own.astype(f32)
    gating_grad = back_own[:, width : width + experts]
    mask = lax.dynamic_slice_in_dim(mask_own, part * own, own, axis=0).astype(f32)
    sigmoids = jax.nn.sigmoid(matmul(mid_own, router_full))
    chosen = sigmoids * mask
    sigmoid_total = jnp.sum(chosen, axis=1, keepdims=True)
    weighted = jnp.sum(gating_grad * chosen, axis=1, keepdims=True) / sigmoid_total
    sigmoid_grad = ROUTE_SCALE / sigmoid_total * (gating_grad - weighted)
    logits_grad = (sigmoid_grad * chosen * (1.0 - sigmoids)).astype(bf16)
    grad_router = transposed_left(mid_own, logits_grad)
    mid_grad = back_own[:, :width] + transposed_right(logits_grad, router_full)
    resid_norm_grad, grad_gain_mid = norm_backward(mid_grad, unit_mid, inverse_mid, gain_rows[1])
    resid_grad = grad_own.astype(f32) + resid_norm_grad

    resid_low, hidden_parts = lax.optimization_barrier((resid_grad.astype(bf16), hidden_parts))
    down_second = transposed_left(hidden_parts[1], grad_parts[1])
    attn_rows, gate_parts, down_second = lax.optimization_barrier(
        (spread(resid_low, tp_steps[:1]), gate_parts, down_second)
    )
    gate_second = transposed_left(gate_parts[1], mid_parts[1])
    attn_grad, gate_second = lax.optimization_barrier(
        (spread(attn_rows, tp_steps[1:]), gate_second)
    )

    def ring_columns(left_side, right_side):
        size = left_side.shape[1] // groups
        return [
            transposed_left(
                lax.dynamic_slice_in_dim(left_side, g * size, size, axis=1), right_side
            ).astype(bf16)
            for g in ring_groups
        ]

    def beside(work, rings):
        rounds = [ring_round(ring, "ep") for ring in rings]
        work, states = lax.optimization_barrier((work, [state for state, _ in rounds]))
        return work, [(state, left) for state, (_, left) in zip(states, rounds)]

    output_ring = ring_begin(ring_columns(attn_grad, attended), "ep")
    attended_grad = (
        matmul(attn_grad, output_turned).astype(bf16).reshape(tokens, heads_local, V_DIM)
    )
    values_grad = jnp.einsum("hqk,qhd->khd", probs_low, attended_grad, preferred_element_type=f32)
    probs_grad = jnp.einsum("qhd,khd->hqk", attended_grad, values, preferred_element_type=f32)
    scores_grad = (
        softmax_probs * (probs_grad - jnp.sum(softmax_probs * probs_grad, axis=-1, keepdims=True))
    ).astype(bf16)
    (scores_grad, values_grad), (output_ring,) = beside((scores_grad, values_grad), [output_ring])
    query_grad = (
        jnp.einsum("hqk,khd->qhd", scores_grad, key_rows, preferred_element_type=f32) * score_scale
    )
    keys_grad = (
        jnp.einsum("hqk,qhd->khd", scores_grad, queries, preferred_element_type=f32) * score_scale
    )
    query_raw_grad = (
        jnp.concatenate(
            [
                query_grad[..., :NOPE],
                rotate(query_grad[..., NOPE:], cosine_table[:, None, :], -sine_table[:, None, :]),
            ],
            axis=-1,
        )
        .astype(bf16)
        .reshape(tokens, heads_local * (NOPE + ROPE))
    )
    expanded_grad = (
        jnp.concatenate([keys_grad[..., :NOPE], values_grad], axis=-1)
        .astype(bf16)
        .reshape(tokens, heads_local * (NOPE + V_DIM))
    )
    latent_normed_grad = transposed_right(expanded_grad, expand_full)
    latent_part_grad, gain_latent_part = norm_backward(
        latent_normed_grad, latent_unit, latent_inverse, gain_latent
    )
    rope_raw_grad = rotate(jnp.sum(keys_grad[..., NOPE:], axis=1), cosine_table, -sine_table)
    latent_grad = jnp.concatenate([latent_part_grad, rope_raw_grad], axis=1).astype(bf16)
    both_grad = pad_columns(jnp.concatenate([query_raw_grad, latent_grad], axis=1), into_size)
    both_grad, (output_ring,) = beside(both_grad, [output_ring])
    into_ring = ring_begin(ring_columns(normed_low, both_grad), "ep")
    in_grad_part = transposed_right(both_grad, into_full).astype(bf16)
    expand_blocks = transposed_left(latent_low, expanded_grad).astype(bf16)
    expand_blocks = expand_blocks.reshape(groups, -1, expand_blocks.shape[1])
    expand_ring = ring_begin(
        [lax.dynamic_slice_in_dim(expand_blocks, g, 1, axis=0)[0] for g in ring_groups], "ep"
    )
    work = (in_grad_part, [left for _, left in (into_ring, expand_ring)])
    (in_grad_part, lefts), (into_ring, output_ring) = beside(work, [into_ring, output_ring])
    into_ring, expand_ring = (into_ring[0], lefts[0][1:]), (expand_ring[0], lefts[1])

    upper_rows, _ = lax.optimization_barrier((upper_parts[1], in_grad_part))
    upper_second = transposed_left(upper_rows, mid_parts[1])
    in_grad = fold_step(in_grad_part, tp_steps[-1])
    halves = (firsts, [down_second, gate_second, upper_second])
    (halves, in_grad), (into_ring, expand_ring, output_ring) = beside(
        (halves, in_grad), [into_ring, expand_ring, output_ring]
    )

    def grad_units(kind, start, count):
        return halves[0][kind][start : start + count] + halves[1][kind][start : start + count]

    in_grad = fold(in_grad, tp_steps[:-1]).astype(f32)
    shared_at = EXP_DEV * expert_pad
    shared_gu_back = lax.all_to_all(
        jnp.stack([grad_units(kind, shared_at, units).T for kind in (1, 2)])
        .astype(bf16)
        .reshape(2, width, 1, units),
        "ep",
        split_axis=1,
        concat_axis=2,
        tiled=True,
    )
    shared_down_back = lax.all_to_all(
        grad_units(0, shared_at, units).astype(bf16),
        "ep",
        split_axis=1,
        concat_axis=0,
        tiled=True,
    )

    grad_expert_down = jnp.stack(
        [grad_units(0, e * expert_pad, hidden_units) for e in range(EXP_DEV)]
    )
    (in_grad, halves, grad_expert_down), (into_ring, expand_ring) = beside(
        (in_grad, halves, grad_expert_down), [into_ring, expand_ring]
    )

    input_norm_grad, grad_gain_in = norm_backward(
        in_grad, unit_in[:own], inverse_in[:own], gain_rows[0]
    )
    hidden_own = (resid_grad + input_norm_grad).astype(bf16)
    grad_small = jnp.concatenate(
        [
            jnp.stack([grad_gain_in, grad_gain_mid])
            .reshape(2, groups, -1)
            .transpose(1, 0, 2)
            .reshape(groups, -1),
            gain_latent_part.reshape(groups, -1),
            grad_router.reshape(groups, -1),
        ],
        axis=1,
    )
    small_sum = by_distance(grad_small, group, distances(ep_steps))
    small_sum = fold_step(small_sum, ep_steps[-1])
    hidden_rows = spread(hidden_own[None], tp_steps[:1])
    block_rows = spread(block_own[None], tp_steps[:1])
    work = (hidden_rows, block_rows, small_sum, halves, shared_gu_back, shared_down_back)
    work, (into_ring, expand_ring) = beside(work, [into_ring, expand_ring])
    hidden_rows, block_rows, small_sum, halves, shared_gu_back, shared_down_back = work
    hidden_rows = by_place(spread(hidden_rows, tp_steps[1:]), part, tp_order)
    block_rows = by_place(spread(block_rows, tp_steps[1:]), part, tp_order)

    grad_expert_gate_up = jnp.stack(
        [
            jnp.stack([grad_units(kind, e * expert_pad, hidden_units).T for kind in (1, 2)])
            for e in range(EXP_DEV)
        ]
    )
    grad_shared_gu_out = shared_gu_back.reshape(shared_gate_up.shape).astype(f32)
    grad_shared_down_out = shared_down_back.astype(f32)
    small_sum = fold(small_sum, ep_steps[:-1])
    into_sum = ring_end(into_ring, "ep")
    grad_expand_out = ring_end(expand_ring, "ep")
    grad_output_out = ring_end(output_ring, "ep").T
    grad_query_out = into_sum[:, :query_size]
    grad_latent_out = into_sum[:, query_size : query_size + latent_width]
    for axis, bit in tp_steps:
        rounded = grad_latent_out.astype(bf16)
        grad_latent_out = rounded.astype(f32) + swap(rounded, axis, bit).astype(f32)
    for axis, bit in tp_steps:
        small_sum = small_sum + swap(small_sum, axis, bit)
    small_sum = small_sum.reshape(-1)
    grad_gains_out = small_sum[: at[1]].reshape(norm_gains.shape)
    grad_gain_latent_out = small_sum[at[1] : at[2]]
    grad_router_out = small_sum[at[2] : at[3]].reshape(router_weight.shape)

    return (
        block_rows.reshape(tokens, width),
        hidden_rows.reshape(tokens, width).astype(f32),
        grad_query_out,
        grad_latent_out,
        grad_expand_out,
        grad_output_out,
        grad_gains_out,
        grad_gain_latent_out,
        grad_router_out,
        grad_shared_gu_out,
        grad_shared_down_out,
        grad_expert_gate_up,
        grad_expert_down,
    )


def power_of_two(size):
    return size & (size - 1) == 0


def on_device(hidden_in, *others):
    groups, parts = lax.axis_size("ep"), lax.axis_size("tp")
    tokens = hidden_in.shape[0]
    mean_load = tokens * TOPK // (EXP_DEV * groups)
    capacity = mean_load + mean_load // 3
    if EXP_DEV * capacity >= tokens and power_of_two(groups) and power_of_two(parts):
        return on_device_dense(hidden_in, *others)
    return on_device_sparse(hidden_in, *others)


def solution(mesh):
    placed = (
        P("ep", None),
        P("ep", None),
        P("ep", "tp"),
        P("ep", None),
        P("ep", "tp"),
        P("tp", "ep"),
        P(None, "ep"),
        P("ep"),
        P("ep", None),
        P(None, "ep", "tp"),
        P("tp", "ep"),
        P("ep", None, None, "tp"),
        P("ep", "tp", None),
        P("ep", None),
    )
    return jax.shard_map(
        on_device,
        mesh=mesh,
        in_specs=placed,
        out_specs=(
            P("ep", None),
            P("ep", None),
            P("ep", "tp"),
            P("ep", None),
            P("ep", "tp"),
            P("tp", "ep"),
            P(None, "ep"),
            P("ep"),
            P("ep", None),
            P(None, "ep", "tp"),
            P("tp", "ep"),
            P("ep", None, None, "tp"),
            P("ep", "tp", None),
        ),
        check_vma=False,
    )
```

```python
import functools
import math

import jax
import jax.numpy as jnp
from jax import lax
from jax.experimental import pallas as pl
from jax.experimental.pallas import tpu as pltpu
from jax.sharding import PartitionSpec as P

NOPE = 128
ROPE = 64
V_DIM = 128
KV_RANK = 512
TOPK = 6
EXP_DEV = 2


EPSILON = 1e-06
ROUTE_SCALE = 2.446
ROPE_BASE = 50000.0


def matmul(left_side, right_side):
    return jnp.dot(left_side, right_side, preferred_element_type=jnp.float32)


def transposed_left(left_side, right_side):
    return lax.dot_general(
        left_side, right_side, (((0,), (0,)), ((), ())), preferred_element_type=jnp.float32
    )


def transposed_right(left_side, right_side):
    return lax.dot_general(
        left_side, right_side, (((1,), (1,)), ((), ())), preferred_element_type=jnp.float32
    )


def rotate(values, cosine_table, sine_table):
    halfway = values.shape[-1] // 2
    first_half = values[..., :halfway]
    second_half = values[..., halfway:]
    return jnp.concatenate(
        [
            first_half * cosine_table - second_half * sine_table,
            second_half * cosine_table + first_half * sine_table,
        ],
        axis=-1,
    )


def norm_forward(values, gain_row):
    inverse = lax.rsqrt(jnp.mean(values * values, axis=-1, keepdims=True) + EPSILON)
    unit_rows = values * inverse
    return (unit_rows * gain_row, unit_rows, inverse)


def norm_backward(incoming, unit_rows, inverse, gain_row):
    scaled = incoming * gain_row
    grad_values = inverse * (
        scaled - unit_rows * jnp.mean(scaled * unit_rows, axis=-1, keepdims=True)
    )
    return (grad_values, jnp.sum(incoming * unit_rows, axis=0))


def on_device_sparse(
    hidden_in,
    out_grad,
    query_weight,
    latent_weight,
    expand_weight,
    output_weight,
    norm_gains,
    latent_gain,
    router_weight,
    shared_gate_up,
    shared_down,
    expert_gate_up,
    expert_down,
    expert_ids,
):
    (
        query_full,
        latent_full,
        expand_full,
        output_full,
        gains_full,
        latent_gain_full,
        router_full,
        shared_gu_full,
        shared_down_full,
    ) = (
        lax.all_gather(query_weight, "ep", axis=0, tiled=True),
        lax.all_gather(latent_weight, "ep", axis=0, tiled=True),
        lax.all_gather(expand_weight, "ep", axis=0, tiled=True),
        lax.all_gather(output_weight, "ep", axis=1, tiled=True),
        lax.all_gather(norm_gains, "ep", axis=1, tiled=True),
        lax.all_gather(latent_gain, "ep", axis=0, tiled=True),
        lax.all_gather(router_weight, "ep", axis=0, tiled=True),
        lax.all_gather(shared_gate_up, "ep", axis=1, tiled=True),
        lax.all_gather(shared_down, "ep", axis=1, tiled=True),
    )
    tokens = hidden_in.shape[0]
    model_width = hidden_in.shape[1]
    heads_local = query_full.shape[1] // (NOPE + ROPE)
    gain_rows = gains_full.astype(jnp.float32)
    gain_latent = latent_gain_full.astype(jnp.float32)
    places = jnp.arange(tokens).astype(jnp.float32)
    frequency = ROPE_BASE ** (-(jnp.arange(ROPE // 2).astype(jnp.float32) * 2.0 / ROPE))
    angles = places[:, None] * frequency[None, :]
    cosine_table = jnp.cos(angles)
    sine_table = jnp.sin(angles)
    resid_in = hidden_in.astype(jnp.float32)
    normed_in, unit_in, inverse_in = norm_forward(resid_in, gain_rows[0])
    normed_low = normed_in.astype(jnp.bfloat16)
    query_raw = matmul(normed_low, query_full).reshape(tokens, heads_local, NOPE + ROPE)
    queries = jnp.concatenate(
        [
            query_raw[..., :NOPE],
            rotate(query_raw[..., NOPE:], cosine_table[:, None, :], sine_table[:, None, :]),
        ],
        axis=-1,
    ).astype(jnp.bfloat16)
    latent = matmul(normed_low, latent_full)
    latent_normed, latent_unit, latent_inverse = norm_forward(latent[:, :KV_RANK], gain_latent)
    latent_low = latent_normed.astype(jnp.bfloat16)
    key_rope = rotate(latent[:, KV_RANK:], cosine_table, sine_table).astype(jnp.bfloat16)
    expanded = (
        matmul(latent_low, expand_full)
        .astype(jnp.bfloat16)
        .reshape(tokens, heads_local, NOPE + V_DIM)
    )
    key_rows = jnp.concatenate(
        [expanded[..., :NOPE], jnp.broadcast_to(key_rope[:, None, :], (tokens, heads_local, ROPE))],
        axis=-1,
    )
    values = expanded[..., NOPE:]
    score_scale = 1.0 / math.sqrt(NOPE + ROPE)
    causal = jnp.arange(tokens)[:, None] >= jnp.arange(tokens)[None, :]

    def attention_scores():
        scores = (
            jnp.einsum("qhd,khd->hqk", queries, key_rows, preferred_element_type=jnp.float32)
            * score_scale
        )
        return jnp.where(causal[None], scores, -1e30)

    scores_first = attention_scores()
    row_max = jnp.max(scores_first, axis=-1, keepdims=True)
    log_total = row_max + jnp.log(jnp.sum(jnp.exp(scores_first - row_max), axis=-1, keepdims=True))
    probs_low = jnp.exp(scores_first - log_total).astype(jnp.bfloat16)
    attended = jnp.einsum("hqk,khd->qhd", probs_low, values, preferred_element_type=jnp.float32)
    attended = attended.astype(jnp.bfloat16).reshape(tokens, heads_local * V_DIM)
    attn_out = lax.psum(matmul(attended, output_full), "tp")
    resid = resid_in + attn_out
    normed_mid, unit_mid, inverse_mid = norm_forward(resid, gain_rows[1])
    mid_low = normed_mid.astype(jnp.bfloat16)
    logits = matmul(mid_low, router_full)
    experts = router_full.shape[1]
    route_mask = (expert_ids[:, :, None] == jnp.arange(experts)[None, None, :]).astype(jnp.float32)
    chosen = jnp.sum(route_mask * logits[:, None, :], axis=2)
    sigmoids = jax.nn.sigmoid(chosen)
    sigmoid_total = jnp.sum(sigmoids, axis=1, keepdims=True)
    gating = ROUTE_SCALE * sigmoids / sigmoid_total
    shared_gate = matmul(mid_low, shared_gu_full[0])
    shared_upper = matmul(mid_low, shared_gu_full[1])
    shared_sig = jax.nn.sigmoid(shared_gate)
    shared_hidden = (shared_gate * shared_sig * shared_upper).astype(jnp.bfloat16)
    shared_part = matmul(shared_hidden, shared_down_full)
    groups = lax.axis_size("ep")
    mean_load = tokens * TOPK // (EXP_DEV * groups)
    capacity = mean_load + mean_load // 3
    choices = tokens * TOPK
    rows_total = groups * capacity
    flat_ids = expert_ids.reshape(-1)
    onehot = (flat_ids[:, None] == jnp.arange(experts)[None, :]).astype(jnp.int32)
    slot_of = jnp.sum((jnp.cumsum(onehot, axis=0) - onehot) * onehot, axis=1)
    target = flat_ids % EXP_DEV * rows_total + flat_ids // EXP_DEV * capacity + slot_of
    slot_table = (
        jnp.full((EXP_DEV * rows_total,), choices, jnp.int32)
        .at[target]
        .set(jnp.arange(choices, dtype=jnp.int32))
        .reshape(EXP_DEV, groups, capacity)
    )
    mid_padded = jnp.concatenate([mid_low, jnp.zeros((1, model_width), jnp.bfloat16)], axis=0)
    outgoing = mid_padded[slot_table.reshape(-1) // TOPK].reshape(EXP_DEV, rows_total, model_width)
    expert_rows = lax.all_to_all(outgoing, "ep", split_axis=1, concat_axis=1, tiled=True)
    expert_gate = jnp.einsum(
        "erd,edf->erf", expert_rows, expert_gate_up[:, 0], preferred_element_type=jnp.float32
    )
    expert_upper = jnp.einsum(
        "erd,edf->erf", expert_rows, expert_gate_up[:, 1], preferred_element_type=jnp.float32
    )
    expert_sig = jax.nn.sigmoid(expert_gate)
    expert_hidden = (expert_gate * expert_sig * expert_upper).astype(jnp.bfloat16)
    expert_part = jnp.einsum(
        "erf,efd->erd", expert_hidden, expert_down, preferred_element_type=jnp.float32
    ).astype(jnp.bfloat16)
    returned = lax.all_to_all(expert_part, "ep", split_axis=1, concat_axis=1, tiled=True)
    per_choice = (
        returned.reshape(-1, model_width)[target]
        .reshape(tokens, TOPK, model_width)
        .astype(jnp.float32)
    )
    routed_part = jnp.sum(gating[:, :, None] * per_choice, axis=1)
    moe_out = lax.psum((shared_part + routed_part).astype(jnp.bfloat16), "tp").astype(jnp.float32)
    block_out = (resid + moe_out).astype(jnp.bfloat16)
    grad_top = out_grad.astype(jnp.float32)
    choice_grad = (gating[:, :, None] * grad_top[:, None, :]).astype(jnp.bfloat16)
    grad_padded = jnp.concatenate(
        [choice_grad.reshape(choices, model_width), jnp.zeros((1, model_width), jnp.bfloat16)],
        axis=0,
    )
    outgoing_grad = grad_padded[slot_table.reshape(-1)].reshape(EXP_DEV, rows_total, model_width)
    rows_grad = lax.all_to_all(outgoing_grad, "ep", split_axis=1, concat_axis=1, tiled=True)
    hidden_grad = jnp.einsum(
        "erd,efd->erf", rows_grad, expert_down, preferred_element_type=jnp.float32
    )
    gate_grad = (
        hidden_grad * expert_upper * expert_sig * (1.0 + expert_gate * (1.0 - expert_sig))
    ).astype(jnp.bfloat16)
    upper_grad = (hidden_grad * expert_gate * expert_sig).astype(jnp.bfloat16)
    grad_expert_down = jnp.einsum(
        "erf,erd->efd", expert_hidden, rows_grad, preferred_element_type=jnp.float32
    )
    grad_expert_gate_up = jnp.stack(
        [
            jnp.einsum("erd,erf->edf", expert_rows, gate_grad, preferred_element_type=jnp.float32),
            jnp.einsum("erd,erf->edf", expert_rows, upper_grad, preferred_element_type=jnp.float32),
        ],
        axis=1,
    )
    row_back = jnp.einsum(
        "erf,edf->erd", gate_grad, expert_gate_up[:, 0], preferred_element_type=jnp.float32
    ) + jnp.einsum(
        "erf,edf->erd", upper_grad, expert_gate_up[:, 1], preferred_element_type=jnp.float32
    )
    row_back_low = row_back.astype(jnp.bfloat16)
    back_rows = lax.all_to_all(row_back_low, "ep", split_axis=1, concat_axis=1, tiled=True)
    choice_back = (
        back_rows.reshape(-1, model_width)[target]
        .reshape(tokens, TOPK, model_width)
        .astype(jnp.float32)
    )
    mid_grad_routed = jnp.sum(choice_back, axis=1)
    gating_grad_part = jnp.sum(per_choice * grad_top[:, None, :], axis=2)
    shared_hidden_grad = transposed_right(out_grad, shared_down_full)
    shared_gate_grad = (
        shared_hidden_grad * shared_upper * shared_sig * (1.0 + shared_gate * (1.0 - shared_sig))
    ).astype(jnp.bfloat16)
    shared_upper_grad = (shared_hidden_grad * shared_gate * shared_sig).astype(jnp.bfloat16)
    grad_shared_down = transposed_left(shared_hidden, out_grad)
    grad_shared_gu = jnp.stack(
        [transposed_left(mid_low, shared_gate_grad), transposed_left(mid_low, shared_upper_grad)],
        axis=0,
    )
    mid_grad_shared = transposed_right(shared_gate_grad, shared_gu_full[0]) + transposed_right(
        shared_upper_grad, shared_gu_full[1]
    )
    mid_grad_sum, gating_grad = (
        lax.psum((mid_grad_routed + mid_grad_shared).astype(jnp.bfloat16), "tp").astype(
            jnp.float32
        ),
        lax.psum(gating_grad_part.astype(jnp.bfloat16), "tp").astype(jnp.float32),
    )
    weighted = jnp.sum(gating_grad * sigmoids, axis=1, keepdims=True) / sigmoid_total
    sigmoid_grad = ROUTE_SCALE / sigmoid_total * (gating_grad - weighted)
    chosen_grad = sigmoid_grad * sigmoids * (1.0 - sigmoids)
    logits_grad = jnp.sum(route_mask * chosen_grad[:, :, None], axis=1).astype(jnp.bfloat16)
    grad_router = transposed_left(mid_low, logits_grad)
    mid_grad = mid_grad_sum + transposed_right(logits_grad, router_full)
    resid_norm_grad, grad_gain_mid = norm_backward(mid_grad, unit_mid, inverse_mid, gain_rows[1])
    resid_grad = grad_top + resid_norm_grad
    attn_grad = resid_grad.astype(jnp.bfloat16)
    grad_output = transposed_left(attended, attn_grad)
    attended_grad = (
        transposed_right(attn_grad, output_full)
        .astype(jnp.bfloat16)
        .reshape(tokens, heads_local, V_DIM)
    )
    softmax_probs = jnp.exp(attention_scores() - log_total)
    values_grad = jnp.einsum(
        "hqk,qhd->khd",
        softmax_probs.astype(jnp.bfloat16),
        attended_grad,
        preferred_element_type=jnp.float32,
    )
    probs_grad = jnp.einsum(
        "qhd,khd->hqk", attended_grad, values, preferred_element_type=jnp.float32
    )
    scores_grad = (
        softmax_probs * (probs_grad - jnp.sum(softmax_probs * probs_grad, axis=-1, keepdims=True))
    ).astype(jnp.bfloat16)
    query_grad = (
        jnp.einsum("hqk,khd->qhd", scores_grad, key_rows, preferred_element_type=jnp.float32)
        * score_scale
    )
    keys_grad = (
        jnp.einsum("hqk,qhd->khd", scores_grad, queries, preferred_element_type=jnp.float32)
        * score_scale
    )
    query_raw_grad = (
        jnp.concatenate(
            [
                query_grad[..., :NOPE],
                rotate(query_grad[..., NOPE:], cosine_table[:, None, :], -sine_table[:, None, :]),
            ],
            axis=-1,
        )
        .astype(jnp.bfloat16)
        .reshape(tokens, heads_local * (NOPE + ROPE))
    )
    expanded_grad = jnp.concatenate([keys_grad[..., :NOPE], values_grad], axis=-1).astype(
        jnp.bfloat16
    )
    expanded_grad = expanded_grad.reshape(tokens, heads_local * (NOPE + V_DIM))
    grad_expand = transposed_left(latent_low, expanded_grad)
    latent_normed_grad = transposed_right(expanded_grad, expand_full)
    latent_part_grad, gain_latent_part = norm_backward(
        latent_normed_grad, latent_unit, latent_inverse, gain_latent
    )
    rope_raw_grad = rotate(jnp.sum(keys_grad[..., NOPE:], axis=1), cosine_table, -sine_table)
    latent_grad_part = jnp.concatenate([latent_part_grad, rope_raw_grad], axis=1)
    in_grad_query = transposed_right(query_raw_grad, query_full)
    in_grad_sum, latent_grad, grad_gain_latent = (
        lax.psum(in_grad_query.astype(jnp.bfloat16), "tp").astype(jnp.float32),
        lax.psum(latent_grad_part.astype(jnp.bfloat16), "tp").astype(jnp.float32),
        lax.psum(gain_latent_part.astype(jnp.bfloat16), "tp").astype(jnp.float32),
    )
    latent_grad_low = latent_grad.astype(jnp.bfloat16)
    grad_latent = transposed_left(normed_low, latent_grad_low)
    grad_query = transposed_left(normed_low, query_raw_grad)
    in_grad = in_grad_sum + transposed_right(latent_grad_low, latent_full)
    input_norm_grad, grad_gain_in = norm_backward(in_grad, unit_in, inverse_in, gain_rows[0])
    grad_hidden = resid_grad + input_norm_grad
    grad_gains = jnp.stack([grad_gain_in, grad_gain_mid], axis=0)
    (
        grad_query_out,
        grad_latent_out,
        grad_expand_out,
        grad_output_out,
        grad_gains_out,
        grad_gain_latent_out,
        grad_router_out,
        grad_shared_gu_out,
        grad_shared_down_out,
    ) = (
        lax.psum_scatter(
            grad_query.astype(jnp.bfloat16), "ep", scatter_dimension=0, tiled=True
        ).astype(jnp.float32),
        lax.psum_scatter(
            grad_latent.astype(jnp.bfloat16), "ep", scatter_dimension=0, tiled=True
        ).astype(jnp.float32),
        lax.psum_scatter(
            grad_expand.astype(jnp.bfloat16), "ep", scatter_dimension=0, tiled=True
        ).astype(jnp.float32),
        lax.psum_scatter(
            grad_output.astype(jnp.bfloat16), "ep", scatter_dimension=1, tiled=True
        ).astype(jnp.float32),
        lax.psum_scatter(
            grad_gains.astype(jnp.bfloat16), "ep", scatter_dimension=1, tiled=True
        ).astype(jnp.float32),
        lax.psum_scatter(
            grad_gain_latent.astype(jnp.bfloat16), "ep", scatter_dimension=0, tiled=True
        ).astype(jnp.float32),
        lax.psum_scatter(
            grad_router.astype(jnp.bfloat16), "ep", scatter_dimension=0, tiled=True
        ).astype(jnp.float32),
        lax.psum_scatter(
            grad_shared_gu.astype(jnp.bfloat16), "ep", scatter_dimension=1, tiled=True
        ).astype(jnp.float32),
        lax.psum_scatter(
            grad_shared_down.astype(jnp.bfloat16), "ep", scatter_dimension=1, tiled=True
        ).astype(jnp.float32),
    )
    return (
        block_out,
        grad_hidden,
        grad_query_out,
        grad_latent_out,
        grad_expand_out,
        grad_output_out,
        grad_gains_out,
        grad_gain_latent_out,
        grad_router_out,
        grad_shared_gu_out,
        grad_shared_down_out,
        grad_expert_gate_up,
        grad_expert_down,
    )


CUTS = 4
GATHERS = 2
LANES = 128
VMEM_BYTES = 56 * 1024 * 1024


def swap(array, axis, bit):
    size = lax.axis_size(axis)
    return lax.ppermute(array, axis, [(place, place ^ bit) for place in range(size)])


def axis_bits(axis):
    size = lax.axis_size(axis)
    return [(axis, 1 << bit) for bit in reversed(range(size.bit_length() - 1))]


def spread(rows, steps):
    for axis, bit in steps:
        rows = jnp.concatenate([rows, swap(rows, axis, bit)], axis=0)
    return rows


def add_rounded(left_side, right_side):
    return (left_side.astype(jnp.float32) + right_side.astype(jnp.float32)).astype(
        left_side.dtype
    )


def fold_step(rows, step):
    axis, bit = step
    half = rows.shape[0] // 2
    return add_rounded(rows[:half], swap(rows[half:], axis, bit))


def fold(rows, steps):
    for step in reversed(steps):
        rows = fold_step(rows, step)
    return rows


def distances(steps):
    found = [0]
    for _, bit in steps:
        found = found + [distance + bit for distance in found]
    return found


def by_distance(blocks, place, order):
    return jnp.concatenate(
        [lax.dynamic_slice_in_dim(blocks, place ^ i, 1, axis=0) for i in order], axis=0
    )


def by_place(blocks, place, order):
    natural = jnp.concatenate([blocks[order.index(i)][None] for i in range(len(order))], axis=0)
    return by_distance(natural, place, range(len(order)))


def ring_owner(spot, size):
    return jnp.where(spot < size // 2, 2 * spot, 2 * (size - 1 - spot) + 1)


def ring_spot(place, size):
    return jnp.where(place % 2 == 0, place // 2, size - 1 - place // 2)


def ring_shift(array, axis, by):
    size = lax.axis_size(axis)
    ring = [2 * i for i in range(size // 2)] + [2 * i + 1 for i in reversed(range(size // 2))]
    return lax.ppermute(array, axis, [(ring[i], ring[(i + by) % size]) for i in range(size)])


def ring_gather(arrays, axis, beside):
    size = lax.axis_size(axis)
    found = [[array] + [None] * (size - 1) for array in arrays]
    ahead, behind, others, rounds = arrays, arrays, [], []
    for k in range(1, size // 2 + 1):
        behind = [ring_shift(array, axis, 1) for array in behind]
        if k < size - k:
            ahead = [ring_shift(array, axis, -1) for array in ahead]
        other = beside[k - 1](others) if k <= len(beside) else None
        behind, ahead, other = lax.optimization_barrier((behind, ahead, other))
        others.append(other)
        rounds.append(behind)
        for pieces, before, after in zip(found, behind, ahead):
            pieces[size - k] = before
            if k < size - k:
                pieces[k] = after
    return found, others, rounds


def ring_begin(parts, axis):
    size = lax.axis_size(axis)
    half = size // 2
    left = [(parts[half - k], parts[half + 1 + k] if k < half - 1 else None) for k in range(1, half)]
    return (parts[half], parts[half + 1]), left + [(parts[0], None)]


def ring_round(ring, axis):
    (ahead, behind), left = ring
    more_ahead, more_behind = left[0]
    ahead = add_rounded(ring_shift(ahead, axis, 1), more_ahead)
    if behind is not None and len(left) > 1:
        behind = ring_shift(behind, axis, -1)
        if more_behind is not None:
            behind = add_rounded(behind, more_behind)
    return (ahead, behind), left[1:]


def ring_end(ring, axis):
    (ahead, behind), left = ring
    while left:
        if len(left) == 1:
            found = ring_shift(ahead, axis, 1).astype(jnp.float32) + left[0][0]
            return found + behind
        (ahead, behind), left = ring_round(((ahead, behind), left), axis)
    return ahead.astype(jnp.float32) + behind


def pad_columns(array, width):
    return jnp.pad(array, ((0, 0), (0, width - array.shape[1])))


def pad_rows(array, height):
    return jnp.pad(array, ((0, height - array.shape[0]), (0, 0)))


def round_up(size, step=LANES):
    return -(-size // step) * step


def feed_forward_kernel(count, wide_steps, sub, *refs):
    first_ref, slot_ref, rows_ref, raw_ref, mask_ref, router_ref, tiles_ref = refs[:7]
    back_out, gate_ref, upper_ref, hidden_ref = refs[7:11]
    gains, shares, kept, tiles, back_ref, arrived, back_left = refs[11:]
    cut, step, last = pl.program_id(0), pl.program_id(1), count + wide_steps - 1
    owners, _, each, width = rows_ref.shape
    half, rows = raw_ref.shape[3], owners * each
    block = sub // each
    f32, bf16 = jnp.float32, jnp.bfloat16

    def arrival(n):
        return pltpu.make_async_copy(tiles_ref.at[n], tiles.at[n], arrived.at[n])

    def back_leaving(n):
        size = width // wide_steps
        extra = back_ref.shape[2] - width if n == wide_steps - 1 else 0
        of = (slice(None), slice(None), pl.ds(n * size, size + extra))
        return pltpu.make_async_copy(back_ref.at[of], back_out.at[(cut, *of)], back_left.at[n])

    @pl.when(step == 0)
    def _():
        @pl.when(cut == 0)
        def _():
            for n in range(count):
                arrival(n).start()

        values = rows_ref[...].reshape(rows, width)
        logits = jnp.dot(values, router_ref[...], preferred_element_type=f32)
        sig = jax.nn.sigmoid(logits) * mask_ref[...].reshape(logits.shape)
        gating = ROUTE_SCALE * sig / jnp.sum(sig, axis=1, keepdims=True)
        lanes = lax.broadcasted_iota(jnp.int32, gating.shape, 1)
        for e in range(EXP_DEV):
            own = jnp.sum(jnp.where(lanes == first_ref[0] + e, gating, 0.0), axis=1, keepdims=True)
            gains[e] = jnp.broadcast_to(own, gains.shape[1:])
        gains[EXP_DEV] = jnp.ones(gains.shape[1:], f32)
        shares[...] = jnp.zeros_like(shares)

    @pl.when(step < count)
    def _():
        @pl.when(cut == 0)
        def _():
            arrival(step).wait()

        kind = jnp.minimum(step // ((count - 1) // EXP_DEV), EXP_DEV)
        for i in range(rows // sub):
            at, of = pl.ds(i * sub, sub), pl.ds(i * block, block)
            values = rows_ref[of].reshape(sub, width)
            both = lax.dot_general(
                values, tiles[step], (((1,), (1,)), ((), ())), preferred_element_type=f32
            )
            gate, upper = both[:, :half], both[:, half:]
            gain, raw = gains[kind, at, :], raw_ref[of].reshape(sub, half).astype(f32)
            sig = jax.nn.sigmoid(gate)
            silu = gate * sig
            hidden = silu * upper
            grad = gain * raw
            shape = (block, 1, each, half)
            hidden_ref[of] = (gain * hidden).astype(bf16).reshape(shape)
            shares[kind, at, :] += hidden * raw
            gate_grad = (grad * upper * (sig + silu * (1.0 - sig))).astype(bf16)
            upper_grad = (grad * silu).astype(bf16)
            gate_ref[of] = gate_grad.reshape(shape)
            upper_ref[of] = upper_grad.reshape(shape)
            kept[step, at, :half] = gate_grad
            kept[step, at, half:] = upper_grad

    @pl.when(step >= count)
    def _():
        size = width // wide_steps
        columns = pl.ds(pl.multiple_of((step - count) * size, size), size)
        for i in range(rows // sub):
            found = sum(
                jnp.dot(
                    kept[n, pl.ds(i * sub, sub), :],
                    tiles[n, :, columns],
                    preferred_element_type=f32,
                )
                for n in range(count)
            ).astype(bf16)
            for j in range(block):
                part = found[j * each : (j + 1) * each]
                back_ref[slot_ref[cut, i * block + j], :, columns] = part

    @pl.when(step == last)
    def _():
        extra = back_ref.shape[2] - width
        lanes = lax.broadcasted_iota(jnp.int32, (rows, extra), 1)
        gating_grad = jnp.zeros(lanes.shape, f32)
        for e in range(EXP_DEV):
            own = jnp.sum(shares[e], axis=1, keepdims=True)
            gating_grad += jnp.where(lanes == first_ref[0] + e, own, 0.0)
        gating_grad = gating_grad.astype(bf16)
        for i in range(owners):
            back_ref[slot_ref[cut, i], :, width:] = gating_grad[i * each : (i + 1) * each]

    for n in range(wide_steps):

        @pl.when(step == count + n)
        def _(n=n):
            back_leaving(n).start()

    @pl.when(step == last)
    def _():
        for n in range(wide_steps):
            back_leaving(n).wait()


def feed_forward(slots, mid_rows, raw_grad, mask, router, tiles, first):
    count, both, width = tiles.shape
    owners, cuts, each, experts = mask.shape
    rows, half, wide_steps = owners * each, both // 2, 4
    bf16, f32 = jnp.bfloat16, jnp.float32

    def tile(step):
        return jnp.minimum(step, count - 1)

    smem, whole = pl.BlockSpec(memory_space=pltpu.SMEM), pl.BlockSpec(memory_space=pl.ANY)
    side = pl.BlockSpec((owners, 1, each, half), lambda c, i: (0, c, 0, tile(i)))
    return pl.pallas_call(
        functools.partial(feed_forward_kernel, count, wide_steps, min(8, owners) * each),
        grid=(cuts, count + wide_steps),
        in_specs=[
            smem,
            smem,
            pl.BlockSpec((owners, 1, each, width), lambda c, i: (0, c, 0, 0)),
            side,
            pl.BlockSpec((owners, 1, each, experts), lambda c, i: (0, c, 0, 0)),
            pl.BlockSpec((width, experts), lambda c, i: (0, 0)),
            whole,
        ],
        out_specs=[whole, side, side, side],
        out_shape=[
            jax.ShapeDtypeStruct((cuts, owners, each, width + LANES), bf16),
            *[jax.ShapeDtypeStruct((owners, cuts, each, count * half), bf16)] * 3,
        ],
        scratch_shapes=[
            pltpu.VMEM((EXP_DEV + 1, rows, half), f32),
            pltpu.VMEM((EXP_DEV + 1, rows, half), f32),
            pltpu.VMEM((count, rows, both), bf16),
            pltpu.VMEM(tiles.shape, bf16),
            pltpu.VMEM((owners, each, width + LANES), bf16),
            pltpu.SemaphoreType.DMA((count,)),
            pltpu.SemaphoreType.DMA((wide_steps,)),
        ],
        compiler_params=pltpu.CompilerParams(vmem_limit_bytes=VMEM_BYTES),
        cost_estimate=pl.CostEstimate(
            flops=4 * cuts * rows * width * both * count,
            bytes_accessed=50_000_000,
            transcendentals=0,
        ),
    )(first, slots, mid_rows, raw_grad, mask, router, tiles)


def rows_by_device_kernel(*refs):
    *left_refs, right_ref, out_ref = refs
    for i, left_ref in enumerate(left_refs):

        @pl.when(pl.program_id(1) == i)
        def _(left_ref=left_ref):
            found = jnp.dot(left_ref[...], right_ref[...], preferred_element_type=jnp.float32)
            out_ref[...] = found.astype(out_ref.dtype).reshape(out_ref.shape)


def rows_by_device(left_parts, right_side, devices):
    rows, depth = left_parts[0].shape
    columns, count = right_side.shape[1], len(left_parts)
    wide = columns // 2
    return pl.pallas_call(
        rows_by_device_kernel,
        grid=(2, count),
        in_specs=[pl.BlockSpec((rows, depth), lambda j, i: (0, 0))] * count
        + [pl.BlockSpec((depth, wide), lambda j, i: (0, j))],
        out_specs=pl.BlockSpec((devices, 1, rows // devices, wide), lambda j, i: (0, i, 0, j)),
        out_shape=jax.ShapeDtypeStruct(
            (devices, count, rows // devices, columns), right_side.dtype
        ),
        compiler_params=pltpu.CompilerParams(vmem_limit_bytes=VMEM_BYTES),
        cost_estimate=pl.CostEstimate(
            flops=2 * count * rows * depth * columns,
            bytes_accessed=2 * count * rows * (depth + columns),
            transcendentals=0,
        ),
    )(*left_parts, right_side).reshape(count * rows, columns)


def place_kernel(places_ref, *refs):
    *pieces, out_ref = refs
    for i, piece in enumerate(pieces):

        @pl.when(pl.program_id(0) == i)
        def _(piece=piece):
            out_ref[0] = piece[...]


def place_blocks(pieces, places):
    shape = pieces[0].shape
    return pl.pallas_call(
        place_kernel,
        grid_spec=pltpu.PrefetchScalarGridSpec(
            num_scalar_prefetch=1,
            grid=(len(pieces),),
            in_specs=[pl.BlockSpec(shape, lambda i, at: (0, 0))] * len(pieces),
            out_specs=pl.BlockSpec((1, *shape), lambda i, at: (at[i], 0, 0)),
        ),
        out_shape=jax.ShapeDtypeStruct((len(pieces), *shape), pieces[0].dtype),
        compiler_params=pltpu.CompilerParams(vmem_limit_bytes=VMEM_BYTES),
    )(jnp.stack(places).astype(jnp.int32), *pieces)


def on_device_dense(
    hidden_in,
    out_grad,
    query_weight,
    latent_weight,
    expand_weight,
    output_weight,
    norm_gains,
    latent_gain,
    router_weight,
    shared_gate_up,
    shared_down,
    expert_gate_up,
    expert_down,
    expert_ids,
):
    groups, parts = lax.axis_size("ep"), lax.axis_size("tp")
    group, part = lax.axis_index("ep"), lax.axis_index("tp")
    tokens, width = hidden_in.shape
    own = tokens // parts
    experts = router_weight.shape[1]
    bf16, f32 = jnp.bfloat16, jnp.float32
    ep_steps, tp_steps = axis_bits("ep"), axis_bits("tp")
    tp_order = distances(tp_steps)
    every = ("ep", "tp")
    devices = groups * parts
    cut_rows = own // CUTS

    spot = ring_spot(group, groups)
    ring_groups = [ring_owner((spot + k) % groups, groups) for k in range(groups)]

    mask_own = jnp.sum(
        (expert_ids[:, :, None] == jnp.arange(experts)[None, None, :]).astype(bf16), axis=1
    )
    sizes = [norm_gains.size, latent_gain.size, router_weight.size, mask_own.size]
    small = jnp.concatenate(
        [array.reshape(1, -1) for array in (norm_gains, latent_gain, router_weight, mask_own)],
        axis=1,
    )
    query_size, latent_width = query_weight.shape[1], latent_weight.shape[1]
    output_size = output_weight.shape[0]
    into_size = round_up(query_size + latent_width)
    into = pad_columns(jnp.concatenate([query_weight, latent_weight], axis=1), into_size)
    out_of = jnp.concatenate(
        [output_weight.T, expand_weight.reshape(output_weight.shape[1], -1)], axis=1
    )

    units = shared_down.shape[0] // groups

    hidden_units = expert_down.shape[1]
    expert_pad, shared_pad = round_up(hidden_units), round_up(units)

    def dense_weights(shared_gu_own, shared_down_own, expert_gate_up, expert_down):
        side_weights = [
            jnp.concatenate(
                [pad_rows(expert_gate_up[e, side].T, expert_pad) for e in range(EXP_DEV)]
                + [pad_rows(shared_gu_own[side].T, shared_pad)],
                axis=0,
            ).reshape(-1, LANES, width)
            for side in range(2)
        ]
        tiles = jnp.concatenate(side_weights, axis=1)
        down_weight = jnp.concatenate(
            [pad_rows(expert_down[e], expert_pad) for e in range(EXP_DEV)]
            + [pad_rows(shared_down_own, shared_pad)],
            axis=0,
        )
        return tiles, down_weight

    (into_pieces, out_of_pieces), others, rounds = ring_gather(
        [into, out_of],
        "ep",
        [
            lambda _: spread(small, ep_steps[:1]),
            lambda done: spread(done[0], ep_steps[1:2]),
            lambda done: spread(done[1], ep_steps[2:]),
        ],
    )
    shared_gate_up_late, shared_down_late, _ = lax.optimization_barrier(
        (shared_gate_up, shared_down, rounds[-1])
    )
    shared_gu_own = lax.all_to_all(
        shared_gate_up_late.reshape(2, -1, groups, units), "ep", split_axis=2, concat_axis=1, tiled=True
    ).reshape(2, width, units)
    shared_down_own = lax.all_to_all(shared_down_late, "ep", split_axis=0, concat_axis=1, tiled=True)


    small_rel = others[2]
    at = [sum(sizes[:i]) for i in range(len(sizes) + 1)]
    small_full = by_place(small_rel, group, distances(ep_steps))
    gain_rows = (
        small_full[:, : at[1]].reshape(groups, 2, -1).transpose(1, 0, 2).reshape(2, width)
    ).astype(f32)
    gain_latent = small_full[:, at[1] : at[2]].reshape(-1).astype(f32)
    router_full = small_full[:, at[2] : at[3]].reshape(width, experts)

    into_full = place_blocks(into_pieces, ring_groups).reshape(width, -1)
    out_of_full = place_blocks(out_of_pieces, ring_groups).reshape(width, -1)
    expand_full = out_of_full[:, output_size:].reshape(KV_RANK, -1)
    output_turned = out_of_full[:, :output_size]

    out_grad_late, _ = lax.optimization_barrier((out_grad, rounds[-3][0]))

    gather_rows = own // GATHERS
    cuts = CUTS // GATHERS

    def by_gather(rows):
        rows = rows.reshape(devices, GATHERS, gather_rows, -1).transpose(1, 0, 2, 3)
        return list(rows.reshape(GATHERS, devices * gather_rows, -1))

    grad_own = lax.dynamic_slice_in_dim(out_grad_late, part * own, own, axis=0)
    grad_parts = by_gather(lax.all_gather(grad_own, every, axis=0, tiled=True))
    mask_parts = [
        rows.astype(f32).reshape(devices, cuts, cut_rows, experts)
        for rows in by_gather(small_full[:, at[3] :])
    ]

    row_blocks = hidden_in.reshape(parts, own, width)
    hidden_rel = by_distance(row_blocks, part, tp_order).reshape(tokens, width)
    heads_local = query_size // (NOPE + ROPE)
    places = ((part ^ jnp.array(tp_order))[:, None] * own + jnp.arange(own)[None, :]).reshape(-1)
    frequency = ROPE_BASE ** (-(jnp.arange(ROPE // 2).astype(f32) * 2.0 / ROPE))
    angles = places.astype(f32)[:, None] * frequency[None, :]
    cosine_table = jnp.cos(angles)
    sine_table = jnp.sin(angles)
    normed_in, unit_in, inverse_in = norm_forward(hidden_rel.astype(f32), gain_rows[0])
    normed_low = normed_in.astype(bf16)
    both_in = matmul(normed_low, into_full)
    query_raw = both_in[:, :query_size].reshape(tokens, heads_local, NOPE + ROPE)
    queries = jnp.concatenate(
        [
            query_raw[..., :NOPE],
            rotate(query_raw[..., NOPE:], cosine_table[:, None, :], sine_table[:, None, :]),
        ],
        axis=-1,
    ).astype(bf16)
    latent = both_in[:, query_size : query_size + latent_width]
    latent_normed, latent_unit, latent_inverse = norm_forward(latent[:, :KV_RANK], gain_latent)
    latent_low = latent_normed.astype(bf16)
    key_rope = rotate(latent[:, KV_RANK:], cosine_table, sine_table).astype(bf16)
    expanded = (
        matmul(latent_low, expand_full).astype(bf16).reshape(tokens, heads_local, NOPE + V_DIM)
    )
    key_rows = jnp.concatenate(
        [expanded[..., :NOPE], jnp.broadcast_to(key_rope[:, None, :], (tokens, heads_local, ROPE))],
        axis=-1,
    )
    values = expanded[..., NOPE:]
    score_scale = 1.0 / math.sqrt(NOPE + ROPE)
    causal = places[:, None] >= places[None, :]
    scores = (
        jnp.einsum("qhd,khd->hqk", queries, key_rows, preferred_element_type=f32) * score_scale
    )
    scores = jnp.where(causal[None], scores, -1e30)
    row_max = jnp.max(scores, axis=-1, keepdims=True)
    powers = jnp.exp(scores - row_max)
    softmax_probs = powers / jnp.sum(powers, axis=-1, keepdims=True)
    probs_low = softmax_probs.astype(bf16)
    attended = jnp.einsum("hqk,khd->qhd", probs_low, values, preferred_element_type=f32)
    attended = attended.astype(bf16).reshape(tokens, heads_local * V_DIM)
    attn_part = transposed_right(attended, output_turned).astype(bf16)
    resid = hidden_rel[:own].astype(f32) + fold(attn_part, tp_steps).astype(f32)

    normed_mid, unit_mid, inverse_mid = norm_forward(resid, gain_rows[1])
    mid_own, expert_gate_up, expert_down = lax.optimization_barrier(
        (normed_mid.astype(bf16), expert_gate_up, expert_down)
    )
    tiles, down_weight = dense_weights(
        shared_gu_own, shared_down_own, expert_gate_up, expert_down
    )
    raw_parts = [
        transposed_right(rows, down_weight).astype(bf16).reshape(devices, cuts, cut_rows, -1)
        for rows in grad_parts
    ]
    first = (group * EXP_DEV).astype(jnp.int32).reshape(1)
    mid_parts = [
        lax.all_gather(
            mid_own[i * gather_rows : (i + 1) * gather_rows], every, axis=0, tiled=True
        )
        for i in range(GATHERS)
    ]
    one_order = (ep_steps + tp_steps)[::-1]
    turn = [0, *range(2, len(tp_steps) + 1), 1, *range(len(tp_steps) + 1, len(one_order))]
    orders = [one_order, [one_order[i] for i in turn]]
    distance = jnp.arange(devices, dtype=jnp.int32) ^ (group * parts + part)
    slots = []
    for order in orders:
        slot = jnp.zeros_like(distance)
        for axis, bit in order:
            slot = 2 * slot + distance // (bit * (parts if axis == "ep" else 1)) % 2
        slots.append(slot)
    slots = jnp.stack([slots[cut % 2] for cut in range(cuts)])

    def on_a_step(sums):
        return [(fold_step(rows, todo[0]), todo[1:]) if todo else (rows, todo) for rows, todo in sums]

    def together(work, sums):
        work, rows = lax.optimization_barrier((work, [rows for rows, _ in sums]))
        return work, [(each, todo) for each, (_, todo) in zip(rows, sums)]

    mid_parts[0], raw_parts = lax.optimization_barrier((mid_parts[0], raw_parts))
    sums, gate_parts, upper_parts, hidden_parts = [], [], [], []
    for i in range(GATHERS):
        mid_rows = mid_parts[i]
        back, *sides = feed_forward(
            slots,
            mid_rows.reshape(devices, cuts, cut_rows, width),
            raw_parts[i],
            mask_parts[i],
            router_full,
            tiles,
            first,
        )
        (back, sides), sums = together((back, sides), on_a_step(sums))
        sums += [(back[cut], orders[cut % 2]) for cut in range(cuts)]
        for parts_of, side in zip((gate_parts, upper_parts, hidden_parts), sides):
            parts_of.append(side.reshape(mid_rows.shape[0], -1))
        if i == 0:
            firsts = [
                transposed_left(parts_of[0], rows[0])
                for parts_of, rows in ((hidden_parts, grad_parts), (gate_parts, mid_parts))
            ]
            (firsts, mid_parts[1:]), sums = together((firsts, mid_parts[1:]), on_a_step(sums))
    firsts.append(transposed_left(upper_parts[0], mid_parts[0]))
    (firsts, hidden_parts), sums = together((firsts, hidden_parts), on_a_step(sums))
    out_part = rows_by_device(hidden_parts, down_weight, devices)
    for _ in range(2):
        out_part, sums = together(out_part, on_a_step(sums))
    out_own = lax.psum_scatter(out_part, every, scatter_dimension=0, tiled=True)
    block_own = (lax.optimization_barrier(resid) + out_own.astype(f32)).astype(bf16)
    while any(todo for _, todo in sums):
        sums = on_a_step(sums)
    back_own = jnp.concatenate([rows[0] for rows, _ in sums], axis=0)

    back_own = back_own.astype(f32)
    gating_grad = back_own[:, width : width + experts]
    mask = lax.dynamic_slice_in_dim(mask_own, part * own, own, axis=0).astype(f32)
    sigmoids = jax.nn.sigmoid(matmul(mid_own, router_full))
    chosen = sigmoids * mask
    sigmoid_total = jnp.sum(chosen, axis=1, keepdims=True)
    weighted = jnp.sum(gating_grad * chosen, axis=1, keepdims=True) / sigmoid_total
    sigmoid_grad = ROUTE_SCALE / sigmoid_total * (gating_grad - weighted)
    logits_grad = (sigmoid_grad * chosen * (1.0 - sigmoids)).astype(bf16)
    grad_router = transposed_left(mid_own, logits_grad)
    mid_grad = back_own[:, :width] + transposed_right(logits_grad, router_full)
    resid_norm_grad, grad_gain_mid = norm_backward(mid_grad, unit_mid, inverse_mid, gain_rows[1])
    resid_grad = grad_own.astype(f32) + resid_norm_grad

    resid_low, hidden_parts = lax.optimization_barrier((resid_grad.astype(bf16), hidden_parts))
    down_second = transposed_left(hidden_parts[1], grad_parts[1])
    attn_rows, gate_parts, down_second = lax.optimization_barrier(
        (spread(resid_low, tp_steps[:1]), gate_parts, down_second)
    )
    gate_second = transposed_left(gate_parts[1], mid_parts[1])
    attn_grad, gate_second = lax.optimization_barrier(
        (spread(attn_rows, tp_steps[1:]), gate_second)
    )

    def ring_columns(left_side, right_side):
        size = left_side.shape[1] // groups
        return [
            transposed_left(
                lax.dynamic_slice_in_dim(left_side, g * size, size, axis=1), right_side
            ).astype(bf16)
            for g in ring_groups
        ]

    def beside(work, rings):
        rounds = [ring_round(ring, "ep") for ring in rings]
        work, states = lax.optimization_barrier((work, [state for state, _ in rounds]))
        return work, [(state, left) for state, (_, left) in zip(states, rounds)]

    output_ring = ring_begin(ring_columns(attn_grad, attended), "ep")
    attended_grad = (
        matmul(attn_grad, output_turned).astype(bf16).reshape(tokens, heads_local, V_DIM)
    )
    values_grad = jnp.einsum("hqk,qhd->khd", probs_low, attended_grad, preferred_element_type=f32)
    probs_grad = jnp.einsum("qhd,khd->hqk", attended_grad, values, preferred_element_type=f32)
    scores_grad = (
        softmax_probs * (probs_grad - jnp.sum(softmax_probs * probs_grad, axis=-1, keepdims=True))
    ).astype(bf16)
    (scores_grad, values_grad), (output_ring,) = beside((scores_grad, values_grad), [output_ring])
    query_grad = (
        jnp.einsum("hqk,khd->qhd", scores_grad, key_rows, preferred_element_type=f32) * score_scale
    )
    keys_grad = (
        jnp.einsum("hqk,qhd->khd", scores_grad, queries, preferred_element_type=f32) * score_scale
    )
    query_raw_grad = (
        jnp.concatenate(
            [
                query_grad[..., :NOPE],
                rotate(query_grad[..., NOPE:], cosine_table[:, None, :], -sine_table[:, None, :]),
            ],
            axis=-1,
        )
        .astype(bf16)
        .reshape(tokens, heads_local * (NOPE + ROPE))
    )
    expanded_grad = (
        jnp.concatenate([keys_grad[..., :NOPE], values_grad], axis=-1)
        .astype(bf16)
        .reshape(tokens, heads_local * (NOPE + V_DIM))
    )
    latent_normed_grad = transposed_right(expanded_grad, expand_full)
    latent_part_grad, gain_latent_part = norm_backward(
        latent_normed_grad, latent_unit, latent_inverse, gain_latent
    )
    rope_raw_grad = rotate(jnp.sum(keys_grad[..., NOPE:], axis=1), cosine_table, -sine_table)
    latent_grad = jnp.concatenate([latent_part_grad, rope_raw_grad], axis=1).astype(bf16)
    both_grad = pad_columns(jnp.concatenate([query_raw_grad, latent_grad], axis=1), into_size)
    both_grad, (output_ring,) = beside(both_grad, [output_ring])
    into_ring = ring_begin(ring_columns(normed_low, both_grad), "ep")
    in_grad_part = transposed_right(both_grad, into_full).astype(bf16)
    expand_blocks = transposed_left(latent_low, expanded_grad).astype(bf16)
    expand_blocks = expand_blocks.reshape(groups, -1, expand_blocks.shape[1])
    expand_ring = ring_begin(
        [lax.dynamic_slice_in_dim(expand_blocks, g, 1, axis=0)[0] for g in ring_groups], "ep"
    )
    work = (in_grad_part, [left for _, left in (into_ring, expand_ring)])
    (in_grad_part, lefts), (into_ring, output_ring) = beside(work, [into_ring, output_ring])
    into_ring, expand_ring = (into_ring[0], lefts[0][1:]), (expand_ring[0], lefts[1])

    upper_rows, _ = lax.optimization_barrier((upper_parts[1], in_grad_part))
    upper_second = transposed_left(upper_rows, mid_parts[1])
    in_grad = fold_step(in_grad_part, tp_steps[-1])
    halves = (firsts, [down_second, gate_second, upper_second])
    (halves, in_grad), (into_ring, expand_ring, output_ring) = beside(
        (halves, in_grad), [into_ring, expand_ring, output_ring]
    )

    def grad_units(kind, start, count):
        return halves[0][kind][start : start + count] + halves[1][kind][start : start + count]

    in_grad = fold(in_grad, tp_steps[:-1]).astype(f32)
    grad_expert_down = jnp.stack(
        [grad_units(0, e * expert_pad, hidden_units) for e in range(EXP_DEV)]
    )
    (in_grad, halves, grad_expert_down), (into_ring, expand_ring) = beside(
        (in_grad, halves, grad_expert_down), [into_ring, expand_ring]
    )

    shared_at = EXP_DEV * expert_pad
    shared_gu_back = lax.all_to_all(
        jnp.stack([grad_units(kind, shared_at, units).T for kind in (1, 2)])
        .astype(bf16)
        .reshape(2, width, 1, units),
        "ep",
        split_axis=1,
        concat_axis=2,
        tiled=True,
    )
    shared_down_back = lax.all_to_all(
        grad_units(0, shared_at, units).astype(bf16),
        "ep",
        split_axis=1,
        concat_axis=0,
        tiled=True,
    )
    input_norm_grad, grad_gain_in = norm_backward(
        in_grad, unit_in[:own], inverse_in[:own], gain_rows[0]
    )
    hidden_own = (resid_grad + input_norm_grad).astype(bf16)
    grad_small = jnp.concatenate(
        [
            jnp.stack([grad_gain_in, grad_gain_mid])
            .reshape(2, groups, -1)
            .transpose(1, 0, 2)
            .reshape(groups, -1),
            gain_latent_part.reshape(groups, -1),
            grad_router.reshape(groups, -1),
        ],
        axis=1,
    )
    small_sum = by_distance(grad_small, group, distances(ep_steps))
    small_sum = fold_step(small_sum, ep_steps[-1])
    hidden_rows = spread(hidden_own[None], tp_steps[:1])
    block_rows = spread(block_own[None], tp_steps[:1])
    (hidden_rows, block_rows, small_sum, halves), (into_ring, expand_ring) = beside(
        (hidden_rows, block_rows, small_sum, halves), [into_ring, expand_ring]
    )
    hidden_rows = by_place(spread(hidden_rows, tp_steps[1:]), part, tp_order)
    block_rows = by_place(spread(block_rows, tp_steps[1:]), part, tp_order)

    grad_expert_gate_up = jnp.stack(
        [
            jnp.stack([grad_units(kind, e * expert_pad, hidden_units).T for kind in (1, 2)])
            for e in range(EXP_DEV)
        ]
    )
    grad_shared_gu_out = shared_gu_back.reshape(shared_gate_up.shape).astype(f32)
    grad_shared_down_out = shared_down_back.astype(f32)
    small_sum = fold(small_sum, ep_steps[:-1])
    into_sum = ring_end(into_ring, "ep")
    grad_expand_out = ring_end(expand_ring, "ep")
    grad_output_out = ring_end(output_ring, "ep").T
    grad_query_out = into_sum[:, :query_size]
    grad_latent_out = into_sum[:, query_size : query_size + latent_width]
    for axis, bit in tp_steps:
        rounded = grad_latent_out.astype(bf16)
        grad_latent_out = rounded.astype(f32) + swap(rounded, axis, bit).astype(f32)
    for axis, bit in tp_steps:
        small_sum = small_sum + swap(small_sum, axis, bit)
    small_sum = small_sum.reshape(-1)
    grad_gains_out = small_sum[: at[1]].reshape(norm_gains.shape)
    grad_gain_latent_out = small_sum[at[1] : at[2]]
    grad_router_out = small_sum[at[2] : at[3]].reshape(router_weight.shape)

    return (
        block_rows.reshape(tokens, width),
        hidden_rows.reshape(tokens, width).astype(f32),
        grad_query_out,
        grad_latent_out,
        grad_expand_out,
        grad_output_out,
        grad_gains_out,
        grad_gain_latent_out,
        grad_router_out,
        grad_shared_gu_out,
        grad_shared_down_out,
        grad_expert_gate_up,
        grad_expert_down,
    )


def power_of_two(size):
    return size & (size - 1) == 0


def on_device(hidden_in, *others):
    groups, parts = lax.axis_size("ep"), lax.axis_size("tp")
    tokens = hidden_in.shape[0]
    mean_load = tokens * TOPK // (EXP_DEV * groups)
    capacity = mean_load + mean_load // 3
    if EXP_DEV * capacity >= tokens and power_of_two(groups) and power_of_two(parts):
        return on_device_dense(hidden_in, *others)
    return on_device_sparse(hidden_in, *others)


def solution(mesh):
    placed = (
        P("ep", None),
        P("ep", None),
        P("ep", "tp"),
        P("ep", None),
        P("ep", "tp"),
        P("tp", "ep"),
        P(None, "ep"),
        P("ep"),
        P("ep", None),
        P(None, "ep", "tp"),
        P("tp", "ep"),
        P("ep", None, None, "tp"),
        P("ep", "tp", None),
        P("ep", None),
    )
    return jax.shard_map(
        on_device,
        mesh=mesh,
        in_specs=placed,
        out_specs=(
            P("ep", None),
            P("ep", None),
            P("ep", "tp"),
            P("ep", None),
            P("ep", "tp"),
            P("tp", "ep"),
            P(None, "ep"),
            P("ep"),
            P("ep", None),
            P(None, "ep", "tp"),
            P("tp", "ep"),
            P("ep", None, None, "tp"),
            P("ep", "tp", None),
        ),
        check_vma=False,
    )
```
